128 devices in a mesh: section: 2 (over x_hi), dp: 32 (over x_lo, y, z), tensor: 2 (over core).
Axes of the slice: x: 4 (x_hi: 2, x_lo: 2; x = x_hi * 2 + x_lo), y: 4, z: 4, core: 2. Of those that a mesh axis runs over, the one named last changes fastest.
Arguments:
- inputs: bfloat16 [32, 2, 128, 1536], P('dp', None, 'tensor'), may hold values from -6 to 6
- out_cotangent: bfloat16 [32, 2, 128, 1536], P('dp', None, 'tensor'), may hold values from -6 to 6
- segments: int32 [32, 2, 128], P('dp'), may hold values from 0 to 2, as said below
- norm_gains: bfloat16 [2, 2, 1536], replicated, may hold values from 0.25 to 1.75
- conv_kernel: bfloat16 [3, 1536], replicated, may hold values from -3 to 3
- qk_gains: bfloat16 [2, 64], replicated, may hold values from 0.25 to 1.75
- conv_in: bfloat16 [1536, 3, 1536], P(('section', 'dp'), None, 'tensor'), may hold values from -0.15625 to 0.15625
- attn_qkv: bfloat16 [1536, 2560], P(('section', 'dp'), 'tensor'), may hold values from -0.15625 to 0.15625
- mixer_out: bfloat16 [2, 1536, 1536], P('section', 'tensor'), may hold values from -0.3125 to 0.3125
- gate_up: bfloat16 [2, 2, 1536, 6912], P('section', None, None, 'tensor'), may hold values from -0.15625 to 0.15625
- down: bfloat16 [2, 6912, 1536], P('section', 'tensor'), may hold values from -0.078125 to 0.078125
Outputs:
- activations: bfloat16 [2, 32, 2, 128, 1536], P('section', 'dp', None, 'tensor')
- input_grads: bfloat16 [2, 32, 2, 128, 1536], P('section', 'dp', None, 'tensor')
- grad_norm_gains: float32 [2, 2, 1536], replicated
- grad_conv_kernel: float32 [3, 1536], replicated
- grad_qk_gains: float32 [2, 64], replicated
- grad_conv_in: float32 [1536, 3, 1536], P(('section', 'dp'), None, 'tensor')
- grad_attn_qkv: float32 [1536, 2560], P(('section', 'dp'), 'tensor')
- grad_mixer_out: float32 [2, 1536, 1536], P('section', 'tensor', 'dp')
- grad_gate_up: float32 [2, 2, 1536, 6912], P('section', None, 'dp', 'tensor')
- grad_down: float32 [2, 6912, 1536], P('section', 'tensor', 'dp')
The draws below stay inside these ranges and needn't reach their ends.
Inputs may be any that keep to these rules, and one draw needn't show every extreme that they name: `segments`: segment numbers never fall along a sequence, and every document has 16 positions or more.
All inputs are finite; a program needn't handle non-finite values.
Results may differ from the reference program's by a relative error of at most 0.04.
Values may be sent and summed in bfloat16 or wider, within the bound.
No kernel may reach another device: no remote copies, remote signals or barrier semaphores. Data moves between devices by JAX's collectives and lax.ppermute only.
A program may use at most 448 MiB of HBM per device.

```python
import jax
import jax.numpy as jnp
from jax import lax

D = 1536
FF = 6912
HEADS = 24
KV_HEADS = 8
HEAD_DIM = 64
KW = 3
SEQ = 128
MICRO = 2
GROUPS = 32
QKV = 2560


def draw_segments(key, part):
    key = jax.random.fold_in(key, 11)
    first_key, second_key = jax.random.split(key)
    first_cut = jax.random.randint(first_key, (GROUPS, MICRO, 1), SEQ // 8, SEQ // 4)
    second_cut = jax.random.randint(second_key, (GROUPS, MICRO, 1), 3 * SEQ // 4, 7 * SEQ // 8)
    position = jnp.arange(SEQ, dtype=jnp.int32)[None, None, :]
    return (position >= first_cut).astype(jnp.int32) + (position >= second_cut).astype(jnp.int32)


def with_spikes(entries, rng, source, target, parts, factor):
    owner, partner = [(jnp.arange(entries.shape[dim]) // (entries.shape[dim] // parts)).reshape([-1 if axis == dim else 1 for axis in range(entries.ndim)]) for dim in (source, target)]
    chosen = jax.random.permutation(rng, parts)[partner]
    strong = (owner == chosen) | (owner == (partner + parts // 2) % parts)
    return jnp.where(strong, factor * entries, entries)


def shard_levels(key, shape, pieces, smallest, largest):
    def one(axis_at, parts):
        steps = jax.random.uniform(jax.random.fold_in(jax.random.fold_in(key, 6), axis_at), (parts,), jnp.float32, smallest / len(pieces), largest / len(pieces))
        return jnp.repeat(jnp.exp(steps), shape[axis_at] // parts).reshape((-1,) + (1,) * (len(shape) - axis_at - 1))

    factor_of = one(*pieces[0])
    for cut in pieces[1:]:
        factor_of = factor_of * one(*cut)
    return factor_of


def normal_values(own_key, shape, scale, bound, pieces=(), held_as=jnp.bfloat16):
    entries = scale * jax.random.normal(own_key, shape, jnp.float32)
    if pieces:
        entries = entries * shard_levels(own_key, shape, pieces, -0.22, 0.18)
    return jnp.clip(entries, -bound, bound).astype(held_as)


def bell_draw_with(stream_key, dims, width, reach, shards, heavy, kind=jnp.bfloat16):
    result = width * jax.random.normal(stream_key, dims, jnp.float32)
    if shards:
        result = result * shard_levels(stream_key, dims, shards, -0.22, 0.18)
    return jnp.clip(with_spikes(result, jax.random.fold_in(stream_key, 3), *heavy), -reach, reach).astype(kind)


def setup_inputs(seed: int = 0) -> dict:
    streams_of = jax.random.split(jax.random.key(seed), 12)
    inputs = bell_draw_with(streams_of[0], (GROUPS, MICRO, SEQ, D), 1.0, 6.0, ((0, 32), (2, 2)), (0, 3, 32, 2.75))
    out_cotangent = bell_draw_with(streams_of[1], (GROUPS, MICRO, SEQ, D), 1.0, 6.0, ((0, 32), (2, 2)), (0, 3, 32, 2.75))
    segments = draw_segments(jax.random.fold_in(streams_of[11], 71), 0)
    norm_gains = jnp.clip(1.0 + 0.15 * jax.random.normal(streams_of[3], (2, 2, D), jnp.float32), 0.25, 1.75).astype(jnp.bfloat16)
    conv_kernel = normal_values(streams_of[4], (KW, D), 0.5, 3.0)
    qk_gains = jnp.clip(1.0 + 0.15 * jax.random.normal(streams_of[5], (2, HEAD_DIM), jnp.float32), 0.25, 1.75).astype(jnp.bfloat16)
    conv_in = normal_values(streams_of[6], (D, 3, D), D ** -0.5, 0.15625, ((0, 64), (2, 2)))
    attn_qkv = normal_values(streams_of[7], (D, QKV), D ** -0.5, 0.15625, ((0, 64), (1, 2)))
    mixer_out = normal_values(streams_of[8], (2, D, D), (D // 4) ** -0.5, 0.3125, ((0, 2), (1, 2)))
    gate_up = normal_values(streams_of[9], (2, 2, D, FF), D ** -0.5, 0.15625, ((0, 2), (3, 2)))
    down = normal_values(streams_of[10], (2, FF, D), FF ** -0.5, 0.078125, ((0, 2), (1, 2)))
    return {"inputs": inputs, "out_cotangent": out_cotangent, "segments": segments, "norm_gains": norm_gains, "conv_kernel": conv_kernel, "qk_gains": qk_gains, "conv_in": conv_in, "attn_qkv": attn_qkv, "mixer_out": mixer_out, "gate_up": gate_up, "down": down}


@jax.custom_vjp
def low(v):
    return lax.optimization_barrier(v.astype(jnp.bfloat16)).astype(jnp.float32)

@jax.custom_vjp
def low_back(v):
    return v

def low_keep(v):
    return (low(v), None)

def low_pass(kept, grad):
    return (grad,)

def back_keep(v):
    return (v, None)

def back_low(kept, grad):
    return (low(grad),)
low.defvjp(low_keep, low_pass)
low_back.defvjp(back_keep, back_low)
EPSILON = 1e-05
ROPE_BASE = 1000000.0
MASKED_SCORE = -1e+30
PRECISE = lax.Precision.HIGHEST

def product(left, right):
    return jnp.dot(left, right, precision=PRECISE)

def normalize(values):
    return values * lax.rsqrt(lax.optimization_barrier(jnp.mean(values * values, axis=-1, keepdims=True)) + EPSILON)

def shift_rows(values, offset):
    return jnp.concatenate([jnp.zeros((offset, values.shape[1]), values.dtype), values[:-offset]], axis=0)

def conv_gate(projected, kernel, segment_ids):
    channels = kernel.shape[1]
    taps = kernel.shape[0]
    gate_before = projected[:, :channels]
    gate_after = projected[:, channels:2 * channels]
    signal = projected[:, 2 * channels:]
    mixed = gate_before * signal
    total = kernel[taps - 1] * mixed
    for offset in range(1, taps):
        same_doc = (segment_ids[offset:] == segment_ids[:-offset]).astype(mixed.dtype)
        same_doc = jnp.concatenate([jnp.zeros((offset,), mixed.dtype), same_doc])
        total = total + kernel[taps - 1 - offset] * shift_rows(mixed, offset) * same_doc[:, None]
    return gate_after * total

def rotary_tables(length, head_size):
    half_size = head_size // 2
    exponent = jnp.arange(half_size, dtype=jnp.float32) * (2.0 / head_size)
    frequency = jnp.exp(-exponent * jnp.log(ROPE_BASE))
    angles = jnp.arange(length, dtype=jnp.float32)[:, None] * frequency[None, :]
    return (jnp.cos(angles), jnp.sin(angles))

def rotate(values, cosine_table, sine_table):
    half_size = values.shape[-1] // 2
    first_half = values[..., :half_size]
    second_half = values[..., half_size:]
    shape_out = (cosine_table.shape[0],) + (1,) * (values.ndim - 2) + (half_size,)
    cosine_table = cosine_table.reshape(shape_out)
    sine_table = sine_table.reshape(shape_out)
    return jnp.concatenate([first_half * cosine_table - second_half * sine_table, second_half * cosine_table + first_half * sine_table], axis=-1)

def prepare_heads(head_inputs, head_gains):
    length = head_inputs.shape[0]
    group_size = HEADS // KV_HEADS
    key_heads = head_inputs.shape[1] // ((group_size + 2) * HEAD_DIM)
    grouped = head_inputs.reshape(length, key_heads, group_size + 2, HEAD_DIM)
    cosine_table, sine_table = rotary_tables(length, HEAD_DIM)
    queries = rotate(normalize(grouped[:, :, :group_size]) * head_gains[0], cosine_table, sine_table)
    keys_out = rotate(normalize(grouped[:, :, group_size]) * head_gains[1], cosine_table, sine_table)
    return (queries, keys_out, grouped[:, :, group_size + 1])

def attention_mix(normed, weight_qkv, head_gains, weight_out, segment_ids):
    length = normed.shape[0]
    head_inputs = low_back(product(normed, weight_qkv))
    queries, keys_out, values_out = prepare_heads(head_inputs, head_gains)
    queries = low(queries)
    keys_out = low(keys_out)
    values_out = low(values_out)
    scores = jnp.einsum('tgjd,sgd->gjts', queries, keys_out, precision=PRECISE) * HEAD_DIM ** (-0.5)
    scores = low_back(scores)
    position = jnp.arange(length)
    allowed = (position[:, None] >= position[None, :]) & (segment_ids[:, None] == segment_ids[None, :])
    scores = jnp.where(allowed, scores, MASKED_SCORE)
    row_max = lax.optimization_barrier(jnp.max(scores, axis=-1, keepdims=True))
    exponent_terms = jnp.exp(scores - row_max)
    weights = exponent_terms / lax.optimization_barrier(jnp.sum(exponent_terms, axis=-1, keepdims=True))
    attended = jnp.einsum('gjts,sgd->tgjd', low(weights), values_out, precision=PRECISE)
    attended = low_back(low(attended.reshape(length, -1)))
    return low_back(product(attended, weight_out))

def conv_mix(normed, weight_in, kernel, weight_out, segment_ids):
    projected = low_back(product(normed, weight_in.reshape(weight_in.shape[0], -1)))
    gated = low(conv_gate(projected, kernel, segment_ids))
    return low_back(product(gated, weight_out))

def layer(layer_in, norm_scale, mixer, weight_pair, weight_down):
    normed = low(normalize(layer_in) * norm_scale[0])
    hidden = layer_in + mixer(normed)
    inner = low(normalize(hidden) * norm_scale[1])
    gate_value = low_back(product(inner, weight_pair[0]))
    up_value = low_back(product(inner, weight_pair[1]))
    active = low(jax.nn.silu(gate_value) * up_value)
    return hidden + low_back(product(active, weight_down))

def conv_section(params, layer_in, segment_ids):
    norm_scale, kernel, weight_in, weight_out, weight_pair, weight_down = params
    return layer(layer_in, norm_scale, lambda normed: conv_mix(normed, weight_in, kernel, weight_out, segment_ids), weight_pair, weight_down)

def attention_section(params, layer_in, segment_ids):
    norm_scale, head_gains, weight_qkv, weight_out, weight_pair, weight_down = params
    return layer(low_back(layer_in), norm_scale, lambda normed: attention_mix(normed, weight_qkv, head_gains, weight_out, segment_ids), weight_pair, weight_down)

def reference(inputs, out_cotangent, segments, norm_gains, conv_kernel, qk_gains, conv_in, attn_qkv, mixer_out, gate_up, down):

    def to_float(values):
        return values.astype(jnp.float32)
    first_params = (to_float(norm_gains[0]), to_float(conv_kernel), to_float(conv_in), to_float(mixer_out[0]), to_float(gate_up[0]), to_float(down[0]))
    second_params = (to_float(norm_gains[1]), to_float(qk_gains), to_float(attn_qkv), to_float(mixer_out[1]), to_float(gate_up[1]), to_float(down[1]))
    sequences = GROUPS * MICRO
    flat_inputs = inputs.reshape(sequences, SEQ, D)
    flat_cotangent = out_cotangent.reshape(sequences, SEQ, D)
    flat_segments = segments.reshape(sequences, SEQ)

    def one_sequence(totals, sequence_item):
        first_total, second_total = totals
        sequence_in, sequence_cotangent, segment_ids = sequence_item
        first_out, first_back = jax.vjp(lambda params, layer_in: conv_section(params, layer_in, segment_ids), first_params, to_float(sequence_in))
        middle = low(first_out)
        second_out, second_back = jax.vjp(lambda params, layer_in: attention_section(params, layer_in, segment_ids), second_params, middle)
        second_grads, middle_grad = second_back(to_float(sequence_cotangent))
        first_grads, input_grad = first_back(middle_grad)
        first_total = jax.tree.map(jnp.add, first_total, first_grads)
        second_total = jax.tree.map(jnp.add, second_total, second_grads)
        per_sequence = (middle.astype(jnp.bfloat16), second_out.astype(jnp.bfloat16), input_grad.astype(jnp.bfloat16), middle_grad.astype(jnp.bfloat16))
        return ((first_total, second_total), per_sequence)
    zeros_init = (jax.tree.map(jnp.zeros_like, first_params), jax.tree.map(jnp.zeros_like, second_params))
    totals, per_sequence = lax.scan(one_sequence, zeros_init, (flat_inputs, flat_cotangent, flat_segments))
    first_total, second_total = totals
    middle_rows, final_rows, input_rows, middle_grad_rows = per_sequence
    shape_out = (GROUPS, MICRO, SEQ, D)
    activations = jnp.stack([middle_rows.reshape(shape_out), final_rows.reshape(shape_out)])
    input_grads = jnp.stack([input_rows.reshape(shape_out), middle_grad_rows.reshape(shape_out)])
    return (activations, input_grads, jnp.stack([first_total[0], second_total[0]]), first_total[1], second_total[1], first_total[2], second_total[2], jnp.stack([first_total[3], second_total[3]]), jnp.stack([first_total[4], second_total[4]]), jnp.stack([first_total[5], second_total[5]]))
```

```python
import jax
import jax.numpy as jnp
from jax import lax
from jax.sharding import Mesh
from jax.sharding import PartitionSpec as P

HEADS = 24
KV_HEADS = 8
HEAD_DIM = 64
GROUP = HEADS // KV_HEADS

EPSILON = 1e-05
ROPE_BASE = 1000000.0
MASKED_SCORE = -1e30

F32 = jnp.float32
BF16 = jnp.bfloat16

PLANE = ("y", "z")
AXES = ("xh", "xl", "y", "z", "c")


def product(left, right):
    return jnp.dot(left, right, preferred_element_type=F32)


def product_left(left, right):
    return lax.dot_general(left, right, (((0,), (0,)), ((), ())), preferred_element_type=F32)


def product_right(left, right):
    return lax.dot_general(left, right, (((1,), (1,)), ((), ())), preferred_element_type=F32)


def swapped(shard, axis):
    return lax.ppermute(shard, axis, [(0, 1), (1, 0)])


def spread(own):
    micro, half, width = own.shape
    return lax.all_gather(own, "c", axis=1, tiled=True).reshape(micro * 2 * half, width)


def halves(full, core):
    tiles = full.reshape(2, 2, -1, full.shape[-1])
    mine = lax.dynamic_index_in_dim(tiles, core, 1, keepdims=False)
    other = lax.dynamic_index_in_dim(tiles, 1 - core, 1, keepdims=False)
    return mine, other


def collect(partial, core):
    mine, other = halves(partial, core)
    return mine + swapped(other.astype(BF16), "c").astype(F32)


def mean_last(values):
    return jnp.mean(values, axis=-1, keepdims=True)


def inverse_rms(values):
    return lax.rsqrt(mean_last(values * values) + EPSILON)


def normalize(values):
    return values * inverse_rms(values)


def norm_backward(grad, gain, values):
    inverse = inverse_rms(values)
    normed = values * inverse
    scaled = grad * gain
    grad_gain = jnp.sum(grad * normed, axis=(0, 1))
    return inverse * (scaled - normed * mean_last(scaled * normed)), grad_gain


def shift_rows(values, offset):
    pad = jnp.zeros((values.shape[0], offset, values.shape[2]), values.dtype)
    return jnp.concatenate([pad, values[:, :-offset]], axis=1)


def conv_gate(projected, kernel, segments):
    channels = kernel.shape[1]
    taps = kernel.shape[0]
    gate_before = projected[..., :channels]
    gate_after = projected[..., channels : 2 * channels]
    signal = projected[..., 2 * channels :]
    mixed = gate_before * signal
    total = kernel[taps - 1] * mixed
    for offset in range(1, taps):
        same = (segments[:, offset:] == segments[:, :-offset]).astype(mixed.dtype)
        same = jnp.pad(same, ((0, 0), (offset, 0)))
        total = total + kernel[taps - 1 - offset] * shift_rows(mixed, offset) * same[..., None]
    return gate_after * total


def rotary_tables(length):
    half = HEAD_DIM // 2
    exponent = jnp.arange(half, dtype=F32) * (2.0 / HEAD_DIM)
    frequency = jnp.exp(-exponent * jnp.log(ROPE_BASE))
    angles = jnp.arange(length, dtype=F32)[:, None] * frequency[None, :]
    return (jnp.cos(angles), jnp.sin(angles))


def rotate(values, cosine, sine):
    half = values.shape[-1] // 2
    first, second = values[..., :half], values[..., half:]
    shape = (1, cosine.shape[0]) + (1,) * (values.ndim - 3) + (half,)
    cosine, sine = cosine.reshape(shape), sine.reshape(shape)
    return jnp.concatenate([first * cosine - second * sine, second * cosine + first * sine], axis=-1)


def prepare_heads(head_inputs, head_gains):
    micro, length, width = head_inputs.shape
    key_heads = width // ((GROUP + 2) * HEAD_DIM)
    grouped = head_inputs.reshape(micro, length, key_heads, GROUP + 2, HEAD_DIM)
    cosine, sine = rotary_tables(length)
    queries = rotate(normalize(grouped[:, :, :, :GROUP]) * head_gains[0], cosine, sine)
    keys = rotate(normalize(grouped[:, :, :, GROUP]) * head_gains[1], cosine, sine)
    return (queries, keys, grouped[:, :, :, GROUP + 1])


def einsum(spec, left, right):
    return jnp.einsum(spec, left, right, preferred_element_type=F32)


def attention_forward(head_inputs, head_gains, segments):
    micro, length, _ = head_inputs.shape
    queries, keys, values = [a.astype(BF16) for a in prepare_heads(head_inputs, head_gains)]
    scores = einsum("mtgjd,msgd->mgjts", queries, keys) * HEAD_DIM ** (-0.5)
    position = jnp.arange(length)
    allowed = (position[:, None] >= position[None, :]) & (
        segments[:, :, None] == segments[:, None, :]
    )
    scores = jnp.where(allowed[:, None, None], scores, MASKED_SCORE)
    terms = jnp.exp(scores - jnp.max(scores, axis=-1, keepdims=True))
    weights = terms / jnp.sum(terms, axis=-1, keepdims=True)
    attended = einsum("mgjts,msgd->mtgjd", weights.astype(BF16), values)
    return attended.reshape(micro, length, -1).astype(BF16), (queries, keys, values, weights)


def attention_backward(grad_attended, saved, head_inputs, head_gains):
    queries, keys, values, weights = saved
    grad_low = grad_attended.reshape(queries.shape).astype(BF16)
    grad_values = einsum("mgjts,mtgjd->msgd", weights.astype(BF16), grad_low)
    grad_weights = einsum("mtgjd,msgd->mgjts", grad_low, values)
    grad_scores = (
        weights * (grad_weights - jnp.sum(grad_weights * weights, axis=-1, keepdims=True))
    ).astype(BF16)
    scale = HEAD_DIM ** (-0.5)
    grad_queries = einsum("mgjts,msgd->mtgjd", grad_scores, keys) * scale
    grad_keys = einsum("mgjts,mtgjd->msgd", grad_scores, queries) * scale
    rebuild = jax.vjp(prepare_heads, head_inputs, head_gains)[1]
    return rebuild((grad_queries, grad_keys, grad_values))


def ffn_forward(inner, weight_gate, weight_up):
    gate = product(inner, weight_gate)
    up = product(inner, weight_up)
    return gate, up, (jax.nn.silu(gate) * up).astype(BF16)


def ffn_grads(grad_active, gate, up):
    sigmoid = jax.nn.sigmoid(gate)
    grad_gate = grad_active * up * sigmoid * (1.0 + gate * (1.0 - sigmoid))
    grad_up = grad_active * gate * sigmoid
    return grad_gate.astype(BF16), grad_up.astype(BF16)


def local(
    inputs,
    out_cotangent,
    segments,
    norm_gains,
    conv_kernel,
    qk_gains,
    conv_in,
    attn_qkv,
    mixer_out,
    gate_up,
    down,
):
    section = lax.axis_index("xh")
    first = section == 0
    core = lax.axis_index("c")
    place = lax.axis_index("y") * 4 + lax.axis_index("z")
    xl = lax.axis_index("xl")
    plane = lax.axis_size("y") * lax.axis_size("z")

    inputs, out_cotangent, segments = inputs[0], out_cotangent[0], segments[0]
    micro, half, width = inputs.shape
    length = 2 * half
    rows = micro * length
    channels = conv_in.shape[2]
    kernel = lax.dynamic_slice_in_dim(conv_kernel, core * channels, channels, 1).astype(F32)
    gains = lax.dynamic_index_in_dim(norm_gains, section, 0, keepdims=False).astype(F32)
    head_gains = qk_gains.astype(F32)
    weight_out, weight_gate, weight_up, weight_down = (
        mixer_out[0],
        gate_up[0, 0],
        gate_up[0, 1],
        down[0],
    )
    hidden_units = weight_down.shape[0]
    part = hidden_units // plane

    in_width = 3 * channels
    qkv_width = attn_qkv.shape[1]
    both = jnp.concatenate([conv_in.reshape(-1, in_width), attn_qkv], axis=1)
    whole = lax.all_gather(both, ("xh", "xl", "y", "z"), axis=0, tiled=True)
    weight_in, weight_qkv = whole[:, :in_width], whole[:, in_width:]

    part_gate = lax.dynamic_slice_in_dim(weight_gate, place * part, part, 1)
    part_up = lax.dynamic_slice_in_dim(weight_up, place * part, part, 1)
    part_down = lax.dynamic_slice_in_dim(weight_down, place * part, part, 0)

    def feed_forward(hidden):
        inner_own = (normalize(hidden) * gains[1]).astype(BF16)
        inner = spread(inner_own)
        gate, up, active = ffn_forward(inner, weight_gate, weight_up)
        return hidden + collect(product(active, weight_down), core), (inner_own, gate, up)

    def feed_forward_back(grad_low, grad, hidden, saved):
        _, gate, up = saved
        grad_active = product_right(spread(grad_low), weight_down)
        grad_gate, grad_up = ffn_grads(grad_active, gate, up)
        partial = product_right(grad_gate, weight_gate) + product_right(grad_up, weight_up)
        back, grad_gain = norm_backward(collect(partial, core), gains[1], hidden)
        grad_hidden = grad + back
        return grad_hidden, grad_gain

    def mixer_back(grad_hidden, grad_proj, weight, layer_in):
        partial = product_right(grad_proj, weight)
        back, grad_gain = norm_backward(collect(partial, core), gains[0], layer_in)
        return (grad_hidden + back).astype(BF16), grad_gain

    first_in = inputs.astype(F32)
    normed_own_0 = (normalize(first_in) * gains[0]).astype(BF16)
    projected = product(spread(normed_own_0), weight_in).reshape(micro, length, in_width)
    gated_0 = conv_gate(projected, kernel, segments).astype(BF16).reshape(rows, -1)
    hidden_0 = first_in + collect(product(gated_0, weight_out), core)
    result_0, ffn_0 = feed_forward(hidden_0)
    result_0 = result_0.astype(BF16)

    received = lax.ppermute(result_0, "xh", [(0, 1)])
    second_in = received.astype(F32)
    normed_own_1 = (normalize(second_in) * gains[0]).astype(BF16)
    head_inputs = product(spread(normed_own_1), weight_qkv).reshape(micro, length, qkv_width)
    gated_1, kept = attention_forward(head_inputs, head_gains, segments)
    gated_1 = gated_1.reshape(rows, -1)
    hidden_1 = second_in + collect(product(gated_1, weight_out), core)
    result_1, ffn_1 = feed_forward(hidden_1)
    result_1 = result_1.astype(BF16)

    def chosen(from_first, from_second):
        return jnp.where(first, from_first, from_second)

    def over_plane(own):
        return lax.all_gather(own, ("y", "z", "c")).reshape(-1, width)

    inner_all = over_plane(chosen(ffn_0[0], ffn_1[0]))
    normed_all = over_plane(chosen(normed_own_0, normed_own_1))
    gated = chosen(gated_0, gated_1)
    gated_all = lax.all_gather(gated, PLANE).reshape(plane * rows, -1)
    part_gates = ffn_forward(inner_all, part_gate, part_up)

    grad_hidden_1, gain_inner_1 = feed_forward_back(
        out_cotangent, out_cotangent.astype(F32), hidden_1, ffn_1
    )
    grad_mix_1 = spread(grad_hidden_1.astype(BF16))
    grad_gated_1 = product_right(grad_mix_1, weight_out).reshape(micro, length, -1)
    grad_heads_in, grad_head_gains = attention_backward(grad_gated_1, kept, head_inputs, head_gains)
    grad_proj_1 = grad_heads_in.astype(BF16).reshape(rows, -1)
    input_grad_1, gain_outer_1 = mixer_back(grad_hidden_1, grad_proj_1, weight_qkv, second_in)

    cotangent = lax.ppermute(input_grad_1, "xh", [(1, 0)])
    grad_all = over_plane(chosen(cotangent, out_cotangent))
    grad_hidden_0, gain_inner_0 = feed_forward_back(
        cotangent, cotangent.astype(F32), hidden_0, ffn_0
    )
    grad_mix_0 = spread(grad_hidden_0.astype(BF16))
    grad_gated_0 = product_right(grad_mix_0, weight_out).reshape(micro, length, -1)
    rebuild = jax.vjp(lambda p, k: conv_gate(p, k, segments), projected, kernel)[1]
    grad_projected, grad_kernel = rebuild(grad_gated_0)
    grad_proj_0 = grad_projected.astype(BF16).reshape(rows, -1)
    input_grad_0, gain_outer_0 = mixer_back(grad_hidden_0, grad_proj_0, weight_in, first_in)

    def from_plane(tiles):
        return lax.all_to_all(tiles, PLANE, 0, 0, tiled=True)

    def by_core(full):
        tiles = full.reshape(micro, 2, half, -1)
        return jnp.swapaxes(tiles, 0, 1).reshape(rows, -1)

    gate_all, up_all, active_all = part_gates
    grad_active_all = product_right(grad_all, part_down)
    grad_gate_all, grad_up_all = ffn_grads(grad_active_all, gate_all, up_all)
    parts = jnp.stack(
        [
            product_left(inner_all, grad_gate_all),
            product_left(inner_all, grad_up_all),
            product_left(grad_all, active_all),
        ]
    ).reshape(3, 2, plane, width // (2 * plane), part)

    def summed_over_pair(tiles, dim):
        mine = lax.dynamic_index_in_dim(tiles, xl, dim, keepdims=False)
        other = lax.dynamic_index_in_dim(tiles, 1 - xl, dim, keepdims=False)
        return mine + swapped(other.astype(BF16), "xl").astype(F32)

    mine = summed_over_pair(parts, 1).astype(BF16)
    arrived = from_plane(jnp.moveaxis(mine, 1, 0))
    lines = jnp.moveaxis(arrived, 0, 2).reshape(3, width // (2 * plane), hidden_units).astype(F32)
    grad_gate_up = lines[:2][None]
    grad_down = lines[2].T[None]

    grad_mix = by_core(chosen(grad_mix_0, grad_mix_1))
    tiles = grad_mix.reshape(rows, 2, plane, -1)
    columns = from_plane(jnp.moveaxis(tiles, 2, 0)).reshape(plane * rows, -1)
    gated_rows = gated_all.reshape(plane, micro, 2, half, -1)
    gated_rows = jnp.swapaxes(gated_rows, 1, 2).reshape(plane * rows, -1)
    out_parts = product_left(columns, gated_rows).reshape(2, -1, channels)
    grad_mixer_out = summed_over_pair(out_parts, 0).T[None]

    spare = in_width - qkv_width
    grad_proj = chosen(grad_proj_0, jnp.pad(grad_proj_1, ((0, 0), (0, spare))))
    tiles = jnp.moveaxis(by_core(grad_proj).reshape(rows, plane, -1), 1, 0)
    columns = from_plane(tiles).reshape(plane * rows, -1)
    in_parts = product_left(normed_all, columns)
    in_parts = in_parts.reshape(2, 2, plane, -1, in_width // plane)
    mine = summed_over_pair(in_parts, 1).astype(BF16)
    arrived = from_plane(jnp.moveaxis(mine, 1, 0))
    lines = jnp.moveaxis(arrived, 0, 2).reshape(2, -1, in_width)
    kept_lines = lax.dynamic_index_in_dim(lines, section, 0, keepdims=False)
    sent_lines = lax.dynamic_index_in_dim(lines, 1 - section, 0, keepdims=False)
    come = swapped(sent_lines, "xh")
    grad_conv_in = chosen(kept_lines, come).astype(F32).reshape(conv_in.shape)
    grad_attn_qkv = chosen(come, kept_lines)[:, :qkv_width].astype(F32)

    full_kernel = lax.dynamic_update_slice(
        jnp.zeros(conv_kernel.shape, F32), grad_kernel, (0, core * channels)
    )
    small = jnp.concatenate(
        [
            chosen(gain_outer_0, gain_outer_1),
            chosen(gain_inner_0, gain_inner_1),
            full_kernel.reshape(-1),
            grad_head_gains.reshape(-1),
        ]
    )
    count = small.shape[0]
    small = jnp.pad(small, (0, -count % 1024)).reshape(-1, 128)
    small = lax.all_gather(small, "c").sum(0)
    small = small + swapped(small, "xl")
    for axis in PLANE:
        copies = jnp.broadcast_to(small, (4, *small.shape))
        small = lax.all_to_all(copies, axis, 0, 0, tiled=True).sum(0)
    come = swapped(small, "xh")
    pair = [chosen(small, come).reshape(-1), chosen(come, small).reshape(-1)]
    grad_norm_gains = jnp.stack([a[: 2 * width].reshape(2, width) for a in pair])
    grad_conv_kernel = pair[0][2 * width : 5 * width].reshape(conv_kernel.shape)
    grad_qk_gains = pair[1][5 * width : count].reshape(qk_gains.shape)

    activations = chosen(result_0, result_1)[None, None]
    input_grads = chosen(input_grad_0, input_grad_1)[None, None]
    return (
        activations,
        input_grads,
        grad_norm_gains,
        grad_conv_kernel,
        grad_qk_gains,
        grad_conv_in,
        grad_attn_qkv,
        grad_mixer_out,
        grad_gate_up,
        grad_down,
    )


def solution(mesh):
    wide = Mesh(mesh.devices.reshape(2, 2, 4, 4, 2), AXES)
    dp = ("xl", "y", "z")
    everyone = ("xh", "xl", "y", "z")
    in_specs = (
        P(dp, None, "c", None),
        P(dp, None, "c", None),
        P(dp, None, None),
        P(),
        P(),
        P(),
        P(everyone, None, "c"),
        P(everyone, "c"),
        P("xh", "c", None),
        P("xh", None, None, "c"),
        P("xh", "c", None),
    )
    out_specs = (
        P("xh", dp, None, "c", None),
        P("xh", dp, None, "c", None),
        P(),
        P(),
        P(),
        P(everyone, None, "c"),
        P(everyone, "c"),
        P("xh", "c", dp),
        P("xh", None, dp, "c"),
        P("xh", "c", dp),
    )
    return jax.shard_map(local, mesh=wide, in_specs=in_specs, out_specs=out_specs, check_vma=False)
```

```python
import functools

import jax
import jax.numpy as jnp
from jax import lax
from jax.experimental import pallas as pl
from jax.experimental.pallas import tpu as pltpu
from jax.sharding import Mesh
from jax.sharding import PartitionSpec as P

HEADS = 24
KV_HEADS = 8
HEAD_DIM = 64
GROUP = HEADS // KV_HEADS

EPSILON = 1e-05
ROPE_BASE = 1000000.0
MASKED_SCORE = -1e30

F32 = jnp.float32
BF16 = jnp.bfloat16

PLANE = ("y", "z")
AXES = ("xh", "xl", "y", "z", "c")


def product(left, right):
    return jnp.dot(left, right, preferred_element_type=F32)


def product_left(left, right):
    return lax.dot_general(left, right, (((0,), (0,)), ((), ())), preferred_element_type=F32)


def product_right(left, right):
    return lax.dot_general(left, right, (((1,), (1,)), ((), ())), preferred_element_type=F32)


def swapped(shard, axis):
    return lax.ppermute(shard, axis, [(0, 1), (1, 0)])


def spread(own):
    micro, half, width = own.shape
    return lax.all_gather(own, "c", axis=1, tiled=True).reshape(micro * 2 * half, width)


def halves(full, core):
    tiles = full.reshape(2, 2, -1, full.shape[-1])
    mine = lax.dynamic_index_in_dim(tiles, core, 1, keepdims=False)
    other = lax.dynamic_index_in_dim(tiles, 1 - core, 1, keepdims=False)
    return mine, other


def joined(mine, other):
    return mine + swapped(other, "c").astype(F32)


def collect(partial, core):
    mine, other = halves(partial, core)
    return joined(mine, other.astype(BF16))


def mean_last(values):
    return jnp.mean(values, axis=-1, keepdims=True)


def inverse_rms(values):
    return lax.rsqrt(mean_last(values * values) + EPSILON)


def normalize(values):
    return values * inverse_rms(values)


def norm_backward(grad, gain, values):
    inverse = inverse_rms(values)
    normed = values * inverse
    scaled = grad * gain
    grad_gain = jnp.sum(grad * normed, axis=(0, 1))
    return inverse * (scaled - normed * mean_last(scaled * normed)), grad_gain


def shift_rows(values, offset):
    pad = jnp.zeros((values.shape[0], offset, values.shape[2]), values.dtype)
    return jnp.concatenate([pad, values[:, :-offset]], axis=1)


def conv_gate(projected, kernel, segments):
    channels = kernel.shape[1]
    taps = kernel.shape[0]
    gate_before = projected[..., :channels]
    gate_after = projected[..., channels : 2 * channels]
    signal = projected[..., 2 * channels :]
    mixed = gate_before * signal
    total = kernel[taps - 1] * mixed
    for offset in range(1, taps):
        same = (segments[:, offset:] == segments[:, :-offset]).astype(mixed.dtype)
        same = jnp.pad(same, ((0, 0), (offset, 0)))
        total = total + kernel[taps - 1 - offset] * shift_rows(mixed, offset) * same[..., None]
    return gate_after * total


def rotary_tables(length):
    half = HEAD_DIM // 2
    exponent = jnp.arange(half, dtype=F32) * (2.0 / HEAD_DIM)
    frequency = jnp.exp(-exponent * jnp.log(ROPE_BASE))
    angles = jnp.arange(length, dtype=F32)[:, None] * frequency[None, :]
    return (jnp.cos(angles), jnp.sin(angles))


def rotate(values, cosine, sine):
    half = values.shape[-1] // 2
    first, second = values[..., :half], values[..., half:]
    shape = (1, cosine.shape[0]) + (1,) * (values.ndim - 3) + (half,)
    cosine, sine = cosine.reshape(shape), sine.reshape(shape)
    return jnp.concatenate([first * cosine - second * sine, second * cosine + first * sine], axis=-1)


def prepare_heads(head_inputs, head_gains):
    micro, length, width = head_inputs.shape
    key_heads = width // ((GROUP + 2) * HEAD_DIM)
    grouped = head_inputs.reshape(micro, length, key_heads, GROUP + 2, HEAD_DIM)
    cosine, sine = rotary_tables(length)
    queries = rotate(normalize(grouped[:, :, :, :GROUP]) * head_gains[0], cosine, sine)
    keys = rotate(normalize(grouped[:, :, :, GROUP]) * head_gains[1], cosine, sine)
    return (queries, keys, grouped[:, :, :, GROUP + 1])


def einsum(spec, left, right):
    return jnp.einsum(spec, left, right, preferred_element_type=F32)


def attention_forward(head_inputs, head_gains, segments):
    micro, length, _ = head_inputs.shape
    queries, keys, values = [a.astype(BF16) for a in prepare_heads(head_inputs, head_gains)]
    scores = einsum("mtgjd,msgd->mgjts", queries, keys) * HEAD_DIM ** (-0.5)
    position = jnp.arange(length)
    allowed = (position[:, None] >= position[None, :]) & (
        segments[:, :, None] == segments[:, None, :]
    )
    scores = jnp.where(allowed[:, None, None], scores, MASKED_SCORE)
    terms = jnp.exp(scores - jnp.max(scores, axis=-1, keepdims=True))
    weights = terms / jnp.sum(terms, axis=-1, keepdims=True)
    attended = einsum("mgjts,msgd->mtgjd", weights.astype(BF16), values)
    return attended.reshape(micro, length, -1).astype(BF16), (queries, keys, values, weights)


def attention_backward(grad_attended, saved, head_inputs, head_gains):
    queries, keys, values, weights = saved
    grad_low = grad_attended.reshape(queries.shape).astype(BF16)
    grad_values = einsum("mgjts,mtgjd->msgd", weights.astype(BF16), grad_low)
    grad_weights = einsum("mtgjd,msgd->mgjts", grad_low, values)
    grad_scores = (
        weights * (grad_weights - jnp.sum(grad_weights * weights, axis=-1, keepdims=True))
    ).astype(BF16)
    scale = HEAD_DIM ** (-0.5)
    grad_queries = einsum("mgjts,msgd->mtgjd", grad_scores, keys) * scale
    grad_keys = einsum("mgjts,mtgjd->msgd", grad_scores, queries) * scale
    rebuild = jax.vjp(prepare_heads, head_inputs, head_gains)[1]
    return rebuild((grad_queries, grad_keys, grad_values))


def ffn_grads(grad_active, gate, up):
    sigmoid = jax.nn.sigmoid(gate)
    grad_gate = grad_active * up * sigmoid * (1.0 + gate * (1.0 - sigmoid))
    grad_up = grad_active * gate * sigmoid
    return grad_gate.astype(BF16), grad_up.astype(BF16)


VMEM_LIMIT = 56 * 1024 * 1024


def halves_out(acc_ref, core, mine_ref, other_ref):
    micro, half, _ = mine_ref.shape
    for m in range(micro):
        start = m * 2 * half
        mine_ref[m] = acc_ref[pl.ds(pl.multiple_of(start + core * half, half), half)]
        rest = acc_ref[pl.ds(pl.multiple_of(start + (1 - core) * half, half), half)]
        other_ref[m] = rest.astype(BF16)


def unit_tiles(units, tile):
    short = units % tile
    tiles = [(0, short)] if short else []
    return tiles + [(at, tile) for at in range(short, units, tile)]


def streamed(tiles, copies, work):
    for copy in copies(0, 0):
        copy.start()
    for k in range(len(tiles)):
        slot = k % 2
        if k + 1 < len(tiles):
            for copy in copies(k + 1, 1 - slot):
                copy.start()
        for copy in copies(k, slot):
            copy.wait()
        work(k, slot)


def ffn_forward_kernel(
    tiles, core_ref, rows_ref, pair_ref, down_ref, gate_ref, up_ref, mine_ref, other_ref,
    pair_buf, down_buf, gate_buf, up_buf, acc_ref, sems, out_sems,
):
    def copies(k, slot):
        at, size = tiles[k]
        return [
            pltpu.make_async_copy(
                pair_ref.at[0, :, pl.ds(at, size)],
                pair_buf.at[slot, :, pl.ds(0, size)],
                sems.at[slot, 0],
            ),
            pltpu.make_async_copy(
                pair_ref.at[1, :, pl.ds(at, size)],
                pair_buf.at[slot, :, pl.ds(size, size)],
                sems.at[slot, 1],
            ),
            pltpu.make_async_copy(
                down_ref.at[pl.ds(at, size)], down_buf.at[slot, pl.ds(0, size)], sems.at[slot, 2]
            ),
        ]

    def kept(k):
        here = (slice(None), pl.ds(*tiles[k]))
        return [
            pltpu.make_async_copy(gate_buf.at[here], gate_ref.at[here], out_sems.at[k, 0]),
            pltpu.make_async_copy(up_buf.at[here], up_ref.at[here], out_sems.at[k, 1]),
        ]

    def work(k, slot):
        at, size = tiles[k]
        both = product(rows_ref[...], pair_buf[slot, :, : 2 * size])
        gate, up = both[:, :size], both[:, size:]
        gate_buf[:, at : at + size] = gate.astype(BF16)
        up_buf[:, at : at + size] = up.astype(BF16)
        for copy in kept(k):
            copy.start()
        active = (gate * jax.nn.sigmoid(gate) * up).astype(BF16)
        part = product(active, down_buf[slot, :size])
        if k == 0:
            acc_ref[...] = part
        else:
            acc_ref[...] += part

    streamed(tiles, copies, work)
    halves_out(acc_ref, core_ref[0], mine_ref, other_ref)
    for k in range(len(tiles)):
        for copy in kept(k):
            copy.wait()


def ffn_backward_kernel(
    tiles, core_ref, rows_ref, gate_ref, up_ref, pair_ref, down_ref, mine_ref, other_ref,
    pair_buf, down_buf, gate_buf, up_buf, acc_ref, sems,
):
    def copies(k, slot):
        at, size = tiles[k]
        columns, place = pl.ds(at, size), pl.ds(0, size)
        return [
            pltpu.make_async_copy(
                down_ref.at[columns], down_buf.at[slot, place], sems.at[slot, 0]
            ),
            pltpu.make_async_copy(
                gate_ref.at[:, columns], gate_buf.at[slot, :, place], sems.at[slot, 1]
            ),
            pltpu.make_async_copy(
                up_ref.at[:, columns], up_buf.at[slot, :, place], sems.at[slot, 2]
            ),
            pltpu.make_async_copy(
                pair_ref.at[0, :, columns], pair_buf.at[slot, :, place], sems.at[slot, 3]
            ),
            pltpu.make_async_copy(
                pair_ref.at[1, :, columns],
                pair_buf.at[slot, :, pl.ds(size, size)],
                sems.at[slot, 4],
            ),
        ]

    def work(k, slot):
        _, size = tiles[k]
        grad_active = product_right(rows_ref[...], down_buf[slot, :size])
        grads = ffn_grads(
            grad_active,
            gate_buf[slot, :, :size].astype(F32),
            up_buf[slot, :, :size].astype(F32),
        )
        part = product_right(jnp.concatenate(grads, axis=1), pair_buf[slot, :, : 2 * size])
        if k == 0:
            acc_ref[...] = part
        else:
            acc_ref[...] += part

    streamed(tiles, copies, work)
    halves_out(acc_ref, core_ref[0], mine_ref, other_ref)


def feed_forward_call(backward, core, rows, pair, down, saved=(), micro=2):
    count, width = rows.shape
    units = down.shape[0]
    tile = 768
    tiles = unit_tiles(units, tile)
    half = count // (2 * micro)
    vmem, any_space = pl.BlockSpec(memory_space=pltpu.VMEM), pl.BlockSpec(memory_space=pl.ANY)
    scalar = pl.BlockSpec(memory_space=pltpu.SMEM)
    out_shape = [
        jax.ShapeDtypeStruct((micro, half, width), F32),
        jax.ShapeDtypeStruct((micro, half, width), BF16),
    ]
    out_specs = [vmem, vmem]
    buffers = [pltpu.VMEM((2, width, 2 * tile), BF16), pltpu.VMEM((2, tile, width), BF16)]
    acc = pltpu.VMEM((count, width), F32)
    if backward:
        body = functools.partial(ffn_backward_kernel, tiles)
        in_specs = [scalar, vmem, any_space, any_space, any_space, any_space]
        buffers += [pltpu.VMEM((2, count, tile), BF16)] * 2
        scratch = [*buffers, acc, pltpu.SemaphoreType.DMA((2, 5))]
    else:
        body = functools.partial(ffn_forward_kernel, tiles)
        in_specs = [scalar, vmem, any_space, any_space]
        out_shape = [jax.ShapeDtypeStruct((count, units), BF16)] * 2 + out_shape
        out_specs = [any_space, any_space, *out_specs]
        buffers += [pltpu.VMEM((count, units), BF16)] * 2
        scratch = [*buffers, acc]
        scratch += [pltpu.SemaphoreType.DMA((2, 3)), pltpu.SemaphoreType.DMA((len(tiles), 2))]
    return pl.pallas_call(
        body,
        in_specs=in_specs,
        out_specs=out_specs,
        out_shape=out_shape,
        scratch_shapes=scratch,
        compiler_params=pltpu.CompilerParams(vmem_limit_bytes=VMEM_LIMIT),
        cost_estimate=pl.CostEstimate(
            flops=6 * count * width * units,
            bytes_accessed=6 * width * units,
            transcendentals=count * units,
        ),
    )(core, rows, *saved, pair, down)


def part_forward_kernel(rows_ref, pair_ref, kept_ref):
    both = product(rows_ref[...], pair_ref[...])
    units = both.shape[1] // 2
    gate, up = both[:, :units], both[:, units:]
    sigmoid = jax.nn.sigmoid(gate)
    silu = gate * sigmoid
    kept_ref[:, :units] = (up * (sigmoid + silu * (1.0 - sigmoid))).astype(BF16)
    kept_ref[:, units : 2 * units] = silu.astype(BF16)
    kept_ref[:, 2 * units :] = (silu * up).astype(BF16)


def part_forward_call(rows, pair):
    tokens, width = rows.shape
    units = pair.shape[1] // 2
    tile = 1024
    return pl.pallas_call(
        part_forward_kernel,
        grid=(tokens // tile,),
        in_specs=[
            pl.BlockSpec((tile, width), lambda i: (i, 0)),
            pl.BlockSpec((width, 2 * units), lambda i: (0, 0)),
        ],
        out_specs=pl.BlockSpec((tile, 3 * units), lambda i: (i, 0)),
        out_shape=jax.ShapeDtypeStruct((tokens, 3 * units), BF16),
        compiler_params=pltpu.CompilerParams(vmem_limit_bytes=VMEM_LIMIT),
        cost_estimate=pl.CostEstimate(
            flops=4 * tokens * width * units,
            bytes_accessed=2 * tokens * (width + 3 * units),
            transcendentals=tokens * units,
        ),
    )(rows, pair)


def part_grads_kernel(here_ref, inner_ref, grad_ref, kept_ref, down_ref, mine_ref, other_ref, acc_ref):
    step = pl.program_id(0)
    inner, grad = inner_ref[...], grad_ref[...]
    units = down_ref.shape[0]
    grad_active = product_right(grad, down_ref[...])
    grad_gate = (grad_active * kept_ref[:, :units].astype(F32)).astype(BF16)
    grad_up = (grad_active * kept_ref[:, units : 2 * units].astype(F32)).astype(BF16)
    parts = [
        product_left(inner, jnp.concatenate([grad_gate, grad_up], axis=1)),
        product_left(grad, kept_ref[:, 2 * units :]),
    ]

    @pl.when(step == 0)
    def _():
        acc_ref[:, : 2 * units] = parts[0]
        acc_ref[:, 2 * units :] = parts[1]

    @pl.when(step > 0)
    def _():
        acc_ref[:, : 2 * units] += parts[0]
        acc_ref[:, 2 * units :] += parts[1]

    @pl.when(step == pl.num_programs(0) - 1)
    def _():
        rows = mine_ref.shape[0]
        here = here_ref[0]
        mine_ref[...] = acc_ref[pl.ds(pl.multiple_of(here * rows, rows), rows)]
        rest = acc_ref[pl.ds(pl.multiple_of((1 - here) * rows, rows), rows)]
        other_ref[...] = rest.astype(BF16)


def part_grads_call(here, inner, grad, both, down):
    tokens, width = inner.shape
    units = down.shape[0]
    tile = 1024
    rows = pl.BlockSpec((tile, width), lambda i, c: (i, 0))
    out = pl.BlockSpec((width // 2, 3 * units), lambda i, c: (0, 0))
    return pl.pallas_call(
        part_grads_kernel,
        grid_spec=pltpu.PrefetchScalarGridSpec(
            num_scalar_prefetch=1,
            grid=(tokens // tile,),
            in_specs=[
                rows,
                rows,
                pl.BlockSpec((tile, 3 * units), lambda i, c: (i, 0)),
                pl.BlockSpec((units, width), lambda i, c: (0, 0)),
            ],
            out_specs=[out, out],
            scratch_shapes=[pltpu.VMEM((width, 3 * units), F32)],
        ),
        out_shape=[
            jax.ShapeDtypeStruct((width // 2, 3 * units), F32),
            jax.ShapeDtypeStruct((width // 2, 3 * units), BF16),
        ],
        compiler_params=pltpu.CompilerParams(vmem_limit_bytes=VMEM_LIMIT),
        cost_estimate=pl.CostEstimate(
            flops=8 * tokens * width * units,
            bytes_accessed=4 * tokens * width,
            transcendentals=tokens * units,
        ),
    )(here, inner, grad, both, down)


def local(
    inputs,
    out_cotangent,
    segments,
    norm_gains,
    conv_kernel,
    qk_gains,
    conv_in,
    attn_qkv,
    mixer_out,
    gate_up,
    down,
):
    section = lax.axis_index("xh")
    first = section == 0
    core = lax.axis_index("c")
    place = lax.axis_index("y") * 4 + lax.axis_index("z")
    xl = lax.axis_index("xl")
    plane = lax.axis_size("y") * lax.axis_size("z")

    inputs, out_cotangent, segments = inputs[0], out_cotangent[0], segments[0]
    micro, half, width = inputs.shape
    length = 2 * half
    rows = micro * length
    channels = conv_in.shape[2]
    kernel = lax.dynamic_slice_in_dim(conv_kernel, core * channels, channels, 1).astype(F32)
    gains = lax.dynamic_index_in_dim(norm_gains, section, 0, keepdims=False).astype(F32)
    head_gains = qk_gains.astype(F32)
    weight_out, weight_pair, weight_down = mixer_out[0], gate_up[0], down[0]
    weight_gate, weight_up = weight_pair[0], weight_pair[1]
    hidden_units = weight_down.shape[0]
    part = hidden_units // plane

    in_width = 3 * channels
    qkv_width = attn_qkv.shape[1]
    both = jnp.concatenate([conv_in.reshape(-1, in_width), attn_qkv], axis=1)
    whole = lax.all_gather(both, ("xh", "xl", "y", "z"), axis=0, tiled=True)
    weight_in, weight_qkv = whole[:, :in_width], whole[:, in_width:]

    lanes = -(-part // 256) * 256
    fill = lanes - part
    part_pair = jnp.concatenate(
        [
            jnp.pad(lax.dynamic_slice_in_dim(w, place * part, part, 1), ((0, 0), (0, fill)))
            for w in (weight_gate, weight_up)
        ],
        axis=1,
    )
    part_down = lax.dynamic_slice_in_dim(weight_down, place * part, part, 0)
    part_down = jnp.pad(part_down, ((0, fill), (0, 0)))

    core_scalar = core.astype(jnp.int32)[None]
    xl_scalar = xl.astype(jnp.int32)[None]

    def feed_forward(hidden):
        inner_own = (normalize(hidden) * gains[1]).astype(BF16)
        gate, up, mine, other = feed_forward_call(
            False, core_scalar, spread(inner_own), weight_pair, weight_down
        )
        return hidden + joined(mine, other), (inner_own, gate, up)

    def feed_forward_back(grad_low, grad, hidden, saved):
        mine, other = feed_forward_call(
            True, core_scalar, spread(grad_low), weight_pair, weight_down, saved[1:]
        )
        back, grad_gain = norm_backward(joined(mine, other), gains[1], hidden)
        grad_hidden = grad + back
        return grad_hidden, grad_gain

    def mixer_back(grad_hidden, grad_proj, weight, layer_in):
        partial = product_right(grad_proj, weight)
        back, grad_gain = norm_backward(collect(partial, core), gains[0], layer_in)
        return (grad_hidden + back).astype(BF16), grad_gain

    first_in = inputs.astype(F32)
    normed_own_0 = (normalize(first_in) * gains[0]).astype(BF16)
    projected = product(spread(normed_own_0), weight_in).reshape(micro, length, in_width)
    gated_0 = conv_gate(projected, kernel, segments).astype(BF16).reshape(rows, -1)
    hidden_0 = first_in + collect(product(gated_0, weight_out), core)
    result_0, ffn_0 = feed_forward(hidden_0)
    result_0 = result_0.astype(BF16)

    received = lax.ppermute(result_0, "xh", [(0, 1)])
    second_in = received.astype(F32)
    normed_own_1 = (normalize(second_in) * gains[0]).astype(BF16)
    head_inputs = product(spread(normed_own_1), weight_qkv).reshape(micro, length, qkv_width)
    gated_1, kept = attention_forward(head_inputs, head_gains, segments)
    gated_1 = gated_1.reshape(rows, -1)
    hidden_1 = second_in + collect(product(gated_1, weight_out), core)
    result_1, ffn_1 = feed_forward(hidden_1)
    result_1 = result_1.astype(BF16)

    def chosen(from_first, from_second):
        return jnp.where(first, from_first, from_second)

    def by_core(full):
        tiles = full.reshape(micro, 2, half, -1)
        return jnp.swapaxes(tiles, 0, 1).reshape(rows, -1)

    def gathered(own, axes):
        return lax.all_gather(own.reshape(-1, own.shape[-1]), axes, tiled=True)

    inner_all = gathered(chosen(ffn_0[0], ffn_1[0]), ("y", "z", "c"))
    normed_y = gathered(chosen(normed_own_0, normed_own_1), ("y", "c"))
    gated_y = gathered(by_core(chosen(gated_0, gated_1)), "y")
    part_kept = part_forward_call(inner_all, part_pair)

    grad_hidden_1, gain_inner_1 = feed_forward_back(
        out_cotangent, out_cotangent.astype(F32), hidden_1, ffn_1
    )
    grad_mix_1 = spread(grad_hidden_1.astype(BF16))
    grad_gated_1 = product_right(grad_mix_1, weight_out).reshape(micro, length, -1)
    grad_heads_in, grad_head_gains = attention_backward(grad_gated_1, kept, head_inputs, head_gains)
    grad_proj_1 = grad_heads_in.astype(BF16).reshape(rows, -1)
    input_grad_1, gain_outer_1 = mixer_back(grad_hidden_1, grad_proj_1, weight_qkv, second_in)

    cotangent = lax.ppermute(input_grad_1, "xh", [(1, 0)])
    grad_all = gathered(chosen(cotangent, out_cotangent), ("y", "z", "c"))
    grad_hidden_0, gain_inner_0 = feed_forward_back(
        cotangent, cotangent.astype(F32), hidden_0, ffn_0
    )
    grad_mix_0 = spread(grad_hidden_0.astype(BF16))
    grad_gated_0 = product_right(grad_mix_0, weight_out).reshape(micro, length, -1)
    rebuild = jax.vjp(lambda p, k: conv_gate(p, k, segments), projected, kernel)[1]
    grad_projected, grad_kernel = rebuild(grad_gated_0)
    grad_proj_0 = grad_projected.astype(BF16).reshape(rows, -1)
    input_grad_0, gain_outer_0 = mixer_back(grad_hidden_0, grad_proj_0, weight_in, first_in)

    def exchanged(tiles, axes):
        return lax.all_to_all(tiles, axes, 0, 0, tiled=True)

    grad_mix = by_core(chosen(grad_mix_0, grad_mix_1))
    tiles = jnp.moveaxis(grad_mix.reshape(rows, 2, 4, 4, -1), 2, 0).reshape(4, rows, -1)
    columns = exchanged(tiles, "y").reshape(4 * rows, -1)
    out_parts = product_left(columns, gated_y).astype(BF16).reshape(8, -1, channels)
    grad_mixer_out = exchanged(out_parts, ("xl", "z")).astype(F32).sum(0).T[None]

    spare = in_width - qkv_width
    grad_proj = by_core(chosen(grad_proj_0, jnp.pad(grad_proj_1, ((0, 0), (0, spare)))))
    tiles = jnp.moveaxis(grad_proj.reshape(rows, 4, -1), 1, 0)
    columns = exchanged(tiles, "y").reshape(4 * rows, -1)
    in_parts = product_left(normed_y, columns).reshape(2, 2, plane, -1, in_width // 4)
    mine = lax.dynamic_index_in_dim(in_parts, xl, 1, keepdims=False)
    other = lax.dynamic_index_in_dim(in_parts, 1 - xl, 1, keepdims=False)
    mine = (mine + swapped(other.astype(BF16), "xl").astype(F32)).astype(BF16)
    arrived = exchanged(jnp.moveaxis(mine, 1, 0), PLANE)
    arrived = arrived.reshape(4, 4, *arrived.shape[1:]).astype(F32).sum(1)
    lines = jnp.moveaxis(arrived, 0, 2).reshape(2, -1, in_width)
    kept_lines = lax.dynamic_index_in_dim(lines, section, 0, keepdims=False)
    sent_lines = lax.dynamic_index_in_dim(lines, 1 - section, 0, keepdims=False)
    come = swapped(sent_lines.astype(BF16), "xh").astype(F32)
    grad_conv_in = chosen(kept_lines, come).reshape(conv_in.shape)
    grad_attn_qkv = chosen(come, kept_lines)[:, :qkv_width]

    mine, other = part_grads_call(xl_scalar, inner_all, grad_all, part_kept, part_down)
    mine = (mine + swapped(other, "xl").astype(F32)).astype(BF16)
    arrived = exchanged(mine.reshape(plane, -1, 3 * lanes), PLANE)
    lines = [
        jnp.moveaxis(arrived[:, :, k * lanes : k * lanes + part], 0, 1)
        .reshape(-1, hidden_units)
        .astype(F32)
        for k in range(3)
    ]
    grad_gate_up = jnp.stack(lines[:2])[None]
    grad_down = lines[2].T[None]

    full_kernel = lax.dynamic_update_slice(
        jnp.zeros(conv_kernel.shape, F32), grad_kernel, (0, core * channels)
    )
    small = jnp.concatenate(
        [
            chosen(gain_outer_0, gain_outer_1),
            chosen(gain_inner_0, gain_inner_1),
            full_kernel.reshape(-1),
            grad_head_gains.reshape(-1),
        ]
    )
    count = small.shape[0]
    small = jnp.pad(small, (0, -count % 1024)).reshape(-1, 128)
    small = lax.all_gather(small, "c").sum(0)
    small = small + swapped(small, "xl")
    for axis in PLANE:
        copies = jnp.broadcast_to(small, (4, *small.shape))
        small = lax.all_to_all(copies, axis, 0, 0, tiled=True).sum(0)
    come = swapped(small, "xh")
    pair = [chosen(small, come).reshape(-1), chosen(come, small).reshape(-1)]
    grad_norm_gains = jnp.stack([a[: 2 * width].reshape(2, width) for a in pair])
    grad_conv_kernel = pair[0][2 * width : 5 * width].reshape(conv_kernel.shape)
    grad_qk_gains = pair[1][5 * width : count].reshape(qk_gains.shape)

    activations = chosen(result_0, result_1)[None, None]
    input_grads = chosen(input_grad_0, input_grad_1)[None, None]
    return (
        activations,
        input_grads,
        grad_norm_gains,
        grad_conv_kernel,
        grad_qk_gains,
        grad_conv_in,
        grad_attn_qkv,
        grad_mixer_out,
        grad_gate_up,
        grad_down,
    )


def solution(mesh):
    wide = Mesh(mesh.devices.reshape(2, 2, 4, 4, 2), AXES)
    dp = ("xl", "y", "z")
    everyone = ("xh", "xl", "y", "z")
    in_specs = (
        P(dp, None, "c", None),
        P(dp, None, "c", None),
        P(dp, None, None),
        P(),
        P(),
        P(),
        P(everyone, None, "c"),
        P(everyone, "c"),
        P("xh", "c", None),
        P("xh", None, None, "c"),
        P("xh", "c", None),
    )
    out_specs = (
        P("xh", dp, None, "c", None),
        P("xh", dp, None, "c", None),
        P(),
        P(),
        P(),
        P(everyone, None, "c"),
        P(everyone, "c"),
        P("xh", "c", dp),
        P("xh", None, dp, "c"),
        P("xh", "c", dp),
    )
    return jax.shard_map(local, mesh=wide, in_specs=in_specs, out_specs=out_specs, check_vma=False)
```

```python
import functools

import jax
import jax.numpy as jnp
from jax import lax
from jax.experimental import pallas as pl
from jax.experimental.pallas import tpu as pltpu
from jax.sharding import Mesh
from jax.sharding import PartitionSpec as P

HEADS = 24
KV_HEADS = 8
HEAD_DIM = 64
GROUP = HEADS // KV_HEADS

EPSILON = 1e-05
ROPE_BASE = 1000000.0
MASKED_SCORE = -1e30

F32 = jnp.float32
BF16 = jnp.bfloat16

PLANE = ("y", "z")
AXES = ("xh", "xl", "y", "z", "c")


def product(left, right):
    return jnp.dot(left, right, preferred_element_type=F32)


def product_left(left, right):
    return lax.dot_general(left, right, (((0,), (0,)), ((), ())), preferred_element_type=F32)


def product_right(left, right):
    return lax.dot_general(left, right, (((1,), (1,)), ((), ())), preferred_element_type=F32)


def swapped(shard, axis):
    return lax.ppermute(shard, axis, [(0, 1), (1, 0)])


def spread(own):
    return lax.all_gather(own, "c", tiled=True)


def joined(mine, other):
    return mine + swapped(other, "c").astype(F32)


def mean_last(values):
    return jnp.mean(values, axis=-1, keepdims=True)


def inverse_rms(values):
    return lax.rsqrt(mean_last(values * values) + EPSILON)


def normalize(values):
    return values * inverse_rms(values)


def norm_backward(grad, gain, values):
    inverse = inverse_rms(values)
    normed = values * inverse
    scaled = grad * gain
    grad_gain = jnp.sum(grad * normed, axis=0)
    return inverse * (scaled - normed * mean_last(scaled * normed)), grad_gain


def exchanged(tiles, axes):
    return lax.all_to_all(tiles, axes, 0, 0, tiled=True)


def ffn_grads(grad_active, gate, up):
    sigmoid = jax.nn.sigmoid(gate)
    grad_gate = grad_active * up * sigmoid * (1.0 + gate * (1.0 - sigmoid))
    grad_up = grad_active * gate * sigmoid
    return grad_gate.astype(BF16), grad_up.astype(BF16)


VMEM_LIMIT = 56 * 1024 * 1024


def unit_tiles(units, tile):
    short = units % tile
    tiles = [(0, short)] if short else []
    return tiles + [(at, tile) for at in range(short, units, tile)]


def streamed(tiles, copies, work):
    for copy in copies(0, 0):
        copy.start()
    for k in range(len(tiles)):
        slot = k % 2
        if k + 1 < len(tiles):
            for copy in copies(k + 1, 1 - slot):
                copy.start()
        for copy in copies(k, slot):
            copy.wait()
        work(k, slot)


def ffn_forward_kernel(
    tiles, core_ref, rows_ref, pair_ref, down_ref, gate_ref, up_ref, mine_ref, other_ref,
    pair_buf, down_buf, gate_buf, up_buf, acc_ref, sems, out_sems,
):
    def copies(k, slot):
        at, size = tiles[k]
        return [
            pltpu.make_async_copy(
                pair_ref.at[0, :, pl.ds(at, size)],
                pair_buf.at[slot, :, pl.ds(0, size)],
                sems.at[slot, 0],
            ),
            pltpu.make_async_copy(
                pair_ref.at[1, :, pl.ds(at, size)],
                pair_buf.at[slot, :, pl.ds(size, size)],
                sems.at[slot, 1],
            ),
            pltpu.make_async_copy(
                down_ref.at[pl.ds(at, size)], down_buf.at[slot, pl.ds(0, size)], sems.at[slot, 2]
            ),
        ]

    def kept(k):
        here = (slice(None), pl.ds(*tiles[k]))
        return [
            pltpu.make_async_copy(gate_buf.at[here], gate_ref.at[here], out_sems.at[k, 0]),
            pltpu.make_async_copy(up_buf.at[here], up_ref.at[here], out_sems.at[k, 1]),
        ]

    def work(k, slot):
        at, size = tiles[k]
        both = product(rows_ref[...], pair_buf[slot, :, : 2 * size])
        gate, up = both[:, :size], both[:, size:]
        gate_buf[:, at : at + size] = gate.astype(BF16)
        up_buf[:, at : at + size] = up.astype(BF16)
        for copy in kept(k):
            copy.start()
        active = (gate * jax.nn.sigmoid(gate) * up).astype(BF16)
        part = product(active, down_buf[slot, :size])
        if k == 0:
            acc_ref[...] = part
        else:
            acc_ref[...] += part

    streamed(tiles, copies, work)
    rows_out(acc_ref, core_ref[0], mine_ref, other_ref)
    for k in range(len(tiles)):
        for copy in kept(k):
            copy.wait()


def ffn_backward_kernel(
    tiles, core_ref, rows_ref, gate_ref, up_ref, pair_ref, down_ref, mine_ref, other_ref,
    pair_buf, down_buf, gate_buf, up_buf, acc_ref, sems,
):
    def copies(k, slot):
        at, size = tiles[k]
        columns, place = pl.ds(at, size), pl.ds(0, size)
        return [
            pltpu.make_async_copy(
                down_ref.at[columns], down_buf.at[slot, place], sems.at[slot, 0]
            ),
            pltpu.make_async_copy(
                gate_ref.at[:, columns], gate_buf.at[slot, :, place], sems.at[slot, 1]
            ),
            pltpu.make_async_copy(
                up_ref.at[:, columns], up_buf.at[slot, :, place], sems.at[slot, 2]
            ),
            pltpu.make_async_copy(
                pair_ref.at[0, :, columns], pair_buf.at[slot, :, place], sems.at[slot, 3]
            ),
            pltpu.make_async_copy(
                pair_ref.at[1, :, columns],
                pair_buf.at[slot, :, pl.ds(size, size)],
                sems.at[slot, 4],
            ),
        ]

    def work(k, slot):
        _, size = tiles[k]
        grad_active = product_right(rows_ref[...], down_buf[slot, :size])
        grads = ffn_grads(
            grad_active,
            gate_buf[slot, :, :size].astype(F32),
            up_buf[slot, :, :size].astype(F32),
        )
        part = product_right(jnp.concatenate(grads, axis=1), pair_buf[slot, :, : 2 * size])
        if k == 0:
            acc_ref[...] = part
        else:
            acc_ref[...] += part

    streamed(tiles, copies, work)
    rows_out(acc_ref, core_ref[0], mine_ref, other_ref)


def feed_forward_call(backward, core, rows, pair, down, saved=()):
    count, width = rows.shape
    units = down.shape[0]
    tile = 768
    tiles = unit_tiles(units, tile)
    vmem, any_space = pl.BlockSpec(memory_space=pltpu.VMEM), pl.BlockSpec(memory_space=pl.ANY)
    scalar = pl.BlockSpec(memory_space=pltpu.SMEM)
    out_shape = [
        jax.ShapeDtypeStruct((count // 2, width), F32),
        jax.ShapeDtypeStruct((count // 2, width), BF16),
    ]
    out_specs = [vmem, vmem]
    buffers = [pltpu.VMEM((2, width, 2 * tile), BF16), pltpu.VMEM((2, tile, width), BF16)]
    acc = pltpu.VMEM((count, width), F32)
    if backward:
        body = functools.partial(ffn_backward_kernel, tiles)
        in_specs = [scalar, vmem, any_space, any_space, any_space, any_space]
        buffers += [pltpu.VMEM((2, count, tile), BF16)] * 2
        scratch = [*buffers, acc, pltpu.SemaphoreType.DMA((2, 5))]
    else:
        body = functools.partial(ffn_forward_kernel, tiles)
        in_specs = [scalar, vmem, any_space, any_space]
        out_shape = [jax.ShapeDtypeStruct((count, units), BF16)] * 2 + out_shape
        out_specs = [any_space, any_space, *out_specs]
        buffers += [pltpu.VMEM((count, units), BF16)] * 2
        scratch = [*buffers, acc]
        scratch += [pltpu.SemaphoreType.DMA((2, 3)), pltpu.SemaphoreType.DMA((len(tiles), 2))]
    return pl.pallas_call(
        body,
        in_specs=in_specs,
        out_specs=out_specs,
        out_shape=out_shape,
        scratch_shapes=scratch,
        compiler_params=pltpu.CompilerParams(vmem_limit_bytes=VMEM_LIMIT),
        cost_estimate=pl.CostEstimate(
            flops=6 * count * width * units,
            bytes_accessed=6 * width * units,
            transcendentals=count * units,
        ),
    )(core, rows, *saved, pair, down)


def part_forward_kernel(rows_ref, pair_ref, kept_ref):
    both = product(rows_ref[...], pair_ref[...])
    units = both.shape[1] // 2
    gate, up = both[:, :units], both[:, units:]
    sigmoid = jax.nn.sigmoid(gate)
    silu = gate * sigmoid
    kept_ref[:, :units] = (up * (sigmoid + silu * (1.0 - sigmoid))).astype(BF16)
    kept_ref[:, units : 2 * units] = silu.astype(BF16)
    kept_ref[:, 2 * units :] = (silu * up).astype(BF16)


def part_forward_call(rows, pair):
    tokens, width = rows.shape
    units = pair.shape[1] // 2
    tile = 1024
    return pl.pallas_call(
        part_forward_kernel,
        grid=(tokens // tile,),
        in_specs=[
            pl.BlockSpec((tile, width), lambda i: (i, 0)),
            pl.BlockSpec((width, 2 * units), lambda i: (0, 0)),
        ],
        out_specs=pl.BlockSpec((tile, 3 * units), lambda i: (i, 0)),
        out_shape=jax.ShapeDtypeStruct((tokens, 3 * units), BF16),
        compiler_params=pltpu.CompilerParams(vmem_limit_bytes=VMEM_LIMIT),
        cost_estimate=pl.CostEstimate(
            flops=4 * tokens * width * units,
            bytes_accessed=2 * tokens * (width + 3 * units),
            transcendentals=tokens * units,
        ),
    )(rows, pair)


def part_grads_kernel(
    here_ref, inner_ref, grad_ref, kept_ref, down_ref, mine_ref, other_ref, acc_ref
):
    step = pl.program_id(0)
    inner, grad = inner_ref[...], grad_ref[...]
    units = down_ref.shape[0]
    grad_active = product_right(grad, down_ref[...])
    grad_gate = (grad_active * kept_ref[:, :units].astype(F32)).astype(BF16)
    grad_up = (grad_active * kept_ref[:, units : 2 * units].astype(F32)).astype(BF16)
    parts = [
        product_left(inner, jnp.concatenate([grad_gate, grad_up], axis=1)),
        product_left(grad, kept_ref[:, 2 * units :]),
    ]

    @pl.when(step == 0)
    def _():
        acc_ref[:, : 2 * units] = parts[0]
        acc_ref[:, 2 * units :] = parts[1]

    @pl.when(step > 0)
    def _():
        acc_ref[:, : 2 * units] += parts[0]
        acc_ref[:, 2 * units :] += parts[1]

    @pl.when(step == pl.num_programs(0) - 1)
    def _():
        rows = mine_ref.shape[0]
        here = here_ref[0]
        mine_ref[...] = acc_ref[pl.ds(pl.multiple_of(here * rows, rows), rows)]
        rest = acc_ref[pl.ds(pl.multiple_of((1 - here) * rows, rows), rows)]
        other_ref[...] = rest.astype(BF16)


def part_grads_call(here, inner, grad, both, down):
    tokens, width = inner.shape
    units = down.shape[0]
    tile = 1024
    rows = pl.BlockSpec((tile, width), lambda i, c: (i, 0))
    out = pl.BlockSpec((width // 2, 3 * units), lambda i, c: (0, 0))
    return pl.pallas_call(
        part_grads_kernel,
        grid_spec=pltpu.PrefetchScalarGridSpec(
            num_scalar_prefetch=1,
            grid=(tokens // tile,),
            in_specs=[
                rows,
                rows,
                pl.BlockSpec((tile, 3 * units), lambda i, c: (i, 0)),
                pl.BlockSpec((units, width), lambda i, c: (0, 0)),
            ],
            out_specs=[out, out],
            scratch_shapes=[pltpu.VMEM((width, 3 * units), F32)],
        ),
        out_shape=[
            jax.ShapeDtypeStruct((width // 2, 3 * units), F32),
            jax.ShapeDtypeStruct((width // 2, 3 * units), BF16),
        ],
        compiler_params=pltpu.CompilerParams(vmem_limit_bytes=VMEM_LIMIT),
        cost_estimate=pl.CostEstimate(
            flops=8 * tokens * width * units,
            bytes_accessed=4 * tokens * width,
            transcendentals=tokens * units,
        ),
    )(here, inner, grad, both, down)


def load_all(copies):
    for copy in copies:
        copy.start()


def in_time(rows):
    half = rows.shape[0] // 4
    return jnp.concatenate([rows[k * half : (k + 1) * half] for k in (0, 2, 1, 3)], axis=0)


def rows_out(acc_ref, core, mine_ref, other_ref):
    half = mine_ref.shape[0]
    mine_ref[...] = acc_ref[pl.ds(pl.multiple_of(core * half, half), half)]
    rest = acc_ref[pl.ds(pl.multiple_of((1 - core) * half, half), half)]
    other_ref[...] = rest.astype(BF16)


def weight_copies(whole_ref, out_ref, in_buf, out_buf, sems, start):
    size = in_buf.shape[2]
    copies = [
        pltpu.make_async_copy(
            whole_ref.at[:, pl.ds(start + k * size, size)], in_buf.at[k], sems.at[k]
        )
        for k in range(in_buf.shape[0])
    ]
    return copies, pltpu.make_async_copy(out_ref, out_buf, sems.at[len(copies)])


def conv_taps(mixed, kernel, masks):
    terms = [mixed]
    for lag in range(1, len(masks) + 1):
        terms.append(pltpu.roll(mixed, lag, 0) * masks[lag - 1])
    taps = kernel.shape[0]
    total = kernel[taps - 1 : taps] * terms[0]
    for lag in range(1, taps):
        total = total + kernel[taps - 1 - lag : taps - lag] * terms[lag]
    return terms, total


def conv_forward_kernel(
    core_ref, rows_ref, kernel_ref, masks_ref, whole_ref, out_ref,
    proj_ref, gated_ref, mine_ref, other_ref, in_buf, out_buf, acc_ref, sems,
):
    copies, last = weight_copies(whole_ref, out_ref, in_buf, out_buf, sems, 0)
    load_all([*copies, last])
    rows = rows_ref[...]
    parts = []
    for k, copy in enumerate(copies):
        copy.wait()
        part = product(rows, in_buf[k])
        proj_ref[k] = part.astype(BF16)
        parts.append(in_time(part))
    masks = [masks_ref[lag] for lag in range(masks_ref.shape[0])]
    gated = []
    for at in range(0, parts[0].shape[1], 128):
        before, after, signal = [part[:, at : at + 128] for part in parts]
        _, total = conv_taps(before * signal, kernel_ref[:, at : at + 128], masks)
        gated.append((after * total).astype(BF16))
    gated = in_time(jnp.concatenate(gated, axis=1))
    gated_ref[...] = gated
    last.wait()
    acc_ref[...] = product(gated, out_buf[...])
    rows_out(acc_ref, core_ref[0], mine_ref, other_ref)


def tiles_out(tiles_ref, mix_ref, grad_mix, columns):
    count = tiles_ref.shape[0]
    width = grad_mix.shape[1] // 2
    step = width // count
    for k in range(count):
        tiles_ref[k] = columns(k)
        mix_ref[k] = jnp.concatenate(
            [grad_mix[:, h * width + k * step : h * width + (k + 1) * step] for h in range(2)],
            axis=1,
        )


def conv_backward_kernel(
    core_ref, grad_ref, kernel_ref, masks_ref, proj_ref, whole_ref, out_ref,
    tiles_ref, mix_ref, taps_ref, mine_ref, other_ref, in_buf, out_buf, acc_ref, sems,
):
    copies, last = weight_copies(whole_ref, out_ref, in_buf, out_buf, sems, 0)
    load_all([last, *copies])
    last.wait()
    grad_gated = in_time(product_right(grad_ref[...], out_buf[...]))
    parts = [in_time(proj_ref[k].astype(F32)) for k in range(3)]
    masks = [masks_ref[lag] for lag in range(masks_ref.shape[0])]
    rows = grad_gated.shape[0]
    grads = [[], [], []]
    for at in range(0, grad_gated.shape[1], 128):
        before, after, signal = [part[:, at : at + 128] for part in parts]
        kernel = kernel_ref[:, at : at + 128]
        terms, total = conv_taps(before * signal, kernel, masks)
        grad = grad_gated[:, at : at + 128]
        grad_total = grad * after
        taps = kernel.shape[0]
        grad_mixed = kernel[taps - 1 : taps] * grad_total
        for lag in range(1, taps):
            sent = pltpu.roll(grad_total * masks[lag - 1], rows - lag, 0)
            grad_mixed = grad_mixed + kernel[taps - 1 - lag : taps - lag] * sent
        for lag in range(taps):
            taps_ref[taps - 1 - lag : taps - lag, at : at + 128] = jnp.sum(
                grad_total * terms[lag], axis=0, keepdims=True
            )
        for k, value in enumerate((grad_mixed * signal, grad * total, grad_mixed * before)):
            grads[k].append(value.astype(BF16))
    grads = [in_time(jnp.concatenate(g, axis=1)) for g in grads]
    step = grads[0].shape[1] // tiles_ref.shape[0]
    tiles_out(
        tiles_ref,
        mix_ref,
        grad_ref[...],
        lambda k: jnp.concatenate([g[:, k * step : (k + 1) * step] for g in grads], axis=1),
    )
    for k, copy in enumerate(copies):
        copy.wait()
        part = product_right(grads[k], in_buf[k])
        acc_ref[...] = part if k == 0 else acc_ref[...] + part
    rows_out(acc_ref, core_ref[0], mine_ref, other_ref)


def head_kind(head):
    return min(max(head % (GROUP + 2) - GROUP + 1, 0), 2)


def lane_facts(rows):
    lane = lax.broadcasted_iota(jnp.int32, (rows, 128), 1)
    return lane < HEAD_DIM, lax.rem(lane, HEAD_DIM) < HEAD_DIM // 2


def head_scales(block, low):
    squares = block * block
    first = jnp.sum(jnp.where(low, squares, 0.0), axis=1, keepdims=True)
    second = jnp.sum(jnp.where(low, 0.0, squares), axis=1, keepdims=True)
    return lax.rsqrt(jnp.where(low, first, second) * (1.0 / HEAD_DIM) + EPSILON)


def block_gains(gains_ref, at):
    heads = [head_kind(2 * at), head_kind(2 * at + 1)]
    return heads, gains_ref[3 * heads[0] + heads[1] : 3 * heads[0] + heads[1] + 1]


def attention_forward_kernel(
    core_ref, rows_ref, gains_ref, tables_ref, mask_ref, whole_ref, out_ref,
    qkv_ref, ready_ref, gated_ref, mine_ref, other_ref, in_buf, out_buf, acc_ref, sems,
):
    copies, last = weight_copies(
        whole_ref, out_ref, in_buf, out_buf, sems, whole_ref.shape[1] - in_buf.shape[2]
    )
    load_all([*copies, last])
    copies[0].wait()
    qkv_ref[...] = product(rows_ref[...], in_buf[0])
    rows, width = qkv_ref.shape
    low, front = lane_facts(rows)
    cosine, sine = tables_ref[0], tables_ref[1]
    for at in range(width // 128):
        block = qkv_ref[:, at * 128 : (at + 1) * 128]
        heads, gains = block_gains(gains_ref, at)
        normed = block * head_scales(block, low) * gains
        turned = jnp.where(front, -pltpu.roll(normed, 96, 1), pltpu.roll(normed, 32, 1))
        ready = normed * cosine + turned * sine
        if heads[0] == 2:
            ready = jnp.where(low, block, ready)
        if heads[1] == 2:
            ready = jnp.where(low, ready, block)
        ready_ref[:, at * 128 : (at + 1) * 128] = ready.astype(BF16)
    half = rows // 4
    span = (GROUP + 2) * HEAD_DIM
    for m in range(2):
        mask = mask_ref[m] > 0
        mask = jnp.concatenate([mask] * GROUP, axis=0)
        for g in range(width // span):
            queries, keys, values = head_rows(ready_ref, m, half, g * span)
            weights = softmax_weights(queries, keys, mask)
            attended = product(weights.astype(BF16), values).astype(BF16)
            for j in range(GROUP):
                at = (g * GROUP + j) * HEAD_DIM
                head = attended[j * 2 * half : (j + 1) * 2 * half]
                gated_ref[m * half : (m + 1) * half, at : at + HEAD_DIM] = head[:half]
                gated_ref[(m + 2) * half : (m + 3) * half, at : at + HEAD_DIM] = head[half:]
    last.wait()
    acc_ref[...] = product(gated_ref[...], out_buf[...])
    rows_out(acc_ref, core_ref[0], mine_ref, other_ref)


def sequence(ref, m, half, at):
    columns = slice(at, at + HEAD_DIM)
    return jnp.concatenate(
        [ref[m * half : (m + 1) * half, columns], ref[(m + 2) * half : (m + 3) * half, columns]],
        axis=0,
    )


def head_rows(ref, m, half, at):
    heads = [sequence(ref, m, half, at + j * HEAD_DIM) for j in range(GROUP + 2)]
    return jnp.concatenate(heads[:GROUP], axis=0), heads[GROUP], heads[GROUP + 1]


def softmax_weights(queries, keys, mask):
    scores = jnp.where(mask, product_right(queries, keys) * HEAD_DIM ** (-0.5), MASKED_SCORE)
    terms = jnp.exp(scores - jnp.max(scores, axis=1, keepdims=True))
    return terms / jnp.sum(terms, axis=1, keepdims=True)


def attention_backward_kernel(
    core_ref, grad_ref, gains_ref, tables_ref, mask_ref, qkv_ref, ready_ref, whole_ref, out_ref,
    tiles_ref, mix_ref, heads_ref, mine_ref, other_ref,
    in_buf, out_buf, acc_ref, attended_ref, ready_grad_ref, proj_ref, sems,
):
    copies, last = weight_copies(
        whole_ref, out_ref, in_buf, out_buf, sems, whole_ref.shape[1] - in_buf.shape[2]
    )
    load_all([last, *copies])
    last.wait()
    attended_ref[...] = product_right(grad_ref[...], out_buf[...]).astype(BF16)
    rows, width = qkv_ref.shape
    half = rows // 4
    span = (GROUP + 2) * HEAD_DIM
    scale = HEAD_DIM ** (-0.5)
    for m in range(2):
        mask = mask_ref[m] > 0
        mask = jnp.concatenate([mask] * GROUP, axis=0)
        for g in range(width // span):
            queries, keys, values = head_rows(ready_ref, m, half, g * span)
            weights = softmax_weights(queries, keys, mask)
            grad = jnp.concatenate(
                [
                    sequence(attended_ref, m, half, (g * GROUP + j) * HEAD_DIM)
                    for j in range(GROUP)
                ],
                axis=0,
            )
            grad_values = product_left(weights.astype(BF16), grad)
            grad_weights = product_right(grad, values)
            mean = jnp.sum(grad_weights * weights, axis=1, keepdims=True)
            grad_scores = (weights * (grad_weights - mean)).astype(BF16)
            grad_queries = product(grad_scores, keys) * scale
            grad_keys = product_left(grad_scores, queries) * scale
            outs = [grad_queries[j * 2 * half : (j + 1) * 2 * half] for j in range(GROUP)]
            for j, out in enumerate([*outs, grad_keys, grad_values]):
                at = g * span + j * HEAD_DIM
                ready_grad_ref[m * half : (m + 1) * half, at : at + HEAD_DIM] = out[:half]
                ready_grad_ref[(m + 2) * half : (m + 3) * half, at : at + HEAD_DIM] = out[half:]
    low, front = lane_facts(rows)
    cosine, sine = tables_ref[0], tables_ref[1]
    for at in range(width // 128):
        lanes = slice(at * 128, (at + 1) * 128)
        block, grad = qkv_ref[:, lanes], ready_grad_ref[:, lanes]
        heads, gains = block_gains(gains_ref, at)
        inverse = head_scales(block, low)
        normed = block * inverse
        turned = grad * sine
        grad_normed = grad * cosine + jnp.where(
            front, pltpu.roll(turned, 96, 1), -pltpu.roll(turned, 32, 1)
        )
        heads_ref[at : at + 1] = jnp.sum(grad_normed * normed, axis=0, keepdims=True)
        grad_normed = grad_normed * gains
        along = grad_normed * normed
        first = jnp.sum(jnp.where(low, along, 0.0), axis=1, keepdims=True)
        second = jnp.sum(jnp.where(low, 0.0, along), axis=1, keepdims=True)
        mean = jnp.where(low, first, second) * (1.0 / HEAD_DIM)
        raw = inverse * (grad_normed - normed * mean)
        if heads[0] == 2:
            raw = jnp.where(low, grad, raw)
        if heads[1] == 2:
            raw = jnp.where(low, raw, grad)
        proj_ref[:, lanes] = raw.astype(BF16)
    step = width // tiles_ref.shape[0]
    spare = jnp.zeros((rows, tiles_ref.shape[2] - step), BF16)
    tiles_out(
        tiles_ref,
        mix_ref,
        grad_ref[...],
        lambda k: jnp.concatenate([proj_ref[:, k * step : (k + 1) * step], spare], axis=1),
    )
    copies[0].wait()
    acc_ref[...] = product_right(proj_ref[...], in_buf[0])
    rows_out(acc_ref, core_ref[0], mine_ref, other_ref)


def mixer_call(kernel, core, operands, whole, weight_out, in_tiles, outs, scratch=(), flops=0):
    vmem, any_space = pl.BlockSpec(memory_space=pltpu.VMEM), pl.BlockSpec(memory_space=pl.ANY)
    rows, width = operands[0].shape
    channels = weight_out.shape[0]
    outs = [*outs, ((rows // 2, width), F32), ((rows // 2, width), BF16)]
    return pl.pallas_call(
        kernel,
        in_specs=[
            pl.BlockSpec(memory_space=pltpu.SMEM),
            *[vmem] * len(operands),
            any_space,
            any_space,
        ],
        out_specs=[vmem] * len(outs),
        out_shape=[jax.ShapeDtypeStruct(*out) for out in outs],
        scratch_shapes=[
            pltpu.VMEM((in_tiles[0], width, in_tiles[1]), BF16),
            pltpu.VMEM((channels, width), BF16),
            pltpu.VMEM((rows, width), F32),
            *scratch,
            pltpu.SemaphoreType.DMA((in_tiles[0] + 1,)),
        ],
        compiler_params=pltpu.CompilerParams(vmem_limit_bytes=VMEM_LIMIT),
        cost_estimate=pl.CostEstimate(
            flops=2 * rows * width * (channels + in_tiles[0] * in_tiles[1]),
            bytes_accessed=2 * width * (channels + in_tiles[0] * in_tiles[1]),
            transcendentals=rows * width,
        ),
    )(core, *operands, whole, weight_out)


def conv_forward_call(core, rows, kernel, masks, whole, weight_out):
    count, channels = rows.shape[0], kernel.shape[1]
    outs = [((3, count, channels), BF16), ((count, channels), BF16)]
    operands = (rows, kernel, masks)
    return mixer_call(
        conv_forward_kernel, core, operands, whole, weight_out, (3, channels), outs
    )


def conv_backward_call(core, grad, kernel, masks, projected, whole, weight_out):
    count, width = grad.shape
    taps, channels = kernel.shape
    outs = [
        ((4, count, 3 * channels // 4), BF16),
        ((4, count, width // 4), BF16),
        ((taps, channels), F32),
    ]
    operands = (grad, kernel, masks, projected)
    return mixer_call(
        conv_backward_kernel, core, operands, whole, weight_out, (3, channels), outs
    )


def attention_forward_call(core, rows, gains, tables, mask, whole, weight_out, qkv_width):
    count, channels = rows.shape[0], weight_out.shape[0]
    outs = [((count, qkv_width), F32), ((count, qkv_width), BF16), ((count, channels), BF16)]
    operands = (rows, gains, tables, mask)
    return mixer_call(
        attention_forward_kernel, core, operands, whole, weight_out, (1, qkv_width), outs
    )


def attention_backward_call(core, grad, gains, tables, mask, qkv, ready, whole, weight_out):
    count, width = grad.shape
    channels, qkv_width = weight_out.shape[0], qkv.shape[1]
    outs = [
        ((4, count, 3 * channels // 4), BF16),
        ((4, count, width // 4), BF16),
        ((qkv_width // 128, 128), F32),
    ]
    scratch = [
        pltpu.VMEM((count, channels), BF16),
        pltpu.VMEM((count, qkv_width), F32),
        pltpu.VMEM((count, qkv_width), BF16),
    ]
    operands = (grad, gains, tables, mask, qkv, ready)
    return mixer_call(
        attention_backward_kernel, core, operands, whole, weight_out, (1, qkv_width), outs, scratch
    )


def conv_masks(segments, taps):
    masks = []
    for lag in range(1, taps):
        same = (segments[:, lag:] == segments[:, :-lag]).astype(F32)
        same = jnp.pad(same, ((0, 0), (lag, 0))).reshape(-1, 1)
        masks.append(jnp.broadcast_to(same, (same.shape[0], 128)))
    return jnp.stack(masks)


def score_mask(segments):
    position = jnp.arange(segments.shape[1])
    allowed = position[:, None] >= position[None, :]
    return (allowed & (segments[:, :, None] == segments[:, None, :])).astype(F32)


def turn_tables(length):
    half = HEAD_DIM // 2
    exponent = jnp.arange(half, dtype=F32) * (2.0 / HEAD_DIM)
    frequency = jnp.exp(-exponent * jnp.log(ROPE_BASE))
    angles = jnp.arange(length, dtype=F32)[:, None] * frequency[None, :]
    tables = jnp.tile(jnp.stack([jnp.cos(angles), jnp.sin(angles)]), (1, 1, 4))
    tables = tables.reshape(2, 2, 1, length // 2, 128)
    return jnp.broadcast_to(tables, (2, 2, 2, length // 2, 128)).reshape(2, 2 * length, 128)


def gain_rows(head_gains):
    kinds = [head_gains[0], head_gains[1], jnp.ones_like(head_gains[0])]
    rows = [jnp.concatenate([a, b]) for a in kinds for b in kinds]
    return jnp.stack(rows)


def head_gain_sums(sums):
    heads = sums.reshape(-1, GROUP + 2, HEAD_DIM)
    return jnp.stack([heads[:, :GROUP].sum((0, 1)), heads[:, GROUP].sum(0)])


def local(
    inputs,
    out_cotangent,
    segments,
    norm_gains,
    conv_kernel,
    qk_gains,
    conv_in,
    attn_qkv,
    mixer_out,
    gate_up,
    down,
):
    section = lax.axis_index("xh")
    first = section == 0
    core = lax.axis_index("c")
    place = lax.axis_index("y") * 4 + lax.axis_index("z")
    xl = lax.axis_index("xl")
    plane = lax.axis_size("y") * lax.axis_size("z")

    shape = inputs.shape[1:]
    width = shape[-1]
    inputs, out_cotangent = inputs.reshape(-1, width), out_cotangent.reshape(-1, width)
    segments = segments[0]
    half = inputs.shape[0]
    rows = 2 * half
    channels = conv_in.shape[2]
    kernel = lax.dynamic_slice_in_dim(conv_kernel, core * channels, channels, 1).astype(F32)
    gains = lax.dynamic_index_in_dim(norm_gains, section, 0, keepdims=False).astype(F32)
    weight_out, weight_pair, weight_down = mixer_out[0], gate_up[0], down[0]
    hidden_units = weight_down.shape[0]
    part = hidden_units // plane
    in_width = 3 * channels
    qkv_width = attn_qkv.shape[1]
    core_scalar = core.astype(jnp.int32)[None]
    xl_scalar = xl.astype(jnp.int32)[None]

    def chosen(from_first, from_second):
        return jnp.where(first, from_first, from_second)

    def gathered(own, axes):
        return lax.all_gather(own, axes, tiled=True)

    both = jnp.concatenate([conv_in.reshape(-1, in_width), attn_qkv], axis=1)
    whole = gathered(both, ("xh", "xl", "y", "z"))

    lanes = -(-part // 256) * 256
    fill = lanes - part
    part_pair = jnp.concatenate(
        [
            jnp.pad(lax.dynamic_slice_in_dim(w, place * part, part, 1), ((0, 0), (0, fill)))
            for w in (weight_pair[0], weight_pair[1])
        ],
        axis=1,
    )
    part_down = lax.dynamic_slice_in_dim(weight_down, place * part, part, 0)
    part_down = jnp.pad(part_down, ((0, fill), (0, 0)))
    masks = conv_masks(segments, kernel.shape[0])
    mask = score_mask(segments)
    tables = turn_tables(segments.shape[1])
    head_gains = gain_rows(qk_gains.astype(F32))
    first_in = inputs.astype(F32)
    normed_own_0 = (normalize(first_in) * gains[0]).astype(BF16)
    normed_0 = spread(normed_own_0)
    cotangent_1 = spread(out_cotangent)
    whole, part_pair, part_down, masks, mask, tables, head_gains, normed_0, cotangent_1 = (
        lax.optimization_barrier(
            (whole, part_pair, part_down, masks, mask, tables, head_gains, normed_0, cotangent_1)
        )
    )

    def feed_forward(hidden):
        inner_own = (normalize(hidden) * gains[1]).astype(BF16)
        gate, up, mine, other = feed_forward_call(
            False, core_scalar, spread(inner_own), weight_pair, weight_down
        )
        return hidden + joined(mine, other), (inner_own, gate, up)

    def feed_forward_back(grad_full, grad, hidden, saved):
        mine, other = feed_forward_call(
            True, core_scalar, grad_full, weight_pair, weight_down, saved[1:]
        )
        back, grad_gain = norm_backward(joined(mine, other), gains[1], hidden)
        return grad + back, grad_gain

    def mixer_back(grad_hidden, mine, other, layer_in):
        back, grad_gain = norm_backward(joined(mine, other), gains[0], layer_in)
        return (grad_hidden + back).astype(BF16), grad_gain

    projected, gated_0, mine, other = conv_forward_call(
        core_scalar, normed_0, kernel, masks, whole, weight_out
    )
    hidden_0 = first_in + joined(mine, other)
    result_0, ffn_0 = feed_forward(hidden_0)
    result_0 = result_0.astype(BF16)

    second_in = lax.ppermute(result_0, "xh", [(0, 1)]).astype(F32)
    normed_own_1 = (normalize(second_in) * gains[0]).astype(BF16)
    normed_y = gathered(chosen(normed_own_0, normed_own_1), ("y", "c"))
    qkv, ready, gated_1, mine, other = attention_forward_call(
        core_scalar, spread(normed_own_1), head_gains, tables, mask, whole, weight_out, qkv_width
    )
    hidden_1 = second_in + joined(mine, other)
    result_1, ffn_1 = feed_forward(hidden_1)
    result_1 = result_1.astype(BF16)

    inner_all = gathered(chosen(ffn_0[0], ffn_1[0]), ("y", "z", "c"))
    part_kept = part_forward_call(inner_all, part_pair)

    grad_hidden_1, gain_inner_1 = feed_forward_back(
        cotangent_1, out_cotangent.astype(F32), hidden_1, ffn_1
    )
    proj_tiles_1, mix_tiles_1, head_sums, mine, other = attention_backward_call(
        core_scalar,
        spread(grad_hidden_1.astype(BF16)),
        head_gains,
        tables,
        mask,
        qkv,
        ready,
        whole,
        weight_out,
    )
    input_grad_1, gain_outer_1 = mixer_back(grad_hidden_1, mine, other, second_in)

    cotangent = lax.ppermute(input_grad_1, "xh", [(1, 0)])
    cotangent, part_kept = lax.optimization_barrier((cotangent, part_kept))
    grad_all = gathered(chosen(cotangent, out_cotangent), ("y", "z", "c"))
    grad_hidden_0, gain_inner_0 = feed_forward_back(
        spread(cotangent), cotangent.astype(F32), hidden_0, ffn_0
    )
    gated, grad_hidden_0 = lax.optimization_barrier((chosen(gated_0, gated_1), grad_hidden_0))
    gated_y = gathered(gated, "y")
    proj_tiles_0, mix_tiles_0, grad_kernel, mine, other = conv_backward_call(
        core_scalar, spread(grad_hidden_0.astype(BF16)), kernel, masks, projected, whole, weight_out
    )
    input_grad_0, gain_outer_0 = mixer_back(grad_hidden_0, mine, other, first_in)

    columns = exchanged(chosen(proj_tiles_0, proj_tiles_1), "y")
    columns = columns.reshape(4 * rows, -1)
    in_parts = product_left(normed_y, columns).reshape(2, 2, plane, -1, in_width // 4)
    mine = lax.dynamic_index_in_dim(in_parts, xl, 1, keepdims=False)
    other = lax.dynamic_index_in_dim(in_parts, 1 - xl, 1, keepdims=False)
    mine = (mine + swapped(other.astype(BF16), "xl").astype(F32)).astype(BF16)
    arrived = exchanged(jnp.moveaxis(mine, 1, 0), PLANE)
    lines = arrived.reshape(4, 4, *arrived.shape[1:]).astype(F32).sum(1)
    kept_lines = lax.dynamic_index_in_dim(lines, section, 1, keepdims=False)
    sent_lines = lax.dynamic_index_in_dim(lines, 1 - section, 1, keepdims=False)
    come = swapped(sent_lines.astype(BF16), "xh").astype(F32)
    lines = chosen(kept_lines, come).reshape(4, -1, 3, channels // 4)
    grad_conv_in = jnp.moveaxis(lines, 0, 2).reshape(conv_in.shape)
    lines = chosen(come, kept_lines)[:, :, : qkv_width // 4]
    grad_attn_qkv = jnp.moveaxis(lines, 0, 1).reshape(attn_qkv.shape)

    columns = exchanged(chosen(mix_tiles_0, mix_tiles_1), "y").reshape(4 * rows, -1)
    out_parts = product_left(columns, gated_y).astype(BF16).reshape(8, -1, channels)
    grad_mixer_out = exchanged(out_parts, ("xl", "z")).astype(F32).sum(0).T[None]

    mine, other = part_grads_call(xl_scalar, inner_all, grad_all, part_kept, part_down)
    mine = (mine + swapped(other, "xl").astype(F32)).astype(BF16)
    arrived = exchanged(mine.reshape(plane, -1, 3 * lanes), PLANE)
    lines = [
        jnp.moveaxis(arrived[:, :, k * lanes : k * lanes + part], 0, 1)
        .reshape(-1, hidden_units)
        .astype(F32)
        for k in range(3)
    ]
    grad_gate_up = jnp.stack(lines[:2])[None]
    grad_down = lines[2].T[None]

    full_kernel = lax.dynamic_update_slice(
        jnp.zeros(conv_kernel.shape, F32), grad_kernel, (0, core * channels)
    )
    small = jnp.concatenate(
        [
            chosen(gain_outer_0, gain_outer_1),
            chosen(gain_inner_0, gain_inner_1),
            full_kernel.reshape(-1),
            head_gain_sums(head_sums).reshape(-1),
        ]
    )
    count = small.shape[0]
    small = jnp.pad(small, (0, -count % 1024)).reshape(-1, 128)
    small = lax.all_gather(small, "c").sum(0)
    small = small + swapped(small, "xl")
    for axis in PLANE:
        copies = jnp.broadcast_to(small, (4, *small.shape))
        small = lax.all_to_all(copies, axis, 0, 0, tiled=True).sum(0)
    come = swapped(small, "xh")
    pair = [chosen(small, come).reshape(-1), chosen(come, small).reshape(-1)]
    grad_norm_gains = jnp.stack([a[: 2 * width].reshape(2, width) for a in pair])
    grad_conv_kernel = pair[0][2 * width : 5 * width].reshape(conv_kernel.shape)
    grad_qk_gains = pair[1][5 * width : count].reshape(qk_gains.shape)

    activations = chosen(result_0, result_1).reshape(1, 1, *shape)
    input_grads = chosen(input_grad_0, input_grad_1).reshape(1, 1, *shape)
    return (
        activations,
        input_grads,
        grad_norm_gains,
        grad_conv_kernel,
        grad_qk_gains,
        grad_conv_in,
        grad_attn_qkv,
        grad_mixer_out,
        grad_gate_up,
        grad_down,
    )


def solution(mesh):
    wide = Mesh(mesh.devices.reshape(2, 2, 4, 4, 2), AXES)
    dp = ("xl", "y", "z")
    everyone = ("xh", "xl", "y", "z")
    in_specs = (
        P(dp, None, "c", None),
        P(dp, None, "c", None),
        P(dp, None, None),
        P(),
        P(),
        P(),
        P(everyone, None, "c"),
        P(everyone, "c"),
        P("xh", "c", None),
        P("xh", None, None, "c"),
        P("xh", "c", None),
    )
    out_specs = (
        P("xh", dp, None, "c", None),
        P("xh", dp, None, "c", None),
        P(),
        P(),
        P(),
        P(everyone, None, "c"),
        P(everyone, "c"),
        P("xh", "c", dp),
        P("xh", None, dp, "c"),
        P("xh", "c", dp),
    )
    return jax.shard_map(local, mesh=wide, in_specs=in_specs, out_specs=out_specs, check_vma=False)
```

```python
import functools

import jax
import jax.numpy as jnp
from jax import lax
from jax.experimental import pallas as pl
from jax.experimental.pallas import tpu as pltpu
from jax.sharding import Mesh
from jax.sharding import PartitionSpec as P

HEADS = 24
KV_HEADS = 8
HEAD_DIM = 64
GROUP = HEADS // KV_HEADS

EPSILON = 1e-05
ROPE_BASE = 1000000.0
MASKED_SCORE = -1e30

F32 = jnp.float32
BF16 = jnp.bfloat16

PLANE = ("y", "z")
AXES = ("xh", "xl", "y", "z", "c")


def product(left, right):
    return jnp.dot(left, right, preferred_element_type=F32)


def product_left(left, right):
    return lax.dot_general(left, right, (((0,), (0,)), ((), ())), preferred_element_type=F32)


def product_right(left, right):
    return lax.dot_general(left, right, (((1,), (1,)), ((), ())), preferred_element_type=F32)


def swapped(shard, axis):
    return lax.ppermute(shard, axis, [(0, 1), (1, 0)])


def spread(own):
    return lax.all_gather(own, "c", tiled=True)


def joined(mine, other):
    return mine + swapped(other, "c").astype(F32)


def mean_last(values):
    return jnp.mean(values, axis=-1, keepdims=True)


def inverse_rms(values):
    return lax.rsqrt(mean_last(values * values) + EPSILON)


def normalize(values):
    return values * inverse_rms(values)


def norm_backward(grad, gain, values):
    inverse = inverse_rms(values)
    normed = values * inverse
    scaled = grad * gain
    grad_gain = jnp.sum(grad * normed, axis=0)
    return inverse * (scaled - normed * mean_last(scaled * normed)), grad_gain


def exchanged(tiles, axes):
    return lax.all_to_all(tiles, axes, 0, 0, tiled=True)


def ffn_grads(grad_active, gate, up):
    sigmoid = jax.nn.sigmoid(gate)
    grad_gate = grad_active * up * sigmoid * (1.0 + gate * (1.0 - sigmoid))
    grad_up = grad_active * gate * sigmoid
    return grad_gate.astype(BF16), grad_up.astype(BF16)


VMEM_LIMIT = 56 * 1024 * 1024


def unit_tiles(units, tile):
    short = units % tile
    tiles = [(0, short)] if short else []
    return tiles + [(at, tile) for at in range(short, units, tile)]


def streamed(tiles, copies, work):
    for copy in copies(0, 0):
        copy.start()
    for k in range(len(tiles)):
        slot = k % 2
        if k + 1 < len(tiles):
            for copy in copies(k + 1, 1 - slot):
                copy.start()
        for copy in copies(k, slot):
            copy.wait()
        work(k, slot)


def ffn_forward_kernel(
    tiles, core_ref, rows_ref, pair_ref, down_ref, gate_ref, up_ref, mine_ref, other_ref,
    pair_buf, down_buf, gate_buf, up_buf, acc_ref, sems, out_sems,
):
    def copies(k, slot):
        at, size = tiles[k]
        return [
            pltpu.make_async_copy(
                pair_ref.at[0, :, pl.ds(at, size)],
                pair_buf.at[slot, :, pl.ds(0, size)],
                sems.at[slot, 0],
            ),
            pltpu.make_async_copy(
                pair_ref.at[1, :, pl.ds(at, size)],
                pair_buf.at[slot, :, pl.ds(size, size)],
                sems.at[slot, 1],
            ),
            pltpu.make_async_copy(
                down_ref.at[pl.ds(at, size)], down_buf.at[slot, pl.ds(0, size)], sems.at[slot, 2]
            ),
        ]

    def kept(k):
        here = (slice(None), pl.ds(*tiles[k]))
        return [
            pltpu.make_async_copy(gate_buf.at[here], gate_ref.at[here], out_sems.at[k, 0]),
            pltpu.make_async_copy(up_buf.at[here], up_ref.at[here], out_sems.at[k, 1]),
        ]

    def work(k, slot):
        at, size = tiles[k]
        both = product(rows_ref[...], pair_buf[slot, :, : 2 * size])
        gate, up = both[:, :size], both[:, size:]
        gate_buf[:, at : at + size] = gate.astype(BF16)
        up_buf[:, at : at + size] = up.astype(BF16)
        for copy in kept(k):
            copy.start()
        active = (gate * jax.nn.sigmoid(gate) * up).astype(BF16)
        part = product(active, down_buf[slot, :size])
        if k == 0:
            acc_ref[...] = part
        else:
            acc_ref[...] += part

    streamed(tiles, copies, work)
    rows_out(acc_ref, core_ref[0], mine_ref, other_ref)
    for k in range(len(tiles)):
        for copy in kept(k):
            copy.wait()


def ffn_backward_kernel(
    tiles, core_ref, rows_ref, gate_ref, up_ref, pair_ref, down_ref, mine_ref, other_ref,
    pair_buf, down_buf, gate_buf, up_buf, acc_ref, sems,
):
    def copies(k, slot):
        at, size = tiles[k]
        columns, place = pl.ds(at, size), pl.ds(0, size)
        return [
            pltpu.make_async_copy(
                down_ref.at[columns], down_buf.at[slot, place], sems.at[slot, 0]
            ),
            pltpu.make_async_copy(
                gate_ref.at[:, columns], gate_buf.at[slot, :, place], sems.at[slot, 1]
            ),
            pltpu.make_async_copy(
                up_ref.at[:, columns], up_buf.at[slot, :, place], sems.at[slot, 2]
            ),
            pltpu.make_async_copy(
                pair_ref.at[0, :, columns], pair_buf.at[slot, :, place], sems.at[slot, 3]
            ),
            pltpu.make_async_copy(
                pair_ref.at[1, :, columns],
                pair_buf.at[slot, :, pl.ds(size, size)],
                sems.at[slot, 4],
            ),
        ]

    def work(k, slot):
        _, size = tiles[k]
        grad_active = product_right(rows_ref[...], down_buf[slot, :size])
        grads = ffn_grads(
            grad_active,
            gate_buf[slot, :, :size].astype(F32),
            up_buf[slot, :, :size].astype(F32),
        )
        part = product_right(jnp.concatenate(grads, axis=1), pair_buf[slot, :, : 2 * size])
        if k == 0:
            acc_ref[...] = part
        else:
            acc_ref[...] += part

    streamed(tiles, copies, work)
    rows_out(acc_ref, core_ref[0], mine_ref, other_ref)


def feed_forward_call(backward, core, rows, pair, down, saved=()):
    count, width = rows.shape
    units = down.shape[0]
    tile = 768
    tiles = unit_tiles(units, tile)
    vmem, any_space = pl.BlockSpec(memory_space=pltpu.VMEM), pl.BlockSpec(memory_space=pl.ANY)
    scalar = pl.BlockSpec(memory_space=pltpu.SMEM)
    out_shape = [
        jax.ShapeDtypeStruct((count // 2, width), F32),
        jax.ShapeDtypeStruct((count // 2, width), BF16),
    ]
    out_specs = [vmem, vmem]
    buffers = [pltpu.VMEM((2, width, 2 * tile), BF16), pltpu.VMEM((2, tile, width), BF16)]
    acc = pltpu.VMEM((count, width), F32)
    if backward:
        body = functools.partial(ffn_backward_kernel, tiles)
        in_specs = [scalar, vmem, any_space, any_space, any_space, any_space]
        buffers += [pltpu.VMEM((2, count, tile), BF16)] * 2
        scratch = [*buffers, acc, pltpu.SemaphoreType.DMA((2, 5))]
    else:
        body = functools.partial(ffn_forward_kernel, tiles)
        in_specs = [scalar, vmem, any_space, any_space]
        out_shape = [jax.ShapeDtypeStruct((count, units), BF16)] * 2 + out_shape
        out_specs = [any_space, any_space, *out_specs]
        buffers += [pltpu.VMEM((count, units), BF16)] * 2
        scratch = [*buffers, acc]
        scratch += [pltpu.SemaphoreType.DMA((2, 3)), pltpu.SemaphoreType.DMA((len(tiles), 2))]
    return pl.pallas_call(
        body,
        in_specs=in_specs,
        out_specs=out_specs,
        out_shape=out_shape,
        scratch_shapes=scratch,
        compiler_params=pltpu.CompilerParams(vmem_limit_bytes=VMEM_LIMIT),
        cost_estimate=pl.CostEstimate(
            flops=6 * count * width * units,
            bytes_accessed=6 * width * units,
            transcendentals=count * units,
        ),
    )(core, rows, *saved, pair, down)


def part_forward_kernel(rows_ref, pair_ref, kept_ref):
    both = product(rows_ref[...], pair_ref[...])
    units = both.shape[1] // 2
    gate, up = both[:, :units], both[:, units:]
    sigmoid = jax.nn.sigmoid(gate)
    silu = gate * sigmoid
    kept_ref[:, :units] = (up * (sigmoid + silu * (1.0 - sigmoid))).astype(BF16)
    kept_ref[:, units : 2 * units] = silu.astype(BF16)
    kept_ref[:, 2 * units :] = (silu * up).astype(BF16)


def part_forward_call(rows, pair):
    tokens, width = rows.shape
    units = pair.shape[1] // 2
    tile = 1024
    return pl.pallas_call(
        part_forward_kernel,
        grid=(tokens // tile,),
        in_specs=[
            pl.BlockSpec((tile, width), lambda i: (i, 0)),
            pl.BlockSpec((width, 2 * units), lambda i: (0, 0)),
        ],
        out_specs=pl.BlockSpec((tile, 3 * units), lambda i: (i, 0)),
        out_shape=jax.ShapeDtypeStruct((tokens, 3 * units), BF16),
        compiler_params=pltpu.CompilerParams(vmem_limit_bytes=VMEM_LIMIT),
        cost_estimate=pl.CostEstimate(
            flops=4 * tokens * width * units,
            bytes_accessed=2 * tokens * (width + 3 * units),
            transcendentals=tokens * units,
        ),
    )(rows, pair)


def accumulated(acc_ref, out_ref, part):
    step = pl.program_id(0)

    @pl.when(step == 0)
    def _():
        acc_ref[...] = part

    @pl.when(step > 0)
    def _():
        acc_ref[...] += part

    @pl.when(step == pl.num_programs(0) - 1)
    def _():
        out_ref[...] = acc_ref[...].astype(BF16)


def part_down_kernel(grad_ref, kept_ref, down_ref, pair_ref, out_ref, acc_ref):
    grad = grad_ref[...]
    units = down_ref.shape[0]
    grad_active = product_right(grad, down_ref[...])
    for k in range(2):
        lanes = slice(k * units, (k + 1) * units)
        pair_ref[:, lanes] = (grad_active * kept_ref[:, lanes].astype(F32)).astype(BF16)
    accumulated(acc_ref, out_ref, product_left(grad, kept_ref[:, 2 * units :]))


def part_pair_kernel(rows_ref, pair_ref, out_ref, acc_ref):
    accumulated(acc_ref, out_ref, product_left(rows_ref[...], pair_ref[...]))


def part_call(kernel, operands, fixed, outs, result, flops):
    tokens = operands[0].shape[0]
    tile = 1024
    by_tokens = lambda width: pl.BlockSpec((tile, width), lambda i: (i, 0))
    entire = lambda shape: pl.BlockSpec(shape, lambda i: (0, 0))
    return pl.pallas_call(
        kernel,
        grid=(tokens // tile,),
        in_specs=[by_tokens(a.shape[1]) for a in operands] + [entire(a.shape) for a in fixed],
        out_specs=[by_tokens(width) for width in outs] + [entire(result)],
        out_shape=[jax.ShapeDtypeStruct((tokens, width), BF16) for width in outs]
        + [jax.ShapeDtypeStruct(result, BF16)],
        scratch_shapes=[pltpu.VMEM(result, F32)],
        compiler_params=pltpu.CompilerParams(vmem_limit_bytes=VMEM_LIMIT),
        cost_estimate=pl.CostEstimate(
            flops=flops,
            bytes_accessed=2 * tokens * sum(a.shape[1] for a in operands),
            transcendentals=0,
        ),
    )(*operands, *fixed)


def part_down_call(grad, kept, down):
    tokens, width = grad.shape
    units = down.shape[0]
    flops = 4 * tokens * width * units
    return part_call(
        part_down_kernel, (grad, kept), (down,), (2 * units,), (width, units), flops
    )


def part_pair_call(inner, pair):
    (tokens, width), columns = inner.shape, pair.shape[1]
    flops = 2 * tokens * width * columns
    return part_call(part_pair_kernel, (inner, pair), (), (), (width, columns), flops)[0]


def load_all(copies):
    for copy in copies:
        copy.start()


def in_time(rows):
    half = rows.shape[0] // 4
    return jnp.concatenate([rows[k * half : (k + 1) * half] for k in (0, 2, 1, 3)], axis=0)


def rows_out(acc_ref, core, mine_ref, other_ref):
    half = mine_ref.shape[0]
    mine_ref[...] = acc_ref[pl.ds(pl.multiple_of(core * half, half), half)]
    rest = acc_ref[pl.ds(pl.multiple_of((1 - core) * half, half), half)]
    other_ref[...] = rest.astype(BF16)


def weight_copies(whole_ref, out_ref, in_buf, out_buf, sems, start):
    size = in_buf.shape[2]
    copies = [
        pltpu.make_async_copy(
            whole_ref.at[:, pl.ds(start + k * size, size)], in_buf.at[k], sems.at[k]
        )
        for k in range(in_buf.shape[0])
    ]
    return copies, pltpu.make_async_copy(out_ref, out_buf, sems.at[len(copies)])


def conv_taps(mixed, kernel, masks):
    terms = [mixed]
    for lag in range(1, len(masks) + 1):
        terms.append(pltpu.roll(mixed, lag, 0) * masks[lag - 1])
    taps = kernel.shape[0]
    total = kernel[taps - 1 : taps] * terms[0]
    for lag in range(1, taps):
        total = total + kernel[taps - 1 - lag : taps - lag] * terms[lag]
    return terms, total


def conv_forward_kernel(
    core_ref, rows_ref, kernel_ref, masks_ref, whole_ref, out_ref,
    proj_ref, gated_ref, mine_ref, other_ref, in_buf, out_buf, acc_ref, sems,
):
    copies, last = weight_copies(whole_ref, out_ref, in_buf, out_buf, sems, 0)
    load_all([*copies, last])
    rows = rows_ref[...]
    parts = []
    for k, copy in enumerate(copies):
        copy.wait()
        part = product(rows, in_buf[k])
        proj_ref[k] = part.astype(BF16)
        parts.append(in_time(part))
    masks = [masks_ref[lag] for lag in range(masks_ref.shape[0])]
    gated = []
    for at in range(0, parts[0].shape[1], 128):
        before, after, signal = [part[:, at : at + 128] for part in parts]
        _, total = conv_taps(before * signal, kernel_ref[:, at : at + 128], masks)
        gated.append((after * total).astype(BF16))
    gated = in_time(jnp.concatenate(gated, axis=1))
    gated_ref[...] = gated
    last.wait()
    acc_ref[...] = product(gated, out_buf[...])
    rows_out(acc_ref, core_ref[0], mine_ref, other_ref)


def tiles_out(tiles_ref, mix_ref, grad_mix, columns):
    for k in range(tiles_ref.shape[0]):
        tiles_ref[k] = columns(k)
    width = grad_mix.shape[1] // 2
    step = width // mix_ref.shape[0]
    for k in range(mix_ref.shape[0]):
        mix_ref[k] = jnp.concatenate(
            [grad_mix[:, h * width + k * step : h * width + (k + 1) * step] for h in range(2)],
            axis=1,
        )


def conv_backward_kernel(
    core_ref, grad_ref, kernel_ref, masks_ref, proj_ref, whole_ref, out_ref,
    tiles_ref, mix_ref, taps_ref, mine_ref, other_ref, in_buf, out_buf, acc_ref, sems,
):
    copies, last = weight_copies(whole_ref, out_ref, in_buf, out_buf, sems, 0)
    load_all([last, *copies])
    last.wait()
    grad_gated = in_time(product_right(grad_ref[...], out_buf[...]))
    parts = [in_time(proj_ref[k].astype(F32)) for k in range(3)]
    masks = [masks_ref[lag] for lag in range(masks_ref.shape[0])]
    rows = grad_gated.shape[0]
    grads = [[], [], []]
    for at in range(0, grad_gated.shape[1], 128):
        before, after, signal = [part[:, at : at + 128] for part in parts]
        kernel = kernel_ref[:, at : at + 128]
        terms, total = conv_taps(before * signal, kernel, masks)
        grad = grad_gated[:, at : at + 128]
        grad_total = grad * after
        taps = kernel.shape[0]
        grad_mixed = kernel[taps - 1 : taps] * grad_total
        for lag in range(1, taps):
            sent = pltpu.roll(grad_total * masks[lag - 1], rows - lag, 0)
            grad_mixed = grad_mixed + kernel[taps - 1 - lag : taps - lag] * sent
        for lag in range(taps):
            taps_ref[taps - 1 - lag : taps - lag, at : at + 128] = jnp.sum(
                grad_total * terms[lag], axis=0, keepdims=True
            )
        for k, value in enumerate((grad_mixed * signal, grad * total, grad_mixed * before)):
            grads[k].append(value.astype(BF16))
    grads = [in_time(jnp.concatenate(g, axis=1)) for g in grads]
    step = grads[0].shape[1] // tiles_ref.shape[0]
    tiles_out(
        tiles_ref,
        mix_ref,
        grad_ref[...],
        lambda k: jnp.concatenate([g[:, k * step : (k + 1) * step] for g in grads], axis=1),
    )
    for k, copy in enumerate(copies):
        copy.wait()
        part = product_right(grads[k], in_buf[k])
        acc_ref[...] = part if k == 0 else acc_ref[...] + part
    rows_out(acc_ref, core_ref[0], mine_ref, other_ref)


def head_kind(head):
    return min(max(head % (GROUP + 2) - GROUP + 1, 0), 2)


def lane_facts(rows):
    lane = lax.broadcasted_iota(jnp.int32, (rows, 128), 1)
    return lane < HEAD_DIM, lax.rem(lane, HEAD_DIM) < HEAD_DIM // 2


def head_scales(block, low):
    squares = block * block
    first = jnp.sum(jnp.where(low, squares, 0.0), axis=1, keepdims=True)
    second = jnp.sum(jnp.where(low, 0.0, squares), axis=1, keepdims=True)
    return lax.rsqrt(jnp.where(low, first, second) * (1.0 / HEAD_DIM) + EPSILON)


def block_gains(gains_ref, at):
    heads = [head_kind(2 * at), head_kind(2 * at + 1)]
    return heads, gains_ref[3 * heads[0] + heads[1] : 3 * heads[0] + heads[1] + 1]


def attention_forward_kernel(
    core_ref, rows_ref, gains_ref, tables_ref, mask_ref, whole_ref, out_ref,
    qkv_ref, ready_ref, gated_ref, mine_ref, other_ref, in_buf, out_buf, acc_ref, sems,
):
    copies, last = weight_copies(
        whole_ref, out_ref, in_buf, out_buf, sems, whole_ref.shape[1] - in_buf.shape[2]
    )
    load_all([*copies, last])
    copies[0].wait()
    qkv_ref[...] = product(rows_ref[...], in_buf[0])
    rows, width = qkv_ref.shape
    low, front = lane_facts(rows)
    cosine, sine = tables_ref[0], tables_ref[1]
    for at in range(width // 128):
        block = qkv_ref[:, at * 128 : (at + 1) * 128]
        heads, gains = block_gains(gains_ref, at)
        normed = block * head_scales(block, low) * gains
        turned = jnp.where(front, -pltpu.roll(normed, 96, 1), pltpu.roll(normed, 32, 1))
        ready = normed * cosine + turned * sine
        if heads[0] == 2:
            ready = jnp.where(low, block, ready)
        if heads[1] == 2:
            ready = jnp.where(low, ready, block)
        ready_ref[:, at * 128 : (at + 1) * 128] = ready.astype(BF16)
    half = rows // 4
    span = (GROUP + 2) * HEAD_DIM
    for m in range(2):
        mask = mask_ref[m] > 0
        mask = jnp.concatenate([mask] * GROUP, axis=0)
        for g in range(width // span):
            queries, keys, values = head_rows(ready_ref, m, half, g * span)
            weights = softmax_weights(queries, keys, mask)
            attended = product(weights.astype(BF16), values).astype(BF16)
            for j in range(GROUP):
                at = (g * GROUP + j) * HEAD_DIM
                head = attended[j * 2 * half : (j + 1) * 2 * half]
                gated_ref[m * half : (m + 1) * half, at : at + HEAD_DIM] = head[:half]
                gated_ref[(m + 2) * half : (m + 3) * half, at : at + HEAD_DIM] = head[half:]
    last.wait()
    acc_ref[...] = product(gated_ref[...], out_buf[...])
    rows_out(acc_ref, core_ref[0], mine_ref, other_ref)


def sequence(ref, m, half, at):
    columns = slice(at, at + HEAD_DIM)
    return jnp.concatenate(
        [ref[m * half : (m + 1) * half, columns], ref[(m + 2) * half : (m + 3) * half, columns]],
        axis=0,
    )


def head_rows(ref, m, half, at):
    heads = [sequence(ref, m, half, at + j * HEAD_DIM) for j in range(GROUP + 2)]
    return jnp.concatenate(heads[:GROUP], axis=0), heads[GROUP], heads[GROUP + 1]


def softmax_weights(queries, keys, mask):
    scores = jnp.where(mask, product_right(queries, keys) * HEAD_DIM ** (-0.5), MASKED_SCORE)
    terms = jnp.exp(scores - jnp.max(scores, axis=1, keepdims=True))
    return terms / jnp.sum(terms, axis=1, keepdims=True)


def attention_backward_kernel(
    core_ref, grad_ref, gains_ref, tables_ref, mask_ref, qkv_ref, ready_ref, whole_ref, out_ref,
    tiles_ref, mix_ref, heads_ref, mine_ref, other_ref,
    in_buf, out_buf, acc_ref, attended_ref, ready_grad_ref, proj_ref, sems,
):
    copies, last = weight_copies(
        whole_ref, out_ref, in_buf, out_buf, sems, whole_ref.shape[1] - in_buf.shape[2]
    )
    load_all([last, *copies])
    last.wait()
    attended_ref[...] = product_right(grad_ref[...], out_buf[...]).astype(BF16)
    rows, width = qkv_ref.shape
    half = rows // 4
    span = (GROUP + 2) * HEAD_DIM
    scale = HEAD_DIM ** (-0.5)
    for m in range(2):
        mask = mask_ref[m] > 0
        mask = jnp.concatenate([mask] * GROUP, axis=0)
        for g in range(width // span):
            queries, keys, values = head_rows(ready_ref, m, half, g * span)
            weights = softmax_weights(queries, keys, mask)
            grad = jnp.concatenate(
                [
                    sequence(attended_ref, m, half, (g * GROUP + j) * HEAD_DIM)
                    for j in range(GROUP)
                ],
                axis=0,
            )
            grad_values = product_left(weights.astype(BF16), grad)
            grad_weights = product_right(grad, values)
            mean = jnp.sum(grad_weights * weights, axis=1, keepdims=True)
            grad_scores = (weights * (grad_weights - mean)).astype(BF16)
            grad_queries = product(grad_scores, keys) * scale
            grad_keys = product_left(grad_scores, queries) * scale
            outs = [grad_queries[j * 2 * half : (j + 1) * 2 * half] for j in range(GROUP)]
            for j, out in enumerate([*outs, grad_keys, grad_values]):
                at = g * span + j * HEAD_DIM
                ready_grad_ref[m * half : (m + 1) * half, at : at + HEAD_DIM] = out[:half]
                ready_grad_ref[(m + 2) * half : (m + 3) * half, at : at + HEAD_DIM] = out[half:]
    low, front = lane_facts(rows)
    cosine, sine = tables_ref[0], tables_ref[1]
    for at in range(width // 128):
        lanes = slice(at * 128, (at + 1) * 128)
        block, grad = qkv_ref[:, lanes], ready_grad_ref[:, lanes]
        heads, gains = block_gains(gains_ref, at)
        inverse = head_scales(block, low)
        normed = block * inverse
        turned = grad * sine
        grad_normed = grad * cosine + jnp.where(
            front, pltpu.roll(turned, 96, 1), -pltpu.roll(turned, 32, 1)
        )
        heads_ref[at : at + 1] = jnp.sum(grad_normed * normed, axis=0, keepdims=True)
        grad_normed = grad_normed * gains
        along = grad_normed * normed
        first = jnp.sum(jnp.where(low, along, 0.0), axis=1, keepdims=True)
        second = jnp.sum(jnp.where(low, 0.0, along), axis=1, keepdims=True)
        mean = jnp.where(low, first, second) * (1.0 / HEAD_DIM)
        raw = inverse * (grad_normed - normed * mean)
        if heads[0] == 2:
            raw = jnp.where(low, grad, raw)
        if heads[1] == 2:
            raw = jnp.where(low, raw, grad)
        proj_ref[:, lanes] = raw.astype(BF16)
    step = width // tiles_ref.shape[0]
    spare = jnp.zeros((rows, tiles_ref.shape[2] - step), BF16)
    tiles_out(
        tiles_ref,
        mix_ref,
        grad_ref[...],
        lambda k: jnp.concatenate([proj_ref[:, k * step : (k + 1) * step], spare], axis=1),
    )
    copies[0].wait()
    acc_ref[...] = product_right(proj_ref[...], in_buf[0])
    rows_out(acc_ref, core_ref[0], mine_ref, other_ref)


def mixer_call(kernel, core, operands, whole, weight_out, in_tiles, outs, scratch=(), flops=0):
    vmem, any_space = pl.BlockSpec(memory_space=pltpu.VMEM), pl.BlockSpec(memory_space=pl.ANY)
    rows, width = operands[0].shape
    channels = weight_out.shape[0]
    outs = [*outs, ((rows // 2, width), F32), ((rows // 2, width), BF16)]
    return pl.pallas_call(
        kernel,
        in_specs=[
            pl.BlockSpec(memory_space=pltpu.SMEM),
            *[vmem] * len(operands),
            any_space,
            any_space,
        ],
        out_specs=[vmem] * len(outs),
        out_shape=[jax.ShapeDtypeStruct(*out) for out in outs],
        scratch_shapes=[
            pltpu.VMEM((in_tiles[0], width, in_tiles[1]), BF16),
            pltpu.VMEM((channels, width), BF16),
            pltpu.VMEM((rows, width), F32),
            *scratch,
            pltpu.SemaphoreType.DMA((in_tiles[0] + 1,)),
        ],
        compiler_params=pltpu.CompilerParams(vmem_limit_bytes=VMEM_LIMIT),
        cost_estimate=pl.CostEstimate(
            flops=2 * rows * width * (channels + in_tiles[0] * in_tiles[1]),
            bytes_accessed=2 * width * (channels + in_tiles[0] * in_tiles[1]),
            transcendentals=rows * width,
        ),
    )(core, *operands, whole, weight_out)


def conv_forward_call(core, rows, kernel, masks, whole, weight_out):
    count, channels = rows.shape[0], kernel.shape[1]
    outs = [((3, count, channels), BF16), ((count, channels), BF16)]
    operands = (rows, kernel, masks)
    return mixer_call(
        conv_forward_kernel, core, operands, whole, weight_out, (3, channels), outs
    )


def conv_backward_call(core, grad, kernel, masks, projected, whole, weight_out):
    count, width = grad.shape
    taps, channels = kernel.shape
    outs = [
        ((8, count, 3 * channels // 8), BF16),
        ((4, count, width // 4), BF16),
        ((taps, channels), F32),
    ]
    operands = (grad, kernel, masks, projected)
    return mixer_call(
        conv_backward_kernel, core, operands, whole, weight_out, (3, channels), outs
    )


def attention_forward_call(core, rows, gains, tables, mask, whole, weight_out, qkv_width):
    count, channels = rows.shape[0], weight_out.shape[0]
    outs = [((count, qkv_width), F32), ((count, qkv_width), BF16), ((count, channels), BF16)]
    operands = (rows, gains, tables, mask)
    return mixer_call(
        attention_forward_kernel, core, operands, whole, weight_out, (1, qkv_width), outs
    )


def attention_backward_call(core, grad, gains, tables, mask, qkv, ready, whole, weight_out):
    count, width = grad.shape
    channels, qkv_width = weight_out.shape[0], qkv.shape[1]
    outs = [
        ((8, count, 3 * channels // 8), BF16),
        ((4, count, width // 4), BF16),
        ((qkv_width // 128, 128), F32),
    ]
    scratch = [
        pltpu.VMEM((count, channels), BF16),
        pltpu.VMEM((count, qkv_width), F32),
        pltpu.VMEM((count, qkv_width), BF16),
    ]
    operands = (grad, gains, tables, mask, qkv, ready)
    return mixer_call(
        attention_backward_kernel, core, operands, whole, weight_out, (1, qkv_width), outs, scratch
    )


def conv_masks(segments, taps):
    masks = []
    for lag in range(1, taps):
        same = (segments[:, lag:] == segments[:, :-lag]).astype(F32)
        same = jnp.pad(same, ((0, 0), (lag, 0))).reshape(-1, 1)
        masks.append(jnp.broadcast_to(same, (same.shape[0], 128)))
    return jnp.stack(masks)


def score_mask(segments):
    position = jnp.arange(segments.shape[1])
    allowed = position[:, None] >= position[None, :]
    return (allowed & (segments[:, :, None] == segments[:, None, :])).astype(F32)


def turn_tables(length):
    half = HEAD_DIM // 2
    exponent = jnp.arange(half, dtype=F32) * (2.0 / HEAD_DIM)
    frequency = jnp.exp(-exponent * jnp.log(ROPE_BASE))
    angles = jnp.arange(length, dtype=F32)[:, None] * frequency[None, :]
    tables = jnp.tile(jnp.stack([jnp.cos(angles), jnp.sin(angles)]), (1, 1, 4))
    tables = tables.reshape(2, 2, 1, length // 2, 128)
    return jnp.broadcast_to(tables, (2, 2, 2, length // 2, 128)).reshape(2, 2 * length, 128)


def gain_rows(head_gains):
    kinds = [head_gains[0], head_gains[1], jnp.ones_like(head_gains[0])]
    rows = [jnp.concatenate([a, b]) for a in kinds for b in kinds]
    return jnp.stack(rows)


def head_gain_sums(sums):
    heads = sums.reshape(-1, GROUP + 2, HEAD_DIM)
    return jnp.stack([heads[:, :GROUP].sum((0, 1)), heads[:, GROUP].sum(0)])


def local(
    inputs,
    out_cotangent,
    segments,
    norm_gains,
    conv_kernel,
    qk_gains,
    conv_in,
    attn_qkv,
    mixer_out,
    gate_up,
    down,
):
    section = lax.axis_index("xh")
    first = section == 0
    core = lax.axis_index("c")
    place = lax.axis_index("y") * 4 + lax.axis_index("z")
    xl = lax.axis_index("xl")
    plane = lax.axis_size("y") * lax.axis_size("z")

    shape = inputs.shape[1:]
    width = shape[-1]
    inputs, out_cotangent = inputs.reshape(-1, width), out_cotangent.reshape(-1, width)
    segments = segments[0]
    half = inputs.shape[0]
    rows = 2 * half
    channels = conv_in.shape[2]
    kernel = lax.dynamic_slice_in_dim(conv_kernel, core * channels, channels, 1).astype(F32)
    gains = lax.dynamic_index_in_dim(norm_gains, section, 0, keepdims=False).astype(F32)
    weight_out, weight_pair, weight_down = mixer_out[0], gate_up[0], down[0]
    hidden_units = weight_down.shape[0]
    part = hidden_units // plane
    in_width = 3 * channels
    qkv_width = attn_qkv.shape[1]
    core_scalar = core.astype(jnp.int32)[None]

    def chosen(from_first, from_second):
        return jnp.where(first, from_first, from_second)

    def gathered(own, axes):
        return lax.all_gather(own, axes, tiled=True)

    everyone = ("xh", "xl", "y", "z")
    whole = gathered(conv_in.reshape(-1, in_width), everyone)

    lanes = -(-part // 256) * 256
    fill = lanes - part
    part_pair = jnp.concatenate(
        [
            jnp.pad(lax.dynamic_slice_in_dim(w, place * part, part, 1), ((0, 0), (0, fill)))
            for w in (weight_pair[0], weight_pair[1])
        ],
        axis=1,
    )
    part_down = lax.dynamic_slice_in_dim(weight_down, place * part, part, 0)
    part_down = jnp.pad(part_down, ((0, fill), (0, 0)))
    masks = conv_masks(segments, kernel.shape[0])
    mask = score_mask(segments)
    tables = turn_tables(segments.shape[1])
    head_gains = gain_rows(qk_gains.astype(F32))
    first_in = inputs.astype(F32)
    normed_own_0 = (normalize(first_in) * gains[0]).astype(BF16)
    normed_0 = spread(normed_own_0)
    cotangent_1 = spread(out_cotangent)
    whole, part_pair, part_down, masks, mask, tables, head_gains, normed_0, cotangent_1 = (
        lax.optimization_barrier(
            (whole, part_pair, part_down, masks, mask, tables, head_gains, normed_0, cotangent_1)
        )
    )

    def feed_forward(hidden):
        inner_own = (normalize(hidden) * gains[1]).astype(BF16)
        gate, up, mine, other = feed_forward_call(
            False, core_scalar, spread(inner_own), weight_pair, weight_down
        )
        return hidden + joined(mine, other), (inner_own, gate, up)

    def feed_forward_back(grad_full, grad, hidden, saved):
        mine, other = feed_forward_call(
            True, core_scalar, grad_full, weight_pair, weight_down, saved[1:]
        )
        back, grad_gain = norm_backward(joined(mine, other), gains[1], hidden)
        return grad + back, grad_gain

    def mixer_back(grad_hidden, mine, other, layer_in):
        back, grad_gain = norm_backward(joined(mine, other), gains[0], layer_in)
        return (grad_hidden + back).astype(BF16), grad_gain

    attn_qkv, _ = lax.optimization_barrier((attn_qkv, whole[:8, :128]))
    whole_qkv = gathered(attn_qkv, everyone)

    projected, gated_0, mine, other = conv_forward_call(
        core_scalar, normed_0, kernel, masks, whole, weight_out
    )
    hidden_0 = first_in + joined(mine, other)
    result_0, ffn_0 = feed_forward(hidden_0)
    result_0 = result_0.astype(BF16)

    second_in = lax.ppermute(result_0, "xh", [(0, 1)]).astype(F32)
    normed_own_1 = (normalize(second_in) * gains[0]).astype(BF16)
    normed_own = chosen(normed_own_0, normed_own_1)
    across = swapped(normed_own, "xl")
    pair = [jnp.where(xl == 0, normed_own, across), jnp.where(xl == 0, across, normed_own)]
    normed_near = gathered(jnp.concatenate(pair), ("y", "c"))
    qkv, ready, gated_1, mine, other = attention_forward_call(
        core_scalar, spread(normed_own_1), head_gains, tables, mask, whole_qkv, weight_out, qkv_width
    )
    hidden_1 = second_in + joined(mine, other)
    result_1, ffn_1 = feed_forward(hidden_1)
    result_1 = result_1.astype(BF16)

    inner_own, normed_near = lax.optimization_barrier(
        (chosen(ffn_0[0], ffn_1[0]), normed_near)
    )
    inner_all = gathered(inner_own, ("y", "z", "c"))
    part_kept = part_forward_call(inner_all, part_pair)

    grad_hidden_1, gain_inner_1 = feed_forward_back(
        cotangent_1, out_cotangent.astype(F32), hidden_1, ffn_1
    )
    proj_tiles_1, mix_tiles_1, head_sums, mine, other = attention_backward_call(
        core_scalar,
        spread(grad_hidden_1.astype(BF16)),
        head_gains,
        tables,
        mask,
        qkv,
        ready,
        whole_qkv,
        weight_out,
    )
    input_grad_1, gain_outer_1 = mixer_back(grad_hidden_1, mine, other, second_in)

    cotangent = lax.ppermute(input_grad_1, "xh", [(1, 0)])
    grad_all = gathered(chosen(cotangent, out_cotangent), ("y", "z", "c"))
    gated, _ = lax.optimization_barrier((chosen(gated_0, gated_1), input_grad_1))
    gated_y = exchanged(jnp.broadcast_to(gated, (4, *gated.shape)), "y").reshape(4 * rows, -1)
    grad_hidden_0, gain_inner_0 = feed_forward_back(
        spread(cotangent), cotangent.astype(F32), hidden_0, ffn_0
    )
    proj_tiles_0, mix_tiles_0, grad_kernel, mine, other = conv_backward_call(
        core_scalar, spread(grad_hidden_0.astype(BF16)), kernel, masks, projected, whole, weight_out
    )
    input_grad_0, gain_outer_0 = mixer_back(grad_hidden_0, mine, other, first_in)

    columns = exchanged(chosen(proj_tiles_0, proj_tiles_1), ("xl", "y"))
    columns = columns.reshape(2, 4, 2, half, -1).transpose(1, 2, 0, 3, 4).reshape(8 * rows, -1)
    in_parts = product_left(normed_near, columns).astype(BF16)
    in_parts = jnp.moveaxis(in_parts.reshape(2, 2 * plane, -1, in_width // 8), 0, 1)
    arrived = exchanged(in_parts, ("xl", "y", "z"))
    lines = arrived.reshape(8, 4, *arrived.shape[1:]).astype(F32).sum(1)
    kept_lines = lax.dynamic_index_in_dim(lines, section, 1, keepdims=False)
    sent_lines = lax.dynamic_index_in_dim(lines, 1 - section, 1, keepdims=False)
    come = swapped(sent_lines.astype(BF16), "xh").astype(F32)
    lines = chosen(kept_lines, come).reshape(8, -1, 3, channels // 8)
    grad_conv_in = jnp.moveaxis(lines, 0, 2).reshape(conv_in.shape)
    lines = chosen(come, kept_lines)[:, :, : qkv_width // 8]
    grad_attn_qkv = jnp.moveaxis(lines, 0, 1).reshape(attn_qkv.shape)

    columns = exchanged(chosen(mix_tiles_0, mix_tiles_1), "y").reshape(4 * rows, -1)
    out_parts = product_left(columns, gated_y).astype(BF16).reshape(8, -1, channels)
    grad_mixer_out = exchanged(out_parts, ("xl", "z")).astype(F32).sum(0).T[None]

    def finished(parts):
        columns = parts.shape[1]
        arrived = exchanged(parts.reshape(2 * plane, -1, columns), ("xl", "y", "z"))
        total = arrived.reshape(2, plane, -1, columns).astype(F32).sum(0)
        return [
            jnp.moveaxis(total[:, :, at : at + part], 0, 1).reshape(-1, hidden_units)
            for at in range(0, columns, lanes)
        ]

    pair_grads, down_parts = part_down_call(grad_all, part_kept, part_down)
    grad_down = finished(down_parts)[0].T[None]
    grad_gate_up = jnp.stack(finished(part_pair_call(inner_all, pair_grads)))[None]

    full_kernel = lax.dynamic_update_slice(
        jnp.zeros(conv_kernel.shape, F32), grad_kernel, (0, core * channels)
    )
    small = jnp.concatenate(
        [
            chosen(gain_outer_0, gain_outer_1),
            chosen(gain_inner_0, gain_inner_1),
            full_kernel.reshape(-1),
            head_gain_sums(head_sums).reshape(-1),
        ]
    )
    count = small.shape[0]
    small = jnp.pad(small, (0, -count % 1024)).reshape(-1, 128)
    small = lax.all_gather(small, "c").sum(0)
    small = small + swapped(small, "xl")
    small = exchanged(jnp.broadcast_to(small, (plane, *small.shape)), PLANE).sum(0)
    come = swapped(small, "xh")
    pair = [chosen(small, come).reshape(-1), chosen(come, small).reshape(-1)]
    grad_norm_gains = jnp.stack([a[: 2 * width].reshape(2, width) for a in pair])
    grad_conv_kernel = pair[0][2 * width : 5 * width].reshape(conv_kernel.shape)
    grad_qk_gains = pair[1][5 * width : count].reshape(qk_gains.shape)

    activations = chosen(result_0, result_1).reshape(1, 1, *shape)
    input_grads = chosen(input_grad_0, input_grad_1).reshape(1, 1, *shape)
    return (
        activations,
        input_grads,
        grad_norm_gains,
        grad_conv_kernel,
        grad_qk_gains,
        grad_conv_in,
        grad_attn_qkv,
        grad_mixer_out,
        grad_gate_up,
        grad_down,
    )


def solution(mesh):
    wide = Mesh(mesh.devices.reshape(2, 2, 4, 4, 2), AXES)
    dp = ("xl", "y", "z")
    everyone = ("xh", "xl", "y", "z")
    in_specs = (
        P(dp, None, "c", None),
        P(dp, None, "c", None),
        P(dp, None, None),
        P(),
        P(),
        P(),
        P(everyone, None, "c"),
        P(everyone, "c"),
        P("xh", "c", None),
        P("xh", None, None, "c"),
        P("xh", "c", None),
    )
    out_specs = (
        P("xh", dp, None, "c", None),
        P("xh", dp, None, "c", None),
        P(),
        P(),
        P(),
        P(everyone, None, "c"),
        P(everyone, "c"),
        P("xh", "c", dp),
        P("xh", None, dp, "c"),
        P("xh", "c", dp),
    )
    return jax.shard_map(local, mesh=wide, in_specs=in_specs, out_specs=out_specs, check_vma=False)
```

```python
import functools

import jax
import jax.numpy as jnp
from jax import lax
from jax.experimental import pallas as pl
from jax.experimental.pallas import tpu as pltpu
from jax.sharding import Mesh
from jax.sharding import PartitionSpec as P

HEADS = 24
KV_HEADS = 8
HEAD_DIM = 64
GROUP = HEADS // KV_HEADS

EPSILON = 1e-05
ROPE_BASE = 1000000.0
MASKED_SCORE = -1e30

F32 = jnp.float32
BF16 = jnp.bfloat16

PLANE = ("y", "z")
AXES = ("xh", "xl", "y", "z", "c")


def product(left, right):
    return jnp.dot(left, right, preferred_element_type=F32)


def product_left(left, right):
    return lax.dot_general(left, right, (((0,), (0,)), ((), ())), preferred_element_type=F32)


def product_right(left, right):
    return lax.dot_general(left, right, (((1,), (1,)), ((), ())), preferred_element_type=F32)


def swapped(shard, axis):
    return lax.ppermute(shard, axis, [(0, 1), (1, 0)])


def spread(own):
    return lax.all_gather(own, "c", tiled=True)


def joined(mine, other):
    return mine + swapped(other, "c").astype(F32)


def mean_last(values):
    return jnp.mean(values, axis=-1, keepdims=True)


def inverse_rms(values):
    return lax.rsqrt(mean_last(values * values) + EPSILON)


def normalize(values):
    return values * inverse_rms(values)


def norm_backward(grad, gain, values):
    inverse = inverse_rms(values)
    normed = values * inverse
    scaled = grad * gain
    grad_gain = jnp.sum(grad * normed, axis=0)
    return inverse * (scaled - normed * mean_last(scaled * normed)), grad_gain


def exchanged(tiles, axes):
    return lax.all_to_all(tiles, axes, 0, 0, tiled=True)


def ffn_grads(grad_active, gate, up):
    sigmoid = jax.nn.sigmoid(gate)
    grad_gate = grad_active * up * sigmoid * (1.0 + gate * (1.0 - sigmoid))
    grad_up = grad_active * gate * sigmoid
    return grad_gate.astype(BF16), grad_up.astype(BF16)


VMEM_LIMIT = 56 * 1024 * 1024
SHORT = pl.CostEstimate(flops=1, bytes_accessed=1, transcendentals=0)


def whole_lanes(columns):
    return -(-columns // 128) * 128


def ordered(kernel, count):
    def body(scalar_ref, *refs):
        kernel(scalar_ref, *refs[count:])

    return body


def unit_tiles(units, tile):
    short = units % tile
    tiles = [(0, short)] if short else []
    return tiles + [(at, tile) for at in range(short, units, tile)]


def streamed(tiles, copies, work):
    for copy in copies(0, 0):
        copy.start()
    for k in range(len(tiles)):
        slot = k % 2
        if k + 1 < len(tiles):
            for copy in copies(k + 1, 1 - slot):
                copy.start()
        for copy in copies(k, slot):
            copy.wait()
        work(k, slot)


def ffn_forward_kernel(
    tiles, core_ref, rows_ref, pair_ref, down_ref, gate_ref, up_ref, mine_ref, other_ref,
    pair_buf, down_buf, gate_buf, up_buf, acc_ref, sems, out_sems,
):
    def copies(k, slot):
        at, size = tiles[k]
        return [
            pltpu.make_async_copy(
                pair_ref.at[0, :, pl.ds(at, size)],
                pair_buf.at[slot, :, pl.ds(0, size)],
                sems.at[slot, 0],
            ),
            pltpu.make_async_copy(
                pair_ref.at[1, :, pl.ds(at, size)],
                pair_buf.at[slot, :, pl.ds(size, size)],
                sems.at[slot, 1],
            ),
            pltpu.make_async_copy(
                down_ref.at[pl.ds(at, size)], down_buf.at[slot, pl.ds(0, size)], sems.at[slot, 2]
            ),
        ]

    def kept(k):
        here = (slice(None), pl.ds(*tiles[k]))
        return [
            pltpu.make_async_copy(gate_buf.at[here], gate_ref.at[here], out_sems.at[k, 0]),
            pltpu.make_async_copy(up_buf.at[here], up_ref.at[here], out_sems.at[k, 1]),
        ]

    def work(k, slot):
        at, size = tiles[k]
        both = product(rows_ref[...], pair_buf[slot, :, : 2 * size])
        gate, up = both[:, :size], both[:, size:]
        gate_buf[:, at : at + size] = gate.astype(BF16)
        up_buf[:, at : at + size] = up.astype(BF16)
        for copy in kept(k):
            copy.start()
        active = (gate * jax.nn.sigmoid(gate) * up).astype(BF16)
        part = product(active, down_buf[slot, :size])
        if k == 0:
            acc_ref[...] = part
        else:
            acc_ref[...] += part

    streamed(tiles, copies, work)
    rows_out(acc_ref, core_ref[0], mine_ref, other_ref)
    for k in range(len(tiles)):
        for copy in kept(k):
            copy.wait()


def ffn_backward_kernel(
    tiles, core_ref, rows_ref, gate_ref, up_ref, pair_ref, down_ref, mine_ref, other_ref,
    pair_buf, down_buf, gate_buf, up_buf, acc_ref, sems,
):
    def copies(k, slot):
        at, size = tiles[k]
        columns, place = pl.ds(at, size), pl.ds(0, size)
        return [
            pltpu.make_async_copy(
                down_ref.at[columns], down_buf.at[slot, place], sems.at[slot, 0]
            ),
            pltpu.make_async_copy(
                gate_ref.at[:, columns], gate_buf.at[slot, :, place], sems.at[slot, 1]
            ),
            pltpu.make_async_copy(
                up_ref.at[:, columns], up_buf.at[slot, :, place], sems.at[slot, 2]
            ),
            pltpu.make_async_copy(
                pair_ref.at[0, :, columns], pair_buf.at[slot, :, place], sems.at[slot, 3]
            ),
            pltpu.make_async_copy(
                pair_ref.at[1, :, columns],
                pair_buf.at[slot, :, pl.ds(size, size)],
                sems.at[slot, 4],
            ),
        ]

    def work(k, slot):
        _, size = tiles[k]
        grad_active = product_right(rows_ref[...], down_buf[slot, :size])
        grads = ffn_grads(
            grad_active,
            gate_buf[slot, :, :size].astype(F32),
            up_buf[slot, :, :size].astype(F32),
        )
        part = product_right(jnp.concatenate(grads, axis=1), pair_buf[slot, :, : 2 * size])
        if k == 0:
            acc_ref[...] = part
        else:
            acc_ref[...] += part

    streamed(tiles, copies, work)
    rows_out(acc_ref, core_ref[0], mine_ref, other_ref)


def feed_forward_call(backward, core, rows, pair, down, saved=(), behind=()):
    count, width = rows.shape
    units = down.shape[0]
    tile = 768
    tiles = unit_tiles(units, tile)
    vmem, any_space = pl.BlockSpec(memory_space=pltpu.VMEM), pl.BlockSpec(memory_space=pl.ANY)
    scalar = pl.BlockSpec(memory_space=pltpu.SMEM)
    out_shape = [
        jax.ShapeDtypeStruct((count // 2, width), F32),
        jax.ShapeDtypeStruct((count // 2, width), BF16),
    ]
    out_specs = [vmem, vmem]
    buffers = [pltpu.VMEM((2, width, 2 * tile), BF16), pltpu.VMEM((2, tile, width), BF16)]
    acc = pltpu.VMEM((count, width), F32)
    if backward:
        body = functools.partial(ffn_backward_kernel, tiles)
        in_specs = [scalar, vmem, any_space, any_space, any_space, any_space]
        buffers += [pltpu.VMEM((2, count, tile), BF16)] * 2
        scratch = [*buffers, acc, pltpu.SemaphoreType.DMA((2, 5))]
    else:
        body = functools.partial(ffn_forward_kernel, tiles)
        in_specs = [scalar, vmem, any_space, any_space]
        out_shape = [jax.ShapeDtypeStruct((count, units), BF16)] * 2 + out_shape
        out_specs = [any_space, any_space, *out_specs]
        buffers += [pltpu.VMEM((count, units), BF16)] * 2
        scratch = [*buffers, acc]
        scratch += [pltpu.SemaphoreType.DMA((2, 3)), pltpu.SemaphoreType.DMA((len(tiles), 2))]
    in_specs = [scalar, *[any_space] * len(behind), *in_specs[1:]]
    return pl.pallas_call(
        ordered(body, len(behind)),
        in_specs=in_specs,
        out_specs=out_specs,
        out_shape=out_shape,
        scratch_shapes=scratch,
        compiler_params=pltpu.CompilerParams(vmem_limit_bytes=VMEM_LIMIT),
        cost_estimate=SHORT,
    )(core, *behind, rows, *saved, pair, down)


def part_forward_kernel(rows_ref, pair_ref, kept_ref):
    both = product(rows_ref[...], pair_ref[...])
    units = both.shape[1] // 2
    gate, up = both[:, :units], both[:, units:]
    sigmoid = jax.nn.sigmoid(gate)
    silu = gate * sigmoid
    kept_ref[:, :units] = (up * (sigmoid + silu * (1.0 - sigmoid))).astype(BF16)
    kept_ref[:, units : 2 * units] = silu.astype(BF16)
    kept_ref[:, 2 * units :] = (silu * up).astype(BF16)


def part_forward_call(rows, pair):
    tokens, width = rows.shape
    units = pair.shape[1] // 2
    tile = 1024
    return pl.pallas_call(
        part_forward_kernel,
        grid=(tokens // tile,),
        in_specs=[
            pl.BlockSpec((tile, width), lambda i: (i, 0)),
            pl.BlockSpec((width, 2 * units), lambda i: (0, 0)),
        ],
        out_specs=pl.BlockSpec((tile, 3 * units), lambda i: (i, 0)),
        out_shape=jax.ShapeDtypeStruct((tokens, 3 * units), BF16),
        compiler_params=pltpu.CompilerParams(vmem_limit_bytes=VMEM_LIMIT),
        cost_estimate=SHORT,
    )(rows, pair)


def pair_out(acc_ref, here, mine_ref, other_ref, runs):
    span = mine_ref.shape[0] // runs
    for k in range(runs):
        for ref, half in ((mine_ref, here), (other_ref, 1 - here)):
            start = pl.multiple_of((2 * k + half) * span, span)
            ref[k * span : (k + 1) * span] = acc_ref[pl.ds(start, span)].astype(BF16)


def accumulated(acc_ref, part, finish):
    step = pl.program_id(0)

    @pl.when(step == 0)
    def _():
        acc_ref[...] = part

    @pl.when(step > 0)
    def _():
        acc_ref[...] += part

    pl.when(step == pl.num_programs(0) - 1)(finish)


def part_down_kernel(here_ref, grad_ref, kept_ref, down_ref, pair_ref, mine_ref, other_ref, acc_ref):
    grad = grad_ref[...]
    units = down_ref.shape[0]
    grad_active = product_right(grad, down_ref[...])
    for k in range(2):
        lanes = slice(k * units, (k + 1) * units)
        pair_ref[:, lanes] = (grad_active * kept_ref[:, lanes].astype(F32)).astype(BF16)
    accumulated(
        acc_ref,
        product_left(grad, kept_ref[:, 2 * units :]),
        lambda: pair_out(acc_ref, here_ref[0], mine_ref, other_ref, 1),
    )


def part_pair_kernel(here_ref, rows_ref, pair_ref, mine_ref, other_ref, acc_ref):
    accumulated(
        acc_ref,
        product_left(rows_ref[...], pair_ref[...]),
        lambda: pair_out(acc_ref, here_ref[0], mine_ref, other_ref, 1),
    )


def part_call(kernel, here, operands, fixed, outs, result, flops, behind=()):
    tokens = operands[0].shape[0]
    tile = 1024
    by_tokens = lambda width: pl.BlockSpec((tile, width), lambda i, h: (i, 0))
    entire = lambda shape: pl.BlockSpec(shape, lambda i, h: (0, 0))
    half = (result[0] // 2, result[1])
    return pl.pallas_call(
        ordered(kernel, len(behind)),
        grid_spec=pltpu.PrefetchScalarGridSpec(
            num_scalar_prefetch=1,
            grid=(tokens // tile,),
            in_specs=[pl.BlockSpec(memory_space=pl.ANY)] * len(behind)
            + [by_tokens(a.shape[1]) for a in operands]
            + [entire(a.shape) for a in fixed],
            out_specs=[by_tokens(width) for width in outs] + [entire(half)] * 2,
            scratch_shapes=[pltpu.VMEM(result, F32)],
        ),
        out_shape=[jax.ShapeDtypeStruct((tokens, width), BF16) for width in outs]
        + [jax.ShapeDtypeStruct(half, BF16)] * 2,
        compiler_params=pltpu.CompilerParams(vmem_limit_bytes=VMEM_LIMIT),
        cost_estimate=SHORT,
    )(here, *behind, *operands, *fixed)


def part_down_call(here, grad, kept, down):
    tokens, width = grad.shape
    units = down.shape[0]
    flops = 4 * tokens * width * units
    return part_call(
        part_down_kernel, here, (grad, kept), (down,), (2 * units,), (width, units), flops
    )


def part_pair_call(here, inner, pair, behind):
    (tokens, width), columns = inner.shape, pair.shape[1]
    flops = 2 * tokens * width * columns
    return part_call(
        part_pair_kernel, here, (inner, pair), (), (), (width, columns), flops, behind
    )


def section_sums_kernel(behind_ref, all_ref, sums_ref):
    half = all_ref.shape[0] // 2
    for k in range(2):
        sums_ref[k] = jnp.sum(all_ref[k * half : (k + 1) * half], axis=0)


def section_sums_call(small, behind):
    vmem = pl.BlockSpec(memory_space=pltpu.VMEM)
    return pl.pallas_call(
        section_sums_kernel,
        in_specs=[pl.BlockSpec(memory_space=pl.ANY), vmem],
        out_specs=vmem,
        out_shape=jax.ShapeDtypeStruct((2, *small.shape[1:]), F32),
        compiler_params=pltpu.CompilerParams(vmem_limit_bytes=VMEM_LIMIT),
        cost_estimate=SHORT,
    )(*behind, small)


def mixer_grads_kernel(
    here_ref, columns_ref, normed_ref, gated_ref, out_ref, mine_ref, other_ref, acc_ref
):
    mix = out_ref.shape[0]
    out_ref[...] = product_left(columns_ref[:, :mix], gated_ref[...]).astype(BF16)
    acc_ref[...] = product_left(normed_ref[...], columns_ref[:, mix:])
    pair_out(acc_ref, here_ref[0], mine_ref, other_ref, 2)


def mixer_grads_call(here, columns, normed, gated, mix, behind):
    vmem = pl.BlockSpec(memory_space=pltpu.VMEM)
    tokens, width = normed.shape
    size = columns.shape[1] - mix
    channels = gated.shape[1]
    return pl.pallas_call(
        ordered(mixer_grads_kernel, len(behind)),
        in_specs=[
            pl.BlockSpec(memory_space=pltpu.SMEM),
            *[pl.BlockSpec(memory_space=pl.ANY)] * len(behind),
            *[vmem] * 3,
        ],
        out_specs=[vmem] * 3,
        out_shape=[
            jax.ShapeDtypeStruct((mix, channels), BF16),
            jax.ShapeDtypeStruct((width // 2, size), BF16),
            jax.ShapeDtypeStruct((width // 2, size), BF16),
        ],
        scratch_shapes=[pltpu.VMEM((width, size), F32)],
        compiler_params=pltpu.CompilerParams(vmem_limit_bytes=VMEM_LIMIT),
        cost_estimate=SHORT,
    )(here, *behind, columns, normed, gated)


def load_all(copies):
    for copy in copies:
        copy.start()


def in_time(rows):
    half = rows.shape[0] // 4
    return jnp.concatenate([rows[k * half : (k + 1) * half] for k in (0, 2, 1, 3)], axis=0)


def rows_out(acc_ref, core, mine_ref, other_ref):
    half = mine_ref.shape[0]
    mine_ref[...] = acc_ref[pl.ds(pl.multiple_of(core * half, half), half)]
    rest = acc_ref[pl.ds(pl.multiple_of((1 - core) * half, half), half)]
    other_ref[...] = rest.astype(BF16)


def weight_copies(whole_ref, out_ref, in_buf, out_buf, sems, start):
    size = in_buf.shape[2]
    copies = [
        pltpu.make_async_copy(
            whole_ref.at[:, pl.ds(start + k * size, size)], in_buf.at[k], sems.at[k]
        )
        for k in range(in_buf.shape[0])
    ]
    return copies, pltpu.make_async_copy(out_ref, out_buf, sems.at[len(copies)])


def conv_taps(mixed, kernel, masks):
    terms = [mixed]
    for lag in range(1, len(masks) + 1):
        terms.append(pltpu.roll(mixed, lag, 0) * masks[lag - 1])
    taps = kernel.shape[0]
    total = kernel[taps - 1 : taps] * terms[0]
    for lag in range(1, taps):
        total = total + kernel[taps - 1 - lag : taps - lag] * terms[lag]
    return terms, total


def conv_forward_kernel(
    core_ref, rows_ref, kernel_ref, masks_ref, whole_ref, out_ref,
    proj_ref, gated_ref, mine_ref, other_ref, in_buf, out_buf, acc_ref, sems,
):
    copies, last = weight_copies(whole_ref, out_ref, in_buf, out_buf, sems, 0)
    load_all([*copies, last])
    rows = rows_ref[...]
    parts = []
    for k, copy in enumerate(copies):
        copy.wait()
        part = product(rows, in_buf[k])
        proj_ref[k] = part.astype(BF16)
        parts.append(in_time(part))
    masks = [masks_ref[lag] for lag in range(masks_ref.shape[0])]
    gated = []
    for at in range(0, parts[0].shape[1], 128):
        before, after, signal = [part[:, at : at + 128] for part in parts]
        _, total = conv_taps(before * signal, kernel_ref[:, at : at + 128], masks)
        gated.append((after * total).astype(BF16))
    gated = in_time(jnp.concatenate(gated, axis=1))
    gated_ref[...] = gated
    last.wait()
    acc_ref[...] = product(gated, out_buf[...])
    rows_out(acc_ref, core_ref[0], mine_ref, other_ref)


def tiles_out(tiles_ref, grad_mix, columns):
    count, _, size = tiles_ref.shape
    width = grad_mix.shape[1] // 2
    step = width // count
    for k in range(count):
        here = slice(k * step, (k + 1) * step)
        parts = [grad_mix[:, :width][:, here], grad_mix[:, width:][:, here], columns(k)]
        spare = size - sum(part.shape[1] for part in parts)
        if spare:
            parts.append(jnp.zeros((grad_mix.shape[0], spare), BF16))
        tiles_ref[k] = jnp.concatenate(parts, axis=1)


def conv_backward_kernel(
    core_ref, grad_ref, kernel_ref, masks_ref, proj_ref, whole_ref, out_ref,
    tiles_ref, taps_ref, mine_ref, other_ref, in_buf, out_buf, acc_ref, sems,
):
    copies, last = weight_copies(whole_ref, out_ref, in_buf, out_buf, sems, 0)
    load_all([last, *copies])
    last.wait()
    grad_gated = in_time(product_right(grad_ref[...], out_buf[...]))
    parts = [in_time(proj_ref[k].astype(F32)) for k in range(3)]
    masks = [masks_ref[lag] for lag in range(masks_ref.shape[0])]
    rows = grad_gated.shape[0]
    grads = [[], [], []]
    for at in range(0, grad_gated.shape[1], 128):
        before, after, signal = [part[:, at : at + 128] for part in parts]
        kernel = kernel_ref[:, at : at + 128]
        terms, total = conv_taps(before * signal, kernel, masks)
        grad = grad_gated[:, at : at + 128]
        grad_total = grad * after
        taps = kernel.shape[0]
        grad_mixed = kernel[taps - 1 : taps] * grad_total
        for lag in range(1, taps):
            sent = pltpu.roll(grad_total * masks[lag - 1], rows - lag, 0)
            grad_mixed = grad_mixed + kernel[taps - 1 - lag : taps - lag] * sent
        for lag in range(taps):
            taps_ref[taps - 1 - lag : taps - lag, at : at + 128] = jnp.sum(
                grad_total * terms[lag], axis=0, keepdims=True
            )
        for k, value in enumerate((grad_mixed * signal, grad * total, grad_mixed * before)):
            grads[k].append(value.astype(BF16))
    grads = [in_time(jnp.concatenate(g, axis=1)) for g in grads]
    step = grads[0].shape[1] // tiles_ref.shape[0]
    tiles_out(
        tiles_ref,
        grad_ref[...],
        lambda k: jnp.concatenate([g[:, k * step : (k + 1) * step] for g in grads], axis=1),
    )
    for k, copy in enumerate(copies):
        copy.wait()
        part = product_right(grads[k], in_buf[k])
        acc_ref[...] = part if k == 0 else acc_ref[...] + part
    rows_out(acc_ref, core_ref[0], mine_ref, other_ref)


def head_kind(head):
    return min(max(head % (GROUP + 2) - GROUP + 1, 0), 2)


def lane_facts(rows):
    lane = lax.broadcasted_iota(jnp.int32, (rows, 128), 1)
    return lane < HEAD_DIM, lax.rem(lane, HEAD_DIM) < HEAD_DIM // 2


def head_scales(block, low):
    squares = block * block
    first = jnp.sum(jnp.where(low, squares, 0.0), axis=1, keepdims=True)
    second = jnp.sum(jnp.where(low, 0.0, squares), axis=1, keepdims=True)
    return lax.rsqrt(jnp.where(low, first, second) * (1.0 / HEAD_DIM) + EPSILON)


def block_gains(gains_ref, at):
    heads = [head_kind(2 * at), head_kind(2 * at + 1)]
    return heads, gains_ref[3 * heads[0] + heads[1] : 3 * heads[0] + heads[1] + 1]


def attention_forward_kernel(
    core_ref, rows_ref, gains_ref, tables_ref, mask_ref, whole_ref, out_ref,
    qkv_ref, ready_ref, gated_ref, mine_ref, other_ref, in_buf, out_buf, acc_ref, sems,
):
    copies, last = weight_copies(
        whole_ref, out_ref, in_buf, out_buf, sems, whole_ref.shape[1] - in_buf.shape[2]
    )
    load_all([*copies, last])
    copies[0].wait()
    qkv_ref[...] = product(rows_ref[...], in_buf[0])
    rows, width = qkv_ref.shape
    low, front = lane_facts(rows)
    cosine, sine = tables_ref[0], tables_ref[1]
    for at in range(width // 128):
        block = qkv_ref[:, at * 128 : (at + 1) * 128]
        heads, gains = block_gains(gains_ref, at)
        normed = block * head_scales(block, low) * gains
        turned = jnp.where(front, -pltpu.roll(normed, 96, 1), pltpu.roll(normed, 32, 1))
        ready = normed * cosine + turned * sine
        if heads[0] == 2:
            ready = jnp.where(low, block, ready)
        if heads[1] == 2:
            ready = jnp.where(low, ready, block)
        ready_ref[:, at * 128 : (at + 1) * 128] = ready.astype(BF16)
    half = rows // 4
    span = (GROUP + 2) * HEAD_DIM
    for m in range(2):
        mask = mask_ref[m] > 0
        mask = jnp.concatenate([mask] * GROUP, axis=0)
        for g in range(width // span):
            queries, keys, values = head_rows(ready_ref, m, half, g * span)
            weights = softmax_weights(queries, keys, mask)
            attended = product(weights.astype(BF16), values).astype(BF16)
            for j in range(GROUP):
                at = (g * GROUP + j) * HEAD_DIM
                head = attended[j * 2 * half : (j + 1) * 2 * half]
                gated_ref[m * half : (m + 1) * half, at : at + HEAD_DIM] = head[:half]
                gated_ref[(m + 2) * half : (m + 3) * half, at : at + HEAD_DIM] = head[half:]
    last.wait()
    acc_ref[...] = product(gated_ref[...], out_buf[...])
    rows_out(acc_ref, core_ref[0], mine_ref, other_ref)


def sequence(ref, m, half, at):
    columns = slice(at, at + HEAD_DIM)
    return jnp.concatenate(
        [ref[m * half : (m + 1) * half, columns], ref[(m + 2) * half : (m + 3) * half, columns]],
        axis=0,
    )


def head_rows(ref, m, half, at):
    heads = [sequence(ref, m, half, at + j * HEAD_DIM) for j in range(GROUP + 2)]
    return jnp.concatenate(heads[:GROUP], axis=0), heads[GROUP], heads[GROUP + 1]


def softmax_weights(queries, keys, mask):
    scores = jnp.where(mask, product_right(queries, keys) * HEAD_DIM ** (-0.5), MASKED_SCORE)
    terms = jnp.exp(scores - jnp.max(scores, axis=1, keepdims=True))
    return terms / jnp.sum(terms, axis=1, keepdims=True)


def attention_backward_kernel(
    core_ref, grad_ref, gains_ref, tables_ref, mask_ref, qkv_ref, ready_ref, whole_ref, out_ref,
    tiles_ref, heads_ref, mine_ref, other_ref,
    in_buf, out_buf, acc_ref, attended_ref, ready_grad_ref, proj_ref, sems,
):
    copies, last = weight_copies(
        whole_ref, out_ref, in_buf, out_buf, sems, whole_ref.shape[1] - in_buf.shape[2]
    )
    load_all([last, *copies])
    last.wait()
    attended_ref[...] = product_right(grad_ref[...], out_buf[...]).astype(BF16)
    rows, width = qkv_ref.shape
    half = rows // 4
    span = (GROUP + 2) * HEAD_DIM
    scale = HEAD_DIM ** (-0.5)
    for m in range(2):
        mask = mask_ref[m] > 0
        mask = jnp.concatenate([mask] * GROUP, axis=0)
        for g in range(width // span):
            queries, keys, values = head_rows(ready_ref, m, half, g * span)
            weights = softmax_weights(queries, keys, mask)
            grad = jnp.concatenate(
                [
                    sequence(attended_ref, m, half, (g * GROUP + j) * HEAD_DIM)
                    for j in range(GROUP)
                ],
                axis=0,
            )
            grad_values = product_left(weights.astype(BF16), grad)
            grad_weights = product_right(grad, values)
            mean = jnp.sum(grad_weights * weights, axis=1, keepdims=True)
            grad_scores = (weights * (grad_weights - mean)).astype(BF16)
            grad_queries = product(grad_scores, keys) * scale
            grad_keys = product_left(grad_scores, queries) * scale
            outs = [grad_queries[j * 2 * half : (j + 1) * 2 * half] for j in range(GROUP)]
            for j, out in enumerate([*outs, grad_keys, grad_values]):
                at = g * span + j * HEAD_DIM
                ready_grad_ref[m * half : (m + 1) * half, at : at + HEAD_DIM] = out[:half]
                ready_grad_ref[(m + 2) * half : (m + 3) * half, at : at + HEAD_DIM] = out[half:]
    low, front = lane_facts(rows)
    cosine, sine = tables_ref[0], tables_ref[1]
    for at in range(width // 128):
        lanes = slice(at * 128, (at + 1) * 128)
        block, grad = qkv_ref[:, lanes], ready_grad_ref[:, lanes]
        heads, gains = block_gains(gains_ref, at)
        inverse = head_scales(block, low)
        normed = block * inverse
        turned = grad * sine
        grad_normed = grad * cosine + jnp.where(
            front, pltpu.roll(turned, 96, 1), -pltpu.roll(turned, 32, 1)
        )
        heads_ref[at : at + 1] = jnp.sum(grad_normed * normed, axis=0, keepdims=True)
        grad_normed = grad_normed * gains
        along = grad_normed * normed
        first = jnp.sum(jnp.where(low, along, 0.0), axis=1, keepdims=True)
        second = jnp.sum(jnp.where(low, 0.0, along), axis=1, keepdims=True)
        mean = jnp.where(low, first, second) * (1.0 / HEAD_DIM)
        raw = inverse * (grad_normed - normed * mean)
        if heads[0] == 2:
            raw = jnp.where(low, grad, raw)
        if heads[1] == 2:
            raw = jnp.where(low, raw, grad)
        proj_ref[:, lanes] = raw.astype(BF16)
    step = width // tiles_ref.shape[0]
    tiles_out(tiles_ref, grad_ref[...], lambda k: proj_ref[:, k * step : (k + 1) * step])
    copies[0].wait()
    acc_ref[...] = product_right(proj_ref[...], in_buf[0])
    rows_out(acc_ref, core_ref[0], mine_ref, other_ref)


def mixer_call(kernel, core, operands, whole, weight_out, in_tiles, outs, scratch=(), behind=()):
    vmem, any_space = pl.BlockSpec(memory_space=pltpu.VMEM), pl.BlockSpec(memory_space=pl.ANY)
    rows, width = operands[0].shape
    channels = weight_out.shape[0]
    outs = [*outs, ((rows // 2, width), F32), ((rows // 2, width), BF16)]
    return pl.pallas_call(
        ordered(kernel, len(behind)),
        in_specs=[
            pl.BlockSpec(memory_space=pltpu.SMEM),
            *[any_space] * len(behind),
            *[vmem] * len(operands),
            any_space,
            any_space,
        ],
        out_specs=[vmem] * len(outs),
        out_shape=[jax.ShapeDtypeStruct(*out) for out in outs],
        scratch_shapes=[
            pltpu.VMEM((in_tiles[0], width, in_tiles[1]), BF16),
            pltpu.VMEM((channels, width), BF16),
            pltpu.VMEM((rows, width), F32),
            *scratch,
            pltpu.SemaphoreType.DMA((in_tiles[0] + 1,)),
        ],
        compiler_params=pltpu.CompilerParams(vmem_limit_bytes=VMEM_LIMIT),
        cost_estimate=SHORT,
    )(core, *behind, *operands, whole, weight_out)


def conv_forward_call(core, rows, kernel, masks, whole, weight_out):
    count, channels = rows.shape[0], kernel.shape[1]
    outs = [((3, count, channels), BF16), ((count, channels), BF16)]
    operands = (rows, kernel, masks)
    return mixer_call(
        conv_forward_kernel, core, operands, whole, weight_out, (3, channels), outs
    )


def conv_backward_call(core, grad, kernel, masks, projected, whole, weight_out, behind):
    count, width = grad.shape
    taps, channels = kernel.shape
    outs = [
        ((4, count, whole_lanes((width + 3 * channels) // 4)), BF16),
        ((taps, channels), F32),
    ]
    operands = (grad, kernel, masks, projected)
    return mixer_call(
        conv_backward_kernel, core, operands, whole, weight_out, (3, channels), outs, (), behind
    )


def attention_forward_call(core, rows, gains, tables, mask, whole, weight_out, qkv_width):
    count, channels = rows.shape[0], weight_out.shape[0]
    outs = [((count, qkv_width), F32), ((count, qkv_width), BF16), ((count, channels), BF16)]
    operands = (rows, gains, tables, mask)
    return mixer_call(
        attention_forward_kernel, core, operands, whole, weight_out, (1, qkv_width), outs
    )


def attention_backward_call(core, grad, gains, tables, mask, qkv, ready, whole, weight_out):
    count, width = grad.shape
    channels, qkv_width = weight_out.shape[0], qkv.shape[1]
    outs = [
        ((4, count, whole_lanes((width + 3 * channels) // 4)), BF16),
        ((qkv_width // 128, 128), F32),
    ]
    scratch = [
        pltpu.VMEM((count, channels), BF16),
        pltpu.VMEM((count, qkv_width), F32),
        pltpu.VMEM((count, qkv_width), BF16),
    ]
    operands = (grad, gains, tables, mask, qkv, ready)
    return mixer_call(
        attention_backward_kernel, core, operands, whole, weight_out, (1, qkv_width), outs, scratch
    )


def conv_masks(segments, taps):
    masks = []
    for lag in range(1, taps):
        same = (segments[:, lag:] == segments[:, :-lag]).astype(F32)
        same = jnp.pad(same, ((0, 0), (lag, 0))).reshape(-1, 1)
        masks.append(jnp.broadcast_to(same, (same.shape[0], 128)))
    return jnp.stack(masks)


def score_mask(segments):
    position = jnp.arange(segments.shape[1])
    allowed = position[:, None] >= position[None, :]
    return (allowed & (segments[:, :, None] == segments[:, None, :])).astype(F32)


def turn_tables(length):
    half = HEAD_DIM // 2
    exponent = jnp.arange(half, dtype=F32) * (2.0 / HEAD_DIM)
    frequency = jnp.exp(-exponent * jnp.log(ROPE_BASE))
    angles = jnp.arange(length, dtype=F32)[:, None] * frequency[None, :]
    tables = jnp.tile(jnp.stack([jnp.cos(angles), jnp.sin(angles)]), (1, 1, 4))
    tables = tables.reshape(2, 2, 1, length // 2, 128)
    return jnp.broadcast_to(tables, (2, 2, 2, length // 2, 128)).reshape(2, 2 * length, 128)


def gain_rows(head_gains):
    kinds = [head_gains[0], head_gains[1], jnp.ones_like(head_gains[0])]
    rows = [jnp.concatenate([a, b]) for a in kinds for b in kinds]
    return jnp.stack(rows)


def head_gain_sums(sums):
    heads = sums.reshape(-1, GROUP + 2, HEAD_DIM)
    return jnp.stack([heads[:, :GROUP].sum((0, 1)), heads[:, GROUP].sum(0)])


def local(
    inputs,
    out_cotangent,
    segments,
    norm_gains,
    conv_kernel,
    qk_gains,
    conv_in,
    attn_qkv,
    mixer_out,
    gate_up,
    down,
):
    section = lax.axis_index("xh")
    first = section == 0
    core = lax.axis_index("c")
    place = lax.axis_index("y") * 4 + lax.axis_index("z")
    xl = lax.axis_index("xl")
    plane = lax.axis_size("y") * lax.axis_size("z")

    shape = inputs.shape[1:]
    width = shape[-1]
    inputs, out_cotangent = inputs.reshape(-1, width), out_cotangent.reshape(-1, width)
    segments = segments[0]
    half = inputs.shape[0]
    rows = 2 * half
    channels = conv_in.shape[2]
    kernel = lax.dynamic_slice_in_dim(conv_kernel, core * channels, channels, 1).astype(F32)
    gains = lax.dynamic_index_in_dim(norm_gains, section, 0, keepdims=False).astype(F32)
    weight_out, weight_pair, weight_down = mixer_out[0], gate_up[0], down[0]
    hidden_units = weight_down.shape[0]
    part = hidden_units // plane
    in_width = 3 * channels
    qkv_width = attn_qkv.shape[1]
    core_scalar = core.astype(jnp.int32)[None]
    xl_scalar = xl.astype(jnp.int32)[None]

    def chosen(from_first, from_second):
        return jnp.where(first, from_first, from_second)

    def gathered(own, axes):
        return lax.all_gather(own, axes, tiled=True)


    both = jnp.concatenate([conv_in.reshape(-1, in_width), attn_qkv], axis=1)
    whole = gathered(both, ("xh", "xl", "y", "z"))

    lanes = -(-part // 256) * 256
    fill = lanes - part
    part_pair = jnp.concatenate(
        [
            jnp.pad(lax.dynamic_slice_in_dim(w, place * part, part, 1), ((0, 0), (0, fill)))
            for w in (weight_pair[0], weight_pair[1])
        ],
        axis=1,
    )
    part_down = lax.dynamic_slice_in_dim(weight_down, place * part, part, 0)
    part_down = jnp.pad(part_down, ((0, fill), (0, 0)))
    masks = conv_masks(segments, kernel.shape[0])
    mask = score_mask(segments)
    tables = turn_tables(segments.shape[1])
    head_gains = gain_rows(qk_gains.astype(F32))
    first_in = inputs.astype(F32)
    normed_own_0 = (normalize(first_in) * gains[0]).astype(BF16)
    normed_0 = spread(normed_own_0)
    cotangent_1 = spread(out_cotangent)
    whole, part_pair, part_down, masks, mask, tables, head_gains, normed_0, cotangent_1 = (
        lax.optimization_barrier(
            (whole, part_pair, part_down, masks, mask, tables, head_gains, normed_0, cotangent_1)
        )
    )

    def feed_forward(hidden, behind=()):
        inner_own = (normalize(hidden) * gains[1]).astype(BF16)
        gate, up, mine, other = feed_forward_call(
            False, core_scalar, spread(inner_own), weight_pair, weight_down, behind=behind
        )
        return hidden + joined(mine, other), (inner_own, gate, up)

    def feed_forward_back(grad_full, grad, hidden, saved):
        mine, other = feed_forward_call(
            True, core_scalar, grad_full, weight_pair, weight_down, saved[1:]
        )
        back, grad_gain = norm_backward(joined(mine, other), gains[1], hidden)
        return grad + back, grad_gain

    def mixer_back(grad_hidden, mine, other, layer_in):
        back, grad_gain = norm_backward(joined(mine, other), gains[0], layer_in)
        return (grad_hidden + back).astype(BF16), grad_gain

    plane_axes = ("y", "z", "c")
    early = gathered(chosen(normed_own_0, out_cotangent), plane_axes)

    projected, gated_0, mine, other = conv_forward_call(
        core_scalar, normed_0, kernel, masks, whole, weight_out
    )
    hidden_0 = first_in + joined(mine, other)
    result_0, ffn_0 = feed_forward(hidden_0)
    result_0 = result_0.astype(BF16)

    second_in = lax.ppermute(result_0, "xh", [(0, 1)]).astype(F32)
    normed_own_1 = (normalize(second_in) * gains[0]).astype(BF16)
    qkv, ready, gated_1, mine, other = attention_forward_call(
        core_scalar, spread(normed_own_1), head_gains, tables, mask, whole, weight_out, qkv_width
    )
    hidden_1 = second_in + joined(mine, other)
    result_1, ffn_1 = feed_forward(hidden_1, (early,))
    result_1 = result_1.astype(BF16)

    inner_all = gathered(chosen(ffn_0[0], ffn_1[0]), plane_axes)

    grad_hidden_1, gain_inner_1 = feed_forward_back(
        cotangent_1, out_cotangent.astype(F32), hidden_1, ffn_1
    )
    tiles_1, head_sums, mine, other = attention_backward_call(
        core_scalar,
        spread(grad_hidden_1.astype(BF16)),
        head_gains,
        tables,
        mask,
        qkv,
        ready,
        whole,
        weight_out,
    )
    input_grad_1, gain_outer_1 = mixer_back(grad_hidden_1, mine, other, second_in)

    cotangent = lax.ppermute(input_grad_1, "xh", [(1, 0)])
    late = gathered(chosen(cotangent, normed_own_1), plane_axes)
    gated = chosen(gated_0, gated_1)
    gated_y = exchanged(jnp.broadcast_to(gated, (4, *gated.shape)), "y").reshape(4 * rows, -1)
    grad_hidden_0, gain_inner_0 = feed_forward_back(
        spread(cotangent), cotangent.astype(F32), hidden_0, ffn_0
    )
    tiles_0, grad_kernel, mine, other = conv_backward_call(
        core_scalar,
        spread(grad_hidden_0.astype(BF16)),
        kernel,
        masks,
        projected,
        whole,
        weight_out,
        (gated_y,),
    )
    input_grad_0, gain_outer_0 = mixer_back(grad_hidden_0, mine, other, first_in)

    def summed_over_pair(mine, other):
        return mine.astype(F32) + swapped(other, "xl").astype(F32)

    columns = exchanged(chosen(tiles_0, tiles_1), "y").reshape(4 * rows, -1)
    z = lax.axis_index("z")
    along_y = [
        lax.dynamic_index_in_dim(a.reshape(4, 4, rows, width), z, 1, keepdims=False)
        for a in (early, late)
    ]
    normed_y = chosen(*along_y).reshape(4 * rows, width)

    part_kept = part_forward_call(inner_all, part_pair)
    pair_grads, down_mine, down_other = lax.cond(
        first,
        lambda: part_down_call(xl_scalar, late, part_kept, part_down),
        lambda: part_down_call(xl_scalar, early, part_kept, part_down),
    )
    out_parts, in_mine, in_other = mixer_grads_call(
        xl_scalar, columns, normed_y, gated_y, width // 4, (pair_grads,)
    )
    pair_mine, pair_other = part_pair_call(xl_scalar, inner_all, pair_grads, (in_mine,))

    total = [summed_over_pair(pair_mine, pair_other), summed_over_pair(down_mine, down_other)]
    total = jnp.concatenate(total, axis=1).astype(BF16)
    arrived = exchanged(total.reshape(plane, -1, 3 * lanes), PLANE)
    lines = [
        jnp.moveaxis(arrived[:, :, k * lanes : k * lanes + part], 0, 1)
        .reshape(-1, hidden_units)
        .astype(F32)
        for k in range(3)
    ]
    grad_gate_up = jnp.stack(lines[:2])[None]
    grad_down = lines[2].T[None]

    total = summed_over_pair(in_mine, in_other).astype(BF16)
    total = total.reshape(2, plane, -1, total.shape[1])
    come = exchanged(jnp.moveaxis(total, 1, 0), PLANE)
    lines = come.reshape(4, 4, *come.shape[1:]).astype(F32).sum(1)
    kept_lines = lax.dynamic_index_in_dim(lines, section, 1, keepdims=False)
    sent_lines = lax.dynamic_index_in_dim(lines, 1 - section, 1, keepdims=False)
    come = swapped(sent_lines.astype(BF16), "xh").astype(F32)
    lines = chosen(kept_lines, come)[:, :, : in_width // 4].reshape(4, -1, 3, channels // 4)
    grad_conv_in = jnp.moveaxis(lines, 0, 2).reshape(conv_in.shape)
    lines = chosen(come, kept_lines)[:, :, : qkv_width // 4]
    grad_attn_qkv = jnp.moveaxis(lines, 0, 1).reshape(attn_qkv.shape)

    out_parts = exchanged(out_parts.reshape(8, -1, channels), ("xl", "z"))
    grad_mixer_out = out_parts.astype(F32).sum(0).T[None]

    full_kernel = lax.dynamic_update_slice(
        jnp.zeros(conv_kernel.shape, F32), grad_kernel, (0, core * channels)
    )
    small = jnp.concatenate(
        [
            chosen(gain_outer_0, gain_outer_1),
            chosen(gain_inner_0, gain_inner_1),
            full_kernel.reshape(-1),
            head_gain_sums(head_sums).reshape(-1),
        ]
    )
    count = small.shape[0]
    small = jnp.pad(small, (0, -count % 1024)).reshape(-1, 128)
    sums = section_sums_call(lax.all_gather(small, AXES), (arrived,))
    pair = [sums[0].reshape(-1), sums[1].reshape(-1)]
    grad_norm_gains = jnp.stack([a[: 2 * width].reshape(2, width) for a in pair])
    grad_conv_kernel = pair[0][2 * width : 5 * width].reshape(conv_kernel.shape)
    grad_qk_gains = pair[1][5 * width : count].reshape(qk_gains.shape)

    activations = chosen(result_0, result_1).reshape(1, 1, *shape)
    input_grads = chosen(input_grad_0, input_grad_1).reshape(1, 1, *shape)
    return (
        activations,
        input_grads,
        grad_norm_gains,
        grad_conv_kernel,
        grad_qk_gains,
        grad_conv_in,
        grad_attn_qkv,
        grad_mixer_out,
        grad_gate_up,
        grad_down,
    )


def solution(mesh):
    wide = Mesh(mesh.devices.reshape(2, 2, 4, 4, 2), AXES)
    dp = ("xl", "y", "z")
    everyone = ("xh", "xl", "y", "z")
    in_specs = (
        P(dp, None, "c", None),
        P(dp, None, "c", None),
        P(dp, None, None),
        P(),
        P(),
        P(),
        P(everyone, None, "c"),
        P(everyone, "c"),
        P("xh", "c", None),
        P("xh", None, None, "c"),
        P("xh", "c", None),
    )
    out_specs = (
        P("xh", dp, None, "c", None),
        P("xh", dp, None, "c", None),
        P(),
        P(),
        P(),
        P(everyone, None, "c"),
        P(everyone, "c"),
        P("xh", "c", dp),
        P("xh", None, dp, "c"),
        P("xh", "c", dp),
    )
    return jax.shard_map(local, mesh=wide, in_specs=in_specs, out_specs=out_specs, check_vma=False)
```

```python
import functools

import jax
import jax.numpy as jnp
from jax import lax
from jax.experimental import pallas as pl
from jax.experimental.pallas import tpu as pltpu
from jax.sharding import Mesh
from jax.sharding import PartitionSpec as P

HEADS = 24
KV_HEADS = 8
HEAD_DIM = 64
GROUP = HEADS // KV_HEADS

EPSILON = 1e-05
ROPE_BASE = 1000000.0
MASKED_SCORE = -1e30

F32 = jnp.float32
BF16 = jnp.bfloat16

PLANE = ("y", "z")
AXES = ("xh", "xl", "y", "z", "c")


def product(left, right):
    return jnp.dot(left, right, preferred_element_type=F32)


def product_left(left, right):
    return lax.dot_general(left, right, (((0,), (0,)), ((), ())), preferred_element_type=F32)


def product_right(left, right):
    return lax.dot_general(left, right, (((1,), (1,)), ((), ())), preferred_element_type=F32)


def swapped(shard, axis):
    return lax.ppermute(shard, axis, [(0, 1), (1, 0)])


def spread(own):
    return lax.all_gather(own, "c", tiled=True)


def joined(mine, other):
    return mine + swapped(other, "c").astype(F32)


def mean_last(values):
    return jnp.mean(values, axis=-1, keepdims=True)


def inverse_rms(values):
    return lax.rsqrt(mean_last(values * values) + EPSILON)


def normalize(values):
    return values * inverse_rms(values)


def exchanged(tiles, axes):
    return lax.all_to_all(tiles, axes, 0, 0, tiled=True)


def ffn_grads(grad_active, gate, up):
    sigmoid = jax.nn.sigmoid(gate)
    grad_gate = grad_active * up * sigmoid * (1.0 + gate * (1.0 - sigmoid))
    grad_up = grad_active * gate * sigmoid
    return grad_gate.astype(BF16), grad_up.astype(BF16)


VMEM_LIMIT = 56 * 1024 * 1024
SHORT = pl.CostEstimate(flops=1, bytes_accessed=1, transcendentals=0)


def ordered(kernel, count):
    def body(scalar_ref, *refs):
        kernel(scalar_ref, *refs[count:])

    return body


def unit_tiles(units, tile):
    short = units % tile
    tiles = [(0, short)] if short else []
    return tiles + [(at, tile) for at in range(short, units, tile)]


def streamed(tiles, copies, work):
    for copy in copies(0, 0):
        copy.start()
    for k in range(len(tiles)):
        slot = k % 2
        if k + 1 < len(tiles):
            for copy in copies(k + 1, 1 - slot):
                copy.start()
        for copy in copies(k, slot):
            copy.wait()
        work(k, slot)


def ffn_forward_kernel(
    tiles, core_ref, rows_ref, pair_ref, down_ref, gate_ref, up_ref, mine_ref, other_ref,
    pair_buf, down_buf, gate_buf, up_buf, acc_ref, sems, out_sems,
):
    def copies(k, slot):
        at, size = tiles[k]
        return [
            pltpu.make_async_copy(
                pair_ref.at[0, :, pl.ds(at, size)],
                pair_buf.at[slot, :, pl.ds(0, size)],
                sems.at[slot, 0],
            ),
            pltpu.make_async_copy(
                pair_ref.at[1, :, pl.ds(at, size)],
                pair_buf.at[slot, :, pl.ds(size, size)],
                sems.at[slot, 1],
            ),
            pltpu.make_async_copy(
                down_ref.at[pl.ds(at, size)], down_buf.at[slot, pl.ds(0, size)], sems.at[slot, 2]
            ),
        ]

    def kept(k):
        here = (slice(None), pl.ds(*tiles[k]))
        return [
            pltpu.make_async_copy(gate_buf.at[here], gate_ref.at[here], out_sems.at[k, 0]),
            pltpu.make_async_copy(up_buf.at[here], up_ref.at[here], out_sems.at[k, 1]),
        ]

    def work(k, slot):
        at, size = tiles[k]
        both = product(rows_ref[...], pair_buf[slot, :, : 2 * size])
        gate, up = both[:, :size], both[:, size:]
        gate_buf[:, at : at + size] = gate.astype(BF16)
        up_buf[:, at : at + size] = up.astype(BF16)
        for copy in kept(k):
            copy.start()
        active = (gate * jax.nn.sigmoid(gate) * up).astype(BF16)
        part = product(active, down_buf[slot, :size])
        if k == 0:
            acc_ref[...] = part
        else:
            acc_ref[...] += part

    streamed(tiles, copies, work)
    rows_out(acc_ref, core_ref[0], mine_ref, other_ref)
    for k in range(len(tiles)):
        for copy in kept(k):
            copy.wait()


def ffn_backward_kernel(
    tiles, core_ref, rows_ref, gate_ref, up_ref, pair_ref, down_ref, mine_ref, other_ref,
    pair_buf, down_buf, gate_buf, up_buf, acc_ref, sems,
):
    def copies(k, slot):
        at, size = tiles[k]
        columns, place = pl.ds(at, size), pl.ds(0, size)
        return [
            pltpu.make_async_copy(
                down_ref.at[columns], down_buf.at[slot, place], sems.at[slot, 0]
            ),
            pltpu.make_async_copy(
                gate_ref.at[:, columns], gate_buf.at[slot, :, place], sems.at[slot, 1]
            ),
            pltpu.make_async_copy(
                up_ref.at[:, columns], up_buf.at[slot, :, place], sems.at[slot, 2]
            ),
            pltpu.make_async_copy(
                pair_ref.at[0, :, columns], pair_buf.at[slot, :, place], sems.at[slot, 3]
            ),
            pltpu.make_async_copy(
                pair_ref.at[1, :, columns],
                pair_buf.at[slot, :, pl.ds(size, size)],
                sems.at[slot, 4],
            ),
        ]

    def work(k, slot):
        _, size = tiles[k]
        grad_active = product_right(rows_ref[...], down_buf[slot, :size])
        grads = ffn_grads(
            grad_active,
            gate_buf[slot, :, :size].astype(F32),
            up_buf[slot, :, :size].astype(F32),
        )
        part = product_right(jnp.concatenate(grads, axis=1), pair_buf[slot, :, : 2 * size])
        if k == 0:
            acc_ref[...] = part
        else:
            acc_ref[...] += part

    streamed(tiles, copies, work)
    rows_out(acc_ref, core_ref[0], mine_ref, other_ref)


def feed_forward_call(backward, core, rows, pair, down, saved=(), behind=()):
    count, width = rows.shape
    units = down.shape[0]
    tile = 768
    tiles = unit_tiles(units, tile)
    vmem, any_space = pl.BlockSpec(memory_space=pltpu.VMEM), pl.BlockSpec(memory_space=pl.ANY)
    scalar = pl.BlockSpec(memory_space=pltpu.SMEM)
    out_shape = [
        jax.ShapeDtypeStruct((count // 2, width), F32),
        jax.ShapeDtypeStruct((count // 2, width), BF16),
    ]
    out_specs = [vmem, vmem]
    buffers = [pltpu.VMEM((2, width, 2 * tile), BF16), pltpu.VMEM((2, tile, width), BF16)]
    acc = pltpu.VMEM((count, width), F32)
    if backward:
        body = functools.partial(ffn_backward_kernel, tiles)
        in_specs = [scalar, vmem, any_space, any_space, any_space, any_space]
        buffers += [pltpu.VMEM((2, count, tile), BF16)] * 2
        scratch = [*buffers, acc, pltpu.SemaphoreType.DMA((2, 5))]
    else:
        body = functools.partial(ffn_forward_kernel, tiles)
        in_specs = [scalar, vmem, any_space, any_space]
        out_shape = [jax.ShapeDtypeStruct((count, units), BF16)] * 2 + out_shape
        out_specs = [any_space, any_space, *out_specs]
        buffers += [pltpu.VMEM((count, units), BF16)] * 2
        scratch = [*buffers, acc]
        scratch += [pltpu.SemaphoreType.DMA((2, 3)), pltpu.SemaphoreType.DMA((len(tiles), 2))]
    in_specs = [scalar, *[any_space] * len(behind), *in_specs[1:]]
    return pl.pallas_call(
        ordered(body, len(behind)),
        in_specs=in_specs,
        out_specs=out_specs,
        out_shape=out_shape,
        scratch_shapes=scratch,
        compiler_params=pltpu.CompilerParams(vmem_limit_bytes=VMEM_LIMIT),
        cost_estimate=SHORT,
    )(core, *behind, rows, *saved, pair, down)


def part_forward_kernel(behind_ref, rows_ref, pair_ref, kept_ref):
    both = product(rows_ref[...], pair_ref[...])
    units = both.shape[1] // 2
    gate, up = both[:, :units], both[:, units:]
    sigmoid = jax.nn.sigmoid(gate)
    silu = gate * sigmoid
    kept_ref[:, :units] = (up * (sigmoid + silu * (1.0 - sigmoid))).astype(BF16)
    kept_ref[:, units : 2 * units] = silu.astype(BF16)
    kept_ref[:, 2 * units :] = (silu * up).astype(BF16)


def part_forward_call(behind, rows, pair):
    tokens, width = rows.shape
    units = pair.shape[1] // 2
    tile = 1024
    return pl.pallas_call(
        part_forward_kernel,
        grid=(tokens // tile,),
        in_specs=[
            pl.BlockSpec(memory_space=pl.ANY),
            pl.BlockSpec((tile, width), lambda i: (i, 0)),
            pl.BlockSpec((width, 2 * units), lambda i: (0, 0)),
        ],
        out_specs=pl.BlockSpec((tile, 3 * units), lambda i: (i, 0)),
        out_shape=jax.ShapeDtypeStruct((tokens, 3 * units), BF16),
        compiler_params=pltpu.CompilerParams(vmem_limit_bytes=VMEM_LIMIT),
        cost_estimate=pl.CostEstimate(
            flops=8 * tokens * width * units, bytes_accessed=2 * tokens * width, transcendentals=0
        ),
    )(behind, rows, pair)


def pair_out(acc_ref, here, mine_ref, other_ref):
    rows = mine_ref.shape[0]
    for ref, half in ((mine_ref, here), (other_ref, 1 - here)):
        ref[...] = acc_ref[pl.ds(pl.multiple_of(half * rows, rows), rows)].astype(BF16)


def accumulated(acc_ref, part, finish):
    step = pl.program_id(0)

    @pl.when(step == 0)
    def _():
        acc_ref[...] = part

    @pl.when(step > 0)
    def _():
        acc_ref[...] += part

    pl.when(step == pl.num_programs(0) - 1)(finish)


def part_down_kernel(here_ref, grad_ref, kept_ref, down_ref, pair_ref, mine_ref, other_ref, acc_ref):
    grad = grad_ref[...]
    units = down_ref.shape[0]
    grad_active = product_right(grad, down_ref[...])
    for k in range(2):
        lanes = slice(k * units, (k + 1) * units)
        pair_ref[:, lanes] = (grad_active * kept_ref[:, lanes].astype(F32)).astype(BF16)
    accumulated(
        acc_ref,
        product_left(grad, kept_ref[:, 2 * units :]),
        lambda: pair_out(acc_ref, here_ref[0], mine_ref, other_ref),
    )


def part_pair_kernel(here_ref, rows_ref, pair_ref, mine_ref, other_ref, acc_ref):
    accumulated(
        acc_ref,
        product_left(rows_ref[...], pair_ref[...]),
        lambda: pair_out(acc_ref, here_ref[0], mine_ref, other_ref),
    )


def part_call(kernel, here, operands, fixed, outs, result, flops, behind=()):
    tokens = operands[0].shape[0]
    tile = 1024
    by_tokens = lambda width: pl.BlockSpec((tile, width), lambda i, h: (i, 0))
    entire = lambda shape: pl.BlockSpec(shape, lambda i, h: (0, 0))
    half = (result[0] // 2, result[1])
    return pl.pallas_call(
        ordered(kernel, len(behind)),
        grid_spec=pltpu.PrefetchScalarGridSpec(
            num_scalar_prefetch=1,
            grid=(tokens // tile,),
            in_specs=[pl.BlockSpec(memory_space=pl.ANY)] * len(behind)
            + [by_tokens(a.shape[1]) for a in operands]
            + [entire(a.shape) for a in fixed],
            out_specs=[by_tokens(width) for width in outs] + [entire(half)] * 2,
            scratch_shapes=[pltpu.VMEM(result, F32)],
        ),
        out_shape=[jax.ShapeDtypeStruct((tokens, width), BF16) for width in outs]
        + [jax.ShapeDtypeStruct(half, BF16)] * 2,
        compiler_params=pltpu.CompilerParams(vmem_limit_bytes=VMEM_LIMIT),
        cost_estimate=SHORT,
    )(here, *behind, *operands, *fixed)


def part_down_call(here, grad, kept, down, behind):
    tokens, width = grad.shape
    units = down.shape[0]
    flops = 4 * tokens * width * units
    return part_call(
        part_down_kernel,
        here,
        (grad, kept),
        (down,),
        (2 * units,),
        (width, units),
        flops,
        behind,
    )


def part_pair_call(here, inner, pair, behind):
    (tokens, width), columns = inner.shape, pair.shape[1]
    flops = 2 * tokens * width * columns
    return part_call(
        part_pair_kernel, here, (inner, pair), (), (), (width, columns), flops, behind
    )


def back_join_kernel(
    behind_ref, mine_ref, come_ref, values_ref, base_ref, gain_ref, wide_ref, low_ref, sums_ref
):
    grad = mine_ref[...] + come_ref[...].astype(F32)
    values = values_ref[...]
    inverse = inverse_rms(values)
    normed = values * inverse
    scaled = grad * gain_ref[...]
    sums_ref[...] = jnp.sum(grad * normed, axis=0, keepdims=True)
    total = base_ref[...] + inverse * (scaled - normed * mean_last(scaled * normed))
    wide_ref[...] = total
    low_ref[...] = total.astype(BF16)


def back_join_call(behind, mine, come, values, base, gain):
    vmem = pl.BlockSpec(memory_space=pltpu.VMEM)
    shape = values.shape
    wide, low, sums = pl.pallas_call(
        back_join_kernel,
        in_specs=[pl.BlockSpec(memory_space=pl.ANY), *[vmem] * 5],
        out_specs=[vmem] * 3,
        out_shape=[
            jax.ShapeDtypeStruct(shape, F32),
            jax.ShapeDtypeStruct(shape, BF16),
            jax.ShapeDtypeStruct((1, shape[1]), F32),
        ],
        compiler_params=pltpu.CompilerParams(vmem_limit_bytes=VMEM_LIMIT),
        cost_estimate=SHORT,
    )(behind, mine, come, values, base, gain[None])
    return wide, low, sums[0]


def section_sums_kernel(behind_ref, all_ref, sums_ref):
    half = all_ref.shape[0] // 2
    for k in range(2):
        sums_ref[k] = jnp.sum(all_ref[k * half : (k + 1) * half], axis=0)


def section_sums_call(small, behind):
    vmem = pl.BlockSpec(memory_space=pltpu.VMEM)
    return pl.pallas_call(
        section_sums_kernel,
        in_specs=[pl.BlockSpec(memory_space=pl.ANY), vmem],
        out_specs=vmem,
        out_shape=jax.ShapeDtypeStruct((2, *small.shape[1:]), F32),
        compiler_params=pltpu.CompilerParams(vmem_limit_bytes=VMEM_LIMIT),
        cost_estimate=SHORT,
    )(*behind, small)


def mixer_grads_kernel(
    places_ref, columns_ref, mix_ref, early_ref, late_ref, mine_ref, other_ref,
    normed_ref, in_ref, out_ref, sems,
):
    count, rows = sems.shape[0], normed_ref.shape[0] // sems.shape[0]
    here, section, z = places_ref[0], places_ref[1], places_ref[2]

    def copies(all_ref):
        span = all_ref.shape[0] // count
        return [
            pltpu.make_async_copy(
                all_ref.at[pl.ds(pl.multiple_of(k * span + z * rows, rows), rows)],
                normed_ref.at[pl.ds(k * rows, rows)],
                sems.at[k],
            )
            for k in range(count)
        ]

    @pl.when(section == 0)
    def _():
        load_all(copies(early_ref))

    @pl.when(section > 0)
    def _():
        load_all(copies(late_ref))

    out_columns = columns_ref.shape[1] // 4
    split = columns_ref.shape[1] - out_columns
    out_ref[...] = product_left(mix_ref[...], columns_ref[:, split:])
    for copy in copies(early_ref):
        copy.wait()
    in_ref[...] = product_left(normed_ref[...], columns_ref[:, :split])
    plane, block, _ = mine_ref.shape
    short = block // 2
    for ref, half in ((mine_ref, here), (other_ref, 1 - here)):
        for k in range(plane):
            for s in range(2):
                start = pl.multiple_of(((2 * s + half) * plane + k) * short, short)
                rows_in = in_ref[pl.ds(start, short)]
                ref[k, s * short : (s + 1) * short, :split] = rows_in.astype(BF16)
            start = pl.multiple_of((half * plane + k) * block, block)
            ref[k, :, split:] = out_ref[pl.ds(start, block)].astype(BF16)


def mixer_grads_call(places, columns, mix, early, late, plane):
    vmem, any_space = pl.BlockSpec(memory_space=pltpu.VMEM), pl.BlockSpec(memory_space=pl.ANY)
    tokens, width = mix.shape
    size = columns.shape[1]
    half = jax.ShapeDtypeStruct((plane, width // (2 * plane), size), BF16)
    return pl.pallas_call(
        mixer_grads_kernel,
        in_specs=[pl.BlockSpec(memory_space=pltpu.SMEM), vmem, vmem, any_space, any_space],
        out_specs=[vmem] * 2,
        out_shape=[half, half],
        scratch_shapes=[
            pltpu.VMEM((tokens, width), BF16),
            pltpu.VMEM((width, size - size // 4), F32),
            pltpu.VMEM((width, size // 4), F32),
            pltpu.SemaphoreType.DMA((4,)),
        ],
        compiler_params=pltpu.CompilerParams(vmem_limit_bytes=VMEM_LIMIT),
        cost_estimate=SHORT,
    )(places, columns, mix, early, late)


def load_all(copies):
    for copy in copies:
        copy.start()


def in_time(rows):
    half = rows.shape[0] // 4
    return jnp.concatenate([rows[k * half : (k + 1) * half] for k in (0, 2, 1, 3)], axis=0)


def rows_out(acc_ref, core, mine_ref, other_ref):
    half = mine_ref.shape[0]
    mine_ref[...] = acc_ref[pl.ds(pl.multiple_of(core * half, half), half)]
    rest = acc_ref[pl.ds(pl.multiple_of((1 - core) * half, half), half)]
    other_ref[...] = rest.astype(BF16)


def weight_copies(whole_ref, out_ref, in_buf, out_buf, sems, start):
    size = in_buf.shape[2]
    copies = [
        pltpu.make_async_copy(
            whole_ref.at[:, pl.ds(start + k * size, size)], in_buf.at[k], sems.at[k]
        )
        for k in range(in_buf.shape[0])
    ]
    return copies, pltpu.make_async_copy(out_ref, out_buf, sems.at[len(copies)])


def conv_taps(mixed, kernel, masks):
    terms = [mixed]
    for lag in range(1, len(masks) + 1):
        terms.append(pltpu.roll(mixed, lag, 0) * masks[lag - 1])
    taps = kernel.shape[0]
    total = kernel[taps - 1 : taps] * terms[0]
    for lag in range(1, taps):
        total = total + kernel[taps - 1 - lag : taps - lag] * terms[lag]
    return terms, total


def conv_forward_kernel(
    core_ref, rows_ref, kernel_ref, masks_ref, whole_ref, out_ref,
    proj_ref, gated_ref, mine_ref, other_ref, in_buf, out_buf, acc_ref, sems,
):
    copies, last = weight_copies(whole_ref, out_ref, in_buf, out_buf, sems, 0)
    load_all([*copies, last])
    rows = rows_ref[...]
    parts = []
    for k, copy in enumerate(copies):
        copy.wait()
        part = product(rows, in_buf[k])
        proj_ref[k] = part.astype(BF16)
        parts.append(in_time(part))
    masks = [masks_ref[lag] for lag in range(masks_ref.shape[0])]
    gated = []
    for at in range(0, parts[0].shape[1], 128):
        before, after, signal = [part[:, at : at + 128] for part in parts]
        _, total = conv_taps(before * signal, kernel_ref[:, at : at + 128], masks)
        gated.append((after * total).astype(BF16))
    gated = in_time(jnp.concatenate(gated, axis=1))
    gated_ref[...] = gated
    last.wait()
    acc_ref[...] = product(gated, out_buf[...])
    rows_out(acc_ref, core_ref[0], mine_ref, other_ref)


def tiles_out(tiles_ref, gated_ref, columns):
    count, rows, size = tiles_ref.shape
    step = gated_ref.shape[1] // count
    for k in range(count):
        parts = [columns(k)]
        spare = size - parts[0].shape[1] - step
        if spare:
            parts.append(jnp.zeros((rows, spare), BF16))
        tiles_ref[k] = jnp.concatenate([*parts, gated_ref[:, k * step : (k + 1) * step]], axis=1)


def conv_backward_kernel(
    core_ref, grad_ref, kernel_ref, masks_ref, proj_ref, gated_ref, other_tiles_ref,
    whole_ref, out_ref, tiles_ref, taps_ref, mine_ref, other_ref, in_buf, out_buf, acc_ref, sems,
):
    copies, last = weight_copies(whole_ref, out_ref, in_buf, out_buf, sems, 0)
    load_all([last, *copies])
    last.wait()
    grad_gated = in_time(product_right(grad_ref[...], out_buf[...]))
    parts = [in_time(proj_ref[k].astype(F32)) for k in range(3)]
    masks = [masks_ref[lag] for lag in range(masks_ref.shape[0])]
    rows = grad_gated.shape[0]
    grads = [[], [], []]
    for at in range(0, grad_gated.shape[1], 128):
        before, after, signal = [part[:, at : at + 128] for part in parts]
        kernel = kernel_ref[:, at : at + 128]
        terms, total = conv_taps(before * signal, kernel, masks)
        grad = grad_gated[:, at : at + 128]
        grad_total = grad * after
        taps = kernel.shape[0]
        grad_mixed = kernel[taps - 1 : taps] * grad_total
        for lag in range(1, taps):
            sent = pltpu.roll(grad_total * masks[lag - 1], rows - lag, 0)
            grad_mixed = grad_mixed + kernel[taps - 1 - lag : taps - lag] * sent
        for lag in range(taps):
            taps_ref[taps - 1 - lag : taps - lag, at : at + 128] = jnp.sum(
                grad_total * terms[lag], axis=0, keepdims=True
            )
        for k, value in enumerate((grad_mixed * signal, grad * total, grad_mixed * before)):
            grads[k].append(value.astype(BF16))
    grads = [in_time(jnp.concatenate(g, axis=1)) for g in grads]
    step = grads[0].shape[1] // tiles_ref.shape[0]

    @pl.when(core_ref[1] == 0)
    def _():
        tiles_out(
            tiles_ref,
            gated_ref,
            lambda k: jnp.concatenate([g[:, k * step : (k + 1) * step] for g in grads], axis=1),
        )

    @pl.when(core_ref[1] > 0)
    def _():
        tiles_ref[...] = other_tiles_ref[...]

    for k, copy in enumerate(copies):
        copy.wait()
        part = product_right(grads[k], in_buf[k])
        acc_ref[...] = part if k == 0 else acc_ref[...] + part
    rows_out(acc_ref, core_ref[0], mine_ref, other_ref)


def head_kind(head):
    return min(max(head % (GROUP + 2) - GROUP + 1, 0), 2)


def lane_facts(rows):
    lane = lax.broadcasted_iota(jnp.int32, (rows, 128), 1)
    return lane < HEAD_DIM, lax.rem(lane, HEAD_DIM) < HEAD_DIM // 2


def head_scales(block, low):
    squares = block * block
    first = jnp.sum(jnp.where(low, squares, 0.0), axis=1, keepdims=True)
    second = jnp.sum(jnp.where(low, 0.0, squares), axis=1, keepdims=True)
    return lax.rsqrt(jnp.where(low, first, second) * (1.0 / HEAD_DIM) + EPSILON)


def block_gains(gains_ref, at):
    heads = [head_kind(2 * at), head_kind(2 * at + 1)]
    return heads, gains_ref[3 * heads[0] + heads[1] : 3 * heads[0] + heads[1] + 1]


def attention_forward_kernel(
    core_ref, rows_ref, gains_ref, tables_ref, mask_ref, whole_ref, out_ref,
    qkv_ref, ready_ref, gated_ref, mine_ref, other_ref, in_buf, out_buf, acc_ref, sems,
):
    copies, last = weight_copies(
        whole_ref, out_ref, in_buf, out_buf, sems, whole_ref.shape[1] - in_buf.shape[2]
    )
    load_all([*copies, last])
    copies[0].wait()
    qkv_ref[...] = product(rows_ref[...], in_buf[0])
    rows, width = qkv_ref.shape
    low, front = lane_facts(rows)
    cosine, sine = tables_ref[0], tables_ref[1]
    for at in range(width // 128):
        block = qkv_ref[:, at * 128 : (at + 1) * 128]
        heads, gains = block_gains(gains_ref, at)
        normed = block * head_scales(block, low) * gains
        turned = jnp.where(front, -pltpu.roll(normed, 96, 1), pltpu.roll(normed, 32, 1))
        ready = normed * cosine + turned * sine
        if heads[0] == 2:
            ready = jnp.where(low, block, ready)
        if heads[1] == 2:
            ready = jnp.where(low, ready, block)
        ready_ref[:, at * 128 : (at + 1) * 128] = ready.astype(BF16)
    half = rows // 4
    span = (GROUP + 2) * HEAD_DIM
    for m in range(2):
        mask = mask_ref[m] > 0
        mask = jnp.concatenate([mask] * GROUP, axis=0)
        for g in range(width // span):
            queries, keys, values = head_rows(ready_ref, m, half, g * span)
            weights = softmax_weights(queries, keys, mask)
            attended = product(weights.astype(BF16), values).astype(BF16)
            for j in range(GROUP):
                at = (g * GROUP + j) * HEAD_DIM
                head = attended[j * 2 * half : (j + 1) * 2 * half]
                gated_ref[m * half : (m + 1) * half, at : at + HEAD_DIM] = head[:half]
                gated_ref[(m + 2) * half : (m + 3) * half, at : at + HEAD_DIM] = head[half:]
    last.wait()
    acc_ref[...] = product(gated_ref[...], out_buf[...])
    rows_out(acc_ref, core_ref[0], mine_ref, other_ref)


def sequence(ref, m, half, at):
    columns = slice(at, at + HEAD_DIM)
    return jnp.concatenate(
        [ref[m * half : (m + 1) * half, columns], ref[(m + 2) * half : (m + 3) * half, columns]],
        axis=0,
    )


def head_rows(ref, m, half, at):
    heads = [sequence(ref, m, half, at + j * HEAD_DIM) for j in range(GROUP + 2)]
    return jnp.concatenate(heads[:GROUP], axis=0), heads[GROUP], heads[GROUP + 1]


def softmax_weights(queries, keys, mask):
    scores = jnp.where(mask, product_right(queries, keys) * HEAD_DIM ** (-0.5), MASKED_SCORE)
    terms = jnp.exp(scores - jnp.max(scores, axis=1, keepdims=True))
    return terms / jnp.sum(terms, axis=1, keepdims=True)


def attention_backward_kernel(
    core_ref, grad_ref, gains_ref, tables_ref, mask_ref, qkv_ref, ready_ref, gated_ref,
    whole_ref, out_ref, tiles_ref, heads_ref, mine_ref, other_ref,
    in_buf, out_buf, acc_ref, attended_ref, ready_grad_ref, proj_ref, sems,
):
    copies, last = weight_copies(
        whole_ref, out_ref, in_buf, out_buf, sems, whole_ref.shape[1] - in_buf.shape[2]
    )
    load_all([last, *copies])
    last.wait()
    attended_ref[...] = product_right(grad_ref[...], out_buf[...]).astype(BF16)
    rows, width = qkv_ref.shape
    half = rows // 4
    span = (GROUP + 2) * HEAD_DIM
    scale = HEAD_DIM ** (-0.5)
    for m in range(2):
        mask = mask_ref[m] > 0
        mask = jnp.concatenate([mask] * GROUP, axis=0)
        for g in range(width // span):
            queries, keys, values = head_rows(ready_ref, m, half, g * span)
            weights = softmax_weights(queries, keys, mask)
            grad = jnp.concatenate(
                [
                    sequence(attended_ref, m, half, (g * GROUP + j) * HEAD_DIM)
                    for j in range(GROUP)
                ],
                axis=0,
            )
            grad_values = product_left(weights.astype(BF16), grad)
            grad_weights = product_right(grad, values)
            mean = jnp.sum(grad_weights * weights, axis=1, keepdims=True)
            grad_scores = (weights * (grad_weights - mean)).astype(BF16)
            grad_queries = product(grad_scores, keys) * scale
            grad_keys = product_left(grad_scores, queries) * scale
            outs = [grad_queries[j * 2 * half : (j + 1) * 2 * half] for j in range(GROUP)]
            for j, out in enumerate([*outs, grad_keys, grad_values]):
                at = g * span + j * HEAD_DIM
                ready_grad_ref[m * half : (m + 1) * half, at : at + HEAD_DIM] = out[:half]
                ready_grad_ref[(m + 2) * half : (m + 3) * half, at : at + HEAD_DIM] = out[half:]
    low, front = lane_facts(rows)
    cosine, sine = tables_ref[0], tables_ref[1]
    for at in range(width // 128):
        lanes = slice(at * 128, (at + 1) * 128)
        block, grad = qkv_ref[:, lanes], ready_grad_ref[:, lanes]
        heads, gains = block_gains(gains_ref, at)
        inverse = head_scales(block, low)
        normed = block * inverse
        turned = grad * sine
        grad_normed = grad * cosine + jnp.where(
            front, pltpu.roll(turned, 96, 1), -pltpu.roll(turned, 32, 1)
        )
        heads_ref[at : at + 1] = jnp.sum(grad_normed * normed, axis=0, keepdims=True)
        grad_normed = grad_normed * gains
        along = grad_normed * normed
        first = jnp.sum(jnp.where(low, along, 0.0), axis=1, keepdims=True)
        second = jnp.sum(jnp.where(low, 0.0, along), axis=1, keepdims=True)
        mean = jnp.where(low, first, second) * (1.0 / HEAD_DIM)
        raw = inverse * (grad_normed - normed * mean)
        if heads[0] == 2:
            raw = jnp.where(low, grad, raw)
        if heads[1] == 2:
            raw = jnp.where(low, raw, grad)
        proj_ref[:, lanes] = raw.astype(BF16)
    step = width // tiles_ref.shape[0]
    tiles_out(tiles_ref, gated_ref, lambda k: proj_ref[:, k * step : (k + 1) * step])
    copies[0].wait()
    acc_ref[...] = product_right(proj_ref[...], in_buf[0])
    rows_out(acc_ref, core_ref[0], mine_ref, other_ref)


def mixer_call(kernel, core, operands, whole, weight_out, in_tiles, outs, scratch=()):
    vmem, any_space = pl.BlockSpec(memory_space=pltpu.VMEM), pl.BlockSpec(memory_space=pl.ANY)
    rows, width = operands[0].shape
    channels = weight_out.shape[0]
    outs = [*outs, ((rows // 2, width), F32), ((rows // 2, width), BF16)]
    return pl.pallas_call(
        kernel,
        in_specs=[
            pl.BlockSpec(memory_space=pltpu.SMEM),
            *[vmem] * len(operands),
            any_space,
            any_space,
        ],
        out_specs=[vmem] * len(outs),
        out_shape=[jax.ShapeDtypeStruct(*out) for out in outs],
        scratch_shapes=[
            pltpu.VMEM((in_tiles[0], width, in_tiles[1]), BF16),
            pltpu.VMEM((channels, width), BF16),
            pltpu.VMEM((rows, width), F32),
            *scratch,
            pltpu.SemaphoreType.DMA((in_tiles[0] + 1,)),
        ],
        compiler_params=pltpu.CompilerParams(vmem_limit_bytes=VMEM_LIMIT),
        cost_estimate=SHORT,
    )(core, *operands, whole, weight_out)


def conv_forward_call(core, rows, kernel, masks, whole, weight_out):
    count, channels = rows.shape[0], kernel.shape[1]
    outs = [((3, count, channels), BF16), ((count, channels), BF16)]
    operands = (rows, kernel, masks)
    return mixer_call(
        conv_forward_kernel, core, operands, whole, weight_out, (3, channels), outs
    )


def conv_backward_call(core, grad, kernel, masks, projected, gated, tiles, whole, weight_out):
    count, width = grad.shape
    taps, channels = kernel.shape
    outs = [
        (tiles.shape, BF16),
        ((taps, channels), F32),
    ]
    operands = (grad, kernel, masks, projected, gated, tiles)
    return mixer_call(
        conv_backward_kernel, core, operands, whole, weight_out, (3, channels), outs
    )


def attention_forward_call(core, rows, gains, tables, mask, whole, weight_out, qkv_width):
    count, channels = rows.shape[0], weight_out.shape[0]
    outs = [((count, qkv_width), F32), ((count, qkv_width), BF16), ((count, channels), BF16)]
    operands = (rows, gains, tables, mask)
    return mixer_call(
        attention_forward_kernel, core, operands, whole, weight_out, (1, qkv_width), outs
    )


def attention_backward_call(
    core, grad, gains, tables, mask, qkv, ready, gated, whole, weight_out
):
    count, width = grad.shape
    channels, qkv_width = weight_out.shape[0], qkv.shape[1]
    outs = [
        ((4, count, channels), BF16),
        ((qkv_width // 128, 128), F32),
    ]
    scratch = [
        pltpu.VMEM((count, channels), BF16),
        pltpu.VMEM((count, qkv_width), F32),
        pltpu.VMEM((count, qkv_width), BF16),
    ]
    operands = (grad, gains, tables, mask, qkv, ready, gated)
    return mixer_call(
        attention_backward_kernel, core, operands, whole, weight_out, (1, qkv_width), outs, scratch
    )


def conv_masks(segments, taps):
    masks = []
    for lag in range(1, taps):
        same = (segments[:, lag:] == segments[:, :-lag]).astype(F32)
        same = jnp.pad(same, ((0, 0), (lag, 0))).reshape(-1, 1)
        masks.append(jnp.broadcast_to(same, (same.shape[0], 128)))
    return jnp.stack(masks)


def score_mask(segments):
    position = jnp.arange(segments.shape[1])
    allowed = position[:, None] >= position[None, :]
    return (allowed & (segments[:, :, None] == segments[:, None, :])).astype(F32)


def turn_tables(length):
    half = HEAD_DIM // 2
    exponent = jnp.arange(half, dtype=F32) * (2.0 / HEAD_DIM)
    frequency = jnp.exp(-exponent * jnp.log(ROPE_BASE))
    angles = jnp.arange(length, dtype=F32)[:, None] * frequency[None, :]
    tables = jnp.tile(jnp.stack([jnp.cos(angles), jnp.sin(angles)]), (1, 1, 4))
    tables = tables.reshape(2, 2, 1, length // 2, 128)
    return jnp.broadcast_to(tables, (2, 2, 2, length // 2, 128)).reshape(2, 2 * length, 128)


def gain_rows(head_gains):
    kinds = [head_gains[0], head_gains[1], jnp.ones_like(head_gains[0])]
    rows = [jnp.concatenate([a, b]) for a in kinds for b in kinds]
    return jnp.stack(rows)


def head_gain_sums(sums):
    heads = sums.reshape(-1, GROUP + 2, HEAD_DIM)
    return jnp.stack([heads[:, :GROUP].sum((0, 1)), heads[:, GROUP].sum(0)])


def local(
    inputs,
    out_cotangent,
    segments,
    norm_gains,
    conv_kernel,
    qk_gains,
    conv_in,
    attn_qkv,
    mixer_out,
    gate_up,
    down,
):
    section = lax.axis_index("xh")
    first = section == 0
    core = lax.axis_index("c")
    place = lax.axis_index("y") * 4 + lax.axis_index("z")
    xl = lax.axis_index("xl")
    plane = lax.axis_size("y") * lax.axis_size("z")

    shape = inputs.shape[1:]
    width = shape[-1]
    inputs, out_cotangent = inputs.reshape(-1, width), out_cotangent.reshape(-1, width)
    segments = segments[0]
    half = inputs.shape[0]
    rows = 2 * half
    channels = conv_in.shape[2]
    kernel = lax.dynamic_slice_in_dim(conv_kernel, core * channels, channels, 1).astype(F32)
    gains = lax.dynamic_index_in_dim(norm_gains, section, 0, keepdims=False).astype(F32)
    weight_out, weight_pair, weight_down = mixer_out[0], gate_up[0], down[0]
    hidden_units = weight_down.shape[0]
    part = hidden_units // plane
    in_width = 3 * channels
    qkv_width = attn_qkv.shape[1]
    z = lax.axis_index("z")
    core_scalar = jnp.stack([core, section]).astype(jnp.int32)
    xl_scalar = jnp.stack([xl, section, z]).astype(jnp.int32)

    def chosen(from_first, from_second):
        return jnp.where(first, from_first, from_second)

    def gathered(own, axes):
        return lax.all_gather(own, axes, tiled=True)


    both = jnp.concatenate([conv_in.reshape(-1, in_width), attn_qkv], axis=1)
    whole = gathered(both, ("xh", "xl", "y", "z"))

    lanes = -(-part // 256) * 256
    fill = lanes - part
    part_pair = jnp.concatenate(
        [
            jnp.pad(lax.dynamic_slice_in_dim(w, place * part, part, 1), ((0, 0), (0, fill)))
            for w in (weight_pair[0], weight_pair[1])
        ],
        axis=1,
    )
    part_down = lax.dynamic_slice_in_dim(weight_down, place * part, part, 0)
    part_down = jnp.pad(part_down, ((0, fill), (0, 0)))
    masks = conv_masks(segments, kernel.shape[0])
    mask = score_mask(segments)
    tables = turn_tables(segments.shape[1])
    head_gains = gain_rows(qk_gains.astype(F32))
    first_in = inputs.astype(F32)
    normed_own_0 = (normalize(first_in) * gains[0]).astype(BF16)
    normed_0 = spread(normed_own_0)
    cotangent_1 = spread(out_cotangent)
    whole, part_pair, part_down, masks, mask, tables, head_gains, normed_0, cotangent_1 = (
        lax.optimization_barrier(
            (whole, part_pair, part_down, masks, mask, tables, head_gains, normed_0, cotangent_1)
        )
    )

    def feed_forward(hidden, behind=()):
        inner_own = (normalize(hidden) * gains[1]).astype(BF16)
        gate, up, mine, other = feed_forward_call(
            False, core_scalar, spread(inner_own), weight_pair, weight_down, behind=behind
        )
        return hidden + joined(mine, other), (inner_own, gate, up)

    def feed_forward_back(grad_full, grad, hidden, saved, behind=()):
        mine, other = feed_forward_call(
            True, core_scalar, grad_full, weight_pair, weight_down, saved[1:], behind
        )
        return back_join_call(core_scalar, mine, swapped(other, "c"), hidden, grad, gains[1])

    def mixer_back(grad_hidden, mine, other, layer_in, behind):
        come = swapped(other, "c")
        return back_join_call(behind, mine, come, layer_in, grad_hidden, gains[0])[1:]

    plane_axes = ("y", "z", "c")
    early = gathered(chosen(normed_own_0, out_cotangent), plane_axes)

    projected, gated_0, mine, other = conv_forward_call(
        core_scalar, normed_0, kernel, masks, whole, weight_out
    )
    hidden_0 = first_in + joined(mine, other)
    result_0, ffn_0 = feed_forward(hidden_0)
    result_0 = result_0.astype(BF16)

    second_in = lax.ppermute(result_0, "xh", [(0, 1)]).astype(F32)
    normed_own_1 = (normalize(second_in) * gains[0]).astype(BF16)
    qkv, ready, gated_1, mine, other = attention_forward_call(
        core_scalar, spread(normed_own_1), head_gains, tables, mask, whole, weight_out, qkv_width
    )
    hidden_1 = second_in + joined(mine, other)
    result_1, ffn_1 = feed_forward(hidden_1, (early,))
    result_1 = result_1.astype(BF16)

    inner_all = gathered(chosen(ffn_0[0], ffn_1[0]), plane_axes)

    grad_hidden_1, grad_mix_1, gain_inner_1 = feed_forward_back(
        cotangent_1, out_cotangent.astype(F32), hidden_1, ffn_1
    )
    tiles_1, head_sums, mine, other = attention_backward_call(
        core_scalar,
        spread(grad_mix_1),
        head_gains,
        tables,
        mask,
        qkv,
        ready,
        gated_1,
        whole,
        weight_out,
    )
    input_grad_1, gain_outer_1 = mixer_back(grad_hidden_1, mine, other, second_in, core_scalar)

    cotangent = lax.ppermute(input_grad_1, "xh", [(1, 0)])
    late = gathered(chosen(cotangent, normed_own_1), plane_axes)
    grad_hidden_0, grad_mix_0, gain_inner_0 = feed_forward_back(
        spread(cotangent), cotangent.astype(F32), hidden_0, ffn_0
    )
    mix_y = gathered(chosen(grad_mix_0, grad_mix_1), ("y", "c"))
    tiles, grad_kernel, mine, other = conv_backward_call(
        core_scalar,
        spread(grad_mix_0),
        kernel,
        masks,
        projected,
        gated_0,
        tiles_1,
        whole,
        weight_out,
    )
    columns = exchanged(tiles, "y").reshape(4 * rows, -1)
    part_kept = part_forward_call(tiles, inner_all, part_pair)

    def summed_over_pair(mine, other):
        return mine.astype(F32) + swapped(other, "xl").astype(F32)

    pair_grads, down_mine, down_other = lax.cond(
        first,
        lambda: part_down_call(xl_scalar, late, part_kept, part_down, (columns,)),
        lambda: part_down_call(xl_scalar, early, part_kept, part_down, (columns,)),
    )
    input_grad_0, gain_outer_0 = mixer_back(grad_hidden_0, mine, other, first_in, pair_grads)
    pair_mine, pair_other = part_pair_call(xl_scalar, inner_all, pair_grads, ())
    mix_mine, mix_other = mixer_grads_call(xl_scalar, columns, mix_y, early, late, plane)

    total = [summed_over_pair(pair_mine, pair_other), summed_over_pair(down_mine, down_other)]
    total = jnp.concatenate(total, axis=1).astype(BF16)
    arrived = exchanged(total.reshape(plane, -1, 3 * lanes), PLANE)
    lines = [
        jnp.moveaxis(arrived[:, :, k * lanes : k * lanes + part], 0, 1)
        .reshape(-1, hidden_units)
        .astype(F32)
        for k in range(3)
    ]
    grad_gate_up = jnp.stack(lines[:2])[None]
    grad_down = lines[2].T[None]

    total = summed_over_pair(mix_mine, mix_other).astype(BF16)
    come = exchanged(total, PLANE)
    lines = come.reshape(4, 4, *come.shape[1:]).astype(F32).sum(1)
    split = in_width // 4
    grad_mixer_out = lines[:, :, split:].transpose(0, 2, 1).reshape(1, channels, -1)
    lines = lines[:, :, :split].reshape(4, 2, -1, split)
    kept_lines = lax.dynamic_index_in_dim(lines, section, 1, keepdims=False)
    sent_lines = lax.dynamic_index_in_dim(lines, 1 - section, 1, keepdims=False)
    come = swapped(sent_lines.astype(BF16), "xh").astype(F32)
    lines = chosen(kept_lines, come).reshape(4, -1, 3, channels // 4)
    grad_conv_in = jnp.moveaxis(lines, 0, 2).reshape(conv_in.shape)
    lines = chosen(come, kept_lines)[:, :, : qkv_width // 4]
    grad_attn_qkv = jnp.moveaxis(lines, 0, 1).reshape(attn_qkv.shape)

    full_kernel = lax.dynamic_update_slice(
        jnp.zeros(conv_kernel.shape, F32), grad_kernel, (0, core * channels)
    )
    small = jnp.concatenate(
        [
            chosen(gain_outer_0, gain_outer_1),
            chosen(gain_inner_0, gain_inner_1),
            full_kernel.reshape(-1),
            head_gain_sums(head_sums).reshape(-1),
        ]
    )
    count = small.shape[0]
    small = jnp.pad(small, (0, -count % 1024)).reshape(-1, 128)
    sums = section_sums_call(lax.all_gather(small, AXES), (arrived,))
    pair = [sums[0].reshape(-1), sums[1].reshape(-1)]
    grad_norm_gains = jnp.stack([a[: 2 * width].reshape(2, width) for a in pair])
    grad_conv_kernel = pair[0][2 * width : 5 * width].reshape(conv_kernel.shape)
    grad_qk_gains = pair[1][5 * width : count].reshape(qk_gains.shape)

    activations = chosen(result_0, result_1).reshape(1, 1, *shape)
    input_grads = chosen(input_grad_0, input_grad_1).reshape(1, 1, *shape)
    return (
        activations,
        input_grads,
        grad_norm_gains,
        grad_conv_kernel,
        grad_qk_gains,
        grad_conv_in,
        grad_attn_qkv,
        grad_mixer_out,
        grad_gate_up,
        grad_down,
    )


def solution(mesh):
    wide = Mesh(mesh.devices.reshape(2, 2, 4, 4, 2), AXES)
    dp = ("xl", "y", "z")
    everyone = ("xh", "xl", "y", "z")
    in_specs = (
        P(dp, None, "c", None),
        P(dp, None, "c", None),
        P(dp, None, None),
        P(),
        P(),
        P(),
        P(everyone, None, "c"),
        P(everyone, "c"),
        P("xh", "c", None),
        P("xh", None, None, "c"),
        P("xh", "c", None),
    )
    out_specs = (
        P("xh", dp, None, "c", None),
        P("xh", dp, None, "c", None),
        P(),
        P(),
        P(),
        P(everyone, None, "c"),
        P(everyone, "c"),
        P("xh", "c", dp),
        P("xh", None, dp, "c"),
        P("xh", "c", dp),
    )
    return jax.shard_map(local, mesh=wide, in_specs=in_specs, out_specs=out_specs, check_vma=False)
```

```python
import functools

import jax
import jax.numpy as jnp
from jax import lax
from jax.experimental import pallas as pl
from jax.experimental.pallas import tpu as pltpu
from jax.sharding import Mesh
from jax.sharding import PartitionSpec as P

HEADS = 24
KV_HEADS = 8
HEAD_DIM = 64
GROUP = HEADS // KV_HEADS

EPSILON = 1e-05
ROPE_BASE = 1000000.0
MASKED_SCORE = -1e30

F32 = jnp.float32
BF16 = jnp.bfloat16

PLANE = ("y", "z")
AXES = ("xh", "xl", "y", "z", "c")


def product(left, right):
    return jnp.dot(left, right, preferred_element_type=F32)


def product_left(left, right):
    return lax.dot_general(left, right, (((0,), (0,)), ((), ())), preferred_element_type=F32)


def product_right(left, right):
    return lax.dot_general(left, right, (((1,), (1,)), ((), ())), preferred_element_type=F32)


def swapped(shard, axis):
    return lax.ppermute(shard, axis, [(0, 1), (1, 0)])


def spread(own):
    return lax.all_gather(own, "c", tiled=True)


def joined(mine, other):
    return mine + swapped(other, "c").astype(F32)


def mean_last(values):
    return jnp.mean(values, axis=-1, keepdims=True)


def inverse_rms(values):
    return lax.rsqrt(mean_last(values * values) + EPSILON)


def normalize(values):
    return values * inverse_rms(values)


def exchanged(tiles, axes):
    return lax.all_to_all(tiles, axes, 0, 0, tiled=True)


def ffn_grads(grad_active, gate, up):
    sigmoid = jax.nn.sigmoid(gate)
    grad_gate = grad_active * up * sigmoid * (1.0 + gate * (1.0 - sigmoid))
    grad_up = grad_active * gate * sigmoid
    return grad_gate.astype(BF16), grad_up.astype(BF16)


VMEM_LIMIT = 56 * 1024 * 1024
SHORT = pl.CostEstimate(flops=1, bytes_accessed=1, transcendentals=0)


def whole_lanes(columns):
    return -(-columns // 128) * 128


def ordered(kernel, count):
    def body(scalar_ref, *refs):
        kernel(scalar_ref, *refs[count:])

    return body


def unit_tiles(units, tile):
    short = units % tile
    tiles = [(0, short)] if short else []
    return tiles + [(at, tile) for at in range(short, units, tile)]


def streamed(tiles, copies, work):
    for copy in copies(0, 0):
        copy.start()
    for k in range(len(tiles)):
        slot = k % 2
        if k + 1 < len(tiles):
            for copy in copies(k + 1, 1 - slot):
                copy.start()
        for copy in copies(k, slot):
            copy.wait()
        work(k, slot)


def ffn_forward_kernel(
    tiles, core_ref, rows_ref, pair_ref, down_ref, gate_ref, up_ref, mine_ref, other_ref,
    pair_buf, down_buf, gate_buf, up_buf, acc_ref, sems, out_sems,
):
    def copies(k, slot):
        at, size = tiles[k]
        return [
            pltpu.make_async_copy(
                pair_ref.at[0, :, pl.ds(at, size)],
                pair_buf.at[slot, :, pl.ds(0, size)],
                sems.at[slot, 0],
            ),
            pltpu.make_async_copy(
                pair_ref.at[1, :, pl.ds(at, size)],
                pair_buf.at[slot, :, pl.ds(size, size)],
                sems.at[slot, 1],
            ),
            pltpu.make_async_copy(
                down_ref.at[pl.ds(at, size)], down_buf.at[slot, pl.ds(0, size)], sems.at[slot, 2]
            ),
        ]

    def kept(k):
        here = (slice(None), pl.ds(*tiles[k]))
        return [
            pltpu.make_async_copy(gate_buf.at[here], gate_ref.at[here], out_sems.at[k, 0]),
            pltpu.make_async_copy(up_buf.at[here], up_ref.at[here], out_sems.at[k, 1]),
        ]

    def work(k, slot):
        at, size = tiles[k]
        both = product(rows_ref[...], pair_buf[slot, :, : 2 * size])
        gate, up = both[:, :size], both[:, size:]
        gate_buf[:, at : at + size] = gate.astype(BF16)
        up_buf[:, at : at + size] = up.astype(BF16)
        for copy in kept(k):
            copy.start()
        active = (gate * jax.nn.sigmoid(gate) * up).astype(BF16)
        part = product(active, down_buf[slot, :size])
        if k == 0:
            acc_ref[...] = part
        else:
            acc_ref[...] += part

    streamed(tiles, copies, work)
    rows_out(acc_ref, core_ref[0], mine_ref, other_ref)
    for k in range(len(tiles)):
        for copy in kept(k):
            copy.wait()


def ffn_backward_kernel(
    tiles, core_ref, rows_ref, gate_ref, up_ref, pair_ref, down_ref, mine_ref, other_ref,
    pair_buf, down_buf, gate_buf, up_buf, acc_ref, sems,
):
    def copies(k, slot):
        at, size = tiles[k]
        columns, place = pl.ds(at, size), pl.ds(0, size)
        return [
            pltpu.make_async_copy(
                down_ref.at[columns], down_buf.at[slot, place], sems.at[slot, 0]
            ),
            pltpu.make_async_copy(
                gate_ref.at[:, columns], gate_buf.at[slot, :, place], sems.at[slot, 1]
            ),
            pltpu.make_async_copy(
                up_ref.at[:, columns], up_buf.at[slot, :, place], sems.at[slot, 2]
            ),
            pltpu.make_async_copy(
                pair_ref.at[0, :, columns], pair_buf.at[slot, :, place], sems.at[slot, 3]
            ),
            pltpu.make_async_copy(
                pair_ref.at[1, :, columns],
                pair_buf.at[slot, :, pl.ds(size, size)],
                sems.at[slot, 4],
            ),
        ]

    def work(k, slot):
        _, size = tiles[k]
        grad_active = product_right(rows_ref[...], down_buf[slot, :size])
        grads = ffn_grads(
            grad_active,
            gate_buf[slot, :, :size].astype(F32),
            up_buf[slot, :, :size].astype(F32),
        )
        part = product_right(jnp.concatenate(grads, axis=1), pair_buf[slot, :, : 2 * size])
        if k == 0:
            acc_ref[...] = part
        else:
            acc_ref[...] += part

    streamed(tiles, copies, work)
    rows_out(acc_ref, core_ref[0], mine_ref, other_ref)


def feed_forward_call(backward, core, rows, pair, down, saved=(), behind=()):
    count, width = rows.shape
    units = down.shape[0]
    tile = 768
    tiles = unit_tiles(units, tile)
    vmem, any_space = pl.BlockSpec(memory_space=pltpu.VMEM), pl.BlockSpec(memory_space=pl.ANY)
    scalar = pl.BlockSpec(memory_space=pltpu.SMEM)
    out_shape = [
        jax.ShapeDtypeStruct((count // 2, width), F32),
        jax.ShapeDtypeStruct((count // 2, width), BF16),
    ]
    out_specs = [vmem, vmem]
    buffers = [pltpu.VMEM((2, width, 2 * tile), BF16), pltpu.VMEM((2, tile, width), BF16)]
    acc = pltpu.VMEM((count, width), F32)
    if backward:
        body = functools.partial(ffn_backward_kernel, tiles)
        in_specs = [scalar, vmem, any_space, any_space, any_space, any_space]
        buffers += [pltpu.VMEM((2, count, tile), BF16)] * 2
        scratch = [*buffers, acc, pltpu.SemaphoreType.DMA((2, 5))]
    else:
        body = functools.partial(ffn_forward_kernel, tiles)
        in_specs = [scalar, vmem, any_space, any_space]
        out_shape = [jax.ShapeDtypeStruct((count, units), BF16)] * 2 + out_shape
        out_specs = [any_space, any_space, *out_specs]
        buffers += [pltpu.VMEM((count, units), BF16)] * 2
        scratch = [*buffers, acc]
        scratch += [pltpu.SemaphoreType.DMA((2, 3)), pltpu.SemaphoreType.DMA((len(tiles), 2))]
    in_specs = [scalar, *[any_space] * len(behind), *in_specs[1:]]
    return pl.pallas_call(
        ordered(body, len(behind)),
        in_specs=in_specs,
        out_specs=out_specs,
        out_shape=out_shape,
        scratch_shapes=scratch,
        compiler_params=pltpu.CompilerParams(vmem_limit_bytes=VMEM_LIMIT),
        cost_estimate=SHORT,
    )(core, *behind, rows, *saved, pair, down)


def part_forward_kernel(behind_ref, rows_ref, pair_ref, kept_ref):
    both = product(rows_ref[...], pair_ref[...])
    units = both.shape[1] // 2
    gate, up = both[:, :units], both[:, units:]
    sigmoid = jax.nn.sigmoid(gate)
    silu = gate * sigmoid
    kept_ref[:, :units] = (up * (sigmoid + silu * (1.0 - sigmoid))).astype(BF16)
    kept_ref[:, units : 2 * units] = silu.astype(BF16)
    kept_ref[:, 2 * units :] = (silu * up).astype(BF16)


def part_forward_call(behind, rows, pair):
    tokens, width = rows.shape
    units = pair.shape[1] // 2
    tile = 1024
    return pl.pallas_call(
        part_forward_kernel,
        grid=(tokens // tile,),
        in_specs=[
            pl.BlockSpec(memory_space=pl.ANY),
            pl.BlockSpec((tile, width), lambda i: (i, 0)),
            pl.BlockSpec((width, 2 * units), lambda i: (0, 0)),
        ],
        out_specs=pl.BlockSpec((tile, 3 * units), lambda i: (i, 0)),
        out_shape=jax.ShapeDtypeStruct((tokens, 3 * units), BF16),
        compiler_params=pltpu.CompilerParams(vmem_limit_bytes=VMEM_LIMIT),
        cost_estimate=pl.CostEstimate(
            flops=8 * tokens * width * units, bytes_accessed=2 * tokens * width, transcendentals=0
        ),
    )(behind, rows, pair)


def pair_out(acc_ref, here, mine_ref, other_ref):
    rows = mine_ref.shape[0]
    for ref, half in ((mine_ref, here), (other_ref, 1 - here)):
        ref[...] = acc_ref[pl.ds(pl.multiple_of(half * rows, rows), rows)].astype(BF16)


def accumulated(acc_ref, part, finish):
    step = pl.program_id(0)

    @pl.when(step == 0)
    def _():
        acc_ref[...] = part

    @pl.when(step > 0)
    def _():
        acc_ref[...] += part

    pl.when(step == pl.num_programs(0) - 1)(finish)


def part_down_kernel(here_ref, grad_ref, kept_ref, down_ref, pair_ref, mine_ref, other_ref, acc_ref):
    grad = grad_ref[...]
    units = down_ref.shape[0]
    grad_active = product_right(grad, down_ref[...])
    for k in range(2):
        lanes = slice(k * units, (k + 1) * units)
        pair_ref[:, lanes] = (grad_active * kept_ref[:, lanes].astype(F32)).astype(BF16)
    accumulated(
        acc_ref,
        product_left(grad, kept_ref[:, 2 * units :]),
        lambda: pair_out(acc_ref, here_ref[0], mine_ref, other_ref),
    )


def part_pair_kernel(here_ref, rows_ref, pair_ref, mine_ref, other_ref, acc_ref):
    accumulated(
        acc_ref,
        product_left(rows_ref[...], pair_ref[...]),
        lambda: pair_out(acc_ref, here_ref[0], mine_ref, other_ref),
    )


def part_call(kernel, here, operands, fixed, outs, result, flops, behind=()):
    tokens = operands[0].shape[0]
    tile = 1024
    by_tokens = lambda width: pl.BlockSpec((tile, width), lambda i, h: (i, 0))
    entire = lambda shape: pl.BlockSpec(shape, lambda i, h: (0, 0))
    half = (result[0] // 2, result[1])
    return pl.pallas_call(
        ordered(kernel, len(behind)),
        grid_spec=pltpu.PrefetchScalarGridSpec(
            num_scalar_prefetch=1,
            grid=(tokens // tile,),
            in_specs=[pl.BlockSpec(memory_space=pl.ANY)] * len(behind)
            + [by_tokens(a.shape[1]) for a in operands]
            + [entire(a.shape) for a in fixed],
            out_specs=[by_tokens(width) for width in outs] + [entire(half)] * 2,
            scratch_shapes=[pltpu.VMEM(result, F32)],
        ),
        out_shape=[jax.ShapeDtypeStruct((tokens, width), BF16) for width in outs]
        + [jax.ShapeDtypeStruct(half, BF16)] * 2,
        compiler_params=pltpu.CompilerParams(vmem_limit_bytes=VMEM_LIMIT),
        cost_estimate=SHORT,
    )(here, *behind, *operands, *fixed)


def part_down_call(here, grad, kept, down, behind):
    tokens, width = grad.shape
    units = down.shape[0]
    flops = 4 * tokens * width * units
    return part_call(
        part_down_kernel,
        here,
        (grad, kept),
        (down,),
        (2 * units,),
        (width, units),
        flops,
        behind,
    )


def part_pair_call(here, inner, pair, behind):
    (tokens, width), columns = inner.shape, pair.shape[1]
    flops = 2 * tokens * width * columns
    return part_call(
        part_pair_kernel, here, (inner, pair), (), (), (width, columns), flops, behind
    )


def back_join_kernel(
    behind_ref, mine_ref, come_ref, values_ref, base_ref, gain_ref, wide_ref, low_ref, sums_ref
):
    grad = mine_ref[...] + come_ref[...].astype(F32)
    values = values_ref[...]
    inverse = inverse_rms(values)
    normed = values * inverse
    scaled = grad * gain_ref[...]
    sums_ref[...] = jnp.sum(grad * normed, axis=0, keepdims=True)
    total = base_ref[...] + inverse * (scaled - normed * mean_last(scaled * normed))
    wide_ref[...] = total
    low_ref[...] = total.astype(BF16)


def back_join_call(behind, mine, come, values, base, gain):
    vmem = pl.BlockSpec(memory_space=pltpu.VMEM)
    shape = values.shape
    wide, low, sums = pl.pallas_call(
        back_join_kernel,
        in_specs=[pl.BlockSpec(memory_space=pl.ANY), *[vmem] * 5],
        out_specs=[vmem] * 3,
        out_shape=[
            jax.ShapeDtypeStruct(shape, F32),
            jax.ShapeDtypeStruct(shape, BF16),
            jax.ShapeDtypeStruct((1, shape[1]), F32),
        ],
        compiler_params=pltpu.CompilerParams(vmem_limit_bytes=VMEM_LIMIT),
        cost_estimate=SHORT,
    )(behind, mine, come, values, base, gain[None])
    return wide, low, sums[0]


def pair_join_kernel(count, *refs):
    *refs, out_ref = refs[count:]
    at = 0
    for mine_ref, come_ref in zip(refs[::2], refs[1::2]):
        size = mine_ref.shape[-1]
        total = mine_ref[...].astype(F32) + come_ref[...].astype(F32)
        out_ref[..., at : at + size] = total.astype(BF16)
        at += size


def pair_join_call(behind, pairs):
    vmem = pl.BlockSpec(memory_space=pltpu.VMEM)
    operands = [a for pair in pairs for a in pair]
    shape = (*operands[0].shape[:-1], sum(mine.shape[-1] for mine, _ in pairs))
    return pl.pallas_call(
        functools.partial(pair_join_kernel, len(behind)),
        in_specs=[pl.BlockSpec(memory_space=pl.ANY)] * len(behind) + [vmem] * len(operands),
        out_specs=vmem,
        out_shape=jax.ShapeDtypeStruct(shape, BF16),
        compiler_params=pltpu.CompilerParams(vmem_limit_bytes=VMEM_LIMIT),
        cost_estimate=SHORT,
    )(*behind, *operands)


def section_sums_kernel(behind_ref, all_ref, sums_ref):
    half = all_ref.shape[0] // 2
    for k in range(2):
        sums_ref[k] = jnp.sum(all_ref[k * half : (k + 1) * half], axis=0)


def section_sums_call(small, behind):
    vmem = pl.BlockSpec(memory_space=pltpu.VMEM)
    return pl.pallas_call(
        section_sums_kernel,
        in_specs=[pl.BlockSpec(memory_space=pl.ANY), vmem],
        out_specs=vmem,
        out_shape=jax.ShapeDtypeStruct((2, *small.shape[1:]), F32),
        compiler_params=pltpu.CompilerParams(vmem_limit_bytes=VMEM_LIMIT),
        cost_estimate=pl.CostEstimate(flops=0, bytes_accessed=8 * small.size, transcendentals=0),
    )(*behind, small)


def mixer_grads_kernel(
    places_ref, behind_ref, columns_ref, gated_ref, early_ref, late_ref,
    in_mine_ref, in_other_ref, out_mine_ref, out_other_ref, normed_ref, in_ref, out_ref, sems,
):
    count, rows = sems.shape[0], normed_ref.shape[0] // sems.shape[0]
    here, section, z = places_ref[0], places_ref[1], places_ref[2]

    def copies(all_ref):
        span = all_ref.shape[0] // count
        return [
            pltpu.make_async_copy(
                all_ref.at[pl.ds(pl.multiple_of(k * span + z * rows, rows), rows)],
                normed_ref.at[pl.ds(k * rows, rows)],
                sems.at[k],
            )
            for k in range(count)
        ]

    @pl.when(section == 0)
    def _():
        load_all(copies(early_ref))

    @pl.when(section > 0)
    def _():
        load_all(copies(late_ref))

    mix = out_ref.shape[0]
    out_ref[...] = product_left(columns_ref[:, :mix], gated_ref[...])
    pair_out(out_ref, here, out_mine_ref, out_other_ref)
    for copy in copies(early_ref):
        copy.wait()
    in_ref[...] = product_left(normed_ref[...], columns_ref[:, mix:])
    plane, block, _ = in_mine_ref.shape
    short = block // 2
    for ref, half in ((in_mine_ref, here), (in_other_ref, 1 - here)):
        for k in range(plane):
            for s in range(2):
                start = pl.multiple_of(((2 * s + half) * plane + k) * short, short)
                rows_in = in_ref[pl.ds(start, short)]
                ref[k, s * short : (s + 1) * short] = rows_in.astype(BF16)


def mixer_grads_call(places, behind, columns, gated, early, late, plane):
    vmem, any_space = pl.BlockSpec(memory_space=pltpu.VMEM), pl.BlockSpec(memory_space=pl.ANY)
    tokens, channels = gated.shape
    width = early.shape[1]
    mix = width // 4
    size = columns.shape[1] - mix
    in_half = jax.ShapeDtypeStruct((plane, width // (2 * plane), size), BF16)
    out_half = jax.ShapeDtypeStruct((mix // 2, channels), BF16)
    return pl.pallas_call(
        mixer_grads_kernel,
        in_specs=[
            pl.BlockSpec(memory_space=pltpu.SMEM),
            any_space,
            vmem,
            vmem,
            any_space,
            any_space,
        ],
        out_specs=[vmem] * 4,
        out_shape=[in_half, in_half, out_half, out_half],
        scratch_shapes=[
            pltpu.VMEM((tokens, width), BF16),
            pltpu.VMEM((width, size), F32),
            pltpu.VMEM((mix, channels), F32),
            pltpu.SemaphoreType.DMA((4,)),
        ],
        compiler_params=pltpu.CompilerParams(vmem_limit_bytes=VMEM_LIMIT),
        cost_estimate=SHORT,
    )(places, behind, columns, gated, early, late)


def load_all(copies):
    for copy in copies:
        copy.start()


def in_time(rows):
    half = rows.shape[0] // 4
    return jnp.concatenate([rows[k * half : (k + 1) * half] for k in (0, 2, 1, 3)], axis=0)


def rows_out(acc_ref, core, mine_ref, other_ref):
    half = mine_ref.shape[0]
    mine_ref[...] = acc_ref[pl.ds(pl.multiple_of(core * half, half), half)]
    rest = acc_ref[pl.ds(pl.multiple_of((1 - core) * half, half), half)]
    other_ref[...] = rest.astype(BF16)


def weight_copies(whole_ref, out_ref, in_buf, out_buf, sems, start):
    size = in_buf.shape[2]
    copies = [
        pltpu.make_async_copy(
            whole_ref.at[:, pl.ds(start + k * size, size)], in_buf.at[k], sems.at[k]
        )
        for k in range(in_buf.shape[0])
    ]
    return copies, pltpu.make_async_copy(out_ref, out_buf, sems.at[len(copies)])


def conv_taps(mixed, kernel, masks):
    terms = [mixed]
    for lag in range(1, len(masks) + 1):
        terms.append(pltpu.roll(mixed, lag, 0) * masks[lag - 1])
    taps = kernel.shape[0]
    total = kernel[taps - 1 : taps] * terms[0]
    for lag in range(1, taps):
        total = total + kernel[taps - 1 - lag : taps - lag] * terms[lag]
    return terms, total


def conv_forward_kernel(
    core_ref, rows_ref, kernel_ref, masks_ref, whole_ref, out_ref,
    proj_ref, gated_ref, mine_ref, other_ref, in_buf, out_buf, acc_ref, sems,
):
    copies, last = weight_copies(whole_ref, out_ref, in_buf, out_buf, sems, 0)
    load_all([*copies, last])
    rows = rows_ref[...]
    parts = []
    for k, copy in enumerate(copies):
        copy.wait()
        part = product(rows, in_buf[k])
        proj_ref[k] = part.astype(BF16)
        parts.append(in_time(part))
    masks = [masks_ref[lag] for lag in range(masks_ref.shape[0])]
    gated = []
    for at in range(0, parts[0].shape[1], 128):
        before, after, signal = [part[:, at : at + 128] for part in parts]
        _, total = conv_taps(before * signal, kernel_ref[:, at : at + 128], masks)
        gated.append((after * total).astype(BF16))
    gated = in_time(jnp.concatenate(gated, axis=1))
    gated_ref[...] = gated
    last.wait()
    acc_ref[...] = product(gated, out_buf[...])
    rows_out(acc_ref, core_ref[0], mine_ref, other_ref)


def tiles_out(tiles_ref, grad_ref, columns):
    count, rows, size = tiles_ref.shape
    width = grad_ref.shape[1] // 2
    step = width // count
    for k in range(count):
        parts = [grad_ref[:, h * width + k * step : h * width + (k + 1) * step] for h in range(2)]
        parts.append(columns(k))
        spare = size - sum(part.shape[1] for part in parts)
        tiles_ref[k] = jnp.concatenate([*parts, jnp.zeros((rows, spare), BF16)], axis=1)


def conv_backward_kernel(
    core_ref, grad_ref, kernel_ref, masks_ref, proj_ref, other_tiles_ref,
    whole_ref, out_ref, tiles_ref, taps_ref, mine_ref, other_ref, in_buf, out_buf, acc_ref, sems,
):
    copies, last = weight_copies(whole_ref, out_ref, in_buf, out_buf, sems, 0)
    load_all([last, *copies])
    last.wait()
    grad_gated = in_time(product_right(grad_ref[...], out_buf[...]))
    parts = [in_time(proj_ref[k].astype(F32)) for k in range(3)]
    masks = [masks_ref[lag] for lag in range(masks_ref.shape[0])]
    rows = grad_gated.shape[0]
    grads = [[], [], []]
    for at in range(0, grad_gated.shape[1], 128):
        before, after, signal = [part[:, at : at + 128] for part in parts]
        kernel = kernel_ref[:, at : at + 128]
        terms, total = conv_taps(before * signal, kernel, masks)
        grad = grad_gated[:, at : at + 128]
        grad_total = grad * after
        taps = kernel.shape[0]
        grad_mixed = kernel[taps - 1 : taps] * grad_total
        for lag in range(1, taps):
            sent = pltpu.roll(grad_total * masks[lag - 1], rows - lag, 0)
            grad_mixed = grad_mixed + kernel[taps - 1 - lag : taps - lag] * sent
        for lag in range(taps):
            taps_ref[taps - 1 - lag : taps - lag, at : at + 128] = jnp.sum(
                grad_total * terms[lag], axis=0, keepdims=True
            )
        for k, value in enumerate((grad_mixed * signal, grad * total, grad_mixed * before)):
            grads[k].append(value.astype(BF16))
    grads = [in_time(jnp.concatenate(g, axis=1)) for g in grads]
    step = grads[0].shape[1] // tiles_ref.shape[0]

    @pl.when(core_ref[1] == 0)
    def _():
        tiles_out(
            tiles_ref,
            grad_ref,
            lambda k: jnp.concatenate([g[:, k * step : (k + 1) * step] for g in grads], axis=1),
        )

    @pl.when(core_ref[1] > 0)
    def _():
        tiles_ref[...] = other_tiles_ref[...]

    for k, copy in enumerate(copies):
        copy.wait()
        part = product_right(grads[k], in_buf[k])
        acc_ref[...] = part if k == 0 else acc_ref[...] + part
    rows_out(acc_ref, core_ref[0], mine_ref, other_ref)


def head_kind(head):
    return min(max(head % (GROUP + 2) - GROUP + 1, 0), 2)


def lane_facts(rows):
    lane = lax.broadcasted_iota(jnp.int32, (rows, 128), 1)
    return lane < HEAD_DIM, lax.rem(lane, HEAD_DIM) < HEAD_DIM // 2


def head_scales(block, low):
    squares = block * block
    first = jnp.sum(jnp.where(low, squares, 0.0), axis=1, keepdims=True)
    second = jnp.sum(jnp.where(low, 0.0, squares), axis=1, keepdims=True)
    return lax.rsqrt(jnp.where(low, first, second) * (1.0 / HEAD_DIM) + EPSILON)


def block_gains(gains_ref, at):
    heads = [head_kind(2 * at), head_kind(2 * at + 1)]
    return heads, gains_ref[3 * heads[0] + heads[1] : 3 * heads[0] + heads[1] + 1]


def attention_forward_kernel(
    core_ref, rows_ref, gains_ref, tables_ref, mask_ref, whole_ref, out_ref,
    qkv_ref, ready_ref, gated_ref, mine_ref, other_ref, in_buf, out_buf, acc_ref, sems,
):
    copies, last = weight_copies(
        whole_ref, out_ref, in_buf, out_buf, sems, whole_ref.shape[1] - in_buf.shape[2]
    )
    load_all([*copies, last])
    copies[0].wait()
    qkv_ref[...] = product(rows_ref[...], in_buf[0])
    rows, width = qkv_ref.shape
    low, front = lane_facts(rows)
    cosine, sine = tables_ref[0], tables_ref[1]
    for at in range(width // 128):
        block = qkv_ref[:, at * 128 : (at + 1) * 128]
        heads, gains = block_gains(gains_ref, at)
        normed = block * head_scales(block, low) * gains
        turned = jnp.where(front, -pltpu.roll(normed, 96, 1), pltpu.roll(normed, 32, 1))
        ready = normed * cosine + turned * sine
        if heads[0] == 2:
            ready = jnp.where(low, block, ready)
        if heads[1] == 2:
            ready = jnp.where(low, ready, block)
        ready_ref[:, at * 128 : (at + 1) * 128] = ready.astype(BF16)
    half = rows // 4
    span = (GROUP + 2) * HEAD_DIM
    for m in range(2):
        mask = mask_ref[m] > 0
        mask = jnp.concatenate([mask] * GROUP, axis=0)
        for g in range(width // span):
            queries, keys, values = head_rows(ready_ref, m, half, g * span)
            weights = softmax_weights(queries, keys, mask)
            attended = product(weights.astype(BF16), values).astype(BF16)
            for j in range(GROUP):
                at = (g * GROUP + j) * HEAD_DIM
                head = attended[j * 2 * half : (j + 1) * 2 * half]
                gated_ref[m * half : (m + 1) * half, at : at + HEAD_DIM] = head[:half]
                gated_ref[(m + 2) * half : (m + 3) * half, at : at + HEAD_DIM] = head[half:]
    last.wait()
    acc_ref[...] = product(gated_ref[...], out_buf[...])
    rows_out(acc_ref, core_ref[0], mine_ref, other_ref)


def sequence(ref, m, half, at):
    columns = slice(at, at + HEAD_DIM)
    return jnp.concatenate(
        [ref[m * half : (m + 1) * half, columns], ref[(m + 2) * half : (m + 3) * half, columns]],
        axis=0,
    )


def head_rows(ref, m, half, at):
    heads = [sequence(ref, m, half, at + j * HEAD_DIM) for j in range(GROUP + 2)]
    return jnp.concatenate(heads[:GROUP], axis=0), heads[GROUP], heads[GROUP + 1]


def softmax_weights(queries, keys, mask):
    scores = jnp.where(mask, product_right(queries, keys) * HEAD_DIM ** (-0.5), MASKED_SCORE)
    terms = jnp.exp(scores - jnp.max(scores, axis=1, keepdims=True))
    return terms / jnp.sum(terms, axis=1, keepdims=True)


def attention_backward_kernel(
    core_ref, grad_ref, gains_ref, tables_ref, mask_ref, qkv_ref, ready_ref,
    whole_ref, out_ref, tiles_ref, heads_ref, mine_ref, other_ref,
    in_buf, out_buf, acc_ref, attended_ref, ready_grad_ref, proj_ref, sems,
):
    copies, last = weight_copies(
        whole_ref, out_ref, in_buf, out_buf, sems, whole_ref.shape[1] - in_buf.shape[2]
    )
    load_all([last, *copies])
    last.wait()
    attended_ref[...] = product_right(grad_ref[...], out_buf[...]).astype(BF16)
    rows, width = qkv_ref.shape
    half = rows // 4
    span = (GROUP + 2) * HEAD_DIM
    scale = HEAD_DIM ** (-0.5)
    for m in range(2):
        mask = mask_ref[m] > 0
        mask = jnp.concatenate([mask] * GROUP, axis=0)
        for g in range(width // span):
            queries, keys, values = head_rows(ready_ref, m, half, g * span)
            weights = softmax_weights(queries, keys, mask)
            grad = jnp.concatenate(
                [
                    sequence(attended_ref, m, half, (g * GROUP + j) * HEAD_DIM)
                    for j in range(GROUP)
                ],
                axis=0,
            )
            grad_values = product_left(weights.astype(BF16), grad)
            grad_weights = product_right(grad, values)
            mean = jnp.sum(grad_weights * weights, axis=1, keepdims=True)
            grad_scores = (weights * (grad_weights - mean)).astype(BF16)
            grad_queries = product(grad_scores, keys) * scale
            grad_keys = product_left(grad_scores, queries) * scale
            outs = [grad_queries[j * 2 * half : (j + 1) * 2 * half] for j in range(GROUP)]
            for j, out in enumerate([*outs, grad_keys, grad_values]):
                at = g * span + j * HEAD_DIM
                ready_grad_ref[m * half : (m + 1) * half, at : at + HEAD_DIM] = out[:half]
                ready_grad_ref[(m + 2) * half : (m + 3) * half, at : at + HEAD_DIM] = out[half:]
    low, front = lane_facts(rows)
    cosine, sine = tables_ref[0], tables_ref[1]
    for at in range(width // 128):
        lanes = slice(at * 128, (at + 1) * 128)
        block, grad = qkv_ref[:, lanes], ready_grad_ref[:, lanes]
        heads, gains = block_gains(gains_ref, at)
        inverse = head_scales(block, low)
        normed = block * inverse
        turned = grad * sine
        grad_normed = grad * cosine + jnp.where(
            front, pltpu.roll(turned, 96, 1), -pltpu.roll(turned, 32, 1)
        )
        heads_ref[at : at + 1] = jnp.sum(grad_normed * normed, axis=0, keepdims=True)
        grad_normed = grad_normed * gains
        along = grad_normed * normed
        first = jnp.sum(jnp.where(low, along, 0.0), axis=1, keepdims=True)
        second = jnp.sum(jnp.where(low, 0.0, along), axis=1, keepdims=True)
        mean = jnp.where(low, first, second) * (1.0 / HEAD_DIM)
        raw = inverse * (grad_normed - normed * mean)
        if heads[0] == 2:
            raw = jnp.where(low, grad, raw)
        if heads[1] == 2:
            raw = jnp.where(low, raw, grad)
        proj_ref[:, lanes] = raw.astype(BF16)
    step = width // tiles_ref.shape[0]
    tiles_out(tiles_ref, grad_ref, lambda k: proj_ref[:, k * step : (k + 1) * step])
    copies[0].wait()
    acc_ref[...] = product_right(proj_ref[...], in_buf[0])
    rows_out(acc_ref, core_ref[0], mine_ref, other_ref)


def mixer_call(kernel, core, operands, whole, weight_out, in_tiles, outs, scratch=()):
    vmem, any_space = pl.BlockSpec(memory_space=pltpu.VMEM), pl.BlockSpec(memory_space=pl.ANY)
    rows, width = operands[0].shape
    channels = weight_out.shape[0]
    outs = [*outs, ((rows // 2, width), F32), ((rows // 2, width), BF16)]
    return pl.pallas_call(
        kernel,
        in_specs=[
            pl.BlockSpec(memory_space=pltpu.SMEM),
            *[vmem] * len(operands),
            any_space,
            any_space,
        ],
        out_specs=[vmem] * len(outs),
        out_shape=[jax.ShapeDtypeStruct(*out) for out in outs],
        scratch_shapes=[
            pltpu.VMEM((in_tiles[0], width, in_tiles[1]), BF16),
            pltpu.VMEM((channels, width), BF16),
            pltpu.VMEM((rows, width), F32),
            *scratch,
            pltpu.SemaphoreType.DMA((in_tiles[0] + 1,)),
        ],
        compiler_params=pltpu.CompilerParams(vmem_limit_bytes=VMEM_LIMIT),
        cost_estimate=SHORT,
    )(core, *operands, whole, weight_out)


def conv_forward_call(core, rows, kernel, masks, whole, weight_out):
    count, channels = rows.shape[0], kernel.shape[1]
    outs = [((3, count, channels), BF16), ((count, channels), BF16)]
    operands = (rows, kernel, masks)
    return mixer_call(
        conv_forward_kernel, core, operands, whole, weight_out, (3, channels), outs
    )


def conv_backward_call(core, grad, kernel, masks, projected, tiles, whole, weight_out):
    count, width = grad.shape
    taps, channels = kernel.shape
    outs = [
        (tiles.shape, BF16),
        ((taps, channels), F32),
    ]
    operands = (grad, kernel, masks, projected, tiles)
    return mixer_call(
        conv_backward_kernel, core, operands, whole, weight_out, (3, channels), outs
    )


def attention_forward_call(core, rows, gains, tables, mask, whole, weight_out, qkv_width):
    count, channels = rows.shape[0], weight_out.shape[0]
    outs = [((count, qkv_width), F32), ((count, qkv_width), BF16), ((count, channels), BF16)]
    operands = (rows, gains, tables, mask)
    return mixer_call(
        attention_forward_kernel, core, operands, whole, weight_out, (1, qkv_width), outs
    )


def attention_backward_call(core, grad, gains, tables, mask, qkv, ready, whole, weight_out):
    count, width = grad.shape
    channels, qkv_width = weight_out.shape[0], qkv.shape[1]
    outs = [
        ((4, count, whole_lanes((width + 3 * channels) // 4)), BF16),
        ((qkv_width // 128, 128), F32),
    ]
    scratch = [
        pltpu.VMEM((count, channels), BF16),
        pltpu.VMEM((count, qkv_width), F32),
        pltpu.VMEM((count, qkv_width), BF16),
    ]
    operands = (grad, gains, tables, mask, qkv, ready)
    return mixer_call(
        attention_backward_kernel, core, operands, whole, weight_out, (1, qkv_width), outs, scratch
    )


def conv_masks(segments, taps):
    masks = []
    for lag in range(1, taps):
        same = (segments[:, lag:] == segments[:, :-lag]).astype(F32)
        same = jnp.pad(same, ((0, 0), (lag, 0))).reshape(-1, 1)
        masks.append(jnp.broadcast_to(same, (same.shape[0], 128)))
    return jnp.stack(masks)


def score_mask(segments):
    position = jnp.arange(segments.shape[1])
    allowed = position[:, None] >= position[None, :]
    return (allowed & (segments[:, :, None] == segments[:, None, :])).astype(F32)


def turn_tables(length):
    half = HEAD_DIM // 2
    exponent = jnp.arange(half, dtype=F32) * (2.0 / HEAD_DIM)
    frequency = jnp.exp(-exponent * jnp.log(ROPE_BASE))
    angles = jnp.arange(length, dtype=F32)[:, None] * frequency[None, :]
    tables = jnp.tile(jnp.stack([jnp.cos(angles), jnp.sin(angles)]), (1, 1, 4))
    tables = tables.reshape(2, 2, 1, length // 2, 128)
    return jnp.broadcast_to(tables, (2, 2, 2, length // 2, 128)).reshape(2, 2 * length, 128)


def gain_rows(head_gains):
    kinds = [head_gains[0], head_gains[1], jnp.ones_like(head_gains[0])]
    rows = [jnp.concatenate([a, b]) for a in kinds for b in kinds]
    return jnp.stack(rows)


def head_gain_sums(sums):
    heads = sums.reshape(-1, GROUP + 2, HEAD_DIM)
    return jnp.stack([heads[:, :GROUP].sum((0, 1)), heads[:, GROUP].sum(0)])


def local(
    inputs,
    out_cotangent,
    segments,
    norm_gains,
    conv_kernel,
    qk_gains,
    conv_in,
    attn_qkv,
    mixer_out,
    gate_up,
    down,
):
    section = lax.axis_index("xh")
    first = section == 0
    core = lax.axis_index("c")
    place = lax.axis_index("y") * 4 + lax.axis_index("z")
    xl = lax.axis_index("xl")
    plane = lax.axis_size("y") * lax.axis_size("z")

    shape = inputs.shape[1:]
    width = shape[-1]
    inputs, out_cotangent = inputs.reshape(-1, width), out_cotangent.reshape(-1, width)
    segments = segments[0]
    half = inputs.shape[0]
    rows = 2 * half
    channels = conv_in.shape[2]
    kernel = lax.dynamic_slice_in_dim(conv_kernel, core * channels, channels, 1).astype(F32)
    gains = lax.dynamic_index_in_dim(norm_gains, section, 0, keepdims=False).astype(F32)
    weight_out, weight_pair, weight_down = mixer_out[0], gate_up[0], down[0]
    hidden_units = weight_down.shape[0]
    part = hidden_units // plane
    in_width = 3 * channels
    qkv_width = attn_qkv.shape[1]
    z = lax.axis_index("z")
    core_scalar = jnp.stack([core, section]).astype(jnp.int32)
    xl_scalar = jnp.stack([xl, section, z]).astype(jnp.int32)

    def chosen(from_first, from_second):
        return jnp.where(first, from_first, from_second)

    def gathered(own, axes):
        return lax.all_gather(own, axes, tiled=True)


    both = jnp.concatenate([conv_in.reshape(-1, in_width), attn_qkv], axis=1)
    whole = gathered(both, ("xh", "xl", "y", "z"))

    lanes = -(-part // 256) * 256
    fill = lanes - part
    part_pair = jnp.concatenate(
        [
            jnp.pad(lax.dynamic_slice_in_dim(w, place * part, part, 1), ((0, 0), (0, fill)))
            for w in (weight_pair[0], weight_pair[1])
        ],
        axis=1,
    )
    part_down = lax.dynamic_slice_in_dim(weight_down, place * part, part, 0)
    part_down = jnp.pad(part_down, ((0, fill), (0, 0)))
    masks = conv_masks(segments, kernel.shape[0])
    mask = score_mask(segments)
    tables = turn_tables(segments.shape[1])
    head_gains = gain_rows(qk_gains.astype(F32))
    first_in = inputs.astype(F32)
    normed_own_0 = (normalize(first_in) * gains[0]).astype(BF16)
    normed_0 = spread(normed_own_0)
    cotangent_1 = spread(out_cotangent)
    whole, part_pair, part_down, masks, mask, tables, head_gains, normed_0, cotangent_1 = (
        lax.optimization_barrier(
            (whole, part_pair, part_down, masks, mask, tables, head_gains, normed_0, cotangent_1)
        )
    )

    def feed_forward(hidden, behind=()):
        inner_own = (normalize(hidden) * gains[1]).astype(BF16)
        gate, up, mine, other = feed_forward_call(
            False, core_scalar, spread(inner_own), weight_pair, weight_down, behind=behind
        )
        return hidden + joined(mine, other), (inner_own, gate, up)

    def feed_forward_back(grad_full, grad, hidden, saved, behind=()):
        mine, other = feed_forward_call(
            True, core_scalar, grad_full, weight_pair, weight_down, saved[1:], behind
        )
        return back_join_call(core_scalar, mine, swapped(other, "c"), hidden, grad, gains[1])

    def mixer_back(grad_hidden, mine, other, layer_in, behind):
        come = swapped(other, "c")
        return back_join_call(behind, mine, come, layer_in, grad_hidden, gains[0])[1:]

    plane_axes = ("y", "z", "c")
    early = gathered(chosen(normed_own_0, out_cotangent), plane_axes)

    projected, gated_0, mine, other = conv_forward_call(
        core_scalar, normed_0, kernel, masks, whole, weight_out
    )
    hidden_0 = first_in + joined(mine, other)
    result_0, ffn_0 = feed_forward(hidden_0)
    result_0 = result_0.astype(BF16)

    second_in = lax.ppermute(result_0, "xh", [(0, 1)]).astype(F32)
    normed_own_1 = (normalize(second_in) * gains[0]).astype(BF16)
    qkv, ready, gated_1, mine, other = attention_forward_call(
        core_scalar, spread(normed_own_1), head_gains, tables, mask, whole, weight_out, qkv_width
    )
    hidden_1 = second_in + joined(mine, other)
    result_1, ffn_1 = feed_forward(hidden_1, (early,))
    result_1 = result_1.astype(BF16)

    inner_all = gathered(chosen(ffn_0[0], ffn_1[0]), plane_axes)
    gated_y = gathered(chosen(gated_0, gated_1), "y")

    grad_hidden_1, grad_mix_1, gain_inner_1 = feed_forward_back(
        cotangent_1, out_cotangent.astype(F32), hidden_1, ffn_1
    )
    tiles_1, head_sums, mine, other = attention_backward_call(
        core_scalar,
        spread(grad_mix_1),
        head_gains,
        tables,
        mask,
        qkv,
        ready,
        whole,
        weight_out,
    )
    input_grad_1, gain_outer_1 = mixer_back(grad_hidden_1, mine, other, second_in, core_scalar)

    cotangent = lax.ppermute(input_grad_1, "xh", [(1, 0)])
    late = gathered(chosen(cotangent, normed_own_1), plane_axes)
    grad_hidden_0, grad_mix_0, gain_inner_0 = feed_forward_back(
        spread(cotangent), cotangent.astype(F32), hidden_0, ffn_0, (gated_y, inner_all)
    )
    tiles, grad_kernel, mine, other = conv_backward_call(
        core_scalar,
        spread(grad_mix_0),
        kernel,
        masks,
        projected,
        tiles_1,
        whole,
        weight_out,
    )
    input_grad_0, gain_outer_0 = mixer_back(grad_hidden_0, mine, other, first_in, core_scalar)

    columns = exchanged(tiles, "y").reshape(4 * rows, -1)
    part_kept = part_forward_call(tiles, inner_all, part_pair)

    def summed_over_pair(mine, other):
        return mine.astype(F32) + swapped(other, "xl").astype(F32)

    pair_grads, down_mine, down_other = lax.cond(
        first,
        lambda: part_down_call(xl_scalar, late, part_kept, part_down, (columns,)),
        lambda: part_down_call(xl_scalar, early, part_kept, part_down, (columns,)),
    )
    in_mine, in_other, out_mine, out_other = mixer_grads_call(
        xl_scalar, part_kept, columns, gated_y, early, late, plane
    )
    pair_mine, pair_other = part_pair_call(xl_scalar, inner_all, pair_grads, (in_mine,))

    down_total = pair_join_call((), [(down_mine, swapped(down_other, "xl"))])
    in_total = pair_join_call((pair_other, down_total), [(in_mine, swapped(in_other, "xl"))])
    come = exchanged(in_total, PLANE)
    lines = come.reshape(4, 4, 2, -1, come.shape[2]).astype(F32).sum(1)[..., : in_width // 4]
    kept_lines = lax.dynamic_index_in_dim(lines, section, 1, keepdims=False)
    sent_lines = lax.dynamic_index_in_dim(lines, 1 - section, 1, keepdims=False)
    come = swapped(sent_lines.astype(BF16), "xh").astype(F32)
    lines = chosen(kept_lines, come).reshape(4, -1, 3, channels // 4)
    grad_conv_in = jnp.moveaxis(lines, 0, 2).reshape(conv_in.shape)
    lines = chosen(come, kept_lines)[:, :, : qkv_width // 4]
    grad_attn_qkv = jnp.moveaxis(lines, 0, 1).reshape(attn_qkv.shape)

    pair_total = pair_join_call((in_total,), [(pair_mine, swapped(pair_other, "xl"))])
    total = jnp.concatenate([pair_total, down_total], axis=1)
    arrived = exchanged(total.reshape(plane, -1, 3 * lanes), PLANE)
    lines = [
        jnp.moveaxis(arrived[:, :, k * lanes : k * lanes + part], 0, 1)
        .reshape(-1, hidden_units)
        .astype(F32)
        for k in range(3)
    ]
    grad_gate_up = jnp.stack(lines[:2])[None]
    grad_down = lines[2].T[None]

    total = summed_over_pair(out_mine, out_other).reshape(4, -1, channels)
    sent = total.astype(BF16)
    lines = lax.dynamic_index_in_dim(total, z, 0, keepdims=False)
    for by in range(1, 4):
        block = lax.dynamic_index_in_dim(sent, (z + by) % 4, 0, keepdims=False)
        lines += lax.ppermute(block, "z", [(k, (k + by) % 4) for k in range(4)]).astype(F32)
    grad_mixer_out = lines.T[None]

    full_kernel = lax.dynamic_update_slice(
        jnp.zeros(conv_kernel.shape, F32), grad_kernel, (0, core * channels)
    )
    small = jnp.concatenate(
        [
            chosen(gain_outer_0, gain_outer_1),
            chosen(gain_inner_0, gain_inner_1),
            full_kernel.reshape(-1),
            head_gain_sums(head_sums).reshape(-1),
        ]
    )
    count = small.shape[0]
    small = jnp.pad(small, (0, -count % 1024)).reshape(-1, 128)
    sums = section_sums_call(lax.all_gather(small, AXES), (pair_total,))
    pair = [sums[0].reshape(-1), sums[1].reshape(-1)]
    grad_norm_gains = jnp.stack([a[: 2 * width].reshape(2, width) for a in pair])
    grad_conv_kernel = pair[0][2 * width : 5 * width].reshape(conv_kernel.shape)
    grad_qk_gains = pair[1][5 * width : count].reshape(qk_gains.shape)

    activations = chosen(result_0, result_1).reshape(1, 1, *shape)
    input_grads = chosen(input_grad_0, input_grad_1).reshape(1, 1, *shape)
    return (
        activations,
        input_grads,
        grad_norm_gains,
        grad_conv_kernel,
        grad_qk_gains,
        grad_conv_in,
        grad_attn_qkv,
        grad_mixer_out,
        grad_gate_up,
        grad_down,
    )


def solution(mesh):
    wide = Mesh(mesh.devices.reshape(2, 2, 4, 4, 2), AXES)
    dp = ("xl", "y", "z")
    everyone = ("xh", "xl", "y", "z")
    in_specs = (
        P(dp, None, "c", None),
        P(dp, None, "c", None),
        P(dp, None, None),
        P(),
        P(),
        P(),
        P(everyone, None, "c"),
        P(everyone, "c"),
        P("xh", "c", None),
        P("xh", None, None, "c"),
        P("xh", "c", None),
    )
    out_specs = (
        P("xh", dp, None, "c", None),
        P("xh", dp, None, "c", None),
        P(),
        P(),
        P(),
        P(everyone, None, "c"),
        P(everyone, "c"),
        P("xh", "c", dp),
        P("xh", None, dp, "c"),
        P("xh", "c", dp),
    )
    return jax.shard_map(local, mesh=wide, in_specs=in_specs, out_specs=out_specs, check_vma=False)
```

```python
import functools

import jax
import jax.numpy as jnp
from jax import lax
from jax.experimental import pallas as pl
from jax.experimental.pallas import tpu as pltpu
from jax.sharding import Mesh
from jax.sharding import PartitionSpec as P

HEADS = 24
KV_HEADS = 8
HEAD_DIM = 64
GROUP = HEADS // KV_HEADS

EPSILON = 1e-05
ROPE_BASE = 1000000.0
MASKED_SCORE = -1e30

F32 = jnp.float32
BF16 = jnp.bfloat16

PLANE = ("y", "z")
AXES = ("xh", "xl", "y", "z", "c")


def product(left, right):
    return jnp.dot(left, right, preferred_element_type=F32)


def product_left(left, right):
    return lax.dot_general(left, right, (((0,), (0,)), ((), ())), preferred_element_type=F32)


def product_right(left, right):
    return lax.dot_general(left, right, (((1,), (1,)), ((), ())), preferred_element_type=F32)


def swapped(shard, axis):
    return lax.ppermute(shard, axis, [(0, 1), (1, 0)])


def spread(own):
    return lax.all_gather(own, "c", tiled=True)


def joined(mine, other):
    return mine + swapped(other, "c").astype(F32)


def mean_last(values):
    return jnp.mean(values, axis=-1, keepdims=True)


def inverse_rms(values):
    return lax.rsqrt(mean_last(values * values) + EPSILON)


def normalize(values):
    return values * inverse_rms(values)


def around(by):
    return [(k, (k + by) % 4) for k in range(4)]


def exchanged(tiles, axes):
    return lax.all_to_all(tiles, axes, 0, 0, tiled=True)


def ffn_grads(grad_active, gate, up):
    sigmoid = jax.nn.sigmoid(gate)
    grad_gate = grad_active * up * sigmoid * (1.0 + gate * (1.0 - sigmoid))
    grad_up = grad_active * gate * sigmoid
    return grad_gate.astype(BF16), grad_up.astype(BF16)


VMEM_LIMIT = 56 * 1024 * 1024
SHORT = pl.CostEstimate(flops=1, bytes_accessed=1, transcendentals=0)


def whole_lanes(columns):
    return -(-columns // 128) * 128


def ordered(kernel, count):
    def body(scalar_ref, *refs):
        kernel(scalar_ref, *refs[count:])

    return body


def unit_tiles(units, tile):
    short = units % tile
    tiles = [(0, short)] if short else []
    return tiles + [(at, tile) for at in range(short, units, tile)]


def streamed(tiles, copies, work):
    for copy in copies(0, 0):
        copy.start()
    for k in range(len(tiles)):
        slot = k % 2
        if k + 1 < len(tiles):
            for copy in copies(k + 1, 1 - slot):
                copy.start()
        for copy in copies(k, slot):
            copy.wait()
        work(k, slot)


def ffn_forward_kernel(
    tiles, core_ref, rows_ref, pair_ref, down_ref, gate_ref, up_ref, mine_ref, other_ref,
    pair_buf, down_buf, gate_buf, up_buf, acc_ref, sems, out_sems,
):
    def copies(k, slot):
        at, size = tiles[k]
        return [
            pltpu.make_async_copy(
                pair_ref.at[0, :, pl.ds(at, size)],
                pair_buf.at[slot, :, pl.ds(0, size)],
                sems.at[slot, 0],
            ),
            pltpu.make_async_copy(
                pair_ref.at[1, :, pl.ds(at, size)],
                pair_buf.at[slot, :, pl.ds(size, size)],
                sems.at[slot, 1],
            ),
            pltpu.make_async_copy(
                down_ref.at[pl.ds(at, size)], down_buf.at[slot, pl.ds(0, size)], sems.at[slot, 2]
            ),
        ]

    def kept(k):
        here = (slice(None), pl.ds(*tiles[k]))
        return [
            pltpu.make_async_copy(gate_buf.at[here], gate_ref.at[here], out_sems.at[k, 0]),
            pltpu.make_async_copy(up_buf.at[here], up_ref.at[here], out_sems.at[k, 1]),
        ]

    def work(k, slot):
        at, size = tiles[k]
        both = product(rows_ref[...], pair_buf[slot, :, : 2 * size])
        gate, up = both[:, :size], both[:, size:]
        gate_buf[:, at : at + size] = gate.astype(BF16)
        up_buf[:, at : at + size] = up.astype(BF16)
        for copy in kept(k):
            copy.start()
        active = (gate * jax.nn.sigmoid(gate) * up).astype(BF16)
        part = product(active, down_buf[slot, :size])
        if k == 0:
            acc_ref[...] = part
        else:
            acc_ref[...] += part

    streamed(tiles, copies, work)
    rows_out(acc_ref, core_ref[0], mine_ref, other_ref)
    for k in range(len(tiles)):
        for copy in kept(k):
            copy.wait()


def ffn_backward_kernel(
    tiles, core_ref, rows_ref, gate_ref, up_ref, pair_ref, down_ref, mine_ref, other_ref,
    pair_buf, down_buf, gate_buf, up_buf, acc_ref, sems,
):
    def copies(k, slot):
        at, size = tiles[k]
        columns, place = pl.ds(at, size), pl.ds(0, size)
        return [
            pltpu.make_async_copy(
                down_ref.at[columns], down_buf.at[slot, place], sems.at[slot, 0]
            ),
            pltpu.make_async_copy(
                gate_ref.at[:, columns], gate_buf.at[slot, :, place], sems.at[slot, 1]
            ),
            pltpu.make_async_copy(
                up_ref.at[:, columns], up_buf.at[slot, :, place], sems.at[slot, 2]
            ),
            pltpu.make_async_copy(
                pair_ref.at[0, :, columns], pair_buf.at[slot, :, place], sems.at[slot, 3]
            ),
            pltpu.make_async_copy(
                pair_ref.at[1, :, columns],
                pair_buf.at[slot, :, pl.ds(size, size)],
                sems.at[slot, 4],
            ),
        ]

    def work(k, slot):
        _, size = tiles[k]
        grad_active = product_right(rows_ref[...], down_buf[slot, :size])
        grads = ffn_grads(
            grad_active,
            gate_buf[slot, :, :size].astype(F32),
            up_buf[slot, :, :size].astype(F32),
        )
        part = product_right(jnp.concatenate(grads, axis=1), pair_buf[slot, :, : 2 * size])
        if k == 0:
            acc_ref[...] = part
        else:
            acc_ref[...] += part

    streamed(tiles, copies, work)
    rows_out(acc_ref, core_ref[0], mine_ref, other_ref)


def ffn_both_kernel(
    tiles, core_ref, rows_ref, grad_ref, pair_ref, down_ref,
    mine_ref, other_ref, grad_mine_ref, grad_other_ref, pair_buf, down_buf, acc_ref, grad_acc_ref, sems,
):
    def copies(k, slot):
        at, size = tiles[k]
        columns, place = pl.ds(at, size), pl.ds(0, size)
        return [
            pltpu.make_async_copy(
                pair_ref.at[0, :, columns], pair_buf.at[slot, :, place], sems.at[slot, 0]
            ),
            pltpu.make_async_copy(
                pair_ref.at[1, :, columns],
                pair_buf.at[slot, :, pl.ds(size, size)],
                sems.at[slot, 1],
            ),
            pltpu.make_async_copy(
                down_ref.at[columns], down_buf.at[slot, place], sems.at[slot, 2]
            ),
        ]

    def work(k, slot):
        _, size = tiles[k]
        both = product(rows_ref[...], pair_buf[slot, :, : 2 * size])
        grad_active = product_right(grad_ref[...], down_buf[slot, :size])
        gate, up = both[:, :size], both[:, size:]
        active = (gate * jax.nn.sigmoid(gate) * up).astype(BF16)
        grads = jnp.concatenate(ffn_grads(grad_active, gate, up), axis=1)
        part = product(active, down_buf[slot, :size])
        grad_part = product_right(grads, pair_buf[slot, :, : 2 * size])
        if k == 0:
            acc_ref[...], grad_acc_ref[...] = part, grad_part
        else:
            acc_ref[...] += part
            grad_acc_ref[...] += grad_part

    streamed(tiles, copies, work)
    rows_out(acc_ref, core_ref[0], mine_ref, other_ref)
    rows_out(grad_acc_ref, core_ref[0], grad_mine_ref, grad_other_ref)


def ffn_both_call(core, rows, grad, pair, down, behind):
    count, width = rows.shape
    units = down.shape[0]
    tile = 768
    vmem, any_space = pl.BlockSpec(memory_space=pltpu.VMEM), pl.BlockSpec(memory_space=pl.ANY)
    half = (count // 2, width)
    return pl.pallas_call(
        ordered(functools.partial(ffn_both_kernel, unit_tiles(units, tile)), len(behind)),
        in_specs=[
            pl.BlockSpec(memory_space=pltpu.SMEM),
            *[any_space] * len(behind),
            vmem,
            vmem,
            any_space,
            any_space,
        ],
        out_specs=[vmem] * 4,
        out_shape=[jax.ShapeDtypeStruct(half, F32), jax.ShapeDtypeStruct(half, BF16)] * 2,
        scratch_shapes=[
            pltpu.VMEM((2, width, 2 * tile), BF16),
            pltpu.VMEM((2, tile, width), BF16),
            pltpu.VMEM((count, width), F32),
            pltpu.VMEM((count, width), F32),
            pltpu.SemaphoreType.DMA((2, 3)),
        ],
        compiler_params=pltpu.CompilerParams(vmem_limit_bytes=VMEM_LIMIT),
        cost_estimate=SHORT,
    )(core, *behind, rows, grad, pair, down)


def feed_forward_call(backward, core, rows, pair, down, saved=(), behind=()):
    count, width = rows.shape
    units = down.shape[0]
    tile = 768
    tiles = unit_tiles(units, tile)
    vmem, any_space = pl.BlockSpec(memory_space=pltpu.VMEM), pl.BlockSpec(memory_space=pl.ANY)
    scalar = pl.BlockSpec(memory_space=pltpu.SMEM)
    out_shape = [
        jax.ShapeDtypeStruct((count // 2, width), F32),
        jax.ShapeDtypeStruct((count // 2, width), BF16),
    ]
    out_specs = [vmem, vmem]
    buffers = [pltpu.VMEM((2, width, 2 * tile), BF16), pltpu.VMEM((2, tile, width), BF16)]
    acc = pltpu.VMEM((count, width), F32)
    if backward:
        body = functools.partial(ffn_backward_kernel, tiles)
        in_specs = [scalar, vmem, any_space, any_space, any_space, any_space]
        buffers += [pltpu.VMEM((2, count, tile), BF16)] * 2
        scratch = [*buffers, acc, pltpu.SemaphoreType.DMA((2, 5))]
    else:
        body = functools.partial(ffn_forward_kernel, tiles)
        in_specs = [scalar, vmem, any_space, any_space]
        out_shape = [jax.ShapeDtypeStruct((count, units), BF16)] * 2 + out_shape
        out_specs = [any_space, any_space, *out_specs]
        buffers += [pltpu.VMEM((count, units), BF16)] * 2
        scratch = [*buffers, acc]
        scratch += [pltpu.SemaphoreType.DMA((2, 3)), pltpu.SemaphoreType.DMA((len(tiles), 2))]
    in_specs = [scalar, *[any_space] * len(behind), *in_specs[1:]]
    return pl.pallas_call(
        ordered(body, len(behind)),
        in_specs=in_specs,
        out_specs=out_specs,
        out_shape=out_shape,
        scratch_shapes=scratch,
        compiler_params=pltpu.CompilerParams(vmem_limit_bytes=VMEM_LIMIT),
        cost_estimate=SHORT,
    )(core, *behind, rows, *saved, pair, down)


def part_forward_kernel(behind_ref, rows_ref, pair_ref, kept_ref):
    both = product(rows_ref[...], pair_ref[...])
    units = both.shape[1] // 2
    gate, up = both[:, :units], both[:, units:]
    sigmoid = jax.nn.sigmoid(gate)
    silu = gate * sigmoid
    kept_ref[:, :units] = (up * (sigmoid + silu * (1.0 - sigmoid))).astype(BF16)
    kept_ref[:, units : 2 * units] = silu.astype(BF16)
    kept_ref[:, 2 * units :] = (silu * up).astype(BF16)


def part_forward_call(behind, rows, pair):
    tokens, width = rows.shape
    units = pair.shape[1] // 2
    tile = 1024
    return pl.pallas_call(
        part_forward_kernel,
        grid=(tokens // tile,),
        in_specs=[
            pl.BlockSpec(memory_space=pl.ANY),
            pl.BlockSpec((tile, width), lambda i: (i, 0)),
            pl.BlockSpec((width, 2 * units), lambda i: (0, 0)),
        ],
        out_specs=pl.BlockSpec((tile, 3 * units), lambda i: (i, 0)),
        out_shape=jax.ShapeDtypeStruct((tokens, 3 * units), BF16),
        compiler_params=pltpu.CompilerParams(vmem_limit_bytes=VMEM_LIMIT),
        cost_estimate=pl.CostEstimate(
            flops=8 * tokens * width * units, bytes_accessed=2 * tokens * width, transcendentals=0
        ),
    )(behind, rows, pair)


def pair_out(acc_ref, here, mine_ref, other_ref):
    rows = mine_ref.shape[0]
    for ref, half in ((mine_ref, here), (other_ref, 1 - here)):
        ref[...] = acc_ref[pl.ds(pl.multiple_of(half * rows, rows), rows)].astype(BF16)


def accumulated(acc_ref, part, finish):
    step = pl.program_id(0)

    @pl.when(step == 0)
    def _():
        acc_ref[...] = part

    @pl.when(step > 0)
    def _():
        acc_ref[...] += part

    pl.when(step == pl.num_programs(0) - 1)(finish)


def part_down_kernel(here_ref, grad_ref, kept_ref, down_ref, pair_ref, mine_ref, other_ref, acc_ref):
    grad = grad_ref[...]
    units = down_ref.shape[0]
    grad_active = product_right(grad, down_ref[...])
    for k in range(2):
        lanes = slice(k * units, (k + 1) * units)
        pair_ref[:, lanes] = (grad_active * kept_ref[:, lanes].astype(F32)).astype(BF16)
    accumulated(
        acc_ref,
        product_left(grad, kept_ref[:, 2 * units :]),
        lambda: pair_out(acc_ref, here_ref[0], mine_ref, other_ref),
    )


def part_pair_kernel(here_ref, rows_ref, pair_ref, mine_ref, other_ref, acc_ref):
    accumulated(
        acc_ref,
        product_left(rows_ref[...], pair_ref[...]),
        lambda: pair_out(acc_ref, here_ref[0], mine_ref, other_ref),
    )


def part_call(kernel, here, operands, fixed, outs, result, flops, behind=()):
    tokens = operands[0].shape[0]
    tile = 1024
    by_tokens = lambda width: pl.BlockSpec((tile, width), lambda i, h: (i, 0))
    entire = lambda shape: pl.BlockSpec(shape, lambda i, h: (0, 0))
    half = (result[0] // 2, result[1])
    return pl.pallas_call(
        ordered(kernel, len(behind)),
        grid_spec=pltpu.PrefetchScalarGridSpec(
            num_scalar_prefetch=1,
            grid=(tokens // tile,),
            in_specs=[pl.BlockSpec(memory_space=pl.ANY)] * len(behind)
            + [by_tokens(a.shape[1]) for a in operands]
            + [entire(a.shape) for a in fixed],
            out_specs=[by_tokens(width) for width in outs] + [entire(half)] * 2,
            scratch_shapes=[pltpu.VMEM(result, F32)],
        ),
        out_shape=[jax.ShapeDtypeStruct((tokens, width), BF16) for width in outs]
        + [jax.ShapeDtypeStruct(half, BF16)] * 2,
        compiler_params=pltpu.CompilerParams(vmem_limit_bytes=VMEM_LIMIT),
        cost_estimate=SHORT,
    )(here, *behind, *operands, *fixed)


def part_down_call(here, grad, kept, down, behind):
    tokens, width = grad.shape
    units = down.shape[0]
    flops = 4 * tokens * width * units
    return part_call(
        part_down_kernel,
        here,
        (grad, kept),
        (down,),
        (2 * units,),
        (width, units),
        flops,
        behind,
    )


def part_pair_call(here, inner, pair, behind):
    (tokens, width), columns = inner.shape, pair.shape[1]
    flops = 2 * tokens * width * columns
    return part_call(
        part_pair_kernel, here, (inner, pair), (), (), (width, columns), flops, behind
    )


def back_join_kernel(
    behind_ref, mine_ref, come_ref, values_ref, base_ref, gain_ref, wide_ref, low_ref, sums_ref
):
    grad = mine_ref[...] + come_ref[...].astype(F32)
    values = values_ref[...]
    inverse = inverse_rms(values)
    normed = values * inverse
    scaled = grad * gain_ref[...]
    sums_ref[...] = jnp.sum(grad * normed, axis=0, keepdims=True)
    total = base_ref[...] + inverse * (scaled - normed * mean_last(scaled * normed))
    wide_ref[...] = total
    low_ref[...] = total.astype(BF16)


def back_join_call(behind, mine, come, values, base, gain):
    vmem = pl.BlockSpec(memory_space=pltpu.VMEM)
    shape = values.shape
    wide, low, sums = pl.pallas_call(
        back_join_kernel,
        in_specs=[pl.BlockSpec(memory_space=pl.ANY), *[vmem] * 5],
        out_specs=[vmem] * 3,
        out_shape=[
            jax.ShapeDtypeStruct(shape, F32),
            jax.ShapeDtypeStruct(shape, BF16),
            jax.ShapeDtypeStruct((1, shape[1]), F32),
        ],
        compiler_params=pltpu.CompilerParams(vmem_limit_bytes=VMEM_LIMIT),
        cost_estimate=SHORT,
    )(behind, mine, come, values, base, gain[None])
    return wide, low, sums[0]


def pair_join_kernel(count, *refs):
    *refs, out_ref = refs[count:]
    at = 0
    for mine_ref, come_ref in zip(refs[::2], refs[1::2]):
        size = mine_ref.shape[-1]
        total = mine_ref[...].astype(F32) + come_ref[...].astype(F32)
        out_ref[..., at : at + size] = total.astype(BF16)
        at += size


def pair_join_call(behind, pairs):
    vmem = pl.BlockSpec(memory_space=pltpu.VMEM)
    operands = [a for pair in pairs for a in pair]
    shape = (*operands[0].shape[:-1], sum(mine.shape[-1] for mine, _ in pairs))
    return pl.pallas_call(
        functools.partial(pair_join_kernel, len(behind)),
        in_specs=[pl.BlockSpec(memory_space=pl.ANY)] * len(behind) + [vmem] * len(operands),
        out_specs=vmem,
        out_shape=jax.ShapeDtypeStruct(shape, BF16),
        compiler_params=pltpu.CompilerParams(vmem_limit_bytes=VMEM_LIMIT),
        cost_estimate=SHORT,
    )(*behind, *operands)


def widened_kernel(behind_ref, low_ref, wide_ref):
    wide_ref[...] = low_ref[...].astype(F32)


def widened_call(behind, low):
    vmem = pl.BlockSpec(memory_space=pltpu.VMEM)
    return pl.pallas_call(
        widened_kernel,
        in_specs=[pl.BlockSpec(memory_space=pl.ANY), vmem],
        out_specs=vmem,
        out_shape=jax.ShapeDtypeStruct(low.shape, F32),
        compiler_params=pltpu.CompilerParams(vmem_limit_bytes=VMEM_LIMIT),
        cost_estimate=SHORT,
    )(behind, low)


def finish_kernel(
    places_ref, behind_ref, come_ref, small_ref, kept_ref, sent_ref, sums_ref, acc_ref
):
    section = places_ref[1]
    count, short, _ = kept_ref.shape
    for k in range(count):
        tiles = [come_ref[m * count + k].astype(F32) for m in range(come_ref.shape[0] // count)]
        acc_ref[...] = functools.reduce(jnp.add, tiles)
        kept_ref[k] = acc_ref[pl.ds(pl.multiple_of(section * short, short), short)]
        sent = acc_ref[pl.ds(pl.multiple_of((1 - section) * short, short), short)]
        sent_ref[k] = sent.astype(BF16)
    half = small_ref.shape[0] // 2
    for k in range(2):
        sums_ref[k] = jnp.sum(small_ref[k * half : (k + 1) * half], axis=0)


def finish_call(places, behind, come, small):
    vmem = pl.BlockSpec(memory_space=pltpu.VMEM)
    plane, block, size = come.shape
    lines = (4, block // 2, size)
    return pl.pallas_call(
        finish_kernel,
        in_specs=[
            pl.BlockSpec(memory_space=pltpu.SMEM),
            pl.BlockSpec(memory_space=pl.ANY),
            vmem,
            vmem,
        ],
        out_specs=[vmem] * 3,
        out_shape=[
            jax.ShapeDtypeStruct(lines, F32),
            jax.ShapeDtypeStruct(lines, BF16),
            jax.ShapeDtypeStruct((2, *small.shape[1:]), F32),
        ],
        scratch_shapes=[pltpu.VMEM((block, size), F32)],
        compiler_params=pltpu.CompilerParams(vmem_limit_bytes=VMEM_LIMIT),
        cost_estimate=SHORT,
    )(places, behind, come, small)


def mixer_grads_kernel(
    places_ref, behind_ref, columns_ref, gated_0_ref, gated_1_ref, gated_2_ref, gated_3_ref,
    early_ref, late_ref, in_mine_ref, in_other_ref, out_mine_ref, out_other_ref,
    normed_ref, in_ref, out_ref, sem,
):
    here, section, y = places_ref[0], places_ref[1], places_ref[2]

    def copy(all_ref):
        rows = normed_ref.shape[0]
        start = pl.multiple_of(y * rows, rows)
        return pltpu.make_async_copy(all_ref.at[pl.ds(start, rows)], normed_ref, sem)

    @pl.when(section == 0)
    def _():
        copy(early_ref).start()

    @pl.when(section > 0)
    def _():
        copy(late_ref).start()

    mix = out_ref.shape[0]
    blocks = (gated_0_ref, gated_1_ref, gated_2_ref, gated_3_ref)
    span = gated_0_ref.shape[0]
    total = None
    for k, gated_ref in enumerate(blocks):
        start = lax.rem(places_ref[3] - k + len(blocks), len(blocks)) * span
        tiles = columns_ref[pl.ds(pl.multiple_of(start, span), span), :mix]
        block = product_left(tiles, gated_ref[...])
        total = block if total is None else total + block
    out_ref[...] = total
    pair_out(out_ref, here, out_mine_ref, out_other_ref)
    copy(early_ref).wait()
    in_ref[...] = product_left(normed_ref[...], columns_ref[:, mix:])
    plane, block, _ = in_mine_ref.shape
    short = block // 2
    for ref, half in ((in_mine_ref, here), (in_other_ref, 1 - here)):
        for k in range(plane):
            for s in range(2):
                start = pl.multiple_of(((2 * s + half) * plane + k) * short, short)
                rows_in = in_ref[pl.ds(start, short)]
                ref[k, s * short : (s + 1) * short] = rows_in.astype(BF16)


def mixer_grads_call(places, behind, columns, gated, early, late, plane):
    vmem, any_space = pl.BlockSpec(memory_space=pltpu.VMEM), pl.BlockSpec(memory_space=pl.ANY)
    tokens, channels = columns.shape[0], gated[0].shape[1]
    width = early.shape[1]
    mix = width // 4
    size = columns.shape[1] - mix
    in_half = jax.ShapeDtypeStruct((plane, width // (2 * plane), size), BF16)
    out_half = jax.ShapeDtypeStruct((mix // 2, channels), BF16)
    return pl.pallas_call(
        mixer_grads_kernel,
        in_specs=[
            pl.BlockSpec(memory_space=pltpu.SMEM),
            any_space,
            vmem,
            *[vmem] * len(gated),
            any_space,
            any_space,
        ],
        out_specs=[vmem] * 4,
        out_shape=[in_half, in_half, out_half, out_half],
        scratch_shapes=[
            pltpu.VMEM((tokens, width), BF16),
            pltpu.VMEM((width, size), F32),
            pltpu.VMEM((mix, channels), F32),
            pltpu.SemaphoreType.DMA,
        ],
        compiler_params=pltpu.CompilerParams(vmem_limit_bytes=VMEM_LIMIT),
        cost_estimate=SHORT,
    )(places, behind, columns, *gated, early, late)


def load_all(copies):
    for copy in copies:
        copy.start()


def in_time(rows):
    half = rows.shape[0] // 4
    return jnp.concatenate([rows[k * half : (k + 1) * half] for k in (0, 2, 1, 3)], axis=0)


def rows_out(acc_ref, core, mine_ref, other_ref):
    half = mine_ref.shape[0]
    mine_ref[...] = acc_ref[pl.ds(pl.multiple_of(core * half, half), half)]
    rest = acc_ref[pl.ds(pl.multiple_of((1 - core) * half, half), half)]
    other_ref[...] = rest.astype(BF16)


def weight_copies(whole_ref, out_ref, in_buf, out_buf, sems, start):
    size = in_buf.shape[2]
    copies = [
        pltpu.make_async_copy(
            whole_ref.at[:, pl.ds(start + k * size, size)], in_buf.at[k], sems.at[k]
        )
        for k in range(in_buf.shape[0])
    ]
    return copies, pltpu.make_async_copy(out_ref, out_buf, sems.at[len(copies)])


def conv_taps(mixed, kernel, masks):
    terms = [mixed]
    for lag in range(1, len(masks) + 1):
        terms.append(pltpu.roll(mixed, lag, 0) * masks[lag - 1])
    taps = kernel.shape[0]
    total = kernel[taps - 1 : taps] * terms[0]
    for lag in range(1, taps):
        total = total + kernel[taps - 1 - lag : taps - lag] * terms[lag]
    return terms, total


def conv_forward_kernel(
    core_ref, rows_ref, kernel_ref, masks_ref, whole_ref, out_ref,
    proj_ref, gated_ref, mine_ref, other_ref, in_buf, out_buf, acc_ref, sems,
):
    copies, last = weight_copies(whole_ref, out_ref, in_buf, out_buf, sems, 0)
    load_all([*copies, last])
    rows = rows_ref[...]
    parts = []
    for k, copy in enumerate(copies):
        copy.wait()
        part = product(rows, in_buf[k])
        proj_ref[k] = part.astype(BF16)
        parts.append(in_time(part))
    masks = [masks_ref[lag] for lag in range(masks_ref.shape[0])]
    gated = []
    for at in range(0, parts[0].shape[1], 128):
        before, after, signal = [part[:, at : at + 128] for part in parts]
        _, total = conv_taps(before * signal, kernel_ref[:, at : at + 128], masks)
        gated.append((after * total).astype(BF16))
    gated = in_time(jnp.concatenate(gated, axis=1))
    gated_ref[...] = gated
    last.wait()
    acc_ref[...] = product(gated, out_buf[...])
    rows_out(acc_ref, core_ref[0], mine_ref, other_ref)


def tiles_out(tiles_ref, grad_ref, columns):
    count, rows, size = tiles_ref.shape
    step = grad_ref.shape[1] // (2 * count * count)
    for k in range(count):
        starts = range(k * step, grad_ref.shape[1], count * step)
        parts = [grad_ref[:, at : at + step] for at in starts]
        parts.append(columns(k))
        spare = size - sum(part.shape[1] for part in parts)
        tiles_ref[k] = jnp.concatenate([*parts, jnp.zeros((rows, spare), BF16)], axis=1)


def conv_backward_kernel(
    core_ref, grad_ref, kernel_ref, masks_ref, proj_ref, other_tiles_ref,
    whole_ref, out_ref, tiles_ref, taps_ref, mine_ref, other_ref, in_buf, out_buf, acc_ref, sems,
):
    copies, last = weight_copies(whole_ref, out_ref, in_buf, out_buf, sems, 0)
    load_all([last, *copies])
    last.wait()
    grad_gated = in_time(product_right(grad_ref[...], out_buf[...]))
    parts = [in_time(proj_ref[k].astype(F32)) for k in range(3)]
    masks = [masks_ref[lag] for lag in range(masks_ref.shape[0])]
    rows = grad_gated.shape[0]
    grads = [[], [], []]
    for at in range(0, grad_gated.shape[1], 128):
        before, after, signal = [part[:, at : at + 128] for part in parts]
        kernel = kernel_ref[:, at : at + 128]
        terms, total = conv_taps(before * signal, kernel, masks)
        grad = grad_gated[:, at : at + 128]
        grad_total = grad * after
        taps = kernel.shape[0]
        grad_mixed = kernel[taps - 1 : taps] * grad_total
        for lag in range(1, taps):
            sent = pltpu.roll(grad_total * masks[lag - 1], rows - lag, 0)
            grad_mixed = grad_mixed + kernel[taps - 1 - lag : taps - lag] * sent
        for lag in range(taps):
            taps_ref[taps - 1 - lag : taps - lag, at : at + 128] = jnp.sum(
                grad_total * terms[lag], axis=0, keepdims=True
            )
        for k, value in enumerate((grad_mixed * signal, grad * total, grad_mixed * before)):
            grads[k].append(value.astype(BF16))
    grads = [in_time(jnp.concatenate(g, axis=1)) for g in grads]
    step = grads[0].shape[1] // tiles_ref.shape[0]

    @pl.when(core_ref[1] == 0)
    def _():
        tiles_out(
            tiles_ref,
            grad_ref,
            lambda k: jnp.concatenate([g[:, k * step : (k + 1) * step] for g in grads], axis=1),
        )

    @pl.when(core_ref[1] > 0)
    def _():
        tiles_ref[...] = other_tiles_ref[...]

    for k, copy in enumerate(copies):
        copy.wait()
        part = product_right(grads[k], in_buf[k])
        acc_ref[...] = part if k == 0 else acc_ref[...] + part
    rows_out(acc_ref, core_ref[0], mine_ref, other_ref)


def head_kind(head):
    return min(max(head % (GROUP + 2) - GROUP + 1, 0), 2)


def lane_facts(rows):
    lane = lax.broadcasted_iota(jnp.int32, (rows, 128), 1)
    return lane < HEAD_DIM, lax.rem(lane, HEAD_DIM) < HEAD_DIM // 2


def head_scales(block, low):
    squares = block * block
    first = jnp.sum(jnp.where(low, squares, 0.0), axis=1, keepdims=True)
    second = jnp.sum(jnp.where(low, 0.0, squares), axis=1, keepdims=True)
    return lax.rsqrt(jnp.where(low, first, second) * (1.0 / HEAD_DIM) + EPSILON)


def block_gains(gains_ref, at):
    heads = [head_kind(2 * at), head_kind(2 * at + 1)]
    return heads, gains_ref[3 * heads[0] + heads[1] : 3 * heads[0] + heads[1] + 1]


def attention_forward_kernel(
    core_ref, rows_ref, gains_ref, tables_ref, mask_ref, whole_ref, out_ref,
    qkv_ref, ready_ref, gated_ref, mine_ref, other_ref, in_buf, out_buf, acc_ref, sems,
):
    copies, last = weight_copies(
        whole_ref, out_ref, in_buf, out_buf, sems, whole_ref.shape[1] - in_buf.shape[2]
    )
    load_all([*copies, last])
    copies[0].wait()
    qkv_ref[...] = product(rows_ref[...], in_buf[0])
    rows, width = qkv_ref.shape
    low, front = lane_facts(rows)
    cosine, sine = tables_ref[0], tables_ref[1]
    for at in range(width // 128):
        block = qkv_ref[:, at * 128 : (at + 1) * 128]
        heads, gains = block_gains(gains_ref, at)
        normed = block * head_scales(block, low) * gains
        turned = jnp.where(front, -pltpu.roll(normed, 96, 1), pltpu.roll(normed, 32, 1))
        ready = normed * cosine + turned * sine
        if heads[0] == 2:
            ready = jnp.where(low, block, ready)
        if heads[1] == 2:
            ready = jnp.where(low, ready, block)
        ready_ref[:, at * 128 : (at + 1) * 128] = ready.astype(BF16)
    half = rows // 4
    span = (GROUP + 2) * HEAD_DIM
    for m in range(2):
        mask = mask_ref[m] > 0
        mask = jnp.concatenate([mask] * GROUP, axis=0)
        for g in range(width // span):
            queries, keys, values = head_rows(ready_ref, m, half, g * span)
            weights = softmax_weights(queries, keys, mask)
            attended = product(weights.astype(BF16), values).astype(BF16)
            for j in range(GROUP):
                at = (g * GROUP + j) * HEAD_DIM
                head = attended[j * 2 * half : (j + 1) * 2 * half]
                gated_ref[m * half : (m + 1) * half, at : at + HEAD_DIM] = head[:half]
                gated_ref[(m + 2) * half : (m + 3) * half, at : at + HEAD_DIM] = head[half:]
    last.wait()
    acc_ref[...] = product(gated_ref[...], out_buf[...])
    rows_out(acc_ref, core_ref[0], mine_ref, other_ref)


def sequence(ref, m, half, at):
    columns = slice(at, at + HEAD_DIM)
    return jnp.concatenate(
        [ref[m * half : (m + 1) * half, columns], ref[(m + 2) * half : (m + 3) * half, columns]],
        axis=0,
    )


def head_rows(ref, m, half, at):
    heads = [sequence(ref, m, half, at + j * HEAD_DIM) for j in range(GROUP + 2)]
    return jnp.concatenate(heads[:GROUP], axis=0), heads[GROUP], heads[GROUP + 1]


def softmax_weights(queries, keys, mask):
    scores = jnp.where(mask, product_right(queries, keys) * HEAD_DIM ** (-0.5), MASKED_SCORE)
    terms = jnp.exp(scores - jnp.max(scores, axis=1, keepdims=True))
    return terms / jnp.sum(terms, axis=1, keepdims=True)


def attention_backward_kernel(
    core_ref, grad_ref, gains_ref, tables_ref, mask_ref, qkv_ref, ready_ref,
    whole_ref, out_ref, tiles_ref, heads_ref, mine_ref, other_ref,
    in_buf, out_buf, acc_ref, attended_ref, ready_grad_ref, proj_ref, sems,
):
    copies, last = weight_copies(
        whole_ref, out_ref, in_buf, out_buf, sems, whole_ref.shape[1] - in_buf.shape[2]
    )
    load_all([last, *copies])
    last.wait()
    attended_ref[...] = product_right(grad_ref[...], out_buf[...]).astype(BF16)
    rows, width = qkv_ref.shape
    half = rows // 4
    span = (GROUP + 2) * HEAD_DIM
    scale = HEAD_DIM ** (-0.5)
    for m in range(2):
        mask = mask_ref[m] > 0
        mask = jnp.concatenate([mask] * GROUP, axis=0)
        for g in range(width // span):
            queries, keys, values = head_rows(ready_ref, m, half, g * span)
            weights = softmax_weights(queries, keys, mask)
            grad = jnp.concatenate(
                [
                    sequence(attended_ref, m, half, (g * GROUP + j) * HEAD_DIM)
                    for j in range(GROUP)
                ],
                axis=0,
            )
            grad_values = product_left(weights.astype(BF16), grad)
            grad_weights = product_right(grad, values)
            mean = jnp.sum(grad_weights * weights, axis=1, keepdims=True)
            grad_scores = (weights * (grad_weights - mean)).astype(BF16)
            grad_queries = product(grad_scores, keys) * scale
            grad_keys = product_left(grad_scores, queries) * scale
            outs = [grad_queries[j * 2 * half : (j + 1) * 2 * half] for j in range(GROUP)]
            for j, out in enumerate([*outs, grad_keys, grad_values]):
                at = g * span + j * HEAD_DIM
                ready_grad_ref[m * half : (m + 1) * half, at : at + HEAD_DIM] = out[:half]
                ready_grad_ref[(m + 2) * half : (m + 3) * half, at : at + HEAD_DIM] = out[half:]
    low, front = lane_facts(rows)
    cosine, sine = tables_ref[0], tables_ref[1]
    for at in range(width // 128):
        lanes = slice(at * 128, (at + 1) * 128)
        block, grad = qkv_ref[:, lanes], ready_grad_ref[:, lanes]
        heads, gains = block_gains(gains_ref, at)
        inverse = head_scales(block, low)
        normed = block * inverse
        turned = grad * sine
        grad_normed = grad * cosine + jnp.where(
            front, pltpu.roll(turned, 96, 1), -pltpu.roll(turned, 32, 1)
        )
        heads_ref[at : at + 1] = jnp.sum(grad_normed * normed, axis=0, keepdims=True)
        grad_normed = grad_normed * gains
        along = grad_normed * normed
        first = jnp.sum(jnp.where(low, along, 0.0), axis=1, keepdims=True)
        second = jnp.sum(jnp.where(low, 0.0, along), axis=1, keepdims=True)
        mean = jnp.where(low, first, second) * (1.0 / HEAD_DIM)
        raw = inverse * (grad_normed - normed * mean)
        if heads[0] == 2:
            raw = jnp.where(low, grad, raw)
        if heads[1] == 2:
            raw = jnp.where(low, raw, grad)
        proj_ref[:, lanes] = raw.astype(BF16)
    step = width // tiles_ref.shape[0]
    tiles_out(tiles_ref, grad_ref, lambda k: proj_ref[:, k * step : (k + 1) * step])
    copies[0].wait()
    acc_ref[...] = product_right(proj_ref[...], in_buf[0])
    rows_out(acc_ref, core_ref[0], mine_ref, other_ref)


def mixer_call(
    kernel, core, operands, whole, weight_out, in_tiles, outs, scratch=(), behind=()
):
    vmem, any_space = pl.BlockSpec(memory_space=pltpu.VMEM), pl.BlockSpec(memory_space=pl.ANY)
    rows, width = operands[0].shape
    channels = weight_out.shape[0]
    outs = [*outs, ((rows // 2, width), F32), ((rows // 2, width), BF16)]
    return pl.pallas_call(
        ordered(kernel, len(behind)),
        in_specs=[
            pl.BlockSpec(memory_space=pltpu.SMEM),
            *[any_space] * len(behind),
            *[vmem] * len(operands),
            any_space,
            any_space,
        ],
        out_specs=[vmem] * len(outs),
        out_shape=[jax.ShapeDtypeStruct(*out) for out in outs],
        scratch_shapes=[
            pltpu.VMEM((in_tiles[0], width, in_tiles[1]), BF16),
            pltpu.VMEM((channels, width), BF16),
            pltpu.VMEM((rows, width), F32),
            *scratch,
            pltpu.SemaphoreType.DMA((in_tiles[0] + 1,)),
        ],
        compiler_params=pltpu.CompilerParams(vmem_limit_bytes=VMEM_LIMIT),
        cost_estimate=SHORT,
    )(core, *behind, *operands, whole, weight_out)


def conv_forward_call(core, rows, kernel, masks, whole, weight_out):
    count, channels = rows.shape[0], kernel.shape[1]
    outs = [((3, count, channels), BF16), ((count, channels), BF16)]
    operands = (rows, kernel, masks)
    return mixer_call(
        conv_forward_kernel, core, operands, whole, weight_out, (3, channels), outs
    )


def conv_backward_call(
    core, grad, kernel, masks, projected, tiles, whole, weight_out, behind
):
    count, width = grad.shape
    taps, channels = kernel.shape
    outs = [
        (tiles.shape, BF16),
        ((taps, channels), F32),
    ]
    operands = (grad, kernel, masks, projected, tiles)
    return mixer_call(
        conv_backward_kernel, core, operands, whole, weight_out, (3, channels), outs, (), behind
    )


def attention_forward_call(core, rows, gains, tables, mask, whole, weight_out, qkv_width):
    count, channels = rows.shape[0], weight_out.shape[0]
    outs = [((count, qkv_width), F32), ((count, qkv_width), BF16), ((count, channels), BF16)]
    operands = (rows, gains, tables, mask)
    return mixer_call(
        attention_forward_kernel, core, operands, whole, weight_out, (1, qkv_width), outs
    )


def attention_backward_call(core, grad, gains, tables, mask, qkv, ready, whole, weight_out):
    count, width = grad.shape
    channels, qkv_width = weight_out.shape[0], qkv.shape[1]
    outs = [
        ((4, count, whole_lanes((width + 3 * channels) // 4)), BF16),
        ((qkv_width // 128, 128), F32),
    ]
    scratch = [
        pltpu.VMEM((count, channels), BF16),
        pltpu.VMEM((count, qkv_width), F32),
        pltpu.VMEM((count, qkv_width), BF16),
    ]
    operands = (grad, gains, tables, mask, qkv, ready)
    return mixer_call(
        attention_backward_kernel, core, operands, whole, weight_out, (1, qkv_width), outs, scratch
    )


def conv_masks(segments, taps):
    masks = []
    for lag in range(1, taps):
        same = (segments[:, lag:] == segments[:, :-lag]).astype(F32)
        same = jnp.pad(same, ((0, 0), (lag, 0))).reshape(-1, 1)
        masks.append(jnp.broadcast_to(same, (same.shape[0], 128)))
    return jnp.stack(masks)


def score_mask(segments):
    position = jnp.arange(segments.shape[1])
    allowed = position[:, None] >= position[None, :]
    return (allowed & (segments[:, :, None] == segments[:, None, :])).astype(F32)


def turn_tables(length):
    half = HEAD_DIM // 2
    exponent = jnp.arange(half, dtype=F32) * (2.0 / HEAD_DIM)
    frequency = jnp.exp(-exponent * jnp.log(ROPE_BASE))
    angles = jnp.arange(length, dtype=F32)[:, None] * frequency[None, :]
    tables = jnp.tile(jnp.stack([jnp.cos(angles), jnp.sin(angles)]), (1, 1, 4))
    tables = tables.reshape(2, 2, 1, length // 2, 128)
    return jnp.broadcast_to(tables, (2, 2, 2, length // 2, 128)).reshape(2, 2 * length, 128)


def gain_rows(head_gains):
    kinds = [head_gains[0], head_gains[1], jnp.ones_like(head_gains[0])]
    rows = [jnp.concatenate([a, b]) for a in kinds for b in kinds]
    return jnp.stack(rows)


def head_gain_sums(sums):
    heads = sums.reshape(-1, GROUP + 2, HEAD_DIM)
    return jnp.stack([heads[:, :GROUP].sum((0, 1)), heads[:, GROUP].sum(0)])


def local(
    inputs,
    out_cotangent,
    segments,
    norm_gains,
    conv_kernel,
    qk_gains,
    conv_in,
    attn_qkv,
    mixer_out,
    gate_up,
    down,
):
    section = lax.axis_index("xh")
    first = section == 0
    core = lax.axis_index("c")
    place = lax.axis_index("y") * 4 + lax.axis_index("z")
    xl = lax.axis_index("xl")
    plane = lax.axis_size("y") * lax.axis_size("z")

    shape = inputs.shape[1:]
    width = shape[-1]
    inputs, out_cotangent = inputs.reshape(-1, width), out_cotangent.reshape(-1, width)
    segments = segments[0]
    half = inputs.shape[0]
    rows = 2 * half
    channels = conv_in.shape[2]
    kernel = lax.dynamic_slice_in_dim(conv_kernel, core * channels, channels, 1).astype(F32)
    gains = lax.dynamic_index_in_dim(norm_gains, section, 0, keepdims=False).astype(F32)
    weight_out, weight_pair, weight_down = mixer_out[0], gate_up[0], down[0]
    hidden_units = weight_down.shape[0]
    part = hidden_units // plane
    in_width = 3 * channels
    qkv_width = attn_qkv.shape[1]
    y, z = lax.axis_index("y"), lax.axis_index("z")
    core_scalar = jnp.stack([core, section]).astype(jnp.int32)
    xl_scalar = jnp.stack([xl, section, y, z]).astype(jnp.int32)

    def chosen(from_first, from_second):
        return jnp.where(first, from_first, from_second)

    def gathered(own, axes):
        return lax.all_gather(own, axes, tiled=True)


    both = jnp.concatenate([conv_in.reshape(-1, in_width), attn_qkv], axis=1)
    whole = gathered(both, ("xh", "xl", "y", "z"))

    lanes = -(-part // 256) * 256
    fill = lanes - part
    part_pair = jnp.concatenate(
        [
            jnp.pad(lax.dynamic_slice_in_dim(w, place * part, part, 1), ((0, 0), (0, fill)))
            for w in (weight_pair[0], weight_pair[1])
        ],
        axis=1,
    )
    part_down = lax.dynamic_slice_in_dim(weight_down, place * part, part, 0)
    part_down = jnp.pad(part_down, ((0, fill), (0, 0)))
    masks = conv_masks(segments, kernel.shape[0])
    mask = score_mask(segments)
    tables = turn_tables(segments.shape[1])
    head_gains = gain_rows(qk_gains.astype(F32))
    first_in = inputs.astype(F32)
    normed_own_0 = (normalize(first_in) * gains[0]).astype(BF16)
    normed_0 = spread(normed_own_0)
    cotangent_1 = spread(out_cotangent)
    whole, part_pair, part_down, masks, mask, tables, head_gains, normed_0, cotangent_1 = (
        lax.optimization_barrier(
            (whole, part_pair, part_down, masks, mask, tables, head_gains, normed_0, cotangent_1)
        )
    )

    def inner_norm(hidden):
        return (normalize(hidden) * gains[1]).astype(BF16)

    def inner_back(mine, other, hidden, grad):
        return back_join_call(core_scalar, mine, swapped(other, "c"), hidden, grad, gains[1])

    def mixer_back(grad_hidden, mine, other, layer_in, behind):
        come = swapped(other, "c")
        return back_join_call(behind, mine, come, layer_in, grad_hidden, gains[0])[1:]

    plane_axes = ("y", "z", "c")
    early = gathered(chosen(normed_own_0, out_cotangent), plane_axes)

    projected, gated_0, mine, other = conv_forward_call(
        core_scalar, normed_0, kernel, masks, whole, weight_out
    )
    hidden_0 = first_in + joined(mine, other)
    inner_0 = inner_norm(hidden_0)
    gate, up, mine, other = feed_forward_call(
        False, core_scalar, spread(inner_0), weight_pair, weight_down
    )
    result_0 = (hidden_0 + joined(mine, other)).astype(BF16)

    second_in = lax.ppermute(result_0, "xh", [(0, 1)]).astype(F32)
    normed_own_1 = (normalize(second_in) * gains[0]).astype(BF16)
    qkv, ready, gated_1, mine, other = attention_forward_call(
        core_scalar, spread(normed_own_1), head_gains, tables, mask, whole, weight_out, qkv_width
    )
    hidden_1 = second_in + joined(mine, other)
    inner_1 = inner_norm(hidden_1)
    mine, other, grad_mine, grad_other = ffn_both_call(
        core_scalar, spread(inner_1), cotangent_1, weight_pair, weight_down, (early,)
    )
    result_1 = (hidden_1 + joined(mine, other)).astype(BF16)

    inner_all = gathered(chosen(inner_0, inner_1), plane_axes)
    gated = chosen(gated_0, gated_1)
    gated_z = [gated, *[lax.ppermute(gated, "z", around(by)) for by in range(1, 4)]]

    grad_hidden_1, grad_mix_1, gain_inner_1 = inner_back(
        grad_mine, grad_other, hidden_1, out_cotangent.astype(F32)
    )
    tiles_1, head_sums, mine, other = attention_backward_call(
        core_scalar,
        spread(grad_mix_1),
        head_gains,
        tables,
        mask,
        qkv,
        ready,
        whole,
        weight_out,
    )
    input_grad_1, gain_outer_1 = mixer_back(grad_hidden_1, mine, other, second_in, core_scalar)

    cotangent = lax.ppermute(input_grad_1, "xh", [(1, 0)])
    late = gathered(chosen(cotangent, normed_own_1), plane_axes)
    mine, other = feed_forward_call(
        True,
        core_scalar,
        spread(cotangent),
        weight_pair,
        weight_down,
        (gate, up),
        (inner_all,),
    )
    grad_hidden_0, grad_mix_0, gain_inner_0 = inner_back(
        mine, other, hidden_0, cotangent.astype(F32)
    )
    tiles, grad_kernel, mine, other = conv_backward_call(
        core_scalar,
        spread(grad_mix_0),
        kernel,
        masks,
        projected,
        tiles_1,
        whole,
        weight_out,
        gated_z[1:],
    )
    columns = exchanged(tiles, "z").reshape(4 * rows, -1)
    part_kept = part_forward_call(tiles, inner_all, part_pair)

    def summed_over_pair(mine, other):
        return mine.astype(F32) + swapped(other, "xl").astype(F32)

    pair_grads, down_mine, down_other = lax.cond(
        first,
        lambda: part_down_call(xl_scalar, late, part_kept, part_down, (columns,)),
        lambda: part_down_call(xl_scalar, early, part_kept, part_down, (columns,)),
    )
    input_grad_0, gain_outer_0 = mixer_back(grad_hidden_0, mine, other, first_in, pair_grads)
    in_mine, in_other, out_mine, out_other = mixer_grads_call(
        xl_scalar, pair_grads, columns, gated_z, early, late, plane
    )
    pair_mine, pair_other = part_pair_call(xl_scalar, inner_all, pair_grads, (in_mine,))

    full_kernel = lax.dynamic_update_slice(
        jnp.zeros(conv_kernel.shape, F32), grad_kernel, (0, core * channels)
    )
    small = jnp.concatenate(
        [
            chosen(gain_outer_0, gain_outer_1),
            chosen(gain_inner_0, gain_inner_1),
            full_kernel.reshape(-1),
            head_gain_sums(head_sums).reshape(-1),
        ]
    )
    count = small.shape[0]
    small = jnp.pad(small, (0, -count % 1024)).reshape(-1, 128)
    small_all = lax.all_gather(small, AXES)

    down_total = pair_join_call((), [(down_mine, swapped(down_other, "xl"))])
    in_total = pair_join_call((pair_other, down_total), [(in_mine, swapped(in_other, "xl"))])
    come = exchanged(in_total, PLANE)

    pair_total = pair_join_call((come,), [(pair_mine, swapped(pair_other, "xl"))])
    total = jnp.concatenate([pair_total, down_total], axis=1)
    arrived = exchanged(total.reshape(plane, -1, 3 * lanes), PLANE)

    kept_lines, sent_lines, sums = finish_call(xl_scalar, total, come, small_all)
    across = swapped(sent_lines, "xh")
    come = across.astype(F32)[:, :, : in_width // 4]
    kept_lines = kept_lines[:, :, : in_width // 4]
    lines = chosen(kept_lines, come).reshape(4, -1, 3, channels // 4)
    grad_conv_in = jnp.moveaxis(lines, 0, 2).reshape(conv_in.shape)
    lines = chosen(come, kept_lines)[:, :, : qkv_width // 4]
    grad_attn_qkv = jnp.moveaxis(lines, 0, 1).reshape(attn_qkv.shape)

    arrived = widened_call(across, arrived)
    lines = [
        jnp.moveaxis(arrived[:, :, k * lanes : k * lanes + part], 0, 1).reshape(-1, hidden_units)
        for k in range(3)
    ]
    grad_gate_up = jnp.stack(lines[:2])[None]
    grad_down = lines[2].T[None]

    total = summed_over_pair(out_mine, out_other).reshape(4, -1, channels)
    sent = total.astype(BF16)
    lines = lax.dynamic_index_in_dim(total, y, 0, keepdims=False)
    for by in range(1, 4):
        block = lax.dynamic_index_in_dim(sent, (y + by) % 4, 0, keepdims=False)
        lines += lax.ppermute(block, "y", around(by)).astype(F32)
    grad_mixer_out = lines.T[None]

    pair = [sums[0].reshape(-1), sums[1].reshape(-1)]
    grad_norm_gains = jnp.stack([a[: 2 * width].reshape(2, width) for a in pair])
    grad_conv_kernel = pair[0][2 * width : 5 * width].reshape(conv_kernel.shape)
    grad_qk_gains = pair[1][5 * width : count].reshape(qk_gains.shape)

    activations = chosen(result_0, result_1).reshape(1, 1, *shape)
    input_grads = chosen(input_grad_0, input_grad_1).reshape(1, 1, *shape)
    return (
        activations,
        input_grads,
        grad_norm_gains,
        grad_conv_kernel,
        grad_qk_gains,
        grad_conv_in,
        grad_attn_qkv,
        grad_mixer_out,
        grad_gate_up,
        grad_down,
    )


def solution(mesh):
    wide = Mesh(mesh.devices.reshape(2, 2, 4, 4, 2), AXES)
    dp = ("xl", "y", "z")
    everyone = ("xh", "xl", "y", "z")
    in_specs = (
        P(dp, None, "c", None),
        P(dp, None, "c", None),
        P(dp, None, None),
        P(),
        P(),
        P(),
        P(everyone, None, "c"),
        P(everyone, "c"),
        P("xh", "c", None),
        P("xh", None, None, "c"),
        P("xh", "c", None),
    )
    out_specs = (
        P("xh", dp, None, "c", None),
        P("xh", dp, None, "c", None),
        P(),
        P(),
        P(),
        P(everyone, None, "c"),
        P(everyone, "c"),
        P("xh", "c", dp),
        P("xh", None, dp, "c"),
        P("xh", "c", dp),
    )
    return jax.shard_map(local, mesh=wide, in_specs=in_specs, out_specs=out_specs, check_vma=False)
```

```python
import functools

import jax
import jax.numpy as jnp
from jax import lax
from jax.experimental import pallas as pl
from jax.experimental.pallas import tpu as pltpu
from jax.sharding import Mesh
from jax.sharding import PartitionSpec as P

HEADS = 24
KV_HEADS = 8
HEAD_DIM = 64
GROUP = HEADS // KV_HEADS

EPSILON = 1e-05
ROPE_BASE = 1000000.0
MASKED_SCORE = -1e30

F32 = jnp.float32
BF16 = jnp.bfloat16

PLANE = ("y", "z")
AXES = ("xh", "xl", "y", "z", "c")


def product(left, right):
    return jnp.dot(left, right, preferred_element_type=F32)


def product_left(left, right):
    return lax.dot_general(left, right, (((0,), (0,)), ((), ())), preferred_element_type=F32)


def product_right(left, right):
    return lax.dot_general(left, right, (((1,), (1,)), ((), ())), preferred_element_type=F32)


def swapped(shard, axis):
    return lax.ppermute(shard, axis, [(0, 1), (1, 0)])


def spread(own):
    return lax.all_gather(own, "c", tiled=True)


def joined(mine, other):
    return mine + swapped(other, "c").astype(F32)


def mean_last(values):
    return jnp.mean(values, axis=-1, keepdims=True)


def inverse_rms(values):
    return lax.rsqrt(mean_last(values * values) + EPSILON)


def normalize(values):
    return values * inverse_rms(values)


def around(by):
    return [(k, (k + by) % 4) for k in range(4)]


def exchanged(tiles, axes):
    return lax.all_to_all(tiles, axes, 0, 0, tiled=True)


def ffn_grads(grad_active, gate, up):
    sigmoid = jax.nn.sigmoid(gate)
    grad_gate = grad_active * up * sigmoid * (1.0 + gate * (1.0 - sigmoid))
    grad_up = grad_active * gate * sigmoid
    return grad_gate.astype(BF16), grad_up.astype(BF16)


VMEM_LIMIT = 56 * 1024 * 1024
SHORT = pl.CostEstimate(flops=1, bytes_accessed=1, transcendentals=0)


def whole_lanes(columns):
    return -(-columns // 128) * 128


def ordered(kernel, count):
    def body(scalar_ref, *refs):
        kernel(scalar_ref, *refs[count:])

    return body


def unit_tiles(units, tile):
    short = units % tile
    tiles = [(0, short)] if short else []
    return tiles + [(at, tile) for at in range(short, units, tile)]


def streamed(tiles, copies, work):
    for copy in copies(0, 0):
        copy.start()
    for k in range(len(tiles)):
        slot = k % 2
        if k + 1 < len(tiles):
            for copy in copies(k + 1, 1 - slot):
                copy.start()
        for copy in copies(k, slot):
            copy.wait()
        work(k, slot)


def ffn_forward_kernel(
    tiles, core_ref, rows_ref, pair_ref, down_ref, gate_ref, up_ref, mine_ref, other_ref,
    pair_buf, down_buf, gate_buf, up_buf, acc_ref, sems, out_sems,
):
    def copies(k, slot):
        at, size = tiles[k]
        return [
            pltpu.make_async_copy(
                pair_ref.at[0, :, pl.ds(at, size)],
                pair_buf.at[slot, :, pl.ds(0, size)],
                sems.at[slot, 0],
            ),
            pltpu.make_async_copy(
                pair_ref.at[1, :, pl.ds(at, size)],
                pair_buf.at[slot, :, pl.ds(size, size)],
                sems.at[slot, 1],
            ),
            pltpu.make_async_copy(
                down_ref.at[pl.ds(at, size)], down_buf.at[slot, pl.ds(0, size)], sems.at[slot, 2]
            ),
        ]

    def kept(k):
        here = (slice(None), pl.ds(*tiles[k]))
        return [
            pltpu.make_async_copy(gate_buf.at[here], gate_ref.at[here], out_sems.at[k, 0]),
            pltpu.make_async_copy(up_buf.at[here], up_ref.at[here], out_sems.at[k, 1]),
        ]

    def work(k, slot):
        at, size = tiles[k]
        both = product(rows_ref[...], pair_buf[slot, :, : 2 * size])
        gate, up = both[:, :size], both[:, size:]
        gate_buf[:, at : at + size] = gate.astype(BF16)
        up_buf[:, at : at + size] = up.astype(BF16)
        for copy in kept(k):
            copy.start()
        active = (gate * jax.nn.sigmoid(gate) * up).astype(BF16)
        part = product(active, down_buf[slot, :size])
        if k == 0:
            acc_ref[...] = part
        else:
            acc_ref[...] += part

    streamed(tiles, copies, work)
    rows_out(acc_ref, core_ref[0], mine_ref, other_ref)
    for k in range(len(tiles)):
        for copy in kept(k):
            copy.wait()


def ffn_backward_kernel(
    tiles, core_ref, rows_ref, gate_ref, up_ref, pair_ref, down_ref, mine_ref, other_ref,
    pair_buf, down_buf, gate_buf, up_buf, acc_ref, sems,
):
    def copies(k, slot):
        at, size = tiles[k]
        columns, place = pl.ds(at, size), pl.ds(0, size)
        return [
            pltpu.make_async_copy(
                down_ref.at[columns], down_buf.at[slot, place], sems.at[slot, 0]
            ),
            pltpu.make_async_copy(
                gate_ref.at[:, columns], gate_buf.at[slot, :, place], sems.at[slot, 1]
            ),
            pltpu.make_async_copy(
                up_ref.at[:, columns], up_buf.at[slot, :, place], sems.at[slot, 2]
            ),
            pltpu.make_async_copy(
                pair_ref.at[0, :, columns], pair_buf.at[slot, :, place], sems.at[slot, 3]
            ),
            pltpu.make_async_copy(
                pair_ref.at[1, :, columns],
                pair_buf.at[slot, :, pl.ds(size, size)],
                sems.at[slot, 4],
            ),
        ]

    def work(k, slot):
        _, size = tiles[k]
        grad_active = product_right(rows_ref[...], down_buf[slot, :size])
        grads = ffn_grads(
            grad_active,
            gate_buf[slot, :, :size].astype(F32),
            up_buf[slot, :, :size].astype(F32),
        )
        part = product_right(jnp.concatenate(grads, axis=1), pair_buf[slot, :, : 2 * size])
        if k == 0:
            acc_ref[...] = part
        else:
            acc_ref[...] += part

    streamed(tiles, copies, work)
    rows_out(acc_ref, core_ref[0], mine_ref, other_ref)


def ffn_both_kernel(
    tiles, core_ref, rows_ref, grad_ref, pair_ref, down_ref,
    mine_ref, other_ref, grad_mine_ref, grad_other_ref, pair_buf, down_buf, acc_ref, grad_acc_ref, sems,
):
    def copies(k, slot):
        at, size = tiles[k]
        columns, place = pl.ds(at, size), pl.ds(0, size)
        return [
            pltpu.make_async_copy(
                pair_ref.at[0, :, columns], pair_buf.at[slot, :, place], sems.at[slot, 0]
            ),
            pltpu.make_async_copy(
                pair_ref.at[1, :, columns],
                pair_buf.at[slot, :, pl.ds(size, size)],
                sems.at[slot, 1],
            ),
            pltpu.make_async_copy(
                down_ref.at[columns], down_buf.at[slot, place], sems.at[slot, 2]
            ),
        ]

    def work(k, slot):
        _, size = tiles[k]
        both = product(rows_ref[...], pair_buf[slot, :, : 2 * size])
        grad_active = product_right(grad_ref[...], down_buf[slot, :size])
        gate, up = both[:, :size], both[:, size:]
        active = (gate * jax.nn.sigmoid(gate) * up).astype(BF16)
        grads = jnp.concatenate(ffn_grads(grad_active, gate, up), axis=1)
        part = product(active, down_buf[slot, :size])
        grad_part = product_right(grads, pair_buf[slot, :, : 2 * size])
        if k == 0:
            acc_ref[...], grad_acc_ref[...] = part, grad_part
        else:
            acc_ref[...] += part
            grad_acc_ref[...] += grad_part

    streamed(tiles, copies, work)
    rows_out(acc_ref, core_ref[0], mine_ref, other_ref)
    rows_out(grad_acc_ref, core_ref[0], grad_mine_ref, grad_other_ref)


def ffn_both_call(core, rows, grad, pair, down, behind):
    count, width = rows.shape
    units = down.shape[0]
    tile = 768
    vmem, any_space = pl.BlockSpec(memory_space=pltpu.VMEM), pl.BlockSpec(memory_space=pl.ANY)
    half = (count // 2, width)
    return pl.pallas_call(
        ordered(functools.partial(ffn_both_kernel, unit_tiles(units, tile)), len(behind)),
        in_specs=[
            pl.BlockSpec(memory_space=pltpu.SMEM),
            *[any_space] * len(behind),
            vmem,
            vmem,
            any_space,
            any_space,
        ],
        out_specs=[vmem] * 4,
        out_shape=[jax.ShapeDtypeStruct(half, F32), jax.ShapeDtypeStruct(half, BF16)] * 2,
        scratch_shapes=[
            pltpu.VMEM((2, width, 2 * tile), BF16),
            pltpu.VMEM((2, tile, width), BF16),
            pltpu.VMEM((count, width), F32),
            pltpu.VMEM((count, width), F32),
            pltpu.SemaphoreType.DMA((2, 3)),
        ],
        compiler_params=pltpu.CompilerParams(vmem_limit_bytes=VMEM_LIMIT),
        cost_estimate=SHORT,
    )(core, *behind, rows, grad, pair, down)


def feed_forward_call(backward, core, rows, pair, down, saved=(), behind=()):
    count, width = rows.shape
    units = down.shape[0]
    tile = 768
    tiles = unit_tiles(units, tile)
    vmem, any_space = pl.BlockSpec(memory_space=pltpu.VMEM), pl.BlockSpec(memory_space=pl.ANY)
    scalar = pl.BlockSpec(memory_space=pltpu.SMEM)
    out_shape = [
        jax.ShapeDtypeStruct((count // 2, width), F32),
        jax.ShapeDtypeStruct((count // 2, width), BF16),
    ]
    out_specs = [vmem, vmem]
    buffers = [pltpu.VMEM((2, width, 2 * tile), BF16), pltpu.VMEM((2, tile, width), BF16)]
    acc = pltpu.VMEM((count, width), F32)
    if backward:
        body = functools.partial(ffn_backward_kernel, tiles)
        in_specs = [scalar, vmem, any_space, any_space, any_space, any_space]
        buffers += [pltpu.VMEM((2, count, tile), BF16)] * 2
        scratch = [*buffers, acc, pltpu.SemaphoreType.DMA((2, 5))]
    else:
        body = functools.partial(ffn_forward_kernel, tiles)
        in_specs = [scalar, vmem, any_space, any_space]
        out_shape = [jax.ShapeDtypeStruct((count, units), BF16)] * 2 + out_shape
        out_specs = [any_space, any_space, *out_specs]
        buffers += [pltpu.VMEM((count, units), BF16)] * 2
        scratch = [*buffers, acc]
        scratch += [pltpu.SemaphoreType.DMA((2, 3)), pltpu.SemaphoreType.DMA((len(tiles), 2))]
    cost = pl.CostEstimate(
        flops=12 * count * width * units, bytes_accessed=6 * width * units, transcendentals=0
    )
    in_specs = [scalar, *[any_space] * len(behind), *in_specs[1:]]
    return pl.pallas_call(
        ordered(body, len(behind)),
        in_specs=in_specs,
        out_specs=out_specs,
        out_shape=out_shape,
        scratch_shapes=scratch,
        compiler_params=pltpu.CompilerParams(vmem_limit_bytes=VMEM_LIMIT),
        cost_estimate=cost if backward else SHORT,
    )(core, *behind, rows, *saved, pair, down)


def part_forward_kernel(*refs):
    rows_ref, pair_ref, kept_ref = refs[-3:]
    both = product(rows_ref[...], pair_ref[...])
    units = both.shape[1] // 2
    gate, up = both[:, :units], both[:, units:]
    sigmoid = jax.nn.sigmoid(gate)
    silu = gate * sigmoid
    kept_ref[:, :units] = (up * (sigmoid + silu * (1.0 - sigmoid))).astype(BF16)
    kept_ref[:, units : 2 * units] = silu.astype(BF16)
    kept_ref[:, 2 * units :] = (silu * up).astype(BF16)


def part_forward_call(behind, rows, pair):
    tokens, width = rows.shape
    units = pair.shape[1] // 2
    tile = 1024
    return pl.pallas_call(
        part_forward_kernel,
        grid=(tokens // tile,),
        in_specs=[
            *[pl.BlockSpec(memory_space=pl.ANY)] * len(behind),
            pl.BlockSpec((tile, width), lambda i: (i, 0)),
            pl.BlockSpec((width, 2 * units), lambda i: (0, 0)),
        ],
        out_specs=pl.BlockSpec((tile, 3 * units), lambda i: (i, 0)),
        out_shape=jax.ShapeDtypeStruct((tokens, 3 * units), BF16),
        compiler_params=pltpu.CompilerParams(vmem_limit_bytes=VMEM_LIMIT),
        cost_estimate=pl.CostEstimate(
            flops=8 * tokens * width * units, bytes_accessed=2 * tokens * width, transcendentals=0
        ),
    )(*behind, rows, pair)


def pair_out(acc_ref, here, mine_ref, other_ref):
    rows = mine_ref.shape[0]
    for ref, half in ((mine_ref, here), (other_ref, 1 - here)):
        ref[...] = acc_ref[pl.ds(pl.multiple_of(half * rows, rows), rows)].astype(BF16)


def accumulated(acc_ref, part, finish):
    step = pl.program_id(0)

    @pl.when(step == 0)
    def _():
        acc_ref[...] = part

    @pl.when(step > 0)
    def _():
        acc_ref[...] += part

    pl.when(step == pl.num_programs(0) - 1)(finish)


def part_down_kernel(here_ref, grad_ref, kept_ref, down_ref, pair_ref, mine_ref, other_ref, acc_ref):
    grad = grad_ref[...]
    units = down_ref.shape[0]
    grad_active = product_right(grad, down_ref[...])
    for k in range(2):
        lanes = slice(k * units, (k + 1) * units)
        pair_ref[:, lanes] = (grad_active * kept_ref[:, lanes].astype(F32)).astype(BF16)
    accumulated(
        acc_ref,
        product_left(grad, kept_ref[:, 2 * units :]),
        lambda: pair_out(acc_ref, here_ref[0], mine_ref, other_ref),
    )


def part_pair_kernel(here_ref, rows_ref, pair_ref, mine_ref, other_ref, acc_ref):
    accumulated(
        acc_ref,
        product_left(rows_ref[...], pair_ref[...]),
        lambda: pair_out(acc_ref, here_ref[0], mine_ref, other_ref),
    )


def part_call(kernel, here, operands, fixed, outs, result, flops, behind=()):
    tokens = operands[0].shape[0]
    tile = 1024
    by_tokens = lambda width: pl.BlockSpec((tile, width), lambda i, h: (i, 0))
    entire = lambda shape: pl.BlockSpec(shape, lambda i, h: (0, 0))
    half = (result[0] // 2, result[1])
    return pl.pallas_call(
        ordered(kernel, len(behind)),
        grid_spec=pltpu.PrefetchScalarGridSpec(
            num_scalar_prefetch=1,
            grid=(tokens // tile,),
            in_specs=[pl.BlockSpec(memory_space=pl.ANY)] * len(behind)
            + [by_tokens(a.shape[1]) for a in operands]
            + [entire(a.shape) for a in fixed],
            out_specs=[by_tokens(width) for width in outs] + [entire(half)] * 2,
            scratch_shapes=[pltpu.VMEM(result, F32)],
        ),
        out_shape=[jax.ShapeDtypeStruct((tokens, width), BF16) for width in outs]
        + [jax.ShapeDtypeStruct(half, BF16)] * 2,
        compiler_params=pltpu.CompilerParams(vmem_limit_bytes=VMEM_LIMIT),
        cost_estimate=SHORT,
    )(here, *behind, *operands, *fixed)


def part_down_call(here, grad, kept, down, behind):
    tokens, width = grad.shape
    units = down.shape[0]
    flops = 4 * tokens * width * units
    return part_call(
        part_down_kernel,
        here,
        (grad, kept),
        (down,),
        (2 * units,),
        (width, units),
        flops,
        behind,
    )


def part_pair_call(here, inner, pair, behind):
    (tokens, width), columns = inner.shape, pair.shape[1]
    flops = 2 * tokens * width * columns
    return part_call(
        part_pair_kernel, here, (inner, pair), (), (), (width, columns), flops, behind
    )


def back_join_kernel(
    behind_ref, mine_ref, come_ref, values_ref, base_ref, gain_ref, wide_ref, low_ref, sums_ref
):
    grad = mine_ref[...] + come_ref[...].astype(F32)
    values = values_ref[...]
    inverse = inverse_rms(values)
    normed = values * inverse
    scaled = grad * gain_ref[...]
    sums_ref[...] = jnp.sum(grad * normed, axis=0, keepdims=True)
    total = base_ref[...] + inverse * (scaled - normed * mean_last(scaled * normed))
    wide_ref[...] = total
    low_ref[...] = total.astype(BF16)


def back_join_call(behind, mine, come, values, base, gain):
    vmem = pl.BlockSpec(memory_space=pltpu.VMEM)
    shape = values.shape
    wide, low, sums = pl.pallas_call(
        back_join_kernel,
        in_specs=[pl.BlockSpec(memory_space=pl.ANY), *[vmem] * 5],
        out_specs=[vmem] * 3,
        out_shape=[
            jax.ShapeDtypeStruct(shape, F32),
            jax.ShapeDtypeStruct(shape, BF16),
            jax.ShapeDtypeStruct((1, shape[1]), F32),
        ],
        compiler_params=pltpu.CompilerParams(vmem_limit_bytes=VMEM_LIMIT),
        cost_estimate=SHORT,
    )(behind, mine, come, values, base, gain[None])
    return wide, low, sums[0]


def pair_join_kernel(count, *refs):
    *refs, out_ref = refs[count:]
    at = 0
    for mine_ref, come_ref in zip(refs[::2], refs[1::2]):
        size = mine_ref.shape[-1]
        total = mine_ref[...].astype(F32) + come_ref[...].astype(F32)
        out_ref[..., at : at + size] = total.astype(BF16)
        at += size


def pair_join_call(behind, pairs):
    vmem = pl.BlockSpec(memory_space=pltpu.VMEM)
    operands = [a for pair in pairs for a in pair]
    shape = (*operands[0].shape[:-1], sum(mine.shape[-1] for mine, _ in pairs))
    return pl.pallas_call(
        functools.partial(pair_join_kernel, len(behind)),
        in_specs=[pl.BlockSpec(memory_space=pl.ANY)] * len(behind) + [vmem] * len(operands),
        out_specs=vmem,
        out_shape=jax.ShapeDtypeStruct(shape, BF16),
        compiler_params=pltpu.CompilerParams(vmem_limit_bytes=VMEM_LIMIT),
        cost_estimate=SHORT,
    )(*behind, *operands)


def widened_kernel(behind_ref, low_ref, wide_ref):
    wide_ref[...] = low_ref[...].astype(F32)


def widened_call(behind, low):
    vmem = pl.BlockSpec(memory_space=pltpu.VMEM)
    return pl.pallas_call(
        widened_kernel,
        in_specs=[pl.BlockSpec(memory_space=pl.ANY), vmem],
        out_specs=vmem,
        out_shape=jax.ShapeDtypeStruct(low.shape, F32),
        compiler_params=pltpu.CompilerParams(vmem_limit_bytes=VMEM_LIMIT),
        cost_estimate=SHORT,
    )(behind, low)


def line_sums_kernel(places_ref, come_ref, mine_ref, other_ref, acc_ref):
    here = places_ref[0]
    count, rows, _ = mine_ref.shape
    for k in range(count):
        tiles = [come_ref[m * count + k].astype(F32) for m in range(come_ref.shape[0] // count)]
        acc_ref[...] = functools.reduce(jnp.add, tiles)
        mine_ref[k] = acc_ref[pl.ds(pl.multiple_of(here * rows, rows), rows)]
        other = acc_ref[pl.ds(pl.multiple_of((1 - here) * rows, rows), rows)]
        other_ref[k] = other.astype(BF16)


def line_sums_call(places, come):
    vmem = pl.BlockSpec(memory_space=pltpu.VMEM)
    plane, block, size = come.shape
    lines = (4, block // 2, size)
    return pl.pallas_call(
        line_sums_kernel,
        in_specs=[pl.BlockSpec(memory_space=pltpu.SMEM), vmem],
        out_specs=[vmem] * 2,
        out_shape=[jax.ShapeDtypeStruct(lines, F32), jax.ShapeDtypeStruct(lines, BF16)],
        scratch_shapes=[pltpu.VMEM((block, size), F32)],
        compiler_params=pltpu.CompilerParams(vmem_limit_bytes=VMEM_LIMIT),
        cost_estimate=SHORT,
    )(places, come)


def finish_kernel(
    places_ref, behind_ref, mine_ref, come_ref, small_ref, kept_ref, sent_ref, sums_ref, acc_ref
):
    section = places_ref[1]
    short = kept_ref.shape[1]
    acc_ref[...] = mine_ref[...] + come_ref[...].astype(F32)
    kept_ref[...] = acc_ref[:, pl.ds(pl.multiple_of(section * short, short), short)]
    sent = acc_ref[:, pl.ds(pl.multiple_of((1 - section) * short, short), short)]
    sent_ref[...] = sent.astype(BF16)
    half = small_ref.shape[0] // 2
    for k in range(2):
        sums_ref[k] = jnp.sum(small_ref[k * half : (k + 1) * half], axis=0)


def finish_call(places, behind, mine, come, small):
    vmem = pl.BlockSpec(memory_space=pltpu.VMEM)
    count, rows, size = mine.shape
    lines = (count, rows // 2, size)
    return pl.pallas_call(
        finish_kernel,
        in_specs=[
            pl.BlockSpec(memory_space=pltpu.SMEM),
            pl.BlockSpec(memory_space=pl.ANY),
            *[vmem] * 3,
        ],
        out_specs=[vmem] * 3,
        out_shape=[
            jax.ShapeDtypeStruct(lines, F32),
            jax.ShapeDtypeStruct(lines, BF16),
            jax.ShapeDtypeStruct((2, *small.shape[1:]), F32),
        ],
        scratch_shapes=[pltpu.VMEM(mine.shape, F32)],
        compiler_params=pltpu.CompilerParams(vmem_limit_bytes=VMEM_LIMIT),
        cost_estimate=SHORT,
    )(places, behind, mine, come, small)


def mixer_grads_kernel(
    places_ref, behind_ref, columns_ref, gated_0_ref, gated_1_ref, gated_2_ref, gated_3_ref,
    early_ref, late_ref, parts_ref, out_mine_ref, out_other_ref, normed_ref,
    in_ref, out_ref, sem,
):
    here, section, y = places_ref[0], places_ref[1], places_ref[2]

    def copy(all_ref):
        rows = normed_ref.shape[0]
        start = pl.multiple_of(y * rows, rows)
        return pltpu.make_async_copy(all_ref.at[pl.ds(start, rows)], normed_ref, sem)

    @pl.when(section == 0)
    def _():
        copy(early_ref).start()

    @pl.when(section > 0)
    def _():
        copy(late_ref).start()

    mix = out_ref.shape[0]
    blocks = (gated_0_ref, gated_1_ref, gated_2_ref, gated_3_ref)
    span = gated_0_ref.shape[0]
    total = None
    for k, gated_ref in enumerate(blocks):
        start = lax.rem(places_ref[3] - k + len(blocks), len(blocks)) * span
        tiles = columns_ref[pl.ds(pl.multiple_of(start, span), span), :mix]
        block = product_left(tiles, gated_ref[...])
        total = block if total is None else total + block
    out_ref[...] = total
    pair_out(out_ref, here, out_mine_ref, out_other_ref)
    copy(early_ref).wait()
    in_ref[...] = product_left(normed_ref[...], columns_ref[:, mix:])
    plane, block, _ = parts_ref.shape
    short = block // 4
    for k in range(plane):
        for half in range(2):
            for s in range(2):
                start = ((2 * s + half) * plane + k) * short
                place = (2 * half + s) * short
                rows_in = in_ref[start : start + short]
                parts_ref[k, place : place + short] = rows_in.astype(BF16)


def mixer_grads_call(places, behind, columns, gated, early, late, plane):
    vmem, any_space = pl.BlockSpec(memory_space=pltpu.VMEM), pl.BlockSpec(memory_space=pl.ANY)
    tokens, channels = columns.shape[0], gated[0].shape[1]
    width = early.shape[1]
    mix = width // 4
    size = columns.shape[1] - mix
    in_parts = jax.ShapeDtypeStruct((plane, width // plane, size), BF16)
    out_half = jax.ShapeDtypeStruct((mix // 2, channels), BF16)
    return pl.pallas_call(
        mixer_grads_kernel,
        in_specs=[
            pl.BlockSpec(memory_space=pltpu.SMEM),
            any_space,
            vmem,
            *[vmem] * len(gated),
            any_space,
            any_space,
        ],
        out_specs=[vmem] * 3,
        out_shape=[in_parts, out_half, out_half],
        scratch_shapes=[
            pltpu.VMEM((tokens, width), BF16),
            pltpu.VMEM((width, size), F32),
            pltpu.VMEM((mix, channels), F32),
            pltpu.SemaphoreType.DMA,
        ],
        compiler_params=pltpu.CompilerParams(vmem_limit_bytes=VMEM_LIMIT),
        cost_estimate=SHORT,
    )(places, behind, columns, *gated, early, late)


def load_all(copies):
    for copy in copies:
        copy.start()


def in_time(rows):
    half = rows.shape[0] // 4
    return jnp.concatenate([rows[k * half : (k + 1) * half] for k in (0, 2, 1, 3)], axis=0)


def rows_out(acc_ref, core, mine_ref, other_ref):
    half = mine_ref.shape[0]
    mine_ref[...] = acc_ref[pl.ds(pl.multiple_of(core * half, half), half)]
    rest = acc_ref[pl.ds(pl.multiple_of((1 - core) * half, half), half)]
    other_ref[...] = rest.astype(BF16)


def weight_copies(whole_ref, out_ref, in_buf, out_buf, sems, start):
    size = in_buf.shape[2]
    copies = [
        pltpu.make_async_copy(
            whole_ref.at[:, pl.ds(start + k * size, size)], in_buf.at[k], sems.at[k]
        )
        for k in range(in_buf.shape[0])
    ]
    return copies, pltpu.make_async_copy(out_ref, out_buf, sems.at[len(copies)])


def conv_taps(mixed, kernel, masks):
    terms = [mixed]
    for lag in range(1, len(masks) + 1):
        terms.append(pltpu.roll(mixed, lag, 0) * masks[lag - 1])
    taps = kernel.shape[0]
    total = kernel[taps - 1 : taps] * terms[0]
    for lag in range(1, taps):
        total = total + kernel[taps - 1 - lag : taps - lag] * terms[lag]
    return terms, total


def conv_forward_kernel(
    core_ref, rows_ref, kernel_ref, masks_ref, whole_ref, out_ref,
    proj_ref, gated_ref, mine_ref, other_ref, in_buf, out_buf, acc_ref, sems,
):
    copies, last = weight_copies(whole_ref, out_ref, in_buf, out_buf, sems, 0)
    load_all([*copies, last])
    rows = rows_ref[...]
    parts = []
    for k, copy in enumerate(copies):
        copy.wait()
        part = product(rows, in_buf[k])
        proj_ref[k] = part.astype(BF16)
        parts.append(in_time(part))
    masks = [masks_ref[lag] for lag in range(masks_ref.shape[0])]
    gated = []
    for at in range(0, parts[0].shape[1], 128):
        before, after, signal = [part[:, at : at + 128] for part in parts]
        _, total = conv_taps(before * signal, kernel_ref[:, at : at + 128], masks)
        gated.append((after * total).astype(BF16))
    gated = in_time(jnp.concatenate(gated, axis=1))
    gated_ref[...] = gated
    last.wait()
    acc_ref[...] = product(gated, out_buf[...])
    rows_out(acc_ref, core_ref[0], mine_ref, other_ref)


def tiles_out(tiles_ref, grad_ref, columns):
    count, rows, size = tiles_ref.shape
    step = grad_ref.shape[1] // (2 * count * count)
    for k in range(count):
        starts = range(k * step, grad_ref.shape[1], count * step)
        parts = [grad_ref[:, at : at + step] for at in starts]
        parts.append(columns(k))
        spare = size - sum(part.shape[1] for part in parts)
        tiles_ref[k] = jnp.concatenate([*parts, jnp.zeros((rows, spare), BF16)], axis=1)


def conv_backward_kernel(
    core_ref, grad_ref, kernel_ref, masks_ref, proj_ref, other_tiles_ref,
    whole_ref, out_ref, tiles_ref, taps_ref, mine_ref, other_ref, in_buf, out_buf, acc_ref, sems,
):
    copies, last = weight_copies(whole_ref, out_ref, in_buf, out_buf, sems, 0)
    load_all([last, *copies])
    last.wait()
    grad_gated = in_time(product_right(grad_ref[...], out_buf[...]))
    parts = [in_time(proj_ref[k].astype(F32)) for k in range(3)]
    masks = [masks_ref[lag] for lag in range(masks_ref.shape[0])]
    rows = grad_gated.shape[0]
    grads = [[], [], []]
    for at in range(0, grad_gated.shape[1], 128):
        before, after, signal = [part[:, at : at + 128] for part in parts]
        kernel = kernel_ref[:, at : at + 128]
        terms, total = conv_taps(before * signal, kernel, masks)
        grad = grad_gated[:, at : at + 128]
        grad_total = grad * after
        taps = kernel.shape[0]
        grad_mixed = kernel[taps - 1 : taps] * grad_total
        for lag in range(1, taps):
            sent = pltpu.roll(grad_total * masks[lag - 1], rows - lag, 0)
            grad_mixed = grad_mixed + kernel[taps - 1 - lag : taps - lag] * sent
        for lag in range(taps):
            taps_ref[taps - 1 - lag : taps - lag, at : at + 128] = jnp.sum(
                grad_total * terms[lag], axis=0, keepdims=True
            )
        for k, value in enumerate((grad_mixed * signal, grad * total, grad_mixed * before)):
            grads[k].append(value.astype(BF16))
    grads = [in_time(jnp.concatenate(g, axis=1)) for g in grads]
    step = grads[0].shape[1] // tiles_ref.shape[0]

    @pl.when(core_ref[1] == 0)
    def _():
        tiles_out(
            tiles_ref,
            grad_ref,
            lambda k: jnp.concatenate([g[:, k * step : (k + 1) * step] for g in grads], axis=1),
        )

    @pl.when(core_ref[1] > 0)
    def _():
        tiles_ref[...] = other_tiles_ref[...]

    for k, copy in enumerate(copies):
        copy.wait()
        part = product_right(grads[k], in_buf[k])
        acc_ref[...] = part if k == 0 else acc_ref[...] + part
    rows_out(acc_ref, core_ref[0], mine_ref, other_ref)


def head_kind(head):
    return min(max(head % (GROUP + 2) - GROUP + 1, 0), 2)


def lane_facts(rows):
    lane = lax.broadcasted_iota(jnp.int32, (rows, 128), 1)
    return lane < HEAD_DIM, lax.rem(lane, HEAD_DIM) < HEAD_DIM // 2


def head_scales(block, low):
    squares = block * block
    first = jnp.sum(jnp.where(low, squares, 0.0), axis=1, keepdims=True)
    second = jnp.sum(jnp.where(low, 0.0, squares), axis=1, keepdims=True)
    return lax.rsqrt(jnp.where(low, first, second) * (1.0 / HEAD_DIM) + EPSILON)


def block_gains(gains_ref, at):
    heads = [head_kind(2 * at), head_kind(2 * at + 1)]
    return heads, gains_ref[3 * heads[0] + heads[1] : 3 * heads[0] + heads[1] + 1]


def attention_forward_kernel(
    core_ref, rows_ref, gains_ref, tables_ref, mask_ref, whole_ref, out_ref,
    qkv_ref, ready_ref, gated_ref, mine_ref, other_ref, in_buf, out_buf, acc_ref, sems,
):
    copies, last = weight_copies(
        whole_ref, out_ref, in_buf, out_buf, sems, whole_ref.shape[1] - in_buf.shape[2]
    )
    load_all([*copies, last])
    copies[0].wait()
    qkv_ref[...] = product(rows_ref[...], in_buf[0])
    rows, width = qkv_ref.shape
    low, front = lane_facts(rows)
    cosine, sine = tables_ref[0], tables_ref[1]
    for at in range(width // 128):
        block = qkv_ref[:, at * 128 : (at + 1) * 128]
        heads, gains = block_gains(gains_ref, at)
        normed = block * head_scales(block, low) * gains
        turned = jnp.where(front, -pltpu.roll(normed, 96, 1), pltpu.roll(normed, 32, 1))
        ready = normed * cosine + turned * sine
        if heads[0] == 2:
            ready = jnp.where(low, block, ready)
        if heads[1] == 2:
            ready = jnp.where(low, ready, block)
        ready_ref[:, at * 128 : (at + 1) * 128] = ready.astype(BF16)
    half = rows // 4
    span = (GROUP + 2) * HEAD_DIM
    for m in range(2):
        mask = mask_ref[m] > 0
        mask = jnp.concatenate([mask] * GROUP, axis=0)
        for g in range(width // span):
            queries, keys, values = head_rows(ready_ref, m, half, g * span)
            weights = softmax_weights(queries, keys, mask)
            attended = product(weights.astype(BF16), values).astype(BF16)
            for j in range(GROUP):
                at = (g * GROUP + j) * HEAD_DIM
                head = attended[j * 2 * half : (j + 1) * 2 * half]
                gated_ref[m * half : (m + 1) * half, at : at + HEAD_DIM] = head[:half]
                gated_ref[(m + 2) * half : (m + 3) * half, at : at + HEAD_DIM] = head[half:]
    last.wait()
    acc_ref[...] = product(gated_ref[...], out_buf[...])
    rows_out(acc_ref, core_ref[0], mine_ref, other_ref)


def sequence(ref, m, half, at):
    columns = slice(at, at + HEAD_DIM)
    return jnp.concatenate(
        [ref[m * half : (m + 1) * half, columns], ref[(m + 2) * half : (m + 3) * half, columns]],
        axis=0,
    )


def head_rows(ref, m, half, at):
    heads = [sequence(ref, m, half, at + j * HEAD_DIM) for j in range(GROUP + 2)]
    return jnp.concatenate(heads[:GROUP], axis=0), heads[GROUP], heads[GROUP + 1]


def softmax_weights(queries, keys, mask):
    scores = jnp.where(mask, product_right(queries, keys) * HEAD_DIM ** (-0.5), MASKED_SCORE)
    terms = jnp.exp(scores - jnp.max(scores, axis=1, keepdims=True))
    return terms / jnp.sum(terms, axis=1, keepdims=True)


def attention_backward_kernel(
    core_ref, grad_ref, gains_ref, tables_ref, mask_ref, qkv_ref, ready_ref,
    whole_ref, out_ref, tiles_ref, heads_ref, mine_ref, other_ref,
    in_buf, out_buf, acc_ref, attended_ref, ready_grad_ref, proj_ref, sems,
):
    copies, last = weight_copies(
        whole_ref, out_ref, in_buf, out_buf, sems, whole_ref.shape[1] - in_buf.shape[2]
    )
    load_all([last, *copies])
    last.wait()
    attended_ref[...] = product_right(grad_ref[...], out_buf[...]).astype(BF16)
    rows, width = qkv_ref.shape
    half = rows // 4
    span = (GROUP + 2) * HEAD_DIM
    scale = HEAD_DIM ** (-0.5)
    for m in range(2):
        mask = mask_ref[m] > 0
        mask = jnp.concatenate([mask] * GROUP, axis=0)
        for g in range(width // span):
            queries, keys, values = head_rows(ready_ref, m, half, g * span)
            weights = softmax_weights(queries, keys, mask)
            grad = jnp.concatenate(
                [
                    sequence(attended_ref, m, half, (g * GROUP + j) * HEAD_DIM)
                    for j in range(GROUP)
                ],
                axis=0,
            )
            grad_values = product_left(weights.astype(BF16), grad)
            grad_weights = product_right(grad, values)
            mean = jnp.sum(grad_weights * weights, axis=1, keepdims=True)
            grad_scores = (weights * (grad_weights - mean)).astype(BF16)
            grad_queries = product(grad_scores, keys) * scale
            grad_keys = product_left(grad_scores, queries) * scale
            outs = [grad_queries[j * 2 * half : (j + 1) * 2 * half] for j in range(GROUP)]
            for j, out in enumerate([*outs, grad_keys, grad_values]):
                at = g * span + j * HEAD_DIM
                ready_grad_ref[m * half : (m + 1) * half, at : at + HEAD_DIM] = out[:half]
                ready_grad_ref[(m + 2) * half : (m + 3) * half, at : at + HEAD_DIM] = out[half:]
    low, front = lane_facts(rows)
    cosine, sine = tables_ref[0], tables_ref[1]
    for at in range(width // 128):
        lanes = slice(at * 128, (at + 1) * 128)
        block, grad = qkv_ref[:, lanes], ready_grad_ref[:, lanes]
        heads, gains = block_gains(gains_ref, at)
        inverse = head_scales(block, low)
        normed = block * inverse
        turned = grad * sine
        grad_normed = grad * cosine + jnp.where(
            front, pltpu.roll(turned, 96, 1), -pltpu.roll(turned, 32, 1)
        )
        heads_ref[at : at + 1] = jnp.sum(grad_normed * normed, axis=0, keepdims=True)
        grad_normed = grad_normed * gains
        along = grad_normed * normed
        first = jnp.sum(jnp.where(low, along, 0.0), axis=1, keepdims=True)
        second = jnp.sum(jnp.where(low, 0.0, along), axis=1, keepdims=True)
        mean = jnp.where(low, first, second) * (1.0 / HEAD_DIM)
        raw = inverse * (grad_normed - normed * mean)
        if heads[0] == 2:
            raw = jnp.where(low, grad, raw)
        if heads[1] == 2:
            raw = jnp.where(low, raw, grad)
        proj_ref[:, lanes] = raw.astype(BF16)
    step = width // tiles_ref.shape[0]
    tiles_out(tiles_ref, grad_ref, lambda k: proj_ref[:, k * step : (k + 1) * step])
    copies[0].wait()
    acc_ref[...] = product_right(proj_ref[...], in_buf[0])
    rows_out(acc_ref, core_ref[0], mine_ref, other_ref)


def mixer_call(
    kernel, core, operands, whole, weight_out, in_tiles, outs, scratch=(), behind=()
):
    vmem, any_space = pl.BlockSpec(memory_space=pltpu.VMEM), pl.BlockSpec(memory_space=pl.ANY)
    rows, width = operands[0].shape
    channels = weight_out.shape[0]
    outs = [*outs, ((rows // 2, width), F32), ((rows // 2, width), BF16)]
    return pl.pallas_call(
        ordered(kernel, len(behind)),
        in_specs=[
            pl.BlockSpec(memory_space=pltpu.SMEM),
            *[any_space] * len(behind),
            *[vmem] * len(operands),
            any_space,
            any_space,
        ],
        out_specs=[vmem] * len(outs),
        out_shape=[jax.ShapeDtypeStruct(*out) for out in outs],
        scratch_shapes=[
            pltpu.VMEM((in_tiles[0], width, in_tiles[1]), BF16),
            pltpu.VMEM((channels, width), BF16),
            pltpu.VMEM((rows, width), F32),
            *scratch,
            pltpu.SemaphoreType.DMA((in_tiles[0] + 1,)),
        ],
        compiler_params=pltpu.CompilerParams(vmem_limit_bytes=VMEM_LIMIT),
        cost_estimate=SHORT,
    )(core, *behind, *operands, whole, weight_out)


def conv_forward_call(core, rows, kernel, masks, whole, weight_out):
    count, channels = rows.shape[0], kernel.shape[1]
    outs = [((3, count, channels), BF16), ((count, channels), BF16)]
    operands = (rows, kernel, masks)
    return mixer_call(
        conv_forward_kernel, core, operands, whole, weight_out, (3, channels), outs
    )


def conv_backward_call(core, grad, kernel, masks, projected, tiles, whole, weight_out):
    count, width = grad.shape
    taps, channels = kernel.shape
    outs = [
        (tiles.shape, BF16),
        ((taps, channels), F32),
    ]
    operands = (grad, kernel, masks, projected, tiles)
    return mixer_call(
        conv_backward_kernel, core, operands, whole, weight_out, (3, channels), outs
    )


def attention_forward_call(core, rows, gains, tables, mask, whole, weight_out, qkv_width):
    count, channels = rows.shape[0], weight_out.shape[0]
    outs = [((count, qkv_width), F32), ((count, qkv_width), BF16), ((count, channels), BF16)]
    operands = (rows, gains, tables, mask)
    return mixer_call(
        attention_forward_kernel, core, operands, whole, weight_out, (1, qkv_width), outs
    )


def attention_backward_call(core, grad, gains, tables, mask, qkv, ready, whole, weight_out):
    count, width = grad.shape
    channels, qkv_width = weight_out.shape[0], qkv.shape[1]
    outs = [
        ((4, count, whole_lanes((width + 3 * channels) // 4)), BF16),
        ((qkv_width // 128, 128), F32),
    ]
    scratch = [
        pltpu.VMEM((count, channels), BF16),
        pltpu.VMEM((count, qkv_width), F32),
        pltpu.VMEM((count, qkv_width), BF16),
    ]
    operands = (grad, gains, tables, mask, qkv, ready)
    return mixer_call(
        attention_backward_kernel, core, operands, whole, weight_out, (1, qkv_width), outs, scratch
    )


def conv_masks(segments, taps):
    masks = []
    for lag in range(1, taps):
        same = (segments[:, lag:] == segments[:, :-lag]).astype(F32)
        same = jnp.pad(same, ((0, 0), (lag, 0))).reshape(-1, 1)
        masks.append(jnp.broadcast_to(same, (same.shape[0], 128)))
    return jnp.stack(masks)


def score_mask(segments):
    position = jnp.arange(segments.shape[1])
    allowed = position[:, None] >= position[None, :]
    return (allowed & (segments[:, :, None] == segments[:, None, :])).astype(F32)


def turn_tables(length):
    half = HEAD_DIM // 2
    exponent = jnp.arange(half, dtype=F32) * (2.0 / HEAD_DIM)
    frequency = jnp.exp(-exponent * jnp.log(ROPE_BASE))
    angles = jnp.arange(length, dtype=F32)[:, None] * frequency[None, :]
    tables = jnp.tile(jnp.stack([jnp.cos(angles), jnp.sin(angles)]), (1, 1, 4))
    tables = tables.reshape(2, 2, 1, length // 2, 128)
    return jnp.broadcast_to(tables, (2, 2, 2, length // 2, 128)).reshape(2, 2 * length, 128)


def gain_rows(head_gains):
    kinds = [head_gains[0], head_gains[1], jnp.ones_like(head_gains[0])]
    rows = [jnp.concatenate([a, b]) for a in kinds for b in kinds]
    return jnp.stack(rows)


def head_gain_sums(sums):
    heads = sums.reshape(-1, GROUP + 2, HEAD_DIM)
    return jnp.stack([heads[:, :GROUP].sum((0, 1)), heads[:, GROUP].sum(0)])


def local(
    inputs,
    out_cotangent,
    segments,
    norm_gains,
    conv_kernel,
    qk_gains,
    conv_in,
    attn_qkv,
    mixer_out,
    gate_up,
    down,
):
    section = lax.axis_index("xh")
    first = section == 0
    core = lax.axis_index("c")
    place = lax.axis_index("y") * 4 + lax.axis_index("z")
    xl = lax.axis_index("xl")
    plane = lax.axis_size("y") * lax.axis_size("z")

    shape = inputs.shape[1:]
    width = shape[-1]
    inputs, out_cotangent = inputs.reshape(-1, width), out_cotangent.reshape(-1, width)
    segments = segments[0]
    half = inputs.shape[0]
    rows = 2 * half
    channels = conv_in.shape[2]
    kernel = lax.dynamic_slice_in_dim(conv_kernel, core * channels, channels, 1).astype(F32)
    gains = lax.dynamic_index_in_dim(norm_gains, section, 0, keepdims=False).astype(F32)
    weight_out, weight_pair, weight_down = mixer_out[0], gate_up[0], down[0]
    hidden_units = weight_down.shape[0]
    part = hidden_units // plane
    in_width = 3 * channels
    qkv_width = attn_qkv.shape[1]
    y, z = lax.axis_index("y"), lax.axis_index("z")
    core_scalar = jnp.stack([core, section]).astype(jnp.int32)
    xl_scalar = jnp.stack([xl, section, y, z]).astype(jnp.int32)

    def chosen(from_first, from_second):
        return jnp.where(first, from_first, from_second)

    def gathered(own, axes):
        return lax.all_gather(own, axes, tiled=True)


    both = jnp.concatenate([conv_in.reshape(-1, in_width), attn_qkv], axis=1)
    whole = gathered(both, ("xh", "xl", "y", "z"))

    lanes = -(-part // 256) * 256
    fill = lanes - part
    part_pair = jnp.concatenate(
        [
            jnp.pad(lax.dynamic_slice_in_dim(w, place * part, part, 1), ((0, 0), (0, fill)))
            for w in (weight_pair[0], weight_pair[1])
        ],
        axis=1,
    )
    part_down = lax.dynamic_slice_in_dim(weight_down, place * part, part, 0)
    part_down = jnp.pad(part_down, ((0, fill), (0, 0)))
    masks = conv_masks(segments, kernel.shape[0])
    mask = score_mask(segments)
    tables = turn_tables(segments.shape[1])
    head_gains = gain_rows(qk_gains.astype(F32))
    first_in = inputs.astype(F32)
    normed_own_0 = (normalize(first_in) * gains[0]).astype(BF16)
    normed_0 = spread(normed_own_0)
    cotangent_1 = spread(out_cotangent)
    whole, part_pair, part_down, masks, mask, tables, head_gains, normed_0, cotangent_1 = (
        lax.optimization_barrier(
            (whole, part_pair, part_down, masks, mask, tables, head_gains, normed_0, cotangent_1)
        )
    )

    def inner_norm(hidden):
        return (normalize(hidden) * gains[1]).astype(BF16)

    def inner_back(mine, other, hidden, grad):
        return back_join_call(core_scalar, mine, swapped(other, "c"), hidden, grad, gains[1])

    def mixer_back(grad_hidden, mine, other, layer_in, behind):
        come = swapped(other, "c")
        return back_join_call(behind, mine, come, layer_in, grad_hidden, gains[0])[1:]

    plane_axes = ("y", "z", "c")
    early = gathered(chosen(normed_own_0, out_cotangent), plane_axes)

    projected, gated_0, mine, other = conv_forward_call(
        core_scalar, normed_0, kernel, masks, whole, weight_out
    )
    hidden_0 = first_in + joined(mine, other)
    inner_0 = inner_norm(hidden_0)
    gate, up, mine, other = feed_forward_call(
        False, core_scalar, spread(inner_0), weight_pair, weight_down
    )
    result_0 = (hidden_0 + joined(mine, other)).astype(BF16)

    second_in = lax.ppermute(result_0, "xh", [(0, 1)]).astype(F32)
    normed_own_1 = (normalize(second_in) * gains[0]).astype(BF16)
    qkv, ready, gated_1, mine, other = attention_forward_call(
        core_scalar, spread(normed_own_1), head_gains, tables, mask, whole, weight_out, qkv_width
    )
    hidden_1 = second_in + joined(mine, other)
    inner_1 = inner_norm(hidden_1)
    mine, other, grad_mine, grad_other = ffn_both_call(
        core_scalar, spread(inner_1), cotangent_1, weight_pair, weight_down, (early,)
    )
    result_1 = (hidden_1 + joined(mine, other)).astype(BF16)

    inner_all = gathered(chosen(inner_0, inner_1), plane_axes)
    gated = chosen(gated_0, gated_1)
    gated_z = [gated, *[lax.ppermute(gated, "z", around(by)) for by in range(1, 4)]]

    grad_hidden_1, grad_mix_1, gain_inner_1 = inner_back(
        grad_mine, grad_other, hidden_1, out_cotangent.astype(F32)
    )
    tiles_1, head_sums, mine, other = attention_backward_call(
        core_scalar,
        spread(grad_mix_1),
        head_gains,
        tables,
        mask,
        qkv,
        ready,
        whole,
        weight_out,
    )
    input_grad_1, gain_outer_1 = mixer_back(grad_hidden_1, mine, other, second_in, core_scalar)

    cotangent = lax.ppermute(input_grad_1, "xh", [(1, 0)])
    late = gathered(chosen(cotangent, normed_own_1), plane_axes)
    mine, other = feed_forward_call(
        True,
        core_scalar,
        spread(cotangent),
        weight_pair,
        weight_down,
        (gate, up),
        (inner_all,),
    )
    grad_hidden_0, grad_mix_0, gain_inner_0 = inner_back(
        mine, other, hidden_0, cotangent.astype(F32)
    )
    tiles, grad_kernel, mine, other = conv_backward_call(
        core_scalar,
        spread(grad_mix_0),
        kernel,
        masks,
        projected,
        tiles_1,
        whole,
        weight_out,
    )
    columns = exchanged(tiles, "z").reshape(4 * rows, -1)
    part_kept = part_forward_call((tiles, *gated_z[1:]), inner_all, part_pair)

    def summed_over_pair(mine, other):
        return mine.astype(F32) + swapped(other, "xl").astype(F32)

    pair_grads, down_mine, down_other = lax.cond(
        first,
        lambda: part_down_call(xl_scalar, late, part_kept, part_down, (columns,)),
        lambda: part_down_call(xl_scalar, early, part_kept, part_down, (columns,)),
    )
    input_grad_0, gain_outer_0 = mixer_back(grad_hidden_0, mine, other, first_in, pair_grads)
    in_parts, out_mine, out_other = mixer_grads_call(
        xl_scalar, pair_grads, columns, gated_z, early, late, plane
    )
    pair_mine, pair_other = part_pair_call(xl_scalar, inner_all, pair_grads, (in_parts,))

    full_kernel = lax.dynamic_update_slice(
        jnp.zeros(conv_kernel.shape, F32), grad_kernel, (0, core * channels)
    )
    small = jnp.concatenate(
        [
            chosen(gain_outer_0, gain_outer_1),
            chosen(gain_inner_0, gain_inner_1),
            full_kernel.reshape(-1),
            head_gain_sums(head_sums).reshape(-1),
        ]
    )
    count = small.shape[0]
    small = jnp.pad(small, (0, -count % 1024)).reshape(-1, 128)
    small_all = lax.all_gather(small, AXES)

    come = exchanged(in_parts, PLANE)
    line_mine, line_other = line_sums_call(xl_scalar, come)
    line_come = swapped(line_other, "xl")

    pairs = [(a, swapped(b, "xl")) for a, b in ((pair_mine, pair_other), (down_mine, down_other))]
    total = pair_join_call((line_mine,), pairs)
    arrived = exchanged(total.reshape(plane, -1, 3 * lanes), PLANE)

    kept_lines, sent_lines, sums = finish_call(xl_scalar, total, line_mine, line_come, small_all)
    across = swapped(sent_lines, "xh")
    come = across.astype(F32)[:, :, : in_width // 4]
    kept_lines = kept_lines[:, :, : in_width // 4]
    lines = chosen(kept_lines, come).reshape(4, -1, 3, channels // 4)
    grad_conv_in = jnp.moveaxis(lines, 0, 2).reshape(conv_in.shape)
    lines = chosen(come, kept_lines)[:, :, : qkv_width // 4]
    grad_attn_qkv = jnp.moveaxis(lines, 0, 1).reshape(attn_qkv.shape)

    arrived = widened_call(across, arrived)
    lines = [
        jnp.moveaxis(arrived[:, :, k * lanes : k * lanes + part], 0, 1).reshape(-1, hidden_units)
        for k in range(3)
    ]
    grad_gate_up = jnp.stack(lines[:2])[None]
    grad_down = lines[2].T[None]

    total = summed_over_pair(out_mine, out_other).reshape(4, -1, channels)
    sent = total.astype(BF16)
    lines = lax.dynamic_index_in_dim(total, y, 0, keepdims=False)
    for by in range(1, 4):
        block = lax.dynamic_index_in_dim(sent, (y + by) % 4, 0, keepdims=False)
        lines += lax.ppermute(block, "y", around(by)).astype(F32)
    grad_mixer_out = lines.T[None]

    pair = [sums[0].reshape(-1), sums[1].reshape(-1)]
    grad_norm_gains = jnp.stack([a[: 2 * width].reshape(2, width) for a in pair])
    grad_conv_kernel = pair[0][2 * width : 5 * width].reshape(conv_kernel.shape)
    grad_qk_gains = pair[1][5 * width : count].reshape(qk_gains.shape)

    activations = chosen(result_0, result_1).reshape(1, 1, *shape)
    input_grads = chosen(input_grad_0, input_grad_1).reshape(1, 1, *shape)
    return (
        activations,
        input_grads,
        grad_norm_gains,
        grad_conv_kernel,
        grad_qk_gains,
        grad_conv_in,
        grad_attn_qkv,
        grad_mixer_out,
        grad_gate_up,
        grad_down,
    )


def solution(mesh):
    wide = Mesh(mesh.devices.reshape(2, 2, 4, 4, 2), AXES)
    dp = ("xl", "y", "z")
    everyone = ("xh", "xl", "y", "z")
    in_specs = (
        P(dp, None, "c", None),
        P(dp, None, "c", None),
        P(dp, None, None),
        P(),
        P(),
        P(),
        P(everyone, None, "c"),
        P(everyone, "c"),
        P("xh", "c", None),
        P("xh", None, None, "c"),
        P("xh", "c", None),
    )
    out_specs = (
        P("xh", dp, None, "c", None),
        P("xh", dp, None, "c", None),
        P(),
        P(),
        P(),
        P(everyone, None, "c"),
        P(everyone, "c"),
        P("xh", "c", dp),
        P("xh", None, dp, "c"),
        P("xh", "c", dp),
    )
    return jax.shard_map(local, mesh=wide, in_specs=in_specs, out_specs=out_specs, check_vma=False)
```

```python
import functools

import jax
import jax.numpy as jnp
from jax import lax
from jax.experimental import pallas as pl
from jax.experimental.pallas import tpu as pltpu
from jax.sharding import Mesh
from jax.sharding import PartitionSpec as P

HEADS = 24
KV_HEADS = 8
HEAD_DIM = 64
GROUP = HEADS // KV_HEADS

EPSILON = 1e-05
ROPE_BASE = 1000000.0
MASKED_SCORE = -1e30

F32 = jnp.float32
BF16 = jnp.bfloat16

PLANE = ("y", "z")
AXES = ("xh", "xl", "y", "z", "c")


def product(left, right):
    return jnp.dot(left, right, preferred_element_type=F32)


def product_left(left, right):
    return lax.dot_general(left, right, (((0,), (0,)), ((), ())), preferred_element_type=F32)


def product_right(left, right):
    return lax.dot_general(left, right, (((1,), (1,)), ((), ())), preferred_element_type=F32)


def swapped(shard, axis):
    return lax.ppermute(shard, axis, [(0, 1), (1, 0)])


def spread(own):
    return lax.all_gather(own, "c", tiled=True)


def joined(mine, other):
    return mine + swapped(other, "c").astype(F32)


def mean_last(values):
    return jnp.mean(values, axis=-1, keepdims=True)


def inverse_rms(values):
    return lax.rsqrt(mean_last(values * values) + EPSILON)


def normalize(values):
    return values * inverse_rms(values)


def around(by):
    return [(k, (k + by) % 4) for k in range(4)]


def exchanged(tiles, axes):
    return lax.all_to_all(tiles, axes, 0, 0, tiled=True)


def ffn_grads(grad_active, gate, up):
    sigmoid = jax.nn.sigmoid(gate)
    grad_gate = grad_active * up * sigmoid * (1.0 + gate * (1.0 - sigmoid))
    grad_up = grad_active * gate * sigmoid
    return grad_gate.astype(BF16), grad_up.astype(BF16)


VMEM_LIMIT = 56 * 1024 * 1024
SHORT = pl.CostEstimate(flops=1, bytes_accessed=1, transcendentals=0)


def whole_lanes(columns):
    return -(-columns // 128) * 128


def ordered(kernel, count):
    def body(scalar_ref, *refs):
        kernel(scalar_ref, *refs[count:])

    return body


def unit_tiles(units, tile):
    short = units % tile
    tiles = [(0, short)] if short else []
    return tiles + [(at, tile) for at in range(short, units, tile)]


def streamed(tiles, copies, work):
    for copy in copies(0, 0):
        copy.start()
    for k in range(len(tiles)):
        slot = k % 2
        if k + 1 < len(tiles):
            for copy in copies(k + 1, 1 - slot):
                copy.start()
        for copy in copies(k, slot):
            copy.wait()
        work(k, slot)


def ffn_forward_kernel(
    tiles, core_ref, rows_ref, pair_ref, down_ref, gate_ref, up_ref, mine_ref, other_ref,
    pair_buf, down_buf, gate_buf, up_buf, acc_ref, sems, out_sems,
):
    def copies(k, slot):
        at, size = tiles[k]
        return [
            pltpu.make_async_copy(
                pair_ref.at[0, :, pl.ds(at, size)],
                pair_buf.at[slot, :, pl.ds(0, size)],
                sems.at[slot, 0],
            ),
            pltpu.make_async_copy(
                pair_ref.at[1, :, pl.ds(at, size)],
                pair_buf.at[slot, :, pl.ds(size, size)],
                sems.at[slot, 1],
            ),
            pltpu.make_async_copy(
                down_ref.at[pl.ds(at, size)], down_buf.at[slot, pl.ds(0, size)], sems.at[slot, 2]
            ),
        ]

    def kept(k):
        here = (slice(None), pl.ds(*tiles[k]))
        return [
            pltpu.make_async_copy(gate_buf.at[here], gate_ref.at[here], out_sems.at[k, 0]),
            pltpu.make_async_copy(up_buf.at[here], up_ref.at[here], out_sems.at[k, 1]),
        ]

    def work(k, slot):
        at, size = tiles[k]
        both = product(rows_ref[...], pair_buf[slot, :, : 2 * size])
        gate, up = both[:, :size], both[:, size:]
        gate_buf[:, at : at + size] = gate.astype(BF16)
        up_buf[:, at : at + size] = up.astype(BF16)
        for copy in kept(k):
            copy.start()
        active = (gate * jax.nn.sigmoid(gate) * up).astype(BF16)
        part = product(active, down_buf[slot, :size])
        if k == 0:
            acc_ref[...] = part
        else:
            acc_ref[...] += part

    streamed(tiles, copies, work)
    rows_out(acc_ref, core_ref[0], mine_ref, other_ref)
    for k in range(len(tiles)):
        for copy in kept(k):
            copy.wait()


def ffn_backward_kernel(
    tiles, core_ref, rows_ref, gate_ref, up_ref, pair_ref, down_ref, mine_ref, other_ref,
    pair_buf, down_buf, gate_buf, up_buf, acc_ref, sems,
):
    def copies(k, slot):
        at, size = tiles[k]
        columns, place = pl.ds(at, size), pl.ds(0, size)
        return [
            pltpu.make_async_copy(
                down_ref.at[columns], down_buf.at[slot, place], sems.at[slot, 0]
            ),
            pltpu.make_async_copy(
                gate_ref.at[:, columns], gate_buf.at[slot, :, place], sems.at[slot, 1]
            ),
            pltpu.make_async_copy(
                up_ref.at[:, columns], up_buf.at[slot, :, place], sems.at[slot, 2]
            ),
            pltpu.make_async_copy(
                pair_ref.at[0, :, columns], pair_buf.at[slot, :, place], sems.at[slot, 3]
            ),
            pltpu.make_async_copy(
                pair_ref.at[1, :, columns],
                pair_buf.at[slot, :, pl.ds(size, size)],
                sems.at[slot, 4],
            ),
        ]

    def work(k, slot):
        _, size = tiles[k]
        grad_active = product_right(rows_ref[...], down_buf[slot, :size])
        grads = ffn_grads(
            grad_active,
            gate_buf[slot, :, :size].astype(F32),
            up_buf[slot, :, :size].astype(F32),
        )
        part = product_right(jnp.concatenate(grads, axis=1), pair_buf[slot, :, : 2 * size])
        if k == 0:
            acc_ref[...] = part
        else:
            acc_ref[...] += part

    streamed(tiles, copies, work)
    rows_out(acc_ref, core_ref[0], mine_ref, other_ref)


def ffn_both_kernel(
    tiles, core_ref, rows_ref, grad_ref, pair_ref, down_ref,
    mine_ref, other_ref, grad_mine_ref, grad_other_ref, pair_buf, down_buf, acc_ref, grad_acc_ref, sems,
):
    def copies(k, slot):
        at, size = tiles[k]
        columns, place = pl.ds(at, size), pl.ds(0, size)
        return [
            pltpu.make_async_copy(
                pair_ref.at[0, :, columns], pair_buf.at[slot, :, place], sems.at[slot, 0]
            ),
            pltpu.make_async_copy(
                pair_ref.at[1, :, columns],
                pair_buf.at[slot, :, pl.ds(size, size)],
                sems.at[slot, 1],
            ),
            pltpu.make_async_copy(
                down_ref.at[columns], down_buf.at[slot, place], sems.at[slot, 2]
            ),
        ]

    def work(k, slot):
        _, size = tiles[k]
        both = product(rows_ref[...], pair_buf[slot, :, : 2 * size])
        grad_active = product_right(grad_ref[...], down_buf[slot, :size])
        gate, up = both[:, :size], both[:, size:]
        active = (gate * jax.nn.sigmoid(gate) * up).astype(BF16)
        grads = jnp.concatenate(ffn_grads(grad_active, gate, up), axis=1)
        part = product(active, down_buf[slot, :size])
        grad_part = product_right(grads, pair_buf[slot, :, : 2 * size])
        if k == 0:
            acc_ref[...], grad_acc_ref[...] = part, grad_part
        else:
            acc_ref[...] += part
            grad_acc_ref[...] += grad_part

    streamed(tiles, copies, work)
    rows_out(acc_ref, core_ref[0], mine_ref, other_ref)
    rows_out(grad_acc_ref, core_ref[0], grad_mine_ref, grad_other_ref)


def ffn_both_call(core, rows, grad, pair, down, behind):
    count, width = rows.shape
    units = down.shape[0]
    tile = 768
    vmem, any_space = pl.BlockSpec(memory_space=pltpu.VMEM), pl.BlockSpec(memory_space=pl.ANY)
    half = (count // 2, width)
    return pl.pallas_call(
        ordered(functools.partial(ffn_both_kernel, unit_tiles(units, tile)), len(behind)),
        in_specs=[
            pl.BlockSpec(memory_space=pltpu.SMEM),
            *[any_space] * len(behind),
            vmem,
            vmem,
            any_space,
            any_space,
        ],
        out_specs=[vmem] * 4,
        out_shape=[jax.ShapeDtypeStruct(half, F32), jax.ShapeDtypeStruct(half, BF16)] * 2,
        scratch_shapes=[
            pltpu.VMEM((2, width, 2 * tile), BF16),
            pltpu.VMEM((2, tile, width), BF16),
            pltpu.VMEM((count, width), F32),
            pltpu.VMEM((count, width), F32),
            pltpu.SemaphoreType.DMA((2, 3)),
        ],
        compiler_params=pltpu.CompilerParams(vmem_limit_bytes=VMEM_LIMIT),
        cost_estimate=SHORT,
    )(core, *behind, rows, grad, pair, down)


def feed_forward_call(backward, core, rows, pair, down, saved=(), behind=()):
    count, width = rows.shape
    units = down.shape[0]
    tile = 768
    tiles = unit_tiles(units, tile)
    vmem, any_space = pl.BlockSpec(memory_space=pltpu.VMEM), pl.BlockSpec(memory_space=pl.ANY)
    scalar = pl.BlockSpec(memory_space=pltpu.SMEM)
    out_shape = [
        jax.ShapeDtypeStruct((count // 2, width), F32),
        jax.ShapeDtypeStruct((count // 2, width), BF16),
    ]
    out_specs = [vmem, vmem]
    buffers = [pltpu.VMEM((2, width, 2 * tile), BF16), pltpu.VMEM((2, tile, width), BF16)]
    acc = pltpu.VMEM((count, width), F32)
    if backward:
        body = functools.partial(ffn_backward_kernel, tiles)
        in_specs = [scalar, vmem, any_space, any_space, any_space, any_space]
        buffers += [pltpu.VMEM((2, count, tile), BF16)] * 2
        scratch = [*buffers, acc, pltpu.SemaphoreType.DMA((2, 5))]
    else:
        body = functools.partial(ffn_forward_kernel, tiles)
        in_specs = [scalar, vmem, any_space, any_space]
        out_shape = [jax.ShapeDtypeStruct((count, units), BF16)] * 2 + out_shape
        out_specs = [any_space, any_space, *out_specs]
        buffers += [pltpu.VMEM((count, units), BF16)] * 2
        scratch = [*buffers, acc]
        scratch += [pltpu.SemaphoreType.DMA((2, 3)), pltpu.SemaphoreType.DMA((len(tiles), 2))]
    in_specs = [scalar, *[any_space] * len(behind), *in_specs[1:]]
    return pl.pallas_call(
        ordered(body, len(behind)),
        in_specs=in_specs,
        out_specs=out_specs,
        out_shape=out_shape,
        scratch_shapes=scratch,
        compiler_params=pltpu.CompilerParams(vmem_limit_bytes=VMEM_LIMIT),
        cost_estimate=SHORT,
    )(core, *behind, rows, *saved, pair, down)


def part_forward_kernel(behind_ref, rows_ref, pair_ref, kept_ref):
    both = product(rows_ref[...], pair_ref[...])
    units = both.shape[1] // 2
    gate, up = both[:, :units], both[:, units:]
    sigmoid = jax.nn.sigmoid(gate)
    silu = gate * sigmoid
    kept_ref[:, :units] = (up * (sigmoid + silu * (1.0 - sigmoid))).astype(BF16)
    kept_ref[:, units : 2 * units] = silu.astype(BF16)
    kept_ref[:, 2 * units :] = (silu * up).astype(BF16)


def part_forward_call(behind, rows, pair):
    tokens, width = rows.shape
    units = pair.shape[1] // 2
    tile = 1024
    return pl.pallas_call(
        part_forward_kernel,
        grid=(tokens // tile,),
        in_specs=[
            pl.BlockSpec(memory_space=pl.ANY),
            pl.BlockSpec((tile, width), lambda i: (i, 0)),
            pl.BlockSpec((width, 2 * units), lambda i: (0, 0)),
        ],
        out_specs=pl.BlockSpec((tile, 3 * units), lambda i: (i, 0)),
        out_shape=jax.ShapeDtypeStruct((tokens, 3 * units), BF16),
        compiler_params=pltpu.CompilerParams(vmem_limit_bytes=VMEM_LIMIT),
        cost_estimate=pl.CostEstimate(
            flops=8 * tokens * width * units, bytes_accessed=2 * tokens * width, transcendentals=0
        ),
    )(behind, rows, pair)


def pair_out(acc_ref, here, mine_ref, other_ref):
    rows = mine_ref.shape[0]
    for ref, half in ((mine_ref, here), (other_ref, 1 - here)):
        ref[...] = acc_ref[pl.ds(pl.multiple_of(half * rows, rows), rows)].astype(BF16)


def accumulated(acc_ref, part, finish):
    step = pl.program_id(0)

    @pl.when(step == 0)
    def _():
        acc_ref[...] = part

    @pl.when(step > 0)
    def _():
        acc_ref[...] += part

    pl.when(step == pl.num_programs(0) - 1)(finish)


def part_down_kernel(here_ref, grad_ref, kept_ref, down_ref, pair_ref, mine_ref, other_ref, acc_ref):
    grad = grad_ref[...]
    units = down_ref.shape[0]
    grad_active = product_right(grad, down_ref[...])
    for k in range(2):
        lanes = slice(k * units, (k + 1) * units)
        pair_ref[:, lanes] = (grad_active * kept_ref[:, lanes].astype(F32)).astype(BF16)
    accumulated(
        acc_ref,
        product_left(grad, kept_ref[:, 2 * units :]),
        lambda: pair_out(acc_ref, here_ref[0], mine_ref, other_ref),
    )


def part_pair_kernel(here_ref, rows_ref, pair_ref, mine_ref, other_ref, acc_ref):
    accumulated(
        acc_ref,
        product_left(rows_ref[...], pair_ref[...]),
        lambda: pair_out(acc_ref, here_ref[0], mine_ref, other_ref),
    )


def part_call(kernel, here, operands, fixed, outs, result, flops, behind=()):
    tokens = operands[0].shape[0]
    tile = 1024
    by_tokens = lambda width: pl.BlockSpec((tile, width), lambda i, h: (i, 0))
    entire = lambda shape: pl.BlockSpec(shape, lambda i, h: (0, 0))
    half = (result[0] // 2, result[1])
    return pl.pallas_call(
        ordered(kernel, len(behind)),
        grid_spec=pltpu.PrefetchScalarGridSpec(
            num_scalar_prefetch=1,
            grid=(tokens // tile,),
            in_specs=[pl.BlockSpec(memory_space=pl.ANY)] * len(behind)
            + [by_tokens(a.shape[1]) for a in operands]
            + [entire(a.shape) for a in fixed],
            out_specs=[by_tokens(width) for width in outs] + [entire(half)] * 2,
            scratch_shapes=[pltpu.VMEM(result, F32)],
        ),
        out_shape=[jax.ShapeDtypeStruct((tokens, width), BF16) for width in outs]
        + [jax.ShapeDtypeStruct(half, BF16)] * 2,
        compiler_params=pltpu.CompilerParams(vmem_limit_bytes=VMEM_LIMIT),
        cost_estimate=SHORT,
    )(here, *behind, *operands, *fixed)


def part_down_call(here, grad, kept, down, behind):
    tokens, width = grad.shape
    units = down.shape[0]
    flops = 4 * tokens * width * units
    return part_call(
        part_down_kernel,
        here,
        (grad, kept),
        (down,),
        (2 * units,),
        (width, units),
        flops,
        behind,
    )


def part_pair_call(here, inner, pair, behind):
    (tokens, width), columns = inner.shape, pair.shape[1]
    flops = 2 * tokens * width * columns
    return part_call(
        part_pair_kernel, here, (inner, pair), (), (), (width, columns), flops, behind
    )


def back_join_kernel(
    behind_ref, mine_ref, come_ref, values_ref, base_ref, gain_ref, wide_ref, low_ref, sums_ref
):
    grad = mine_ref[...] + come_ref[...].astype(F32)
    values = values_ref[...]
    inverse = inverse_rms(values)
    normed = values * inverse
    scaled = grad * gain_ref[...]
    sums_ref[...] = jnp.sum(grad * normed, axis=0, keepdims=True)
    total = base_ref[...] + inverse * (scaled - normed * mean_last(scaled * normed))
    wide_ref[...] = total
    low_ref[...] = total.astype(BF16)


def back_join_call(behind, mine, come, values, base, gain):
    vmem = pl.BlockSpec(memory_space=pltpu.VMEM)
    shape = values.shape
    wide, low, sums = pl.pallas_call(
        back_join_kernel,
        in_specs=[pl.BlockSpec(memory_space=pl.ANY), *[vmem] * 5],
        out_specs=[vmem] * 3,
        out_shape=[
            jax.ShapeDtypeStruct(shape, F32),
            jax.ShapeDtypeStruct(shape, BF16),
            jax.ShapeDtypeStruct((1, shape[1]), F32),
        ],
        compiler_params=pltpu.CompilerParams(vmem_limit_bytes=VMEM_LIMIT),
        cost_estimate=SHORT,
    )(behind, mine, come, values, base, gain[None])
    return wide, low, sums[0]


def pair_join_kernel(count, *refs):
    *refs, out_ref = refs[count:]
    at = 0
    for mine_ref, come_ref in zip(refs[::2], refs[1::2]):
        size = mine_ref.shape[-1]
        total = mine_ref[...].astype(F32) + come_ref[...].astype(F32)
        out_ref[..., at : at + size] = total.astype(BF16)
        at += size


def pair_join_call(behind, pairs):
    vmem = pl.BlockSpec(memory_space=pltpu.VMEM)
    operands = [a for pair in pairs for a in pair]
    shape = (*operands[0].shape[:-1], sum(mine.shape[-1] for mine, _ in pairs))
    return pl.pallas_call(
        functools.partial(pair_join_kernel, len(behind)),
        in_specs=[pl.BlockSpec(memory_space=pl.ANY)] * len(behind) + [vmem] * len(operands),
        out_specs=vmem,
        out_shape=jax.ShapeDtypeStruct(shape, BF16),
        compiler_params=pltpu.CompilerParams(vmem_limit_bytes=VMEM_LIMIT),
        cost_estimate=SHORT,
    )(*behind, *operands)


def widened_kernel(behind_ref, low_ref, wide_ref):
    wide_ref[...] = low_ref[...].astype(F32)


def widened_call(behind, low):
    vmem = pl.BlockSpec(memory_space=pltpu.VMEM)
    return pl.pallas_call(
        widened_kernel,
        in_specs=[pl.BlockSpec(memory_space=pl.ANY), vmem],
        out_specs=vmem,
        out_shape=jax.ShapeDtypeStruct(low.shape, F32),
        compiler_params=pltpu.CompilerParams(vmem_limit_bytes=VMEM_LIMIT),
        cost_estimate=SHORT,
    )(behind, low)


def finish_kernel(
    places_ref, behind_ref, come_ref, small_ref, kept_ref, sent_ref, sums_ref, acc_ref
):
    section = places_ref[1]
    count, short, _ = kept_ref.shape
    for k in range(count):
        tiles = [come_ref[m * count + k].astype(F32) for m in range(come_ref.shape[0] // count)]
        acc_ref[...] = functools.reduce(jnp.add, tiles)
        kept_ref[k] = acc_ref[pl.ds(pl.multiple_of(section * short, short), short)]
        sent = acc_ref[pl.ds(pl.multiple_of((1 - section) * short, short), short)]
        sent_ref[k] = sent.astype(BF16)
    half = small_ref.shape[0] // 2
    for k in range(2):
        sums_ref[k] = jnp.sum(small_ref[k * half : (k + 1) * half], axis=0)


def finish_call(places, behind, come, small):
    vmem = pl.BlockSpec(memory_space=pltpu.VMEM)
    plane, block, size = come.shape
    lines = (4, block // 2, size)
    return pl.pallas_call(
        finish_kernel,
        in_specs=[
            pl.BlockSpec(memory_space=pltpu.SMEM),
            pl.BlockSpec(memory_space=pl.ANY),
            vmem,
            vmem,
        ],
        out_specs=[vmem] * 3,
        out_shape=[
            jax.ShapeDtypeStruct(lines, F32),
            jax.ShapeDtypeStruct(lines, BF16),
            jax.ShapeDtypeStruct((2, *small.shape[1:]), F32),
        ],
        scratch_shapes=[pltpu.VMEM((block, size), F32)],
        compiler_params=pltpu.CompilerParams(vmem_limit_bytes=VMEM_LIMIT),
        cost_estimate=SHORT,
    )(places, behind, come, small)


def mixer_grads_kernel(
    places_ref, behind_ref, columns_ref, gated_ref, early_ref, late_ref,
    in_mine_ref, in_other_ref, out_mine_ref, out_other_ref, normed_ref, in_ref, out_ref, sem,
):
    here, section, y = places_ref[0], places_ref[1], places_ref[2]

    def copy(all_ref):
        rows = normed_ref.shape[0]
        start = pl.multiple_of(y * rows, rows)
        return pltpu.make_async_copy(all_ref.at[pl.ds(start, rows)], normed_ref, sem)

    @pl.when(section == 0)
    def _():
        copy(early_ref).start()

    @pl.when(section > 0)
    def _():
        copy(late_ref).start()

    mix = out_ref.shape[0]
    out_ref[...] = product_left(columns_ref[:, :mix], gated_ref[...])
    pair_out(out_ref, here, out_mine_ref, out_other_ref)
    copy(early_ref).wait()
    in_ref[...] = product_left(normed_ref[...], columns_ref[:, mix:])
    plane, block, _ = in_mine_ref.shape
    short = block // 2
    for ref, half in ((in_mine_ref, here), (in_other_ref, 1 - here)):
        for k in range(plane):
            for s in range(2):
                start = pl.multiple_of(((2 * s + half) * plane + k) * short, short)
                rows_in = in_ref[pl.ds(start, short)]
                ref[k, s * short : (s + 1) * short] = rows_in.astype(BF16)


def mixer_grads_call(places, behind, columns, gated, early, late, plane):
    vmem, any_space = pl.BlockSpec(memory_space=pltpu.VMEM), pl.BlockSpec(memory_space=pl.ANY)
    tokens, channels = gated.shape
    width = early.shape[1]
    mix = width // 4
    size = columns.shape[1] - mix
    in_half = jax.ShapeDtypeStruct((plane, width // (2 * plane), size), BF16)
    out_half = jax.ShapeDtypeStruct((mix // 2, channels), BF16)
    return pl.pallas_call(
        mixer_grads_kernel,
        in_specs=[
            pl.BlockSpec(memory_space=pltpu.SMEM),
            any_space,
            vmem,
            vmem,
            any_space,
            any_space,
        ],
        out_specs=[vmem] * 4,
        out_shape=[in_half, in_half, out_half, out_half],
        scratch_shapes=[
            pltpu.VMEM((tokens, width), BF16),
            pltpu.VMEM((width, size), F32),
            pltpu.VMEM((mix, channels), F32),
            pltpu.SemaphoreType.DMA,
        ],
        compiler_params=pltpu.CompilerParams(vmem_limit_bytes=VMEM_LIMIT),
        cost_estimate=SHORT,
    )(places, behind, columns, gated, early, late)


def load_all(copies):
    for copy in copies:
        copy.start()


def in_time(rows):
    half = rows.shape[0] // 4
    return jnp.concatenate([rows[k * half : (k + 1) * half] for k in (0, 2, 1, 3)], axis=0)


def rows_out(acc_ref, core, mine_ref, other_ref):
    half = mine_ref.shape[0]
    mine_ref[...] = acc_ref[pl.ds(pl.multiple_of(core * half, half), half)]
    rest = acc_ref[pl.ds(pl.multiple_of((1 - core) * half, half), half)]
    other_ref[...] = rest.astype(BF16)


def weight_copies(whole_ref, out_ref, in_buf, out_buf, sems, start):
    size = in_buf.shape[2]
    copies = [
        pltpu.make_async_copy(
            whole_ref.at[:, pl.ds(start + k * size, size)], in_buf.at[k], sems.at[k]
        )
        for k in range(in_buf.shape[0])
    ]
    return copies, pltpu.make_async_copy(out_ref, out_buf, sems.at[len(copies)])


def conv_taps(mixed, kernel, masks):
    terms = [mixed]
    for lag in range(1, len(masks) + 1):
        terms.append(pltpu.roll(mixed, lag, 0) * masks[lag - 1])
    taps = kernel.shape[0]
    total = kernel[taps - 1 : taps] * terms[0]
    for lag in range(1, taps):
        total = total + kernel[taps - 1 - lag : taps - lag] * terms[lag]
    return terms, total


def conv_forward_kernel(
    core_ref, rows_ref, kernel_ref, masks_ref, whole_ref, out_ref,
    proj_ref, gated_ref, mine_ref, other_ref, in_buf, out_buf, acc_ref, sems,
):
    copies, last = weight_copies(whole_ref, out_ref, in_buf, out_buf, sems, 0)
    load_all([*copies, last])
    rows = rows_ref[...]
    parts = []
    for k, copy in enumerate(copies):
        copy.wait()
        part = product(rows, in_buf[k])
        proj_ref[k] = part.astype(BF16)
        parts.append(in_time(part))
    masks = [masks_ref[lag] for lag in range(masks_ref.shape[0])]
    gated = []
    for at in range(0, parts[0].shape[1], 128):
        before, after, signal = [part[:, at : at + 128] for part in parts]
        _, total = conv_taps(before * signal, kernel_ref[:, at : at + 128], masks)
        gated.append((after * total).astype(BF16))
    gated = in_time(jnp.concatenate(gated, axis=1))
    gated_ref[...] = gated
    last.wait()
    acc_ref[...] = product(gated, out_buf[...])
    rows_out(acc_ref, core_ref[0], mine_ref, other_ref)


def tiles_out(tiles_ref, grad_ref, columns):
    count, rows, size = tiles_ref.shape
    step = grad_ref.shape[1] // (2 * count * count)
    for k in range(count):
        starts = range(k * step, grad_ref.shape[1], count * step)
        parts = [grad_ref[:, at : at + step] for at in starts]
        parts.append(columns(k))
        spare = size - sum(part.shape[1] for part in parts)
        tiles_ref[k] = jnp.concatenate([*parts, jnp.zeros((rows, spare), BF16)], axis=1)


def conv_backward_kernel(
    core_ref, grad_ref, kernel_ref, masks_ref, proj_ref, other_tiles_ref,
    whole_ref, out_ref, tiles_ref, taps_ref, mine_ref, other_ref, in_buf, out_buf, acc_ref, sems,
):
    copies, last = weight_copies(whole_ref, out_ref, in_buf, out_buf, sems, 0)
    load_all([last, *copies])
    last.wait()
    grad_gated = in_time(product_right(grad_ref[...], out_buf[...]))
    parts = [in_time(proj_ref[k].astype(F32)) for k in range(3)]
    masks = [masks_ref[lag] for lag in range(masks_ref.shape[0])]
    rows = grad_gated.shape[0]
    grads = [[], [], []]
    for at in range(0, grad_gated.shape[1], 128):
        before, after, signal = [part[:, at : at + 128] for part in parts]
        kernel = kernel_ref[:, at : at + 128]
        terms, total = conv_taps(before * signal, kernel, masks)
        grad = grad_gated[:, at : at + 128]
        grad_total = grad * after
        taps = kernel.shape[0]
        grad_mixed = kernel[taps - 1 : taps] * grad_total
        for lag in range(1, taps):
            sent = pltpu.roll(grad_total * masks[lag - 1], rows - lag, 0)
            grad_mixed = grad_mixed + kernel[taps - 1 - lag : taps - lag] * sent
        for lag in range(taps):
            taps_ref[taps - 1 - lag : taps - lag, at : at + 128] = jnp.sum(
                grad_total * terms[lag], axis=0, keepdims=True
            )
        for k, value in enumerate((grad_mixed * signal, grad * total, grad_mixed * before)):
            grads[k].append(value.astype(BF16))
    grads = [in_time(jnp.concatenate(g, axis=1)) for g in grads]
    step = grads[0].shape[1] // tiles_ref.shape[0]

    @pl.when(core_ref[1] == 0)
    def _():
        tiles_out(
            tiles_ref,
            grad_ref,
            lambda k: jnp.concatenate([g[:, k * step : (k + 1) * step] for g in grads], axis=1),
        )

    @pl.when(core_ref[1] > 0)
    def _():
        tiles_ref[...] = other_tiles_ref[...]

    for k, copy in enumerate(copies):
        copy.wait()
        part = product_right(grads[k], in_buf[k])
        acc_ref[...] = part if k == 0 else acc_ref[...] + part
    rows_out(acc_ref, core_ref[0], mine_ref, other_ref)


def head_kind(head):
    return min(max(head % (GROUP + 2) - GROUP + 1, 0), 2)


def lane_facts(rows):
    lane = lax.broadcasted_iota(jnp.int32, (rows, 128), 1)
    return lane < HEAD_DIM, lax.rem(lane, HEAD_DIM) < HEAD_DIM // 2


def head_scales(block, low):
    squares = block * block
    first = jnp.sum(jnp.where(low, squares, 0.0), axis=1, keepdims=True)
    second = jnp.sum(jnp.where(low, 0.0, squares), axis=1, keepdims=True)
    return lax.rsqrt(jnp.where(low, first, second) * (1.0 / HEAD_DIM) + EPSILON)


def block_gains(gains_ref, at):
    heads = [head_kind(2 * at), head_kind(2 * at + 1)]
    return heads, gains_ref[3 * heads[0] + heads[1] : 3 * heads[0] + heads[1] + 1]


def attention_forward_kernel(
    core_ref, rows_ref, gains_ref, tables_ref, mask_ref, whole_ref, out_ref,
    qkv_ref, ready_ref, gated_ref, mine_ref, other_ref, in_buf, out_buf, acc_ref, sems,
):
    copies, last = weight_copies(
        whole_ref, out_ref, in_buf, out_buf, sems, whole_ref.shape[1] - in_buf.shape[2]
    )
    load_all([*copies, last])
    copies[0].wait()
    qkv_ref[...] = product(rows_ref[...], in_buf[0])
    rows, width = qkv_ref.shape
    low, front = lane_facts(rows)
    cosine, sine = tables_ref[0], tables_ref[1]
    for at in range(width // 128):
        block = qkv_ref[:, at * 128 : (at + 1) * 128]
        heads, gains = block_gains(gains_ref, at)
        normed = block * head_scales(block, low) * gains
        turned = jnp.where(front, -pltpu.roll(normed, 96, 1), pltpu.roll(normed, 32, 1))
        ready = normed * cosine + turned * sine
        if heads[0] == 2:
            ready = jnp.where(low, block, ready)
        if heads[1] == 2:
            ready = jnp.where(low, ready, block)
        ready_ref[:, at * 128 : (at + 1) * 128] = ready.astype(BF16)
    half = rows // 4
    span = (GROUP + 2) * HEAD_DIM
    for m in range(2):
        mask = mask_ref[m] > 0
        mask = jnp.concatenate([mask] * GROUP, axis=0)
        for g in range(width // span):
            queries, keys, values = head_rows(ready_ref, m, half, g * span)
            weights = softmax_weights(queries, keys, mask)
            attended = product(weights.astype(BF16), values).astype(BF16)
            for j in range(GROUP):
                at = (g * GROUP + j) * HEAD_DIM
                head = attended[j * 2 * half : (j + 1) * 2 * half]
                gated_ref[m * half : (m + 1) * half, at : at + HEAD_DIM] = head[:half]
                gated_ref[(m + 2) * half : (m + 3) * half, at : at + HEAD_DIM] = head[half:]
    last.wait()
    acc_ref[...] = product(gated_ref[...], out_buf[...])
    rows_out(acc_ref, core_ref[0], mine_ref, other_ref)


def sequence(ref, m, half, at):
    columns = slice(at, at + HEAD_DIM)
    return jnp.concatenate(
        [ref[m * half : (m + 1) * half, columns], ref[(m + 2) * half : (m + 3) * half, columns]],
        axis=0,
    )


def head_rows(ref, m, half, at):
    heads = [sequence(ref, m, half, at + j * HEAD_DIM) for j in range(GROUP + 2)]
    return jnp.concatenate(heads[:GROUP], axis=0), heads[GROUP], heads[GROUP + 1]


def softmax_weights(queries, keys, mask):
    scores = jnp.where(mask, product_right(queries, keys) * HEAD_DIM ** (-0.5), MASKED_SCORE)
    terms = jnp.exp(scores - jnp.max(scores, axis=1, keepdims=True))
    return terms / jnp.sum(terms, axis=1, keepdims=True)


def attention_backward_kernel(
    core_ref, grad_ref, gains_ref, tables_ref, mask_ref, qkv_ref, ready_ref,
    whole_ref, out_ref, tiles_ref, heads_ref, mine_ref, other_ref,
    in_buf, out_buf, acc_ref, attended_ref, ready_grad_ref, proj_ref, sems,
):
    copies, last = weight_copies(
        whole_ref, out_ref, in_buf, out_buf, sems, whole_ref.shape[1] - in_buf.shape[2]
    )
    load_all([last, *copies])
    last.wait()
    attended_ref[...] = product_right(grad_ref[...], out_buf[...]).astype(BF16)
    rows, width = qkv_ref.shape
    half = rows // 4
    span = (GROUP + 2) * HEAD_DIM
    scale = HEAD_DIM ** (-0.5)
    for m in range(2):
        mask = mask_ref[m] > 0
        mask = jnp.concatenate([mask] * GROUP, axis=0)
        for g in range(width // span):
            queries, keys, values = head_rows(ready_ref, m, half, g * span)
            weights = softmax_weights(queries, keys, mask)
            grad = jnp.concatenate(
                [
                    sequence(attended_ref, m, half, (g * GROUP + j) * HEAD_DIM)
                    for j in range(GROUP)
                ],
                axis=0,
            )
            grad_values = product_left(weights.astype(BF16), grad)
            grad_weights = product_right(grad, values)
            mean = jnp.sum(grad_weights * weights, axis=1, keepdims=True)
            grad_scores = (weights * (grad_weights - mean)).astype(BF16)
            grad_queries = product(grad_scores, keys) * scale
            grad_keys = product_left(grad_scores, queries) * scale
            outs = [grad_queries[j * 2 * half : (j + 1) * 2 * half] for j in range(GROUP)]
            for j, out in enumerate([*outs, grad_keys, grad_values]):
                at = g * span + j * HEAD_DIM
                ready_grad_ref[m * half : (m + 1) * half, at : at + HEAD_DIM] = out[:half]
                ready_grad_ref[(m + 2) * half : (m + 3) * half, at : at + HEAD_DIM] = out[half:]
    low, front = lane_facts(rows)
    cosine, sine = tables_ref[0], tables_ref[1]
    for at in range(width // 128):
        lanes = slice(at * 128, (at + 1) * 128)
        block, grad = qkv_ref[:, lanes], ready_grad_ref[:, lanes]
        heads, gains = block_gains(gains_ref, at)
        inverse = head_scales(block, low)
        normed = block * inverse
        turned = grad * sine
        grad_normed = grad * cosine + jnp.where(
            front, pltpu.roll(turned, 96, 1), -pltpu.roll(turned, 32, 1)
        )
        heads_ref[at : at + 1] = jnp.sum(grad_normed * normed, axis=0, keepdims=True)
        grad_normed = grad_normed * gains
        along = grad_normed * normed
        first = jnp.sum(jnp.where(low, along, 0.0), axis=1, keepdims=True)
        second = jnp.sum(jnp.where(low, 0.0, along), axis=1, keepdims=True)
        mean = jnp.where(low, first, second) * (1.0 / HEAD_DIM)
        raw = inverse * (grad_normed - normed * mean)
        if heads[0] == 2:
            raw = jnp.where(low, grad, raw)
        if heads[1] == 2:
            raw = jnp.where(low, raw, grad)
        proj_ref[:, lanes] = raw.astype(BF16)
    step = width // tiles_ref.shape[0]
    tiles_out(tiles_ref, grad_ref, lambda k: proj_ref[:, k * step : (k + 1) * step])
    copies[0].wait()
    acc_ref[...] = product_right(proj_ref[...], in_buf[0])
    rows_out(acc_ref, core_ref[0], mine_ref, other_ref)


def mixer_call(
    kernel, core, operands, whole, weight_out, in_tiles, outs, scratch=(), behind=()
):
    vmem, any_space = pl.BlockSpec(memory_space=pltpu.VMEM), pl.BlockSpec(memory_space=pl.ANY)
    rows, width = operands[0].shape
    channels = weight_out.shape[0]
    outs = [*outs, ((rows // 2, width), F32), ((rows // 2, width), BF16)]
    return pl.pallas_call(
        ordered(kernel, len(behind)),
        in_specs=[
            pl.BlockSpec(memory_space=pltpu.SMEM),
            *[any_space] * len(behind),
            *[vmem] * len(operands),
            any_space,
            any_space,
        ],
        out_specs=[vmem] * len(outs),
        out_shape=[jax.ShapeDtypeStruct(*out) for out in outs],
        scratch_shapes=[
            pltpu.VMEM((in_tiles[0], width, in_tiles[1]), BF16),
            pltpu.VMEM((channels, width), BF16),
            pltpu.VMEM((rows, width), F32),
            *scratch,
            pltpu.SemaphoreType.DMA((in_tiles[0] + 1,)),
        ],
        compiler_params=pltpu.CompilerParams(vmem_limit_bytes=VMEM_LIMIT),
        cost_estimate=SHORT,
    )(core, *behind, *operands, whole, weight_out)


def conv_forward_call(core, rows, kernel, masks, whole, weight_out):
    count, channels = rows.shape[0], kernel.shape[1]
    outs = [((3, count, channels), BF16), ((count, channels), BF16)]
    operands = (rows, kernel, masks)
    return mixer_call(
        conv_forward_kernel, core, operands, whole, weight_out, (3, channels), outs
    )


def conv_backward_call(core, grad, kernel, masks, projected, tiles, whole, weight_out):
    count, width = grad.shape
    taps, channels = kernel.shape
    outs = [
        (tiles.shape, BF16),
        ((taps, channels), F32),
    ]
    operands = (grad, kernel, masks, projected, tiles)
    return mixer_call(
        conv_backward_kernel, core, operands, whole, weight_out, (3, channels), outs
    )


def attention_forward_call(core, rows, gains, tables, mask, whole, weight_out, qkv_width):
    count, channels = rows.shape[0], weight_out.shape[0]
    outs = [((count, qkv_width), F32), ((count, qkv_width), BF16), ((count, channels), BF16)]
    operands = (rows, gains, tables, mask)
    return mixer_call(
        attention_forward_kernel, core, operands, whole, weight_out, (1, qkv_width), outs
    )


def attention_backward_call(core, grad, gains, tables, mask, qkv, ready, whole, weight_out):
    count, width = grad.shape
    channels, qkv_width = weight_out.shape[0], qkv.shape[1]
    outs = [
        ((4, count, whole_lanes((width + 3 * channels) // 4)), BF16),
        ((qkv_width // 128, 128), F32),
    ]
    scratch = [
        pltpu.VMEM((count, channels), BF16),
        pltpu.VMEM((count, qkv_width), F32),
        pltpu.VMEM((count, qkv_width), BF16),
    ]
    operands = (grad, gains, tables, mask, qkv, ready)
    return mixer_call(
        attention_backward_kernel, core, operands, whole, weight_out, (1, qkv_width), outs, scratch
    )


def conv_masks(segments, taps):
    masks = []
    for lag in range(1, taps):
        same = (segments[:, lag:] == segments[:, :-lag]).astype(F32)
        same = jnp.pad(same, ((0, 0), (lag, 0))).reshape(-1, 1)
        masks.append(jnp.broadcast_to(same, (same.shape[0], 128)))
    return jnp.stack(masks)


def score_mask(segments):
    position = jnp.arange(segments.shape[1])
    allowed = position[:, None] >= position[None, :]
    return (allowed & (segments[:, :, None] == segments[:, None, :])).astype(F32)


def turn_tables(length):
    half = HEAD_DIM // 2
    exponent = jnp.arange(half, dtype=F32) * (2.0 / HEAD_DIM)
    frequency = jnp.exp(-exponent * jnp.log(ROPE_BASE))
    angles = jnp.arange(length, dtype=F32)[:, None] * frequency[None, :]
    tables = jnp.tile(jnp.stack([jnp.cos(angles), jnp.sin(angles)]), (1, 1, 4))
    tables = tables.reshape(2, 2, 1, length // 2, 128)
    return jnp.broadcast_to(tables, (2, 2, 2, length // 2, 128)).reshape(2, 2 * length, 128)


def gain_rows(head_gains):
    kinds = [head_gains[0], head_gains[1], jnp.ones_like(head_gains[0])]
    rows = [jnp.concatenate([a, b]) for a in kinds for b in kinds]
    return jnp.stack(rows)


def head_gain_sums(sums):
    heads = sums.reshape(-1, GROUP + 2, HEAD_DIM)
    return jnp.stack([heads[:, :GROUP].sum((0, 1)), heads[:, GROUP].sum(0)])


def local(
    inputs,
    out_cotangent,
    segments,
    norm_gains,
    conv_kernel,
    qk_gains,
    conv_in,
    attn_qkv,
    mixer_out,
    gate_up,
    down,
):
    section = lax.axis_index("xh")
    first = section == 0
    core = lax.axis_index("c")
    place = lax.axis_index("y") * 4 + lax.axis_index("z")
    xl = lax.axis_index("xl")
    plane = lax.axis_size("y") * lax.axis_size("z")

    shape = inputs.shape[1:]
    width = shape[-1]
    inputs, out_cotangent = inputs.reshape(-1, width), out_cotangent.reshape(-1, width)
    segments = segments[0]
    half = inputs.shape[0]
    rows = 2 * half
    channels = conv_in.shape[2]
    kernel = lax.dynamic_slice_in_dim(conv_kernel, core * channels, channels, 1).astype(F32)
    gains = lax.dynamic_index_in_dim(norm_gains, section, 0, keepdims=False).astype(F32)
    weight_out, weight_pair, weight_down = mixer_out[0], gate_up[0], down[0]
    hidden_units = weight_down.shape[0]
    part = hidden_units // plane
    in_width = 3 * channels
    qkv_width = attn_qkv.shape[1]
    y = lax.axis_index("y")
    core_scalar = jnp.stack([core, section]).astype(jnp.int32)
    xl_scalar = jnp.stack([xl, section, y]).astype(jnp.int32)

    def chosen(from_first, from_second):
        return jnp.where(first, from_first, from_second)

    def gathered(own, axes):
        return lax.all_gather(own, axes, tiled=True)


    both = jnp.concatenate([conv_in.reshape(-1, in_width), attn_qkv], axis=1)
    whole = gathered(both, ("xh", "xl", "y", "z"))

    lanes = -(-part // 256) * 256
    fill = lanes - part
    part_pair = jnp.concatenate(
        [
            jnp.pad(lax.dynamic_slice_in_dim(w, place * part, part, 1), ((0, 0), (0, fill)))
            for w in (weight_pair[0], weight_pair[1])
        ],
        axis=1,
    )
    part_down = lax.dynamic_slice_in_dim(weight_down, place * part, part, 0)
    part_down = jnp.pad(part_down, ((0, fill), (0, 0)))
    masks = conv_masks(segments, kernel.shape[0])
    mask = score_mask(segments)
    tables = turn_tables(segments.shape[1])
    head_gains = gain_rows(qk_gains.astype(F32))
    first_in = inputs.astype(F32)
    normed_own_0 = (normalize(first_in) * gains[0]).astype(BF16)
    normed_0 = spread(normed_own_0)
    cotangent_1 = spread(out_cotangent)
    whole, part_pair, part_down, masks, mask, tables, head_gains, normed_0, cotangent_1 = (
        lax.optimization_barrier(
            (whole, part_pair, part_down, masks, mask, tables, head_gains, normed_0, cotangent_1)
        )
    )

    def inner_norm(hidden):
        return (normalize(hidden) * gains[1]).astype(BF16)

    def inner_back(mine, other, hidden, grad):
        return back_join_call(core_scalar, mine, swapped(other, "c"), hidden, grad, gains[1])

    def mixer_back(grad_hidden, mine, other, layer_in, behind):
        come = swapped(other, "c")
        return back_join_call(behind, mine, come, layer_in, grad_hidden, gains[0])[1:]

    plane_axes = ("y", "z", "c")
    early = gathered(chosen(normed_own_0, out_cotangent), plane_axes)

    projected, gated_0, mine, other = conv_forward_call(
        core_scalar, normed_0, kernel, masks, whole, weight_out
    )
    hidden_0 = first_in + joined(mine, other)
    inner_0 = inner_norm(hidden_0)
    gate, up, mine, other = feed_forward_call(
        False, core_scalar, spread(inner_0), weight_pair, weight_down
    )
    result_0 = (hidden_0 + joined(mine, other)).astype(BF16)

    second_in = lax.ppermute(result_0, "xh", [(0, 1)]).astype(F32)
    normed_own_1 = (normalize(second_in) * gains[0]).astype(BF16)
    qkv, ready, gated_1, mine, other = attention_forward_call(
        core_scalar, spread(normed_own_1), head_gains, tables, mask, whole, weight_out, qkv_width
    )
    hidden_1 = second_in + joined(mine, other)
    inner_1 = inner_norm(hidden_1)
    mine, other, grad_mine, grad_other = ffn_both_call(
        core_scalar, spread(inner_1), cotangent_1, weight_pair, weight_down, (early,)
    )
    result_1 = (hidden_1 + joined(mine, other)).astype(BF16)

    inner_all = gathered(chosen(inner_0, inner_1), plane_axes)
    gated = chosen(gated_0, gated_1)
    gated_z = gathered(gated, "z")

    grad_hidden_1, grad_mix_1, gain_inner_1 = inner_back(
        grad_mine, grad_other, hidden_1, out_cotangent.astype(F32)
    )
    tiles_1, head_sums, mine, other = attention_backward_call(
        core_scalar,
        spread(grad_mix_1),
        head_gains,
        tables,
        mask,
        qkv,
        ready,
        whole,
        weight_out,
    )
    input_grad_1, gain_outer_1 = mixer_back(grad_hidden_1, mine, other, second_in, core_scalar)

    cotangent = lax.ppermute(input_grad_1, "xh", [(1, 0)])
    late = gathered(chosen(cotangent, normed_own_1), plane_axes)
    mine, other = feed_forward_call(
        True,
        core_scalar,
        spread(cotangent),
        weight_pair,
        weight_down,
        (gate, up),
        (inner_all,),
    )
    grad_hidden_0, grad_mix_0, gain_inner_0 = inner_back(
        mine, other, hidden_0, cotangent.astype(F32)
    )
    tiles, grad_kernel, mine, other = conv_backward_call(
        core_scalar,
        spread(grad_mix_0),
        kernel,
        masks,
        projected,
        tiles_1,
        whole,
        weight_out,
    )
    columns = exchanged(tiles, "z").reshape(4 * rows, -1)
    part_kept = part_forward_call(tiles, inner_all, part_pair)

    def summed_over_pair(mine, other):
        return mine.astype(F32) + swapped(other, "xl").astype(F32)

    pair_grads, down_mine, down_other = lax.cond(
        first,
        lambda: part_down_call(xl_scalar, late, part_kept, part_down, (columns,)),
        lambda: part_down_call(xl_scalar, early, part_kept, part_down, (columns,)),
    )
    input_grad_0, gain_outer_0 = mixer_back(grad_hidden_0, mine, other, first_in, pair_grads)
    pair_mine, pair_other = part_pair_call(xl_scalar, inner_all, pair_grads, ())
    in_mine, in_other, out_mine, out_other = mixer_grads_call(
        xl_scalar, pair_other, columns, gated_z, early, late, plane
    )

    full_kernel = lax.dynamic_update_slice(
        jnp.zeros(conv_kernel.shape, F32), grad_kernel, (0, core * channels)
    )
    small = jnp.concatenate(
        [
            chosen(gain_outer_0, gain_outer_1),
            chosen(gain_inner_0, gain_inner_1),
            full_kernel.reshape(-1),
            head_gain_sums(head_sums).reshape(-1),
        ]
    )
    count = small.shape[0]
    small = jnp.pad(small, (0, -count % 1024)).reshape(-1, 128)
    small_all = lax.all_gather(small, AXES)

    pairs = [(a, swapped(b, "xl")) for a, b in ((pair_mine, pair_other), (down_mine, down_other))]
    total = pair_join_call((), pairs)
    arrived = exchanged(total.reshape(plane, -1, 3 * lanes), PLANE)
    arrived = widened_call(core_scalar, arrived)
    lines = [
        jnp.moveaxis(arrived[:, :, k * lanes : k * lanes + part], 0, 1).reshape(-1, hidden_units)
        for k in range(3)
    ]
    grad_gate_up = jnp.stack(lines[:2])[None]
    grad_down = lines[2].T[None]

    in_total = pair_join_call((total,), [(in_mine, swapped(in_other, "xl"))])
    come = exchanged(in_total, PLANE)
    kept_lines, sent_lines, sums = finish_call(xl_scalar, arrived, come, small_all)
    come = swapped(sent_lines, "xh").astype(F32)[:, :, : in_width // 4]
    kept_lines = kept_lines[:, :, : in_width // 4]
    lines = chosen(kept_lines, come).reshape(4, -1, 3, channels // 4)
    grad_conv_in = jnp.moveaxis(lines, 0, 2).reshape(conv_in.shape)
    lines = chosen(come, kept_lines)[:, :, : qkv_width // 4]
    grad_attn_qkv = jnp.moveaxis(lines, 0, 1).reshape(attn_qkv.shape)

    total = summed_over_pair(out_mine, out_other).reshape(4, -1, channels)
    sent = total.astype(BF16)
    lines = lax.dynamic_index_in_dim(total, y, 0, keepdims=False)
    for by in range(1, 4):
        block = lax.dynamic_index_in_dim(sent, (y + by) % 4, 0, keepdims=False)
        lines += lax.ppermute(block, "y", around(by)).astype(F32)
    grad_mixer_out = lines.T[None]

    pair = [sums[0].reshape(-1), sums[1].reshape(-1)]
    grad_norm_gains = jnp.stack([a[: 2 * width].reshape(2, width) for a in pair])
    grad_conv_kernel = pair[0][2 * width : 5 * width].reshape(conv_kernel.shape)
    grad_qk_gains = pair[1][5 * width : count].reshape(qk_gains.shape)

    activations = chosen(result_0, result_1).reshape(1, 1, *shape)
    input_grads = chosen(input_grad_0, input_grad_1).reshape(1, 1, *shape)
    return (
        activations,
        input_grads,
        grad_norm_gains,
        grad_conv_kernel,
        grad_qk_gains,
        grad_conv_in,
        grad_attn_qkv,
        grad_mixer_out,
        grad_gate_up,
        grad_down,
    )


def solution(mesh):
    wide = Mesh(mesh.devices.reshape(2, 2, 4, 4, 2), AXES)
    dp = ("xl", "y", "z")
    everyone = ("xh", "xl", "y", "z")
    in_specs = (
        P(dp, None, "c", None),
        P(dp, None, "c", None),
        P(dp, None, None),
        P(),
        P(),
        P(),
        P(everyone, None, "c"),
        P(everyone, "c"),
        P("xh", "c", None),
        P("xh", None, None, "c"),
        P("xh", "c", None),
    )
    out_specs = (
        P("xh", dp, None, "c", None),
        P("xh", dp, None, "c", None),
        P(),
        P(),
        P(),
        P(everyone, None, "c"),
        P(everyone, "c"),
        P("xh", "c", dp),
        P("xh", None, dp, "c"),
        P("xh", "c", dp),
    )
    return jax.shard_map(local, mesh=wide, in_specs=in_specs, out_specs=out_specs, check_vma=False)
```

```python
import functools

import jax
import jax.numpy as jnp
from jax import lax
from jax.experimental import pallas as pl
from jax.experimental.pallas import tpu as pltpu
from jax.sharding import Mesh
from jax.sharding import PartitionSpec as P

HEADS = 24
KV_HEADS = 8
HEAD_DIM = 64
GROUP = HEADS // KV_HEADS

EPSILON = 1e-05
ROPE_BASE = 1000000.0
MASKED_SCORE = -1e30

F32 = jnp.float32
BF16 = jnp.bfloat16

PLANE = ("y", "z")
AXES = ("xh", "xl", "y", "z", "c")


def product(left, right):
    return jnp.dot(left, right, preferred_element_type=F32)


def product_left(left, right):
    return lax.dot_general(left, right, (((0,), (0,)), ((), ())), preferred_element_type=F32)


def product_right(left, right):
    return lax.dot_general(left, right, (((1,), (1,)), ((), ())), preferred_element_type=F32)


def swapped(shard, axis):
    return lax.ppermute(shard, axis, [(0, 1), (1, 0)])


def spread(own):
    return lax.all_gather(own, "c", tiled=True)


def joined(mine, other):
    return mine + swapped(other, "c").astype(F32)


def mean_last(values):
    return jnp.mean(values, axis=-1, keepdims=True)


def inverse_rms(values):
    return lax.rsqrt(mean_last(values * values) + EPSILON)


def normalize(values):
    return values * inverse_rms(values)


def around(by):
    return [(k, (k + by) % 4) for k in range(4)]


def exchanged(tiles, axes):
    return lax.all_to_all(tiles, axes, 0, 0, tiled=True)


def ffn_grads(grad_active, gate, up):
    sigmoid = jax.nn.sigmoid(gate)
    grad_gate = grad_active * up * sigmoid * (1.0 + gate * (1.0 - sigmoid))
    grad_up = grad_active * gate * sigmoid
    return grad_gate.astype(BF16), grad_up.astype(BF16)


VMEM_LIMIT = 56 * 1024 * 1024
SHORT = pl.CostEstimate(flops=1, bytes_accessed=1, transcendentals=0)


def whole_lanes(columns):
    return -(-columns // 128) * 128


def ordered(kernel, count):
    def body(scalar_ref, *refs):
        kernel(scalar_ref, *refs[count:])

    return body


def unit_tiles(units, tile):
    short = units % tile
    tiles = [(0, short)] if short else []
    return tiles + [(at, tile) for at in range(short, units, tile)]


def streamed(tiles, copies, work):
    for copy in copies(0, 0):
        copy.start()
    for k in range(len(tiles)):
        slot = k % 2
        if k + 1 < len(tiles):
            for copy in copies(k + 1, 1 - slot):
                copy.start()
        for copy in copies(k, slot):
            copy.wait()
        work(k, slot)


def ffn_forward_kernel(
    tiles, core_ref, rows_ref, pair_ref, down_ref, gate_ref, up_ref, mine_ref, other_ref,
    pair_buf, down_buf, gate_buf, up_buf, acc_ref, sems, out_sems,
):
    def copies(k, slot):
        at, size = tiles[k]
        return [
            pltpu.make_async_copy(
                pair_ref.at[0, :, pl.ds(at, size)],
                pair_buf.at[slot, :, pl.ds(0, size)],
                sems.at[slot, 0],
            ),
            pltpu.make_async_copy(
                pair_ref.at[1, :, pl.ds(at, size)],
                pair_buf.at[slot, :, pl.ds(size, size)],
                sems.at[slot, 1],
            ),
            pltpu.make_async_copy(
                down_ref.at[pl.ds(at, size)], down_buf.at[slot, pl.ds(0, size)], sems.at[slot, 2]
            ),
        ]

    def kept(k):
        here = (slice(None), pl.ds(*tiles[k]))
        return [
            pltpu.make_async_copy(gate_buf.at[here], gate_ref.at[here], out_sems.at[k, 0]),
            pltpu.make_async_copy(up_buf.at[here], up_ref.at[here], out_sems.at[k, 1]),
        ]

    def work(k, slot):
        at, size = tiles[k]
        both = product(rows_ref[...], pair_buf[slot, :, : 2 * size])
        gate, up = both[:, :size], both[:, size:]
        gate_buf[:, at : at + size] = gate.astype(BF16)
        up_buf[:, at : at + size] = up.astype(BF16)
        for copy in kept(k):
            copy.start()
        active = (gate * jax.nn.sigmoid(gate) * up).astype(BF16)
        part = product(active, down_buf[slot, :size])
        if k == 0:
            acc_ref[...] = part
        else:
            acc_ref[...] += part

    streamed(tiles, copies, work)
    rows_out(acc_ref, core_ref[0], mine_ref, other_ref)
    for k in range(len(tiles)):
        for copy in kept(k):
            copy.wait()


def ffn_backward_kernel(
    tiles, core_ref, rows_ref, gate_ref, up_ref, pair_ref, down_ref, mine_ref, other_ref,
    pair_buf, down_buf, gate_buf, up_buf, acc_ref, sems,
):
    def copies(k, slot):
        at, size = tiles[k]
        columns, place = pl.ds(at, size), pl.ds(0, size)
        return [
            pltpu.make_async_copy(
                down_ref.at[columns], down_buf.at[slot, place], sems.at[slot, 0]
            ),
            pltpu.make_async_copy(
                gate_ref.at[:, columns], gate_buf.at[slot, :, place], sems.at[slot, 1]
            ),
            pltpu.make_async_copy(
                up_ref.at[:, columns], up_buf.at[slot, :, place], sems.at[slot, 2]
            ),
            pltpu.make_async_copy(
                pair_ref.at[0, :, columns], pair_buf.at[slot, :, place], sems.at[slot, 3]
            ),
            pltpu.make_async_copy(
                pair_ref.at[1, :, columns],
                pair_buf.at[slot, :, pl.ds(size, size)],
                sems.at[slot, 4],
            ),
        ]

    def work(k, slot):
        _, size = tiles[k]
        grad_active = product_right(rows_ref[...], down_buf[slot, :size])
        grads = ffn_grads(
            grad_active,
            gate_buf[slot, :, :size].astype(F32),
            up_buf[slot, :, :size].astype(F32),
        )
        part = product_right(jnp.concatenate(grads, axis=1), pair_buf[slot, :, : 2 * size])
        if k == 0:
            acc_ref[...] = part
        else:
            acc_ref[...] += part

    streamed(tiles, copies, work)
    rows_out(acc_ref, core_ref[0], mine_ref, other_ref)


def ffn_both_kernel(
    tiles, core_ref, rows_ref, grad_ref, pair_ref, down_ref,
    mine_ref, other_ref, grad_mine_ref, grad_other_ref, pair_buf, down_buf, acc_ref, grad_acc_ref, sems,
):
    def copies(k, slot):
        at, size = tiles[k]
        columns, place = pl.ds(at, size), pl.ds(0, size)
        return [
            pltpu.make_async_copy(
                pair_ref.at[0, :, columns], pair_buf.at[slot, :, place], sems.at[slot, 0]
            ),
            pltpu.make_async_copy(
                pair_ref.at[1, :, columns],
                pair_buf.at[slot, :, pl.ds(size, size)],
                sems.at[slot, 1],
            ),
            pltpu.make_async_copy(
                down_ref.at[columns], down_buf.at[slot, place], sems.at[slot, 2]
            ),
        ]

    def work(k, slot):
        _, size = tiles[k]
        both = product(rows_ref[...], pair_buf[slot, :, : 2 * size])
        grad_active = product_right(grad_ref[...], down_buf[slot, :size])
        gate, up = both[:, :size], both[:, size:]
        active = (gate * jax.nn.sigmoid(gate) * up).astype(BF16)
        grads = jnp.concatenate(ffn_grads(grad_active, gate, up), axis=1)
        part = product(active, down_buf[slot, :size])
        grad_part = product_right(grads, pair_buf[slot, :, : 2 * size])
        if k == 0:
            acc_ref[...], grad_acc_ref[...] = part, grad_part
        else:
            acc_ref[...] += part
            grad_acc_ref[...] += grad_part

    streamed(tiles, copies, work)
    rows_out(acc_ref, core_ref[0], mine_ref, other_ref)
    rows_out(grad_acc_ref, core_ref[0], grad_mine_ref, grad_other_ref)


def ffn_both_call(core, rows, grad, pair, down, behind):
    count, width = rows.shape
    units = down.shape[0]
    tile = 768
    vmem, any_space = pl.BlockSpec(memory_space=pltpu.VMEM), pl.BlockSpec(memory_space=pl.ANY)
    half = (count // 2, width)
    return pl.pallas_call(
        ordered(functools.partial(ffn_both_kernel, unit_tiles(units, tile)), len(behind)),
        in_specs=[
            pl.BlockSpec(memory_space=pltpu.SMEM),
            *[any_space] * len(behind),
            vmem,
            vmem,
            any_space,
            any_space,
        ],
        out_specs=[vmem] * 4,
        out_shape=[jax.ShapeDtypeStruct(half, F32), jax.ShapeDtypeStruct(half, BF16)] * 2,
        scratch_shapes=[
            pltpu.VMEM((2, width, 2 * tile), BF16),
            pltpu.VMEM((2, tile, width), BF16),
            pltpu.VMEM((count, width), F32),
            pltpu.VMEM((count, width), F32),
            pltpu.SemaphoreType.DMA((2, 3)),
        ],
        compiler_params=pltpu.CompilerParams(vmem_limit_bytes=VMEM_LIMIT),
        cost_estimate=SHORT,
    )(core, *behind, rows, grad, pair, down)


def feed_forward_call(backward, core, rows, pair, down, saved=(), behind=()):
    count, width = rows.shape
    units = down.shape[0]
    tile = 768
    tiles = unit_tiles(units, tile)
    vmem, any_space = pl.BlockSpec(memory_space=pltpu.VMEM), pl.BlockSpec(memory_space=pl.ANY)
    scalar = pl.BlockSpec(memory_space=pltpu.SMEM)
    out_shape = [
        jax.ShapeDtypeStruct((count // 2, width), F32),
        jax.ShapeDtypeStruct((count // 2, width), BF16),
    ]
    out_specs = [vmem, vmem]
    buffers = [pltpu.VMEM((2, width, 2 * tile), BF16), pltpu.VMEM((2, tile, width), BF16)]
    acc = pltpu.VMEM((count, width), F32)
    if backward:
        body = functools.partial(ffn_backward_kernel, tiles)
        in_specs = [scalar, vmem, any_space, any_space, any_space, any_space]
        buffers += [pltpu.VMEM((2, count, tile), BF16)] * 2
        scratch = [*buffers, acc, pltpu.SemaphoreType.DMA((2, 5))]
    else:
        body = functools.partial(ffn_forward_kernel, tiles)
        in_specs = [scalar, vmem, any_space, any_space]
        out_shape = [jax.ShapeDtypeStruct((count, units), BF16)] * 2 + out_shape
        out_specs = [any_space, any_space, *out_specs]
        buffers += [pltpu.VMEM((count, units), BF16)] * 2
        scratch = [*buffers, acc]
        scratch += [pltpu.SemaphoreType.DMA((2, 3)), pltpu.SemaphoreType.DMA((len(tiles), 2))]
    in_specs = [scalar, *[any_space] * len(behind), *in_specs[1:]]
    return pl.pallas_call(
        ordered(body, len(behind)),
        in_specs=in_specs,
        out_specs=out_specs,
        out_shape=out_shape,
        scratch_shapes=scratch,
        compiler_params=pltpu.CompilerParams(vmem_limit_bytes=VMEM_LIMIT),
        cost_estimate=SHORT,
    )(core, *behind, rows, *saved, pair, down)


def part_forward_kernel(*refs):
    rows_ref, pair_ref, kept_ref = refs[-3:]
    both = product(rows_ref[...], pair_ref[...])
    units = both.shape[1] // 2
    gate, up = both[:, :units], both[:, units:]
    sigmoid = jax.nn.sigmoid(gate)
    silu = gate * sigmoid
    kept_ref[:, :units] = (up * (sigmoid + silu * (1.0 - sigmoid))).astype(BF16)
    kept_ref[:, units : 2 * units] = silu.astype(BF16)
    kept_ref[:, 2 * units :] = (silu * up).astype(BF16)


def part_forward_call(behind, rows, pair):
    tokens, width = rows.shape
    units = pair.shape[1] // 2
    tile = 1024
    return pl.pallas_call(
        part_forward_kernel,
        grid=(tokens // tile,),
        in_specs=[
            *[pl.BlockSpec(memory_space=pl.ANY)] * len(behind),
            pl.BlockSpec((tile, width), lambda i: (i, 0)),
            pl.BlockSpec((width, 2 * units), lambda i: (0, 0)),
        ],
        out_specs=pl.BlockSpec((tile, 3 * units), lambda i: (i, 0)),
        out_shape=jax.ShapeDtypeStruct((tokens, 3 * units), BF16),
        compiler_params=pltpu.CompilerParams(vmem_limit_bytes=VMEM_LIMIT),
        cost_estimate=pl.CostEstimate(
            flops=8 * tokens * width * units, bytes_accessed=2 * tokens * width, transcendentals=0
        ),
    )(*behind, rows, pair)


def pair_out(acc_ref, here, mine_ref, other_ref):
    rows = mine_ref.shape[0]
    for ref, half in ((mine_ref, here), (other_ref, 1 - here)):
        ref[...] = acc_ref[pl.ds(pl.multiple_of(half * rows, rows), rows)].astype(BF16)


def accumulated(acc_ref, part, finish):
    step = pl.program_id(0)

    @pl.when(step == 0)
    def _():
        acc_ref[...] = part

    @pl.when(step > 0)
    def _():
        acc_ref[...] += part

    pl.when(step == pl.num_programs(0) - 1)(finish)


def part_down_kernel(here_ref, grad_ref, kept_ref, down_ref, pair_ref, mine_ref, other_ref, acc_ref):
    grad = grad_ref[...]
    units = down_ref.shape[0]
    grad_active = product_right(grad, down_ref[...])
    for k in range(2):
        lanes = slice(k * units, (k + 1) * units)
        pair_ref[:, lanes] = (grad_active * kept_ref[:, lanes].astype(F32)).astype(BF16)
    accumulated(
        acc_ref,
        product_left(grad, kept_ref[:, 2 * units :]),
        lambda: pair_out(acc_ref, here_ref[0], mine_ref, other_ref),
    )


def part_pair_kernel(here_ref, rows_ref, pair_ref, mine_ref, other_ref, acc_ref):
    accumulated(
        acc_ref,
        product_left(rows_ref[...], pair_ref[...]),
        lambda: pair_out(acc_ref, here_ref[0], mine_ref, other_ref),
    )


def part_call(kernel, here, operands, fixed, outs, result, flops, behind=()):
    tokens = operands[0].shape[0]
    tile = 1024
    by_tokens = lambda width: pl.BlockSpec((tile, width), lambda i, h: (i, 0))
    entire = lambda shape: pl.BlockSpec(shape, lambda i, h: (0, 0))
    half = (result[0] // 2, result[1])
    return pl.pallas_call(
        ordered(kernel, len(behind)),
        grid_spec=pltpu.PrefetchScalarGridSpec(
            num_scalar_prefetch=1,
            grid=(tokens // tile,),
            in_specs=[pl.BlockSpec(memory_space=pl.ANY)] * len(behind)
            + [by_tokens(a.shape[1]) for a in operands]
            + [entire(a.shape) for a in fixed],
            out_specs=[by_tokens(width) for width in outs] + [entire(half)] * 2,
            scratch_shapes=[pltpu.VMEM(result, F32)],
        ),
        out_shape=[jax.ShapeDtypeStruct((tokens, width), BF16) for width in outs]
        + [jax.ShapeDtypeStruct(half, BF16)] * 2,
        compiler_params=pltpu.CompilerParams(vmem_limit_bytes=VMEM_LIMIT),
        cost_estimate=SHORT,
    )(here, *behind, *operands, *fixed)


def part_down_call(here, grad, kept, down, behind):
    tokens, width = grad.shape
    units = down.shape[0]
    flops = 4 * tokens * width * units
    return part_call(
        part_down_kernel,
        here,
        (grad, kept),
        (down,),
        (2 * units,),
        (width, units),
        flops,
        behind,
    )


def part_pair_call(here, inner, pair, behind):
    (tokens, width), columns = inner.shape, pair.shape[1]
    flops = 2 * tokens * width * columns
    return part_call(
        part_pair_kernel, here, (inner, pair), (), (), (width, columns), flops, behind
    )


def back_join_kernel(
    behind_ref, mine_ref, come_ref, values_ref, base_ref, gain_ref, wide_ref, low_ref, sums_ref
):
    grad = mine_ref[...] + come_ref[...].astype(F32)
    values = values_ref[...]
    inverse = inverse_rms(values)
    normed = values * inverse
    scaled = grad * gain_ref[...]
    sums_ref[...] = jnp.sum(grad * normed, axis=0, keepdims=True)
    total = base_ref[...] + inverse * (scaled - normed * mean_last(scaled * normed))
    wide_ref[...] = total
    low_ref[...] = total.astype(BF16)


def back_join_call(behind, mine, come, values, base, gain):
    vmem = pl.BlockSpec(memory_space=pltpu.VMEM)
    shape = values.shape
    wide, low, sums = pl.pallas_call(
        back_join_kernel,
        in_specs=[pl.BlockSpec(memory_space=pl.ANY), *[vmem] * 5],
        out_specs=[vmem] * 3,
        out_shape=[
            jax.ShapeDtypeStruct(shape, F32),
            jax.ShapeDtypeStruct(shape, BF16),
            jax.ShapeDtypeStruct((1, shape[1]), F32),
        ],
        compiler_params=pltpu.CompilerParams(vmem_limit_bytes=VMEM_LIMIT),
        cost_estimate=SHORT,
    )(behind, mine, come, values, base, gain[None])
    return wide, low, sums[0]


def pair_join_kernel(count, *refs):
    *refs, out_ref = refs[count:]
    at = 0
    for mine_ref, come_ref in zip(refs[::2], refs[1::2]):
        size = mine_ref.shape[-1]
        total = mine_ref[...].astype(F32) + come_ref[...].astype(F32)
        out_ref[..., at : at + size] = total.astype(BF16)
        at += size


def pair_join_call(behind, pairs):
    vmem = pl.BlockSpec(memory_space=pltpu.VMEM)
    operands = [a for pair in pairs for a in pair]
    shape = (*operands[0].shape[:-1], sum(mine.shape[-1] for mine, _ in pairs))
    return pl.pallas_call(
        functools.partial(pair_join_kernel, len(behind)),
        in_specs=[pl.BlockSpec(memory_space=pl.ANY)] * len(behind) + [vmem] * len(operands),
        out_specs=vmem,
        out_shape=jax.ShapeDtypeStruct(shape, BF16),
        compiler_params=pltpu.CompilerParams(vmem_limit_bytes=VMEM_LIMIT),
        cost_estimate=SHORT,
    )(*behind, *operands)


def widened_kernel(behind_ref, low_ref, wide_ref):
    wide_ref[...] = low_ref[...].astype(F32)


def widened_call(behind, low):
    vmem = pl.BlockSpec(memory_space=pltpu.VMEM)
    return pl.pallas_call(
        widened_kernel,
        in_specs=[pl.BlockSpec(memory_space=pl.ANY), vmem],
        out_specs=vmem,
        out_shape=jax.ShapeDtypeStruct(low.shape, F32),
        compiler_params=pltpu.CompilerParams(vmem_limit_bytes=VMEM_LIMIT),
        cost_estimate=SHORT,
    )(behind, low)


def line_sums_kernel(places_ref, come_ref, mine_ref, other_ref, acc_ref):
    here = places_ref[0]
    count, rows, _ = mine_ref.shape
    for k in range(count):
        tiles = [come_ref[m * count + k].astype(F32) for m in range(come_ref.shape[0] // count)]
        acc_ref[...] = functools.reduce(jnp.add, tiles)
        mine_ref[k] = acc_ref[pl.ds(pl.multiple_of(here * rows, rows), rows)]
        other = acc_ref[pl.ds(pl.multiple_of((1 - here) * rows, rows), rows)]
        other_ref[k] = other.astype(BF16)


def line_sums_call(places, come):
    vmem = pl.BlockSpec(memory_space=pltpu.VMEM)
    plane, block, size = come.shape
    lines = (4, block // 2, size)
    return pl.pallas_call(
        line_sums_kernel,
        in_specs=[pl.BlockSpec(memory_space=pltpu.SMEM), vmem],
        out_specs=[vmem] * 2,
        out_shape=[jax.ShapeDtypeStruct(lines, F32), jax.ShapeDtypeStruct(lines, BF16)],
        scratch_shapes=[pltpu.VMEM((block, size), F32)],
        compiler_params=pltpu.CompilerParams(vmem_limit_bytes=VMEM_LIMIT),
        cost_estimate=SHORT,
    )(places, come)


def finish_kernel(
    places_ref, behind_ref, mine_ref, come_ref, kept_ref, sent_ref, acc_ref
):
    section = places_ref[1]
    short = kept_ref.shape[1]
    acc_ref[...] = mine_ref[...] + come_ref[...].astype(F32)
    kept_ref[...] = acc_ref[:, pl.ds(pl.multiple_of(section * short, short), short)]
    sent = acc_ref[:, pl.ds(pl.multiple_of((1 - section) * short, short), short)]
    sent_ref[...] = sent.astype(BF16)


def plane_sums_kernel(behind_ref, small_ref, sums_ref):
    sums_ref[...] = jnp.sum(small_ref[...], axis=0)


def plane_sums_call(behind, small):
    vmem = pl.BlockSpec(memory_space=pltpu.VMEM)
    return pl.pallas_call(
        plane_sums_kernel,
        in_specs=[pl.BlockSpec(memory_space=pl.ANY), vmem],
        out_specs=vmem,
        out_shape=jax.ShapeDtypeStruct(small.shape[1:], F32),
        compiler_params=pltpu.CompilerParams(vmem_limit_bytes=VMEM_LIMIT),
        cost_estimate=SHORT,
    )(behind, small)


def finish_call(places, behind, mine, come):
    vmem = pl.BlockSpec(memory_space=pltpu.VMEM)
    count, rows, size = mine.shape
    lines = (count, rows // 2, size)
    return pl.pallas_call(
        finish_kernel,
        in_specs=[
            pl.BlockSpec(memory_space=pltpu.SMEM),
            pl.BlockSpec(memory_space=pl.ANY),
            *[vmem] * 2,
        ],
        out_specs=[vmem] * 2,
        out_shape=[jax.ShapeDtypeStruct(lines, F32), jax.ShapeDtypeStruct(lines, BF16)],
        scratch_shapes=[pltpu.VMEM(mine.shape, F32)],
        compiler_params=pltpu.CompilerParams(vmem_limit_bytes=VMEM_LIMIT),
        cost_estimate=SHORT,
    )(places, behind, mine, come)


def mixer_grads_kernel(
    places_ref, behind_ref, columns_ref, gated_ref, early_ref, late_ref,
    parts_ref, out_mine_ref, out_other_ref, normed_ref, in_ref, out_ref, sem,
):
    here, section, y = places_ref[0], places_ref[1], places_ref[2]

    def copy(all_ref):
        rows = normed_ref.shape[0]
        start = pl.multiple_of(y * rows, rows)
        return pltpu.make_async_copy(all_ref.at[pl.ds(start, rows)], normed_ref, sem)

    @pl.when(section == 0)
    def _():
        copy(early_ref).start()

    @pl.when(section > 0)
    def _():
        copy(late_ref).start()

    mix = out_ref.shape[0]
    out_ref[...] = product_left(columns_ref[:, :mix], gated_ref[...])
    pair_out(out_ref, here, out_mine_ref, out_other_ref)
    copy(early_ref).wait()
    in_ref[...] = product_left(normed_ref[...], columns_ref[:, mix:])
    plane, block, _ = parts_ref.shape
    short = block // 4
    for k in range(plane):
        for half in range(2):
            for s in range(2):
                start = ((2 * s + half) * plane + k) * short
                place = (2 * half + s) * short
                rows_in = in_ref[start : start + short]
                parts_ref[k, place : place + short] = rows_in.astype(BF16)


def mixer_grads_call(places, behind, columns, gated, early, late, plane):
    vmem, any_space = pl.BlockSpec(memory_space=pltpu.VMEM), pl.BlockSpec(memory_space=pl.ANY)
    tokens, channels = gated.shape
    width = early.shape[1]
    mix = width // 4
    size = columns.shape[1] - mix
    in_parts = jax.ShapeDtypeStruct((plane, width // plane, size), BF16)
    out_half = jax.ShapeDtypeStruct((mix // 2, channels), BF16)
    return pl.pallas_call(
        mixer_grads_kernel,
        in_specs=[
            pl.BlockSpec(memory_space=pltpu.SMEM),
            any_space,
            vmem,
            vmem,
            any_space,
            any_space,
        ],
        out_specs=[vmem] * 3,
        out_shape=[in_parts, out_half, out_half],
        scratch_shapes=[
            pltpu.VMEM((tokens, width), BF16),
            pltpu.VMEM((width, size), F32),
            pltpu.VMEM((mix, channels), F32),
            pltpu.SemaphoreType.DMA,
        ],
        compiler_params=pltpu.CompilerParams(vmem_limit_bytes=VMEM_LIMIT),
        cost_estimate=SHORT,
    )(places, behind, columns, gated, early, late)


def load_all(copies):
    for copy in copies:
        copy.start()


def in_time(rows):
    half = rows.shape[0] // 4
    return jnp.concatenate([rows[k * half : (k + 1) * half] for k in (0, 2, 1, 3)], axis=0)


def rows_out(acc_ref, core, mine_ref, other_ref):
    half = mine_ref.shape[0]
    mine_ref[...] = acc_ref[pl.ds(pl.multiple_of(core * half, half), half)]
    rest = acc_ref[pl.ds(pl.multiple_of((1 - core) * half, half), half)]
    other_ref[...] = rest.astype(BF16)


def weight_copies(whole_ref, out_ref, in_buf, out_buf, sems, start):
    size = in_buf.shape[2]
    copies = [
        pltpu.make_async_copy(
            whole_ref.at[:, pl.ds(start + k * size, size)], in_buf.at[k], sems.at[k]
        )
        for k in range(in_buf.shape[0])
    ]
    return copies, pltpu.make_async_copy(out_ref, out_buf, sems.at[len(copies)])


def conv_taps(mixed, kernel, masks):
    terms = [mixed]
    for lag in range(1, len(masks) + 1):
        terms.append(pltpu.roll(mixed, lag, 0) * masks[lag - 1])
    taps = kernel.shape[0]
    total = kernel[taps - 1 : taps] * terms[0]
    for lag in range(1, taps):
        total = total + kernel[taps - 1 - lag : taps - lag] * terms[lag]
    return terms, total


def conv_forward_kernel(
    core_ref, rows_ref, kernel_ref, masks_ref, whole_ref, out_ref,
    proj_ref, gated_ref, mine_ref, other_ref, in_buf, out_buf, acc_ref, sems,
):
    copies, last = weight_copies(whole_ref, out_ref, in_buf, out_buf, sems, 0)
    load_all([*copies, last])
    rows = rows_ref[...]
    parts = []
    for k, copy in enumerate(copies):
        copy.wait()
        part = product(rows, in_buf[k])
        proj_ref[k] = part.astype(BF16)
        parts.append(in_time(part))
    masks = [masks_ref[lag] for lag in range(masks_ref.shape[0])]
    gated = []
    for at in range(0, parts[0].shape[1], 128):
        before, after, signal = [part[:, at : at + 128] for part in parts]
        _, total = conv_taps(before * signal, kernel_ref[:, at : at + 128], masks)
        gated.append((after * total).astype(BF16))
    gated = in_time(jnp.concatenate(gated, axis=1))
    gated_ref[...] = gated
    last.wait()
    acc_ref[...] = product(gated, out_buf[...])
    rows_out(acc_ref, core_ref[0], mine_ref, other_ref)


def tiles_out(tiles_ref, grad_ref, columns):
    count, rows, size = tiles_ref.shape
    step = grad_ref.shape[1] // (2 * count * count)
    for k in range(count):
        starts = range(k * step, grad_ref.shape[1], count * step)
        parts = [grad_ref[:, at : at + step] for at in starts]
        parts.append(columns(k))
        spare = size - sum(part.shape[1] for part in parts)
        tiles_ref[k] = jnp.concatenate([*parts, jnp.zeros((rows, spare), BF16)], axis=1)


def conv_backward_kernel(
    core_ref, grad_ref, kernel_ref, masks_ref, proj_ref, other_tiles_ref,
    whole_ref, out_ref, tiles_ref, taps_ref, mine_ref, other_ref, in_buf, out_buf, acc_ref, sems,
):
    copies, last = weight_copies(whole_ref, out_ref, in_buf, out_buf, sems, 0)
    load_all([last, *copies])
    last.wait()
    grad_gated = in_time(product_right(grad_ref[...], out_buf[...]))
    parts = [in_time(proj_ref[k].astype(F32)) for k in range(3)]
    masks = [masks_ref[lag] for lag in range(masks_ref.shape[0])]
    rows = grad_gated.shape[0]
    grads = [[], [], []]
    for at in range(0, grad_gated.shape[1], 128):
        before, after, signal = [part[:, at : at + 128] for part in parts]
        kernel = kernel_ref[:, at : at + 128]
        terms, total = conv_taps(before * signal, kernel, masks)
        grad = grad_gated[:, at : at + 128]
        grad_total = grad * after
        taps = kernel.shape[0]
        grad_mixed = kernel[taps - 1 : taps] * grad_total
        for lag in range(1, taps):
            sent = pltpu.roll(grad_total * masks[lag - 1], rows - lag, 0)
            grad_mixed = grad_mixed + kernel[taps - 1 - lag : taps - lag] * sent
        for lag in range(taps):
            taps_ref[taps - 1 - lag : taps - lag, at : at + 128] = jnp.sum(
                grad_total * terms[lag], axis=0, keepdims=True
            )
        for k, value in enumerate((grad_mixed * signal, grad * total, grad_mixed * before)):
            grads[k].append(value.astype(BF16))
    grads = [in_time(jnp.concatenate(g, axis=1)) for g in grads]
    step = grads[0].shape[1] // tiles_ref.shape[0]

    @pl.when(core_ref[1] == 0)
    def _():
        tiles_out(
            tiles_ref,
            grad_ref,
            lambda k: jnp.concatenate([g[:, k * step : (k + 1) * step] for g in grads], axis=1),
        )

    @pl.when(core_ref[1] > 0)
    def _():
        tiles_ref[...] = other_tiles_ref[...]

    for k, copy in enumerate(copies):
        copy.wait()
        part = product_right(grads[k], in_buf[k])
        acc_ref[...] = part if k == 0 else acc_ref[...] + part
    rows_out(acc_ref, core_ref[0], mine_ref, other_ref)


def head_kind(head):
    return min(max(head % (GROUP + 2) - GROUP + 1, 0), 2)


def lane_facts(rows):
    lane = lax.broadcasted_iota(jnp.int32, (rows, 128), 1)
    return lane < HEAD_DIM, lax.rem(lane, HEAD_DIM) < HEAD_DIM // 2


def head_scales(block, low):
    squares = block * block
    first = jnp.sum(jnp.where(low, squares, 0.0), axis=1, keepdims=True)
    second = jnp.sum(jnp.where(low, 0.0, squares), axis=1, keepdims=True)
    return lax.rsqrt(jnp.where(low, first, second) * (1.0 / HEAD_DIM) + EPSILON)


def block_gains(gains_ref, at):
    heads = [head_kind(2 * at), head_kind(2 * at + 1)]
    return heads, gains_ref[3 * heads[0] + heads[1] : 3 * heads[0] + heads[1] + 1]


def attention_forward_kernel(
    core_ref, rows_ref, gains_ref, tables_ref, mask_ref, whole_ref, out_ref,
    qkv_ref, ready_ref, gated_ref, mine_ref, other_ref, in_buf, out_buf, acc_ref, sems,
):
    copies, last = weight_copies(
        whole_ref, out_ref, in_buf, out_buf, sems, whole_ref.shape[1] - in_buf.shape[2]
    )
    load_all([*copies, last])
    copies[0].wait()
    qkv_ref[...] = product(rows_ref[...], in_buf[0])
    rows, width = qkv_ref.shape
    low, front = lane_facts(rows)
    cosine, sine = tables_ref[0], tables_ref[1]
    for at in range(width // 128):
        block = qkv_ref[:, at * 128 : (at + 1) * 128]
        heads, gains = block_gains(gains_ref, at)
        normed = block * head_scales(block, low) * gains
        turned = jnp.where(front, -pltpu.roll(normed, 96, 1), pltpu.roll(normed, 32, 1))
        ready = normed * cosine + turned * sine
        if heads[0] == 2:
            ready = jnp.where(low, block, ready)
        if heads[1] == 2:
            ready = jnp.where(low, ready, block)
        ready_ref[:, at * 128 : (at + 1) * 128] = ready.astype(BF16)
    half = rows // 4
    span = (GROUP + 2) * HEAD_DIM
    for m in range(2):
        mask = mask_ref[m] > 0
        mask = jnp.concatenate([mask] * GROUP, axis=0)
        for g in range(width // span):
            queries, keys, values = head_rows(ready_ref, m, half, g * span)
            weights = softmax_weights(queries, keys, mask)
            attended = product(weights.astype(BF16), values).astype(BF16)
            for j in range(GROUP):
                at = (g * GROUP + j) * HEAD_DIM
                head = attended[j * 2 * half : (j + 1) * 2 * half]
                gated_ref[m * half : (m + 1) * half, at : at + HEAD_DIM] = head[:half]
                gated_ref[(m + 2) * half : (m + 3) * half, at : at + HEAD_DIM] = head[half:]
    last.wait()
    acc_ref[...] = product(gated_ref[...], out_buf[...])
    rows_out(acc_ref, core_ref[0], mine_ref, other_ref)


def sequence(ref, m, half, at):
    columns = slice(at, at + HEAD_DIM)
    return jnp.concatenate(
        [ref[m * half : (m + 1) * half, columns], ref[(m + 2) * half : (m + 3) * half, columns]],
        axis=0,
    )


def head_rows(ref, m, half, at):
    heads = [sequence(ref, m, half, at + j * HEAD_DIM) for j in range(GROUP + 2)]
    return jnp.concatenate(heads[:GROUP], axis=0), heads[GROUP], heads[GROUP + 1]


def softmax_weights(queries, keys, mask):
    scores = jnp.where(mask, product_right(queries, keys) * HEAD_DIM ** (-0.5), MASKED_SCORE)
    terms = jnp.exp(scores - jnp.max(scores, axis=1, keepdims=True))
    return terms / jnp.sum(terms, axis=1, keepdims=True)


def attention_backward_kernel(
    core_ref, grad_ref, gains_ref, tables_ref, mask_ref, qkv_ref, ready_ref,
    whole_ref, out_ref, tiles_ref, heads_ref, mine_ref, other_ref,
    in_buf, out_buf, acc_ref, attended_ref, ready_grad_ref, proj_ref, sems,
):
    copies, last = weight_copies(
        whole_ref, out_ref, in_buf, out_buf, sems, whole_ref.shape[1] - in_buf.shape[2]
    )
    load_all([last, *copies])
    last.wait()
    attended_ref[...] = product_right(grad_ref[...], out_buf[...]).astype(BF16)
    rows, width = qkv_ref.shape
    half = rows // 4
    span = (GROUP + 2) * HEAD_DIM
    scale = HEAD_DIM ** (-0.5)
    for m in range(2):
        mask = mask_ref[m] > 0
        mask = jnp.concatenate([mask] * GROUP, axis=0)
        for g in range(width // span):
            queries, keys, values = head_rows(ready_ref, m, half, g * span)
            weights = softmax_weights(queries, keys, mask)
            grad = jnp.concatenate(
                [
                    sequence(attended_ref, m, half, (g * GROUP + j) * HEAD_DIM)
                    for j in range(GROUP)
                ],
                axis=0,
            )
            grad_values = product_left(weights.astype(BF16), grad)
            grad_weights = product_right(grad, values)
            mean = jnp.sum(grad_weights * weights, axis=1, keepdims=True)
            grad_scores = (weights * (grad_weights - mean)).astype(BF16)
            grad_queries = product(grad_scores, keys) * scale
            grad_keys = product_left(grad_scores, queries) * scale
            outs = [grad_queries[j * 2 * half : (j + 1) * 2 * half] for j in range(GROUP)]
            for j, out in enumerate([*outs, grad_keys, grad_values]):
                at = g * span + j * HEAD_DIM
                ready_grad_ref[m * half : (m + 1) * half, at : at + HEAD_DIM] = out[:half]
                ready_grad_ref[(m + 2) * half : (m + 3) * half, at : at + HEAD_DIM] = out[half:]
    low, front = lane_facts(rows)
    cosine, sine = tables_ref[0], tables_ref[1]
    for at in range(width // 128):
        lanes = slice(at * 128, (at + 1) * 128)
        block, grad = qkv_ref[:, lanes], ready_grad_ref[:, lanes]
        heads, gains = block_gains(gains_ref, at)
        inverse = head_scales(block, low)
        normed = block * inverse
        turned = grad * sine
        grad_normed = grad * cosine + jnp.where(
            front, pltpu.roll(turned, 96, 1), -pltpu.roll(turned, 32, 1)
        )
        heads_ref[at : at + 1] = jnp.sum(grad_normed * normed, axis=0, keepdims=True)
        grad_normed = grad_normed * gains
        along = grad_normed * normed
        first = jnp.sum(jnp.where(low, along, 0.0), axis=1, keepdims=True)
        second = jnp.sum(jnp.where(low, 0.0, along), axis=1, keepdims=True)
        mean = jnp.where(low, first, second) * (1.0 / HEAD_DIM)
        raw = inverse * (grad_normed - normed * mean)
        if heads[0] == 2:
            raw = jnp.where(low, grad, raw)
        if heads[1] == 2:
            raw = jnp.where(low, raw, grad)
        proj_ref[:, lanes] = raw.astype(BF16)
    step = width // tiles_ref.shape[0]
    tiles_out(tiles_ref, grad_ref, lambda k: proj_ref[:, k * step : (k + 1) * step])
    copies[0].wait()
    acc_ref[...] = product_right(proj_ref[...], in_buf[0])
    rows_out(acc_ref, core_ref[0], mine_ref, other_ref)


def mixer_call(
    kernel, core, operands, whole, weight_out, in_tiles, outs, scratch=(), behind=()
):
    vmem, any_space = pl.BlockSpec(memory_space=pltpu.VMEM), pl.BlockSpec(memory_space=pl.ANY)
    rows, width = operands[0].shape
    channels = weight_out.shape[0]
    outs = [*outs, ((rows // 2, width), F32), ((rows // 2, width), BF16)]
    return pl.pallas_call(
        ordered(kernel, len(behind)),
        in_specs=[
            pl.BlockSpec(memory_space=pltpu.SMEM),
            *[any_space] * len(behind),
            *[vmem] * len(operands),
            any_space,
            any_space,
        ],
        out_specs=[vmem] * len(outs),
        out_shape=[jax.ShapeDtypeStruct(*out) for out in outs],
        scratch_shapes=[
            pltpu.VMEM((in_tiles[0], width, in_tiles[1]), BF16),
            pltpu.VMEM((channels, width), BF16),
            pltpu.VMEM((rows, width), F32),
            *scratch,
            pltpu.SemaphoreType.DMA((in_tiles[0] + 1,)),
        ],
        compiler_params=pltpu.CompilerParams(vmem_limit_bytes=VMEM_LIMIT),
        cost_estimate=SHORT,
    )(core, *behind, *operands, whole, weight_out)


def conv_forward_call(core, rows, kernel, masks, whole, weight_out):
    count, channels = rows.shape[0], kernel.shape[1]
    outs = [((3, count, channels), BF16), ((count, channels), BF16)]
    operands = (rows, kernel, masks)
    return mixer_call(
        conv_forward_kernel, core, operands, whole, weight_out, (3, channels), outs
    )


def conv_backward_call(core, grad, kernel, masks, projected, tiles, whole, weight_out):
    count, width = grad.shape
    taps, channels = kernel.shape
    outs = [
        (tiles.shape, BF16),
        ((taps, channels), F32),
    ]
    operands = (grad, kernel, masks, projected, tiles)
    return mixer_call(
        conv_backward_kernel, core, operands, whole, weight_out, (3, channels), outs
    )


def attention_forward_call(core, rows, gains, tables, mask, whole, weight_out, qkv_width):
    count, channels = rows.shape[0], weight_out.shape[0]
    outs = [((count, qkv_width), F32), ((count, qkv_width), BF16), ((count, channels), BF16)]
    operands = (rows, gains, tables, mask)
    return mixer_call(
        attention_forward_kernel, core, operands, whole, weight_out, (1, qkv_width), outs
    )


def attention_backward_call(core, grad, gains, tables, mask, qkv, ready, whole, weight_out):
    count, width = grad.shape
    channels, qkv_width = weight_out.shape[0], qkv.shape[1]
    outs = [
        ((4, count, whole_lanes((width + 3 * channels) // 4)), BF16),
        ((qkv_width // 128, 128), F32),
    ]
    scratch = [
        pltpu.VMEM((count, channels), BF16),
        pltpu.VMEM((count, qkv_width), F32),
        pltpu.VMEM((count, qkv_width), BF16),
    ]
    operands = (grad, gains, tables, mask, qkv, ready)
    return mixer_call(
        attention_backward_kernel, core, operands, whole, weight_out, (1, qkv_width), outs, scratch
    )


def conv_masks(segments, taps):
    masks = []
    for lag in range(1, taps):
        same = (segments[:, lag:] == segments[:, :-lag]).astype(F32)
        same = jnp.pad(same, ((0, 0), (lag, 0))).reshape(-1, 1)
        masks.append(jnp.broadcast_to(same, (same.shape[0], 128)))
    return jnp.stack(masks)


def score_mask(segments):
    position = jnp.arange(segments.shape[1])
    allowed = position[:, None] >= position[None, :]
    return (allowed & (segments[:, :, None] == segments[:, None, :])).astype(F32)


def turn_tables(length):
    half = HEAD_DIM // 2
    exponent = jnp.arange(half, dtype=F32) * (2.0 / HEAD_DIM)
    frequency = jnp.exp(-exponent * jnp.log(ROPE_BASE))
    angles = jnp.arange(length, dtype=F32)[:, None] * frequency[None, :]
    tables = jnp.tile(jnp.stack([jnp.cos(angles), jnp.sin(angles)]), (1, 1, 4))
    tables = tables.reshape(2, 2, 1, length // 2, 128)
    return jnp.broadcast_to(tables, (2, 2, 2, length // 2, 128)).reshape(2, 2 * length, 128)


def gain_rows(head_gains):
    kinds = [head_gains[0], head_gains[1], jnp.ones_like(head_gains[0])]
    rows = [jnp.concatenate([a, b]) for a in kinds for b in kinds]
    return jnp.stack(rows)


def head_gain_sums(sums):
    heads = sums.reshape(-1, GROUP + 2, HEAD_DIM)
    return jnp.stack([heads[:, :GROUP].sum((0, 1)), heads[:, GROUP].sum(0)])


def local(
    inputs,
    out_cotangent,
    segments,
    norm_gains,
    conv_kernel,
    qk_gains,
    conv_in,
    attn_qkv,
    mixer_out,
    gate_up,
    down,
):
    section = lax.axis_index("xh")
    first = section == 0
    core = lax.axis_index("c")
    place = lax.axis_index("y") * 4 + lax.axis_index("z")
    xl = lax.axis_index("xl")
    plane = lax.axis_size("y") * lax.axis_size("z")

    shape = inputs.shape[1:]
    width = shape[-1]
    inputs, out_cotangent = inputs.reshape(-1, width), out_cotangent.reshape(-1, width)
    segments = segments[0]
    half = inputs.shape[0]
    rows = 2 * half
    channels = conv_in.shape[2]
    kernel = lax.dynamic_slice_in_dim(conv_kernel, core * channels, channels, 1).astype(F32)
    gains = lax.dynamic_index_in_dim(norm_gains, section, 0, keepdims=False).astype(F32)
    weight_out, weight_pair, weight_down = mixer_out[0], gate_up[0], down[0]
    hidden_units = weight_down.shape[0]
    part = hidden_units // plane
    in_width = 3 * channels
    qkv_width = attn_qkv.shape[1]
    y = lax.axis_index("y")
    core_scalar = jnp.stack([core, section]).astype(jnp.int32)
    xl_scalar = jnp.stack([xl, section, y]).astype(jnp.int32)

    def chosen(from_first, from_second):
        return jnp.where(first, from_first, from_second)

    def gathered(own, axes):
        return lax.all_gather(own, axes, tiled=True)


    both = jnp.concatenate([conv_in.reshape(-1, in_width), attn_qkv], axis=1)
    whole = gathered(both, ("xh", "xl", "y", "z"))

    lanes = -(-part // 256) * 256
    fill = lanes - part
    part_pair = jnp.concatenate(
        [
            jnp.pad(lax.dynamic_slice_in_dim(w, place * part, part, 1), ((0, 0), (0, fill)))
            for w in (weight_pair[0], weight_pair[1])
        ],
        axis=1,
    )
    part_down = lax.dynamic_slice_in_dim(weight_down, place * part, part, 0)
    part_down = jnp.pad(part_down, ((0, fill), (0, 0)))
    masks = conv_masks(segments, kernel.shape[0])
    mask = score_mask(segments)
    tables = turn_tables(segments.shape[1])
    head_gains = gain_rows(qk_gains.astype(F32))
    first_in = inputs.astype(F32)
    normed_own_0 = (normalize(first_in) * gains[0]).astype(BF16)
    normed_0 = spread(normed_own_0)
    cotangent_1 = spread(out_cotangent)
    whole, part_pair, part_down, masks, mask, tables, head_gains, normed_0, cotangent_1 = (
        lax.optimization_barrier(
            (whole, part_pair, part_down, masks, mask, tables, head_gains, normed_0, cotangent_1)
        )
    )

    def inner_norm(hidden):
        return (normalize(hidden) * gains[1]).astype(BF16)

    def inner_back(mine, other, hidden, grad):
        return back_join_call(core_scalar, mine, swapped(other, "c"), hidden, grad, gains[1])

    def mixer_back(grad_hidden, mine, other, layer_in, behind):
        come = swapped(other, "c")
        return back_join_call(behind, mine, come, layer_in, grad_hidden, gains[0])[1:]

    plane_axes = ("y", "z", "c")
    early = gathered(chosen(normed_own_0, out_cotangent), plane_axes)

    projected, gated_0, mine, other = conv_forward_call(
        core_scalar, normed_0, kernel, masks, whole, weight_out
    )
    hidden_0 = first_in + joined(mine, other)
    inner_0 = inner_norm(hidden_0)
    gate, up, mine, other = feed_forward_call(
        False, core_scalar, spread(inner_0), weight_pair, weight_down
    )
    result_0 = (hidden_0 + joined(mine, other)).astype(BF16)

    second_in = lax.ppermute(result_0, "xh", [(0, 1)]).astype(F32)
    normed_own_1 = (normalize(second_in) * gains[0]).astype(BF16)
    qkv, ready, gated_1, mine, other = attention_forward_call(
        core_scalar, spread(normed_own_1), head_gains, tables, mask, whole, weight_out, qkv_width
    )
    hidden_1 = second_in + joined(mine, other)
    inner_1 = inner_norm(hidden_1)
    mine, other, grad_mine, grad_other = ffn_both_call(
        core_scalar, spread(inner_1), cotangent_1, weight_pair, weight_down, (early,)
    )
    result_1 = (hidden_1 + joined(mine, other)).astype(BF16)

    inner_all = gathered(chosen(inner_0, inner_1), plane_axes)
    gated_z = gathered(chosen(gated_0, gated_1), "z")

    grad_hidden_1, grad_mix_1, gain_inner_1 = inner_back(
        grad_mine, grad_other, hidden_1, out_cotangent.astype(F32)
    )
    tiles_1, head_sums, mine, other = attention_backward_call(
        core_scalar,
        spread(grad_mix_1),
        head_gains,
        tables,
        mask,
        qkv,
        ready,
        whole,
        weight_out,
    )
    input_grad_1, gain_outer_1 = mixer_back(grad_hidden_1, mine, other, second_in, core_scalar)

    cotangent = lax.ppermute(input_grad_1, "xh", [(1, 0)])
    late = gathered(chosen(cotangent, normed_own_1), plane_axes)
    mine, other = feed_forward_call(
        True,
        core_scalar,
        spread(cotangent),
        weight_pair,
        weight_down,
        (gate, up),
        (inner_all,),
    )
    grad_hidden_0, grad_mix_0, gain_inner_0 = inner_back(
        mine, other, hidden_0, cotangent.astype(F32)
    )
    tiles, grad_kernel, mine, other = conv_backward_call(
        core_scalar,
        spread(grad_mix_0),
        kernel,
        masks,
        projected,
        tiles_1,
        whole,
        weight_out,
    )
    columns = exchanged(tiles, "z").reshape(4 * rows, -1)
    part_kept = part_forward_call((tiles,), inner_all, part_pair)

    def summed_over_pair(mine, other):
        return mine.astype(F32) + swapped(other, "xl").astype(F32)

    pair_grads, down_mine, down_other = lax.cond(
        first,
        lambda: part_down_call(xl_scalar, late, part_kept, part_down, (columns,)),
        lambda: part_down_call(xl_scalar, early, part_kept, part_down, (columns,)),
    )
    input_grad_0, gain_outer_0 = mixer_back(grad_hidden_0, mine, other, first_in, pair_grads)
    pair_mine, pair_other = part_pair_call(xl_scalar, inner_all, pair_grads, ())
    in_parts, out_mine, out_other = mixer_grads_call(
        xl_scalar, pair_other, columns, gated_z, early, late, plane
    )

    full_kernel = lax.dynamic_update_slice(
        jnp.zeros(conv_kernel.shape, F32), grad_kernel, (0, core * channels)
    )
    small = jnp.concatenate(
        [
            chosen(gain_outer_0, gain_outer_1),
            chosen(gain_inner_0, gain_inner_1),
            full_kernel.reshape(-1),
            head_gain_sums(head_sums).reshape(-1),
        ]
    )
    count = small.shape[0]
    small = jnp.pad(small, (0, -count % 1024)).reshape(-1, 128)
    small = lax.all_gather(small, "c").sum(0)
    small = small + swapped(small, "xl")
    across = swapped(small, "xh")
    small = jnp.concatenate([chosen(small, across), chosen(across, small)])
    small_all = lax.all_gather(small, PLANE)

    come = exchanged(in_parts, PLANE)
    line_mine, line_other = line_sums_call(xl_scalar, come)
    line_come = swapped(line_other, "xl")

    pairs = [(a, swapped(b, "xl")) for a, b in ((pair_mine, pair_other), (down_mine, down_other))]
    total = pair_join_call((in_parts,), pairs)
    arrived = exchanged(total.reshape(plane, -1, 3 * lanes), PLANE)

    kept_lines, sent_lines = finish_call(xl_scalar, total, line_mine, line_come)
    across = swapped(sent_lines, "xh")
    come = across.astype(F32)[:, :, : in_width // 4]
    kept_lines = kept_lines[:, :, : in_width // 4]
    lines = chosen(kept_lines, come).reshape(4, -1, 3, channels // 4)
    grad_conv_in = jnp.moveaxis(lines, 0, 2).reshape(conv_in.shape)
    lines = chosen(come, kept_lines)[:, :, : qkv_width // 4]
    grad_attn_qkv = jnp.moveaxis(lines, 0, 1).reshape(attn_qkv.shape)

    arrived = widened_call(across, arrived)
    lines = [
        jnp.moveaxis(arrived[:, :, k * lanes : k * lanes + part], 0, 1).reshape(-1, hidden_units)
        for k in range(3)
    ]
    grad_gate_up = jnp.stack(lines[:2])[None]
    grad_down = lines[2].T[None]

    total = summed_over_pair(out_mine, out_other).reshape(4, -1, channels)
    sent = total.astype(BF16)
    lines = lax.dynamic_index_in_dim(total, y, 0, keepdims=False)
    for by in range(1, 4):
        block = lax.dynamic_index_in_dim(sent, (y + by) % 4, 0, keepdims=False)
        lines += lax.ppermute(block, "y", around(by)).astype(F32)
    grad_mixer_out = lines.T[None]

    pair = plane_sums_call(arrived, small_all).reshape(2, -1)
    grad_norm_gains = jnp.stack([a[: 2 * width].reshape(2, width) for a in pair])
    grad_conv_kernel = pair[0][2 * width : 5 * width].reshape(conv_kernel.shape)
    grad_qk_gains = pair[1][5 * width : count].reshape(qk_gains.shape)

    activations = chosen(result_0, result_1).reshape(1, 1, *shape)
    input_grads = chosen(input_grad_0, input_grad_1).reshape(1, 1, *shape)
    return (
        activations,
        input_grads,
        grad_norm_gains,
        grad_conv_kernel,
        grad_qk_gains,
        grad_conv_in,
        grad_attn_qkv,
        grad_mixer_out,
        grad_gate_up,
        grad_down,
    )


def solution(mesh):
    wide = Mesh(mesh.devices.reshape(2, 2, 4, 4, 2), AXES)
    dp = ("xl", "y", "z")
    everyone = ("xh", "xl", "y", "z")
    in_specs = (
        P(dp, None, "c", None),
        P(dp, None, "c", None),
        P(dp, None, None),
        P(),
        P(),
        P(),
        P(everyone, None, "c"),
        P(everyone, "c"),
        P("xh", "c", None),
        P("xh", None, None, "c"),
        P("xh", "c", None),
    )
    out_specs = (
        P("xh", dp, None, "c", None),
        P("xh", dp, None, "c", None),
        P(),
        P(),
        P(),
        P(everyone, None, "c"),
        P(everyone, "c"),
        P("xh", "c", dp),
        P("xh", None, dp, "c"),
        P("xh", "c", dp),
    )
    return jax.shard_map(local, mesh=wide, in_specs=in_specs, out_specs=out_specs, check_vma=False)
```

```python
import functools

import jax
import jax.numpy as jnp
from jax import lax
from jax.experimental import pallas as pl
from jax.experimental.pallas import tpu as pltpu
from jax.sharding import Mesh
from jax.sharding import PartitionSpec as P

HEADS = 24
KV_HEADS = 8
HEAD_DIM = 64
GROUP = HEADS // KV_HEADS

EPSILON = 1e-05
ROPE_BASE = 1000000.0
MASKED_SCORE = -1e30

F32 = jnp.float32
BF16 = jnp.bfloat16

PLANE = ("y", "z")
AXES = ("xh", "xl", "y", "z", "c")


def product(left, right):
    return jnp.dot(left, right, preferred_element_type=F32)


def product_left(left, right):
    return lax.dot_general(left, right, (((0,), (0,)), ((), ())), preferred_element_type=F32)


def product_right(left, right):
    return lax.dot_general(left, right, (((1,), (1,)), ((), ())), preferred_element_type=F32)


def swapped(shard, axis):
    return lax.ppermute(shard, axis, [(0, 1), (1, 0)])


def spread(own):
    return lax.all_gather(own, "c", tiled=True)


def joined(mine, other):
    return mine + swapped(other, "c").astype(F32)


def mean_last(values):
    return jnp.mean(values, axis=-1, keepdims=True)


def inverse_rms(values):
    return lax.rsqrt(mean_last(values * values) + EPSILON)


def normalize(values):
    return values * inverse_rms(values)


def around(by):
    return [(k, (k + by) % 4) for k in range(4)]


def exchanged(tiles, axes):
    return lax.all_to_all(tiles, axes, 0, 0, tiled=True)


def ffn_grads(grad_active, gate, up):
    sigmoid = jax.nn.sigmoid(gate)
    grad_gate = grad_active * up * sigmoid * (1.0 + gate * (1.0 - sigmoid))
    grad_up = grad_active * gate * sigmoid
    return grad_gate.astype(BF16), grad_up.astype(BF16)


VMEM_LIMIT = 56 * 1024 * 1024
SHORT = pl.CostEstimate(flops=1, bytes_accessed=1, transcendentals=0)


def whole_lanes(columns):
    return -(-columns // 128) * 128


def ordered(kernel, count):
    def body(scalar_ref, *refs):
        kernel(scalar_ref, *refs[count:])

    return body


def unit_tiles(units, tile):
    short = units % tile
    tiles = [(0, short)] if short else []
    return tiles + [(at, tile) for at in range(short, units, tile)]


def streamed(tiles, copies, work):
    for copy in copies(0, 0):
        copy.start()
    for k in range(len(tiles)):
        slot = k % 2
        if k + 1 < len(tiles):
            for copy in copies(k + 1, 1 - slot):
                copy.start()
        for copy in copies(k, slot):
            copy.wait()
        work(k, slot)


def ffn_forward_kernel(
    tiles, core_ref, rows_ref, pair_ref, down_ref, gate_ref, up_ref, mine_ref, other_ref,
    pair_buf, down_buf, gate_buf, up_buf, acc_ref, sems, out_sems,
):
    def copies(k, slot):
        at, size = tiles[k]
        return [
            pltpu.make_async_copy(
                pair_ref.at[0, :, pl.ds(at, size)],
                pair_buf.at[slot, :, pl.ds(0, size)],
                sems.at[slot, 0],
            ),
            pltpu.make_async_copy(
                pair_ref.at[1, :, pl.ds(at, size)],
                pair_buf.at[slot, :, pl.ds(size, size)],
                sems.at[slot, 1],
            ),
            pltpu.make_async_copy(
                down_ref.at[pl.ds(at, size)], down_buf.at[slot, pl.ds(0, size)], sems.at[slot, 2]
            ),
        ]

    def kept(k):
        here = (slice(None), pl.ds(*tiles[k]))
        return [
            pltpu.make_async_copy(gate_buf.at[here], gate_ref.at[here], out_sems.at[k, 0]),
            pltpu.make_async_copy(up_buf.at[here], up_ref.at[here], out_sems.at[k, 1]),
        ]

    def work(k, slot):
        at, size = tiles[k]
        both = product(rows_ref[...], pair_buf[slot, :, : 2 * size])
        gate, up = both[:, :size], both[:, size:]
        gate_buf[:, at : at + size] = gate.astype(BF16)
        up_buf[:, at : at + size] = up.astype(BF16)
        for copy in kept(k):
            copy.start()
        active = (gate * jax.nn.sigmoid(gate) * up).astype(BF16)
        part = product(active, down_buf[slot, :size])
        if k == 0:
            acc_ref[...] = part
        else:
            acc_ref[...] += part

    streamed(tiles, copies, work)
    rows_out(acc_ref, core_ref[0], mine_ref, other_ref)
    for k in range(len(tiles)):
        for copy in kept(k):
            copy.wait()


def ffn_backward_kernel(
    tiles, core_ref, rows_ref, gate_ref, up_ref, pair_ref, down_ref, mine_ref, other_ref,
    pair_buf, down_buf, gate_buf, up_buf, acc_ref, sems,
):
    def copies(k, slot):
        at, size = tiles[k]
        columns, place = pl.ds(at, size), pl.ds(0, size)
        return [
            pltpu.make_async_copy(
                down_ref.at[columns], down_buf.at[slot, place], sems.at[slot, 0]
            ),
            pltpu.make_async_copy(
                gate_ref.at[:, columns], gate_buf.at[slot, :, place], sems.at[slot, 1]
            ),
            pltpu.make_async_copy(
                up_ref.at[:, columns], up_buf.at[slot, :, place], sems.at[slot, 2]
            ),
            pltpu.make_async_copy(
                pair_ref.at[0, :, columns], pair_buf.at[slot, :, place], sems.at[slot, 3]
            ),
            pltpu.make_async_copy(
                pair_ref.at[1, :, columns],
                pair_buf.at[slot, :, pl.ds(size, size)],
                sems.at[slot, 4],
            ),
        ]

    def work(k, slot):
        _, size = tiles[k]
        grad_active = product_right(rows_ref[...], down_buf[slot, :size])
        grads = ffn_grads(
            grad_active,
            gate_buf[slot, :, :size].astype(F32),
            up_buf[slot, :, :size].astype(F32),
        )
        part = product_right(jnp.concatenate(grads, axis=1), pair_buf[slot, :, : 2 * size])
        if k == 0:
            acc_ref[...] = part
        else:
            acc_ref[...] += part

    streamed(tiles, copies, work)
    rows_out(acc_ref, core_ref[0], mine_ref, other_ref)


def ffn_both_kernel(
    tiles, core_ref, rows_ref, grad_ref, pair_ref, down_ref,
    mine_ref, other_ref, grad_mine_ref, grad_other_ref, pair_buf, down_buf, acc_ref, grad_acc_ref, sems,
):
    def copies(k, slot):
        at, size = tiles[k]
        columns, place = pl.ds(at, size), pl.ds(0, size)
        return [
            pltpu.make_async_copy(
                pair_ref.at[0, :, columns], pair_buf.at[slot, :, place], sems.at[slot, 0]
            ),
            pltpu.make_async_copy(
                pair_ref.at[1, :, columns],
                pair_buf.at[slot, :, pl.ds(size, size)],
                sems.at[slot, 1],
            ),
            pltpu.make_async_copy(
                down_ref.at[columns], down_buf.at[slot, place], sems.at[slot, 2]
            ),
        ]

    def work(k, slot):
        _, size = tiles[k]
        both = product(rows_ref[...], pair_buf[slot, :, : 2 * size])
        grad_active = product_right(grad_ref[...], down_buf[slot, :size])
        gate, up = both[:, :size], both[:, size:]
        active = (gate * jax.nn.sigmoid(gate) * up).astype(BF16)
        grads = jnp.concatenate(ffn_grads(grad_active, gate, up), axis=1)
        part = product(active, down_buf[slot, :size])
        grad_part = product_right(grads, pair_buf[slot, :, : 2 * size])
        if k == 0:
            acc_ref[...], grad_acc_ref[...] = part, grad_part
        else:
            acc_ref[...] += part
            grad_acc_ref[...] += grad_part

    streamed(tiles, copies, work)
    rows_out(acc_ref, core_ref[0], mine_ref, other_ref)
    rows_out(grad_acc_ref, core_ref[0], grad_mine_ref, grad_other_ref)


def ffn_both_call(core, rows, grad, pair, down, behind):
    count, width = rows.shape
    units = down.shape[0]
    tile = 768
    vmem, any_space = pl.BlockSpec(memory_space=pltpu.VMEM), pl.BlockSpec(memory_space=pl.ANY)
    half = (count // 2, width)
    return pl.pallas_call(
        ordered(functools.partial(ffn_both_kernel, unit_tiles(units, tile)), len(behind)),
        in_specs=[
            pl.BlockSpec(memory_space=pltpu.SMEM),
            *[any_space] * len(behind),
            vmem,
            vmem,
            any_space,
            any_space,
        ],
        out_specs=[vmem] * 4,
        out_shape=[jax.ShapeDtypeStruct(half, F32), jax.ShapeDtypeStruct(half, BF16)] * 2,
        scratch_shapes=[
            pltpu.VMEM((2, width, 2 * tile), BF16),
            pltpu.VMEM((2, tile, width), BF16),
            pltpu.VMEM((count, width), F32),
            pltpu.VMEM((count, width), F32),
            pltpu.SemaphoreType.DMA((2, 3)),
        ],
        compiler_params=pltpu.CompilerParams(vmem_limit_bytes=VMEM_LIMIT),
        cost_estimate=SHORT,
    )(core, *behind, rows, grad, pair, down)


def feed_forward_call(backward, core, rows, pair, down, saved=(), behind=()):
    count, width = rows.shape
    units = down.shape[0]
    tile = 768
    tiles = unit_tiles(units, tile)
    vmem, any_space = pl.BlockSpec(memory_space=pltpu.VMEM), pl.BlockSpec(memory_space=pl.ANY)
    scalar = pl.BlockSpec(memory_space=pltpu.SMEM)
    out_shape = [
        jax.ShapeDtypeStruct((count // 2, width), F32),
        jax.ShapeDtypeStruct((count // 2, width), BF16),
    ]
    out_specs = [vmem, vmem]
    buffers = [pltpu.VMEM((2, width, 2 * tile), BF16), pltpu.VMEM((2, tile, width), BF16)]
    acc = pltpu.VMEM((count, width), F32)
    if backward:
        body = functools.partial(ffn_backward_kernel, tiles)
        in_specs = [scalar, vmem, any_space, any_space, any_space, any_space]
        buffers += [pltpu.VMEM((2, count, tile), BF16)] * 2
        scratch = [*buffers, acc, pltpu.SemaphoreType.DMA((2, 5))]
    else:
        body = functools.partial(ffn_forward_kernel, tiles)
        in_specs = [scalar, vmem, any_space, any_space]
        out_shape = [jax.ShapeDtypeStruct((count, units), BF16)] * 2 + out_shape
        out_specs = [any_space, any_space, *out_specs]
        buffers += [pltpu.VMEM((count, units), BF16)] * 2
        scratch = [*buffers, acc]
        scratch += [pltpu.SemaphoreType.DMA((2, 3)), pltpu.SemaphoreType.DMA((len(tiles), 2))]
    in_specs = [scalar, *[any_space] * len(behind), *in_specs[1:]]
    return pl.pallas_call(
        ordered(body, len(behind)),
        in_specs=in_specs,
        out_specs=out_specs,
        out_shape=out_shape,
        scratch_shapes=scratch,
        compiler_params=pltpu.CompilerParams(vmem_limit_bytes=VMEM_LIMIT),
        cost_estimate=SHORT,
    )(core, *behind, rows, *saved, pair, down)


def part_forward_kernel(*refs):
    rows_ref, pair_ref, kept_ref = refs[-3:]
    both = product(rows_ref[...], pair_ref[...])
    units = both.shape[1] // 2
    gate, up = both[:, :units], both[:, units:]
    sigmoid = jax.nn.sigmoid(gate)
    silu = gate * sigmoid
    kept_ref[:, :units] = (up * (sigmoid + silu * (1.0 - sigmoid))).astype(BF16)
    kept_ref[:, units : 2 * units] = silu.astype(BF16)
    kept_ref[:, 2 * units :] = (silu * up).astype(BF16)


def part_forward_call(behind, rows, pair):
    tokens, width = rows.shape
    units = pair.shape[1] // 2
    tile = 1024
    return pl.pallas_call(
        part_forward_kernel,
        grid=(tokens // tile,),
        in_specs=[
            *[pl.BlockSpec(memory_space=pl.ANY)] * len(behind),
            pl.BlockSpec((tile, width), lambda i: (i, 0)),
            pl.BlockSpec((width, 2 * units), lambda i: (0, 0)),
        ],
        out_specs=pl.BlockSpec((tile, 3 * units), lambda i: (i, 0)),
        out_shape=jax.ShapeDtypeStruct((tokens, 3 * units), BF16),
        compiler_params=pltpu.CompilerParams(vmem_limit_bytes=VMEM_LIMIT),
        cost_estimate=pl.CostEstimate(
            flops=8 * tokens * width * units, bytes_accessed=2 * tokens * width, transcendentals=0
        ),
    )(*behind, rows, pair)


def pair_out(acc_ref, here, mine_ref, other_ref):
    rows = mine_ref.shape[0]
    for ref, half in ((mine_ref, here), (other_ref, 1 - here)):
        ref[...] = acc_ref[pl.ds(pl.multiple_of(half * rows, rows), rows)].astype(BF16)


def accumulated(acc_ref, part, finish):
    step = pl.program_id(0)

    @pl.when(step == 0)
    def _():
        acc_ref[...] = part

    @pl.when(step > 0)
    def _():
        acc_ref[...] += part

    pl.when(step == pl.num_programs(0) - 1)(finish)


def part_down_kernel(here_ref, grad_ref, kept_ref, down_ref, pair_ref, mine_ref, other_ref, acc_ref):
    grad = grad_ref[...]
    units = down_ref.shape[0]
    grad_active = product_right(grad, down_ref[...])
    for k in range(2):
        lanes = slice(k * units, (k + 1) * units)
        pair_ref[:, lanes] = (grad_active * kept_ref[:, lanes].astype(F32)).astype(BF16)
    accumulated(
        acc_ref,
        product_left(grad, kept_ref[:, 2 * units :]),
        lambda: pair_out(acc_ref, here_ref[0], mine_ref, other_ref),
    )


def part_pair_kernel(here_ref, rows_ref, pair_ref, mine_ref, other_ref, acc_ref):
    accumulated(
        acc_ref,
        product_left(rows_ref[...], pair_ref[...]),
        lambda: pair_out(acc_ref, here_ref[0], mine_ref, other_ref),
    )


def part_call(kernel, here, operands, fixed, outs, result, flops, behind=()):
    tokens = operands[0].shape[0]
    tile = 1024
    by_tokens = lambda width: pl.BlockSpec((tile, width), lambda i, h: (i, 0))
    entire = lambda shape: pl.BlockSpec(shape, lambda i, h: (0, 0))
    half = (result[0] // 2, result[1])
    return pl.pallas_call(
        ordered(kernel, len(behind)),
        grid_spec=pltpu.PrefetchScalarGridSpec(
            num_scalar_prefetch=1,
            grid=(tokens // tile,),
            in_specs=[pl.BlockSpec(memory_space=pl.ANY)] * len(behind)
            + [by_tokens(a.shape[1]) for a in operands]
            + [entire(a.shape) for a in fixed],
            out_specs=[by_tokens(width) for width in outs] + [entire(half)] * 2,
            scratch_shapes=[pltpu.VMEM(result, F32)],
        ),
        out_shape=[jax.ShapeDtypeStruct((tokens, width), BF16) for width in outs]
        + [jax.ShapeDtypeStruct(half, BF16)] * 2,
        compiler_params=pltpu.CompilerParams(vmem_limit_bytes=VMEM_LIMIT),
        cost_estimate=SHORT,
    )(here, *behind, *operands, *fixed)


def part_down_call(here, grad, kept, down, behind):
    tokens, width = grad.shape
    units = down.shape[0]
    flops = 4 * tokens * width * units
    return part_call(
        part_down_kernel,
        here,
        (grad, kept),
        (down,),
        (2 * units,),
        (width, units),
        flops,
        behind,
    )


def part_pair_call(here, inner, pair, behind):
    (tokens, width), columns = inner.shape, pair.shape[1]
    flops = 2 * tokens * width * columns
    return part_call(
        part_pair_kernel, here, (inner, pair), (), (), (width, columns), flops, behind
    )


def back_join_kernel(
    behind_ref, mine_ref, come_ref, values_ref, base_ref, gain_ref, wide_ref, low_ref, sums_ref
):
    grad = mine_ref[...] + come_ref[...].astype(F32)
    values = values_ref[...]
    inverse = inverse_rms(values)
    normed = values * inverse
    scaled = grad * gain_ref[...]
    sums_ref[...] = jnp.sum(grad * normed, axis=0, keepdims=True)
    total = base_ref[...] + inverse * (scaled - normed * mean_last(scaled * normed))
    wide_ref[...] = total
    low_ref[...] = total.astype(BF16)


def back_join_call(behind, mine, come, values, base, gain):
    vmem = pl.BlockSpec(memory_space=pltpu.VMEM)
    shape = values.shape
    wide, low, sums = pl.pallas_call(
        back_join_kernel,
        in_specs=[pl.BlockSpec(memory_space=pl.ANY), *[vmem] * 5],
        out_specs=[vmem] * 3,
        out_shape=[
            jax.ShapeDtypeStruct(shape, F32),
            jax.ShapeDtypeStruct(shape, BF16),
            jax.ShapeDtypeStruct((1, shape[1]), F32),
        ],
        compiler_params=pltpu.CompilerParams(vmem_limit_bytes=VMEM_LIMIT),
        cost_estimate=SHORT,
    )(behind, mine, come, values, base, gain[None])
    return wide, low, sums[0]


def pair_join_kernel(count, *refs):
    *refs, out_ref = refs[count:]
    at = 0
    for mine_ref, come_ref in zip(refs[::2], refs[1::2]):
        size = mine_ref.shape[-1]
        total = mine_ref[...].astype(F32) + come_ref[...].astype(F32)
        out_ref[..., at : at + size] = total.astype(BF16)
        at += size


def pair_join_call(behind, pairs):
    vmem = pl.BlockSpec(memory_space=pltpu.VMEM)
    operands = [a for pair in pairs for a in pair]
    shape = (*operands[0].shape[:-1], sum(mine.shape[-1] for mine, _ in pairs))
    return pl.pallas_call(
        functools.partial(pair_join_kernel, len(behind)),
        in_specs=[pl.BlockSpec(memory_space=pl.ANY)] * len(behind) + [vmem] * len(operands),
        out_specs=vmem,
        out_shape=jax.ShapeDtypeStruct(shape, BF16),
        compiler_params=pltpu.CompilerParams(vmem_limit_bytes=VMEM_LIMIT),
        cost_estimate=SHORT,
    )(*behind, *operands)


def lines_kernel(behind_ref, arrived_ref, pair_ref, down_ref):
    plane, _, lanes = arrived_ref.shape
    lanes //= 3
    part = down_ref.shape[1] // plane
    for k in range(plane):
        rows = arrived_ref[k].astype(F32)
        at = slice(k * part, (k + 1) * part)
        pair_ref[0, :, at] = rows[:, :part]
        pair_ref[1, :, at] = rows[:, lanes : lanes + part]
        down_ref[:, at] = rows[:, 2 * lanes : 2 * lanes + part]


def lines_call(behind, arrived, units):
    vmem = pl.BlockSpec(memory_space=pltpu.VMEM)
    rows = arrived.shape[1]
    return pl.pallas_call(
        lines_kernel,
        in_specs=[pl.BlockSpec(memory_space=pl.ANY), vmem],
        out_specs=[vmem] * 2,
        out_shape=[
            jax.ShapeDtypeStruct((2, rows, units), F32),
            jax.ShapeDtypeStruct((rows, units), F32),
        ],
        compiler_params=pltpu.CompilerParams(vmem_limit_bytes=VMEM_LIMIT),
        cost_estimate=SHORT,
    )(behind, arrived)


def line_sums_kernel(places_ref, come_ref, mine_ref, other_ref, acc_ref):
    here = places_ref[0]
    count, rows, _ = mine_ref.shape
    for k in range(count):
        tiles = [come_ref[m * count + k].astype(F32) for m in range(come_ref.shape[0] // count)]
        acc_ref[...] = functools.reduce(jnp.add, tiles)
        mine_ref[k] = acc_ref[pl.ds(pl.multiple_of(here * rows, rows), rows)]
        other = acc_ref[pl.ds(pl.multiple_of((1 - here) * rows, rows), rows)]
        other_ref[k] = other.astype(BF16)


def line_sums_call(places, come):
    vmem = pl.BlockSpec(memory_space=pltpu.VMEM)
    plane, block, size = come.shape
    lines = (4, block // 2, size)
    return pl.pallas_call(
        line_sums_kernel,
        in_specs=[pl.BlockSpec(memory_space=pltpu.SMEM), vmem],
        out_specs=[vmem] * 2,
        out_shape=[jax.ShapeDtypeStruct(lines, F32), jax.ShapeDtypeStruct(lines, BF16)],
        scratch_shapes=[pltpu.VMEM((block, size), F32)],
        compiler_params=pltpu.CompilerParams(vmem_limit_bytes=VMEM_LIMIT),
        cost_estimate=SHORT,
    )(places, come)


def finish_kernel(
    places_ref, behind_ref, mine_ref, come_ref, kept_ref, sent_ref, acc_ref
):
    section = places_ref[1]
    short = kept_ref.shape[1]
    acc_ref[...] = mine_ref[...] + come_ref[...].astype(F32)
    kept_ref[...] = acc_ref[:, pl.ds(pl.multiple_of(section * short, short), short)]
    sent = acc_ref[:, pl.ds(pl.multiple_of((1 - section) * short, short), short)]
    sent_ref[...] = sent.astype(BF16)


def plane_sums_kernel(behind_ref, small_ref, sums_ref):
    sums_ref[...] = jnp.sum(small_ref[...], axis=0)


def plane_sums_call(behind, small):
    vmem = pl.BlockSpec(memory_space=pltpu.VMEM)
    return pl.pallas_call(
        plane_sums_kernel,
        in_specs=[pl.BlockSpec(memory_space=pl.ANY), vmem],
        out_specs=vmem,
        out_shape=jax.ShapeDtypeStruct(small.shape[1:], F32),
        compiler_params=pltpu.CompilerParams(vmem_limit_bytes=VMEM_LIMIT),
        cost_estimate=SHORT,
    )(behind, small)


def finish_call(places, behind, mine, come):
    vmem = pl.BlockSpec(memory_space=pltpu.VMEM)
    count, rows, size = mine.shape
    lines = (count, rows // 2, size)
    return pl.pallas_call(
        finish_kernel,
        in_specs=[
            pl.BlockSpec(memory_space=pltpu.SMEM),
            pl.BlockSpec(memory_space=pl.ANY),
            *[vmem] * 2,
        ],
        out_specs=[vmem] * 2,
        out_shape=[jax.ShapeDtypeStruct(lines, F32), jax.ShapeDtypeStruct(lines, BF16)],
        scratch_shapes=[pltpu.VMEM(mine.shape, F32)],
        compiler_params=pltpu.CompilerParams(vmem_limit_bytes=VMEM_LIMIT),
        cost_estimate=SHORT,
    )(places, behind, mine, come)


def mixer_in_kernel(
    places_ref, behind_ref, columns_ref, early_ref, late_ref, parts_ref, normed_ref, in_ref, sem
):
    section, y = places_ref[1], places_ref[2]

    def copy(all_ref):
        rows = normed_ref.shape[0]
        start = pl.multiple_of(y * rows, rows)
        return pltpu.make_async_copy(all_ref.at[pl.ds(start, rows)], normed_ref, sem)

    @pl.when(section == 0)
    def _():
        copy(early_ref).start()

    @pl.when(section > 0)
    def _():
        copy(late_ref).start()

    copy(early_ref).wait()
    mix = columns_ref.shape[1] - in_ref.shape[1]
    in_ref[...] = product_left(normed_ref[...], columns_ref[:, mix:])
    plane, block, _ = parts_ref.shape
    short = block // 4
    for k in range(plane):
        for half in range(2):
            for s in range(2):
                start = ((2 * s + half) * plane + k) * short
                place = (2 * half + s) * short
                rows_in = in_ref[start : start + short]
                parts_ref[k, place : place + short] = rows_in.astype(BF16)


def mixer_in_call(places, behind, columns, early, late, plane):
    vmem, any_space = pl.BlockSpec(memory_space=pltpu.VMEM), pl.BlockSpec(memory_space=pl.ANY)
    tokens, width = columns.shape[0], early.shape[1]
    size = columns.shape[1] - width // 4
    return pl.pallas_call(
        mixer_in_kernel,
        in_specs=[pl.BlockSpec(memory_space=pltpu.SMEM), any_space, vmem, any_space, any_space],
        out_specs=vmem,
        out_shape=jax.ShapeDtypeStruct((plane, width // plane, size), BF16),
        scratch_shapes=[
            pltpu.VMEM((tokens, width), BF16),
            pltpu.VMEM((width, size), F32),
            pltpu.SemaphoreType.DMA,
        ],
        compiler_params=pltpu.CompilerParams(vmem_limit_bytes=VMEM_LIMIT),
        cost_estimate=SHORT,
    )(places, behind, columns, early, late)


def mixer_out_kernel(places_ref, behind_ref, columns_ref, gated_ref, mine_ref, other_ref, out_ref):
    out_ref[...] = product_left(columns_ref[:, : out_ref.shape[0]], gated_ref[...])
    pair_out(out_ref, places_ref[0], mine_ref, other_ref)


def mixer_out_call(places, behind, columns, gated, mix):
    vmem = pl.BlockSpec(memory_space=pltpu.VMEM)
    channels = gated.shape[1]
    half = jax.ShapeDtypeStruct((mix // 2, channels), BF16)
    return pl.pallas_call(
        mixer_out_kernel,
        in_specs=[
            pl.BlockSpec(memory_space=pltpu.SMEM),
            pl.BlockSpec(memory_space=pl.ANY),
            vmem,
            vmem,
        ],
        out_specs=[vmem] * 2,
        out_shape=[half, half],
        scratch_shapes=[pltpu.VMEM((mix, channels), F32)],
        compiler_params=pltpu.CompilerParams(vmem_limit_bytes=VMEM_LIMIT),
        cost_estimate=SHORT,
    )(places, behind, columns, gated)


def load_all(copies):
    for copy in copies:
        copy.start()


def in_time(rows):
    half = rows.shape[0] // 4
    return jnp.concatenate([rows[k * half : (k + 1) * half] for k in (0, 2, 1, 3)], axis=0)


def rows_out(acc_ref, core, mine_ref, other_ref):
    half = mine_ref.shape[0]
    mine_ref[...] = acc_ref[pl.ds(pl.multiple_of(core * half, half), half)]
    rest = acc_ref[pl.ds(pl.multiple_of((1 - core) * half, half), half)]
    other_ref[...] = rest.astype(BF16)


def weight_copies(whole_ref, out_ref, in_buf, out_buf, sems, start):
    size = in_buf.shape[2]
    copies = [
        pltpu.make_async_copy(
            whole_ref.at[:, pl.ds(start + k * size, size)], in_buf.at[k], sems.at[k]
        )
        for k in range(in_buf.shape[0])
    ]
    return copies, pltpu.make_async_copy(out_ref, out_buf, sems.at[len(copies)])


def conv_taps(mixed, kernel, masks):
    terms = [mixed]
    for lag in range(1, len(masks) + 1):
        terms.append(pltpu.roll(mixed, lag, 0) * masks[lag - 1])
    taps = kernel.shape[0]
    total = kernel[taps - 1 : taps] * terms[0]
    for lag in range(1, taps):
        total = total + kernel[taps - 1 - lag : taps - lag] * terms[lag]
    return terms, total


def conv_forward_kernel(
    core_ref, rows_ref, kernel_ref, masks_ref, whole_ref, out_ref,
    proj_ref, gated_ref, mine_ref, other_ref, in_buf, out_buf, acc_ref, sems,
):
    copies, last = weight_copies(whole_ref, out_ref, in_buf, out_buf, sems, 0)
    load_all([*copies, last])
    rows = rows_ref[...]
    parts = []
    for k, copy in enumerate(copies):
        copy.wait()
        part = product(rows, in_buf[k])
        proj_ref[k] = part.astype(BF16)
        parts.append(in_time(part))
    masks = [masks_ref[lag] for lag in range(masks_ref.shape[0])]
    gated = []
    for at in range(0, parts[0].shape[1], 128):
        before, after, signal = [part[:, at : at + 128] for part in parts]
        _, total = conv_taps(before * signal, kernel_ref[:, at : at + 128], masks)
        gated.append((after * total).astype(BF16))
    gated = in_time(jnp.concatenate(gated, axis=1))
    gated_ref[...] = gated
    last.wait()
    acc_ref[...] = product(gated, out_buf[...])
    rows_out(acc_ref, core_ref[0], mine_ref, other_ref)


def tiles_out(tiles_ref, grad_ref, columns):
    count, rows, size = tiles_ref.shape
    step = grad_ref.shape[1] // (2 * count * count)
    for k in range(count):
        starts = range(k * step, grad_ref.shape[1], count * step)
        parts = [grad_ref[:, at : at + step] for at in starts]
        parts.append(columns(k))
        spare = size - sum(part.shape[1] for part in parts)
        tiles_ref[k] = jnp.concatenate([*parts, jnp.zeros((rows, spare), BF16)], axis=1)


def conv_backward_kernel(
    core_ref, grad_ref, kernel_ref, masks_ref, proj_ref, other_tiles_ref,
    whole_ref, out_ref, tiles_ref, taps_ref, mine_ref, other_ref, in_buf, out_buf, acc_ref, sems,
):
    copies, last = weight_copies(whole_ref, out_ref, in_buf, out_buf, sems, 0)
    load_all([last, *copies])
    last.wait()
    grad_gated = in_time(product_right(grad_ref[...], out_buf[...]))
    parts = [in_time(proj_ref[k].astype(F32)) for k in range(3)]
    masks = [masks_ref[lag] for lag in range(masks_ref.shape[0])]
    rows = grad_gated.shape[0]
    grads = [[], [], []]
    for at in range(0, grad_gated.shape[1], 128):
        before, after, signal = [part[:, at : at + 128] for part in parts]
        kernel = kernel_ref[:, at : at + 128]
        terms, total = conv_taps(before * signal, kernel, masks)
        grad = grad_gated[:, at : at + 128]
        grad_total = grad * after
        taps = kernel.shape[0]
        grad_mixed = kernel[taps - 1 : taps] * grad_total
        for lag in range(1, taps):
            sent = pltpu.roll(grad_total * masks[lag - 1], rows - lag, 0)
            grad_mixed = grad_mixed + kernel[taps - 1 - lag : taps - lag] * sent
        for lag in range(taps):
            taps_ref[taps - 1 - lag : taps - lag, at : at + 128] = jnp.sum(
                grad_total * terms[lag], axis=0, keepdims=True
            )
        for k, value in enumerate((grad_mixed * signal, grad * total, grad_mixed * before)):
            grads[k].append(value.astype(BF16))
    grads = [in_time(jnp.concatenate(g, axis=1)) for g in grads]
    step = grads[0].shape[1] // tiles_ref.shape[0]

    @pl.when(core_ref[1] == 0)
    def _():
        tiles_out(
            tiles_ref,
            grad_ref,
            lambda k: jnp.concatenate([g[:, k * step : (k + 1) * step] for g in grads], axis=1),
        )

    @pl.when(core_ref[1] > 0)
    def _():
        tiles_ref[...] = other_tiles_ref[...]

    for k, copy in enumerate(copies):
        copy.wait()
        part = product_right(grads[k], in_buf[k])
        acc_ref[...] = part if k == 0 else acc_ref[...] + part
    rows_out(acc_ref, core_ref[0], mine_ref, other_ref)


def head_kind(head):
    return min(max(head % (GROUP + 2) - GROUP + 1, 0), 2)


def lane_facts(rows):
    lane = lax.broadcasted_iota(jnp.int32, (rows, 128), 1)
    return lane < HEAD_DIM, lax.rem(lane, HEAD_DIM) < HEAD_DIM // 2


def head_scales(block, low):
    squares = block * block
    first = jnp.sum(jnp.where(low, squares, 0.0), axis=1, keepdims=True)
    second = jnp.sum(jnp.where(low, 0.0, squares), axis=1, keepdims=True)
    return lax.rsqrt(jnp.where(low, first, second) * (1.0 / HEAD_DIM) + EPSILON)


def block_gains(gains_ref, at):
    heads = [head_kind(2 * at), head_kind(2 * at + 1)]
    return heads, gains_ref[3 * heads[0] + heads[1] : 3 * heads[0] + heads[1] + 1]


def attention_forward_kernel(
    core_ref, rows_ref, gains_ref, tables_ref, mask_ref, whole_ref, out_ref,
    qkv_ref, ready_ref, gated_ref, mine_ref, other_ref, in_buf, out_buf, acc_ref, sems,
):
    copies, last = weight_copies(
        whole_ref, out_ref, in_buf, out_buf, sems, whole_ref.shape[1] - in_buf.shape[2]
    )
    load_all([*copies, last])
    copies[0].wait()
    qkv_ref[...] = product(rows_ref[...], in_buf[0])
    rows, width = qkv_ref.shape
    low, front = lane_facts(rows)
    cosine, sine = tables_ref[0], tables_ref[1]
    for at in range(width // 128):
        block = qkv_ref[:, at * 128 : (at + 1) * 128]
        heads, gains = block_gains(gains_ref, at)
        normed = block * head_scales(block, low) * gains
        turned = jnp.where(front, -pltpu.roll(normed, 96, 1), pltpu.roll(normed, 32, 1))
        ready = normed * cosine + turned * sine
        if heads[0] == 2:
            ready = jnp.where(low, block, ready)
        if heads[1] == 2:
            ready = jnp.where(low, ready, block)
        ready_ref[:, at * 128 : (at + 1) * 128] = ready.astype(BF16)
    half = rows // 4
    span = (GROUP + 2) * HEAD_DIM
    for m in range(2):
        mask = mask_ref[m] > 0
        mask = jnp.concatenate([mask] * GROUP, axis=0)
        for g in range(width // span):
            queries, keys, values = head_rows(ready_ref, m, half, g * span)
            weights = softmax_weights(queries, keys, mask)
            attended = product(weights.astype(BF16), values).astype(BF16)
            for j in range(GROUP):
                at = (g * GROUP + j) * HEAD_DIM
                head = attended[j * 2 * half : (j + 1) * 2 * half]
                gated_ref[m * half : (m + 1) * half, at : at + HEAD_DIM] = head[:half]
                gated_ref[(m + 2) * half : (m + 3) * half, at : at + HEAD_DIM] = head[half:]
    last.wait()
    acc_ref[...] = product(gated_ref[...], out_buf[...])
    rows_out(acc_ref, core_ref[0], mine_ref, other_ref)


def sequence(ref, m, half, at):
    columns = slice(at, at + HEAD_DIM)
    return jnp.concatenate(
        [ref[m * half : (m + 1) * half, columns], ref[(m + 2) * half : (m + 3) * half, columns]],
        axis=0,
    )


def head_rows(ref, m, half, at):
    heads = [sequence(ref, m, half, at + j * HEAD_DIM) for j in range(GROUP + 2)]
    return jnp.concatenate(heads[:GROUP], axis=0), heads[GROUP], heads[GROUP + 1]


def softmax_weights(queries, keys, mask):
    scores = jnp.where(mask, product_right(queries, keys) * HEAD_DIM ** (-0.5), MASKED_SCORE)
    terms = jnp.exp(scores - jnp.max(scores, axis=1, keepdims=True))
    return terms / jnp.sum(terms, axis=1, keepdims=True)


def attention_backward_kernel(
    core_ref, grad_ref, gains_ref, tables_ref, mask_ref, qkv_ref, ready_ref,
    whole_ref, out_ref, tiles_ref, heads_ref, mine_ref, other_ref,
    in_buf, out_buf, acc_ref, attended_ref, ready_grad_ref, proj_ref, sems,
):
    copies, last = weight_copies(
        whole_ref, out_ref, in_buf, out_buf, sems, whole_ref.shape[1] - in_buf.shape[2]
    )
    load_all([last, *copies])
    last.wait()
    attended_ref[...] = product_right(grad_ref[...], out_buf[...]).astype(BF16)
    rows, width = qkv_ref.shape
    half = rows // 4
    span = (GROUP + 2) * HEAD_DIM
    scale = HEAD_DIM ** (-0.5)
    for m in range(2):
        mask = mask_ref[m] > 0
        mask = jnp.concatenate([mask] * GROUP, axis=0)
        for g in range(width // span):
            queries, keys, values = head_rows(ready_ref, m, half, g * span)
            weights = softmax_weights(queries, keys, mask)
            grad = jnp.concatenate(
                [
                    sequence(attended_ref, m, half, (g * GROUP + j) * HEAD_DIM)
                    for j in range(GROUP)
                ],
                axis=0,
            )
            grad_values = product_left(weights.astype(BF16), grad)
            grad_weights = product_right(grad, values)
            mean = jnp.sum(grad_weights * weights, axis=1, keepdims=True)
            grad_scores = (weights * (grad_weights - mean)).astype(BF16)
            grad_queries = product(grad_scores, keys) * scale
            grad_keys = product_left(grad_scores, queries) * scale
            outs = [grad_queries[j * 2 * half : (j + 1) * 2 * half] for j in range(GROUP)]
            for j, out in enumerate([*outs, grad_keys, grad_values]):
                at = g * span + j * HEAD_DIM
                ready_grad_ref[m * half : (m + 1) * half, at : at + HEAD_DIM] = out[:half]
                ready_grad_ref[(m + 2) * half : (m + 3) * half, at : at + HEAD_DIM] = out[half:]
    low, front = lane_facts(rows)
    cosine, sine = tables_ref[0], tables_ref[1]
    for at in range(width // 128):
        lanes = slice(at * 128, (at + 1) * 128)
        block, grad = qkv_ref[:, lanes], ready_grad_ref[:, lanes]
        heads, gains = block_gains(gains_ref, at)
        inverse = head_scales(block, low)
        normed = block * inverse
        turned = grad * sine
        grad_normed = grad * cosine + jnp.where(
            front, pltpu.roll(turned, 96, 1), -pltpu.roll(turned, 32, 1)
        )
        heads_ref[at : at + 1] = jnp.sum(grad_normed * normed, axis=0, keepdims=True)
        grad_normed = grad_normed * gains
        along = grad_normed * normed
        first = jnp.sum(jnp.where(low, along, 0.0), axis=1, keepdims=True)
        second = jnp.sum(jnp.where(low, 0.0, along), axis=1, keepdims=True)
        mean = jnp.where(low, first, second) * (1.0 / HEAD_DIM)
        raw = inverse * (grad_normed - normed * mean)
        if heads[0] == 2:
            raw = jnp.where(low, grad, raw)
        if heads[1] == 2:
            raw = jnp.where(low, raw, grad)
        proj_ref[:, lanes] = raw.astype(BF16)
    step = width // tiles_ref.shape[0]
    tiles_out(tiles_ref, grad_ref, lambda k: proj_ref[:, k * step : (k + 1) * step])
    copies[0].wait()
    acc_ref[...] = product_right(proj_ref[...], in_buf[0])
    rows_out(acc_ref, core_ref[0], mine_ref, other_ref)


def mixer_call(
    kernel, core, operands, whole, weight_out, in_tiles, outs, scratch=(), behind=()
):
    vmem, any_space = pl.BlockSpec(memory_space=pltpu.VMEM), pl.BlockSpec(memory_space=pl.ANY)
    rows, width = operands[0].shape
    channels = weight_out.shape[0]
    outs = [*outs, ((rows // 2, width), F32), ((rows // 2, width), BF16)]
    return pl.pallas_call(
        ordered(kernel, len(behind)),
        in_specs=[
            pl.BlockSpec(memory_space=pltpu.SMEM),
            *[any_space] * len(behind),
            *[vmem] * len(operands),
            any_space,
            any_space,
        ],
        out_specs=[vmem] * len(outs),
        out_shape=[jax.ShapeDtypeStruct(*out) for out in outs],
        scratch_shapes=[
            pltpu.VMEM((in_tiles[0], width, in_tiles[1]), BF16),
            pltpu.VMEM((channels, width), BF16),
            pltpu.VMEM((rows, width), F32),
            *scratch,
            pltpu.SemaphoreType.DMA((in_tiles[0] + 1,)),
        ],
        compiler_params=pltpu.CompilerParams(vmem_limit_bytes=VMEM_LIMIT),
        cost_estimate=SHORT,
    )(core, *behind, *operands, whole, weight_out)


def conv_forward_call(core, rows, kernel, masks, whole, weight_out):
    count, channels = rows.shape[0], kernel.shape[1]
    outs = [((3, count, channels), BF16), ((count, channels), BF16)]
    operands = (rows, kernel, masks)
    return mixer_call(
        conv_forward_kernel, core, operands, whole, weight_out, (3, channels), outs
    )


def conv_backward_call(core, grad, kernel, masks, projected, tiles, whole, weight_out):
    count, width = grad.shape
    taps, channels = kernel.shape
    outs = [
        (tiles.shape, BF16),
        ((taps, channels), F32),
    ]
    operands = (grad, kernel, masks, projected, tiles)
    return mixer_call(
        conv_backward_kernel, core, operands, whole, weight_out, (3, channels), outs
    )


def attention_forward_call(core, rows, gains, tables, mask, whole, weight_out, qkv_width):
    count, channels = rows.shape[0], weight_out.shape[0]
    outs = [((count, qkv_width), F32), ((count, qkv_width), BF16), ((count, channels), BF16)]
    operands = (rows, gains, tables, mask)
    return mixer_call(
        attention_forward_kernel, core, operands, whole, weight_out, (1, qkv_width), outs
    )


def attention_backward_call(core, grad, gains, tables, mask, qkv, ready, whole, weight_out):
    count, width = grad.shape
    channels, qkv_width = weight_out.shape[0], qkv.shape[1]
    outs = [
        ((4, count, whole_lanes((width + 3 * channels) // 4)), BF16),
        ((qkv_width // 128, 128), F32),
    ]
    scratch = [
        pltpu.VMEM((count, channels), BF16),
        pltpu.VMEM((count, qkv_width), F32),
        pltpu.VMEM((count, qkv_width), BF16),
    ]
    operands = (grad, gains, tables, mask, qkv, ready)
    return mixer_call(
        attention_backward_kernel, core, operands, whole, weight_out, (1, qkv_width), outs, scratch
    )


def conv_masks(segments, taps):
    masks = []
    for lag in range(1, taps):
        same = (segments[:, lag:] == segments[:, :-lag]).astype(F32)
        same = jnp.pad(same, ((0, 0), (lag, 0))).reshape(-1, 1)
        masks.append(jnp.broadcast_to(same, (same.shape[0], 128)))
    return jnp.stack(masks)


def score_mask(segments):
    position = jnp.arange(segments.shape[1])
    allowed = position[:, None] >= position[None, :]
    return (allowed & (segments[:, :, None] == segments[:, None, :])).astype(F32)


def turn_tables(length):
    half = HEAD_DIM // 2
    exponent = jnp.arange(half, dtype=F32) * (2.0 / HEAD_DIM)
    frequency = jnp.exp(-exponent * jnp.log(ROPE_BASE))
    angles = jnp.arange(length, dtype=F32)[:, None] * frequency[None, :]
    tables = jnp.tile(jnp.stack([jnp.cos(angles), jnp.sin(angles)]), (1, 1, 4))
    tables = tables.reshape(2, 2, 1, length // 2, 128)
    return jnp.broadcast_to(tables, (2, 2, 2, length // 2, 128)).reshape(2, 2 * length, 128)


def gain_rows(head_gains):
    kinds = [head_gains[0], head_gains[1], jnp.ones_like(head_gains[0])]
    rows = [jnp.concatenate([a, b]) for a in kinds for b in kinds]
    return jnp.stack(rows)


def head_gain_sums(sums):
    heads = sums.reshape(-1, GROUP + 2, HEAD_DIM)
    return jnp.stack([heads[:, :GROUP].sum((0, 1)), heads[:, GROUP].sum(0)])


def local(
    inputs,
    out_cotangent,
    segments,
    norm_gains,
    conv_kernel,
    qk_gains,
    conv_in,
    attn_qkv,
    mixer_out,
    gate_up,
    down,
):
    section = lax.axis_index("xh")
    first = section == 0
    core = lax.axis_index("c")
    place = lax.axis_index("y") * 4 + lax.axis_index("z")
    xl = lax.axis_index("xl")
    plane = lax.axis_size("y") * lax.axis_size("z")

    shape = inputs.shape[1:]
    width = shape[-1]
    inputs, out_cotangent = inputs.reshape(-1, width), out_cotangent.reshape(-1, width)
    segments = segments[0]
    half = inputs.shape[0]
    rows = 2 * half
    channels = conv_in.shape[2]
    kernel = lax.dynamic_slice_in_dim(conv_kernel, core * channels, channels, 1).astype(F32)
    gains = lax.dynamic_index_in_dim(norm_gains, section, 0, keepdims=False).astype(F32)
    weight_out, weight_pair, weight_down = mixer_out[0], gate_up[0], down[0]
    hidden_units = weight_down.shape[0]
    part = hidden_units // plane
    in_width = 3 * channels
    qkv_width = attn_qkv.shape[1]
    y = lax.axis_index("y")
    core_scalar = jnp.stack([core, section]).astype(jnp.int32)
    xl_scalar = jnp.stack([xl, section, y]).astype(jnp.int32)

    def chosen(from_first, from_second):
        return jnp.where(first, from_first, from_second)

    def gathered(own, axes):
        return lax.all_gather(own, axes, tiled=True)


    both = jnp.concatenate([conv_in.reshape(-1, in_width), attn_qkv], axis=1)
    whole = gathered(both, ("xh", "xl", "y", "z"))

    lanes = -(-part // 256) * 256
    fill = lanes - part
    part_pair = jnp.concatenate(
        [
            jnp.pad(lax.dynamic_slice_in_dim(w, place * part, part, 1), ((0, 0), (0, fill)))
            for w in (weight_pair[0], weight_pair[1])
        ],
        axis=1,
    )
    part_down = lax.dynamic_slice_in_dim(weight_down, place * part, part, 0)
    part_down = jnp.pad(part_down, ((0, fill), (0, 0)))
    masks = conv_masks(segments, kernel.shape[0])
    mask = score_mask(segments)
    tables = turn_tables(segments.shape[1])
    head_gains = gain_rows(qk_gains.astype(F32))
    first_in = inputs.astype(F32)
    normed_own_0 = (normalize(first_in) * gains[0]).astype(BF16)
    normed_0 = spread(normed_own_0)
    cotangent_1 = spread(out_cotangent)
    whole, part_pair, part_down, masks, mask, tables, head_gains, normed_0, cotangent_1 = (
        lax.optimization_barrier(
            (whole, part_pair, part_down, masks, mask, tables, head_gains, normed_0, cotangent_1)
        )
    )

    def inner_norm(hidden):
        return (normalize(hidden) * gains[1]).astype(BF16)

    def inner_back(mine, other, hidden, grad):
        return back_join_call(core_scalar, mine, swapped(other, "c"), hidden, grad, gains[1])

    def mixer_back(grad_hidden, mine, other, layer_in, behind):
        come = swapped(other, "c")
        return back_join_call(behind, mine, come, layer_in, grad_hidden, gains[0])[1:]

    plane_axes = ("y", "z", "c")
    early = gathered(chosen(normed_own_0, out_cotangent), plane_axes)

    projected, gated_0, mine, other = conv_forward_call(
        core_scalar, normed_0, kernel, masks, whole, weight_out
    )
    hidden_0 = first_in + joined(mine, other)
    inner_0 = inner_norm(hidden_0)
    gate, up, mine, other = feed_forward_call(
        False, core_scalar, spread(inner_0), weight_pair, weight_down
    )
    result_0 = (hidden_0 + joined(mine, other)).astype(BF16)

    second_in = lax.ppermute(result_0, "xh", [(0, 1)]).astype(F32)
    normed_own_1 = (normalize(second_in) * gains[0]).astype(BF16)
    qkv, ready, gated_1, mine, other = attention_forward_call(
        core_scalar, spread(normed_own_1), head_gains, tables, mask, whole, weight_out, qkv_width
    )
    hidden_1 = second_in + joined(mine, other)
    inner_1 = inner_norm(hidden_1)
    mine, other, grad_mine, grad_other = ffn_both_call(
        core_scalar, spread(inner_1), cotangent_1, weight_pair, weight_down, (early,)
    )
    result_1 = (hidden_1 + joined(mine, other)).astype(BF16)

    inner_all = gathered(chosen(inner_0, inner_1), plane_axes)
    gated_z = gathered(chosen(gated_0, gated_1), "z")

    grad_hidden_1, grad_mix_1, gain_inner_1 = inner_back(
        grad_mine, grad_other, hidden_1, out_cotangent.astype(F32)
    )
    tiles_1, head_sums, mine, other = attention_backward_call(
        core_scalar,
        spread(grad_mix_1),
        head_gains,
        tables,
        mask,
        qkv,
        ready,
        whole,
        weight_out,
    )
    input_grad_1, gain_outer_1 = mixer_back(grad_hidden_1, mine, other, second_in, core_scalar)

    cotangent = lax.ppermute(input_grad_1, "xh", [(1, 0)])
    late = gathered(chosen(cotangent, normed_own_1), plane_axes)
    mine, other = feed_forward_call(
        True,
        core_scalar,
        spread(cotangent),
        weight_pair,
        weight_down,
        (gate, up),
        (inner_all,),
    )
    grad_hidden_0, grad_mix_0, gain_inner_0 = inner_back(
        mine, other, hidden_0, cotangent.astype(F32)
    )
    tiles, grad_kernel, mine, other = conv_backward_call(
        core_scalar,
        spread(grad_mix_0),
        kernel,
        masks,
        projected,
        tiles_1,
        whole,
        weight_out,
    )
    columns = exchanged(tiles, "z").reshape(4 * rows, -1)
    part_kept = part_forward_call((tiles,), inner_all, part_pair)

    def summed_over_pair(mine, other):
        return mine.astype(F32) + swapped(other, "xl").astype(F32)

    pair_grads, down_mine, down_other = lax.cond(
        first,
        lambda: part_down_call(xl_scalar, late, part_kept, part_down, (columns,)),
        lambda: part_down_call(xl_scalar, early, part_kept, part_down, (columns,)),
    )
    input_grad_0, gain_outer_0 = mixer_back(grad_hidden_0, mine, other, first_in, pair_grads)
    in_parts = mixer_in_call(xl_scalar, pair_grads, columns, early, late, plane)
    pair_mine, pair_other = part_pair_call(xl_scalar, inner_all, pair_grads, (in_parts,))
    out_mine, out_other = mixer_out_call(xl_scalar, pair_other, columns, gated_z, width // 4)

    full_kernel = lax.dynamic_update_slice(
        jnp.zeros(conv_kernel.shape, F32), grad_kernel, (0, core * channels)
    )
    small = jnp.concatenate(
        [
            chosen(gain_outer_0, gain_outer_1),
            chosen(gain_inner_0, gain_inner_1),
            full_kernel.reshape(-1),
            head_gain_sums(head_sums).reshape(-1),
        ]
    )
    count = small.shape[0]
    small = jnp.pad(small, (0, -count % 1024)).reshape(-1, 128)
    small = lax.all_gather(small, "c").sum(0)
    small = small + swapped(small, "xl")
    across = swapped(small, "xh")
    small = jnp.concatenate([chosen(small, across), chosen(across, small)])
    small_all = lax.all_gather(small, PLANE)

    come = exchanged(in_parts, PLANE)
    line_mine, line_other = line_sums_call(xl_scalar, come)
    line_come = swapped(line_other, "xl")

    pairs = [(a, swapped(b, "xl")) for a, b in ((pair_mine, pair_other), (down_mine, down_other))]
    total = pair_join_call((in_parts,), pairs)
    arrived = exchanged(total.reshape(plane, -1, 3 * lanes), PLANE)

    kept_lines, sent_lines = finish_call(xl_scalar, total, line_mine, line_come)
    across = swapped(sent_lines, "xh")
    come = across.astype(F32)[:, :, : in_width // 4]
    kept_lines = kept_lines[:, :, : in_width // 4]
    lines = chosen(kept_lines, come).reshape(4, -1, 3, channels // 4)
    grad_conv_in = jnp.moveaxis(lines, 0, 2).reshape(conv_in.shape)
    lines = chosen(come, kept_lines)[:, :, : qkv_width // 4]
    grad_attn_qkv = jnp.moveaxis(lines, 0, 1).reshape(attn_qkv.shape)

    grad_gate_up, grad_down = lines_call(across, arrived, hidden_units)
    grad_gate_up, grad_down = grad_gate_up[None], grad_down.T[None]

    total = summed_over_pair(out_mine, out_other).reshape(4, -1, channels)
    sent = total.astype(BF16)
    lines = lax.dynamic_index_in_dim(total, y, 0, keepdims=False)
    for by in range(1, 4):
        block = lax.dynamic_index_in_dim(sent, (y + by) % 4, 0, keepdims=False)
        lines += lax.ppermute(block, "y", around(by)).astype(F32)
    grad_mixer_out = lines.T[None]

    pair = plane_sums_call(grad_gate_up, small_all).reshape(2, -1)
    grad_norm_gains = jnp.stack([a[: 2 * width].reshape(2, width) for a in pair])
    grad_conv_kernel = pair[0][2 * width : 5 * width].reshape(conv_kernel.shape)
    grad_qk_gains = pair[1][5 * width : count].reshape(qk_gains.shape)

    activations = chosen(result_0, result_1).reshape(1, 1, *shape)
    input_grads = chosen(input_grad_0, input_grad_1).reshape(1, 1, *shape)
    return (
        activations,
        input_grads,
        grad_norm_gains,
        grad_conv_kernel,
        grad_qk_gains,
        grad_conv_in,
        grad_attn_qkv,
        grad_mixer_out,
        grad_gate_up,
        grad_down,
    )


def solution(mesh):
    wide = Mesh(mesh.devices.reshape(2, 2, 4, 4, 2), AXES)
    dp = ("xl", "y", "z")
    everyone = ("xh", "xl", "y", "z")
    in_specs = (
        P(dp, None, "c", None),
        P(dp, None, "c", None),
        P(dp, None, None),
        P(),
        P(),
        P(),
        P(everyone, None, "c"),
        P(everyone, "c"),
        P("xh", "c", None),
        P("xh", None, None, "c"),
        P("xh", "c", None),
    )
    out_specs = (
        P("xh", dp, None, "c", None),
        P("xh", dp, None, "c", None),
        P(),
        P(),
        P(),
        P(everyone, None, "c"),
        P(everyone, "c"),
        P("xh", "c", dp),
        P("xh", None, dp, "c"),
        P("xh", "c", dp),
    )
    return jax.shard_map(local, mesh=wide, in_specs=in_specs, out_specs=out_specs, check_vma=False)
```

```python
import functools

import jax
import jax.numpy as jnp
from jax import lax
from jax.experimental import pallas as pl
from jax.experimental.pallas import tpu as pltpu
from jax.sharding import Mesh
from jax.sharding import PartitionSpec as P

HEADS = 24
KV_HEADS = 8
HEAD_DIM = 64
GROUP = HEADS // KV_HEADS

EPSILON = 1e-05
ROPE_BASE = 1000000.0
MASKED_SCORE = -1e30

F32 = jnp.float32
BF16 = jnp.bfloat16

PLANE = ("y", "z")
AXES = ("xh", "xl", "y", "z", "c")


def product(left, right):
    return jnp.dot(left, right, preferred_element_type=F32)


def product_left(left, right):
    return lax.dot_general(left, right, (((0,), (0,)), ((), ())), preferred_element_type=F32)


def product_right(left, right):
    return lax.dot_general(left, right, (((1,), (1,)), ((), ())), preferred_element_type=F32)


def swapped(shard, axis):
    return lax.ppermute(shard, axis, [(0, 1), (1, 0)])


def spread(own):
    return lax.all_gather(own, "c", tiled=True)


def joined(mine, other):
    return mine + swapped(other, "c").astype(F32)


def mean_last(values):
    return jnp.mean(values, axis=-1, keepdims=True)


def inverse_rms(values):
    return lax.rsqrt(mean_last(values * values) + EPSILON)


def normalize(values):
    return values * inverse_rms(values)


def around(by):
    return [(k, (k + by) % 4) for k in range(4)]


def exchanged(tiles, axes):
    return lax.all_to_all(tiles, axes, 0, 0, tiled=True)


def ffn_grads(grad_active, gate, up):
    sigmoid = jax.nn.sigmoid(gate)
    grad_gate = grad_active * up * sigmoid * (1.0 + gate * (1.0 - sigmoid))
    grad_up = grad_active * gate * sigmoid
    return grad_gate.astype(BF16), grad_up.astype(BF16)


VMEM_LIMIT = 56 * 1024 * 1024
SHORT = pl.CostEstimate(flops=1, bytes_accessed=1, transcendentals=0)


def whole_lanes(columns):
    return -(-columns // 128) * 128


def ordered(kernel, count):
    def body(scalar_ref, *refs):
        kernel(scalar_ref, *refs[count:])

    return body


def unit_tiles(units, tile):
    short = units % tile
    tiles = [(0, short)] if short else []
    return tiles + [(at, tile) for at in range(short, units, tile)]


def streamed(tiles, copies, work):
    for copy in copies(0, 0):
        copy.start()
    for k in range(len(tiles)):
        slot = k % 2
        if k + 1 < len(tiles):
            for copy in copies(k + 1, 1 - slot):
                copy.start()
        for copy in copies(k, slot):
            copy.wait()
        work(k, slot)


def ffn_forward_kernel(
    tiles, core_ref, rows_ref, pair_ref, down_ref, gate_ref, up_ref, mine_ref, other_ref,
    pair_buf, down_buf, gate_buf, up_buf, acc_ref, sems, out_sems,
):
    def copies(k, slot):
        at, size = tiles[k]
        return [
            pltpu.make_async_copy(
                pair_ref.at[0, :, pl.ds(at, size)],
                pair_buf.at[slot, :, pl.ds(0, size)],
                sems.at[slot, 0],
            ),
            pltpu.make_async_copy(
                pair_ref.at[1, :, pl.ds(at, size)],
                pair_buf.at[slot, :, pl.ds(size, size)],
                sems.at[slot, 1],
            ),
            pltpu.make_async_copy(
                down_ref.at[pl.ds(at, size)], down_buf.at[slot, pl.ds(0, size)], sems.at[slot, 2]
            ),
        ]

    def kept(k):
        here = (slice(None), pl.ds(*tiles[k]))
        return [
            pltpu.make_async_copy(gate_buf.at[here], gate_ref.at[here], out_sems.at[k, 0]),
            pltpu.make_async_copy(up_buf.at[here], up_ref.at[here], out_sems.at[k, 1]),
        ]

    def work(k, slot):
        at, size = tiles[k]
        both = product(rows_ref[...], pair_buf[slot, :, : 2 * size])
        gate, up = both[:, :size], both[:, size:]
        gate_buf[:, at : at + size] = gate.astype(BF16)
        up_buf[:, at : at + size] = up.astype(BF16)
        for copy in kept(k):
            copy.start()
        active = (gate * jax.nn.sigmoid(gate) * up).astype(BF16)
        part = product(active, down_buf[slot, :size])
        if k == 0:
            acc_ref[...] = part
        else:
            acc_ref[...] += part

    streamed(tiles, copies, work)
    rows_out(acc_ref, core_ref[0], mine_ref, other_ref)
    for k in range(len(tiles)):
        for copy in kept(k):
            copy.wait()


def ffn_backward_kernel(
    tiles, core_ref, rows_ref, gate_ref, up_ref, pair_ref, down_ref, mine_ref, other_ref,
    pair_buf, down_buf, gate_buf, up_buf, acc_ref, sems,
):
    def copies(k, slot):
        at, size = tiles[k]
        columns, place = pl.ds(at, size), pl.ds(0, size)
        return [
            pltpu.make_async_copy(
                down_ref.at[columns], down_buf.at[slot, place], sems.at[slot, 0]
            ),
            pltpu.make_async_copy(
                gate_ref.at[:, columns], gate_buf.at[slot, :, place], sems.at[slot, 1]
            ),
            pltpu.make_async_copy(
                up_ref.at[:, columns], up_buf.at[slot, :, place], sems.at[slot, 2]
            ),
            pltpu.make_async_copy(
                pair_ref.at[0, :, columns], pair_buf.at[slot, :, place], sems.at[slot, 3]
            ),
            pltpu.make_async_copy(
                pair_ref.at[1, :, columns],
                pair_buf.at[slot, :, pl.ds(size, size)],
                sems.at[slot, 4],
            ),
        ]

    def work(k, slot):
        _, size = tiles[k]
        grad_active = product_right(rows_ref[...], down_buf[slot, :size])
        grads = ffn_grads(
            grad_active,
            gate_buf[slot, :, :size].astype(F32),
            up_buf[slot, :, :size].astype(F32),
        )
        part = product_right(jnp.concatenate(grads, axis=1), pair_buf[slot, :, : 2 * size])
        if k == 0:
            acc_ref[...] = part
        else:
            acc_ref[...] += part

    streamed(tiles, copies, work)
    rows_out(acc_ref, core_ref[0], mine_ref, other_ref)


def ffn_both_kernel(
    tiles, core_ref, rows_ref, grad_ref, pair_ref, down_ref,
    mine_ref, other_ref, grad_mine_ref, grad_other_ref, pair_buf, down_buf, acc_ref, grad_acc_ref, sems,
):
    def copies(k, slot):
        at, size = tiles[k]
        columns, place = pl.ds(at, size), pl.ds(0, size)
        return [
            pltpu.make_async_copy(
                pair_ref.at[0, :, columns], pair_buf.at[slot, :, place], sems.at[slot, 0]
            ),
            pltpu.make_async_copy(
                pair_ref.at[1, :, columns],
                pair_buf.at[slot, :, pl.ds(size, size)],
                sems.at[slot, 1],
            ),
            pltpu.make_async_copy(
                down_ref.at[columns], down_buf.at[slot, place], sems.at[slot, 2]
            ),
        ]

    def work(k, slot):
        _, size = tiles[k]
        both = product(rows_ref[...], pair_buf[slot, :, : 2 * size])
        grad_active = product_right(grad_ref[...], down_buf[slot, :size])
        gate, up = both[:, :size], both[:, size:]
        active = (gate * jax.nn.sigmoid(gate) * up).astype(BF16)
        grads = jnp.concatenate(ffn_grads(grad_active, gate, up), axis=1)
        part = product(active, down_buf[slot, :size])
        grad_part = product_right(grads, pair_buf[slot, :, : 2 * size])
        if k == 0:
            acc_ref[...], grad_acc_ref[...] = part, grad_part
        else:
            acc_ref[...] += part
            grad_acc_ref[...] += grad_part

    streamed(tiles, copies, work)
    rows_out(acc_ref, core_ref[0], mine_ref, other_ref)
    rows_out(grad_acc_ref, core_ref[0], grad_mine_ref, grad_other_ref)


def ffn_both_call(core, rows, grad, pair, down, behind):
    count, width = rows.shape
    units = down.shape[0]
    tile = 768
    vmem, any_space = pl.BlockSpec(memory_space=pltpu.VMEM), pl.BlockSpec(memory_space=pl.ANY)
    half = (count // 2, width)
    return pl.pallas_call(
        ordered(functools.partial(ffn_both_kernel, unit_tiles(units, tile)), len(behind)),
        in_specs=[
            pl.BlockSpec(memory_space=pltpu.SMEM),
            *[any_space] * len(behind),
            vmem,
            vmem,
            any_space,
            any_space,
        ],
        out_specs=[vmem] * 4,
        out_shape=[jax.ShapeDtypeStruct(half, F32), jax.ShapeDtypeStruct(half, BF16)] * 2,
        scratch_shapes=[
            pltpu.VMEM((2, width, 2 * tile), BF16),
            pltpu.VMEM((2, tile, width), BF16),
            pltpu.VMEM((count, width), F32),
            pltpu.VMEM((count, width), F32),
            pltpu.SemaphoreType.DMA((2, 3)),
        ],
        compiler_params=pltpu.CompilerParams(vmem_limit_bytes=VMEM_LIMIT),
        cost_estimate=SHORT,
    )(core, *behind, rows, grad, pair, down)


def feed_forward_call(backward, core, rows, pair, down, saved=(), behind=()):
    count, width = rows.shape
    units = down.shape[0]
    tile = 768
    tiles = unit_tiles(units, tile)
    vmem, any_space = pl.BlockSpec(memory_space=pltpu.VMEM), pl.BlockSpec(memory_space=pl.ANY)
    scalar = pl.BlockSpec(memory_space=pltpu.SMEM)
    out_shape = [
        jax.ShapeDtypeStruct((count // 2, width), F32),
        jax.ShapeDtypeStruct((count // 2, width), BF16),
    ]
    out_specs = [vmem, vmem]
    buffers = [pltpu.VMEM((2, width, 2 * tile), BF16), pltpu.VMEM((2, tile, width), BF16)]
    acc = pltpu.VMEM((count, width), F32)
    if backward:
        body = functools.partial(ffn_backward_kernel, tiles)
        in_specs = [scalar, vmem, any_space, any_space, any_space, any_space]
        buffers += [pltpu.VMEM((2, count, tile), BF16)] * 2
        scratch = [*buffers, acc, pltpu.SemaphoreType.DMA((2, 5))]
    else:
        body = functools.partial(ffn_forward_kernel, tiles)
        in_specs = [scalar, vmem, any_space, any_space]
        out_shape = [jax.ShapeDtypeStruct((count, units), BF16)] * 2 + out_shape
        out_specs = [any_space, any_space, *out_specs]
        buffers += [pltpu.VMEM((count, units), BF16)] * 2
        scratch = [*buffers, acc]
        scratch += [pltpu.SemaphoreType.DMA((2, 3)), pltpu.SemaphoreType.DMA((len(tiles), 2))]
    in_specs = [scalar, *[any_space] * len(behind), *in_specs[1:]]
    return pl.pallas_call(
        ordered(body, len(behind)),
        in_specs=in_specs,
        out_specs=out_specs,
        out_shape=out_shape,
        scratch_shapes=scratch,
        compiler_params=pltpu.CompilerParams(vmem_limit_bytes=VMEM_LIMIT),
        cost_estimate=SHORT,
    )(core, *behind, rows, *saved, pair, down)


def part_forward_kernel(*refs):
    rows_ref, pair_ref, kept_ref = refs[-3:]
    both = product(rows_ref[...], pair_ref[...])
    units = both.shape[1] // 2
    gate, up = both[:, :units], both[:, units:]
    sigmoid = jax.nn.sigmoid(gate)
    silu = gate * sigmoid
    kept_ref[:, :units] = (up * (sigmoid + silu * (1.0 - sigmoid))).astype(BF16)
    kept_ref[:, units : 2 * units] = silu.astype(BF16)
    kept_ref[:, 2 * units :] = (silu * up).astype(BF16)


def part_forward_call(behind, rows, pair):
    tokens, width = rows.shape
    units = pair.shape[1] // 2
    tile = 1024
    return pl.pallas_call(
        part_forward_kernel,
        grid=(tokens // tile,),
        in_specs=[
            *[pl.BlockSpec(memory_space=pl.ANY)] * len(behind),
            pl.BlockSpec((tile, width), lambda i: (i, 0)),
            pl.BlockSpec((width, 2 * units), lambda i: (0, 0)),
        ],
        out_specs=pl.BlockSpec((tile, 3 * units), lambda i: (i, 0)),
        out_shape=jax.ShapeDtypeStruct((tokens, 3 * units), BF16),
        compiler_params=pltpu.CompilerParams(vmem_limit_bytes=VMEM_LIMIT),
        cost_estimate=pl.CostEstimate(
            flops=8 * tokens * width * units, bytes_accessed=2 * tokens * width, transcendentals=0
        ),
    )(*behind, rows, pair)


def pair_out(acc_ref, here, mine_ref, other_ref):
    rows = mine_ref.shape[0]
    for ref, half in ((mine_ref, here), (other_ref, 1 - here)):
        ref[...] = acc_ref[pl.ds(pl.multiple_of(half * rows, rows), rows)].astype(BF16)


def accumulated(acc_ref, part, finish):
    step = pl.program_id(0)

    @pl.when(step == 0)
    def _():
        acc_ref[...] = part

    @pl.when(step > 0)
    def _():
        acc_ref[...] += part

    pl.when(step == pl.num_programs(0) - 1)(finish)


def part_down_kernel(here_ref, grad_ref, kept_ref, down_ref, pair_ref, mine_ref, other_ref, acc_ref):
    grad = grad_ref[...]
    units = down_ref.shape[0]
    grad_active = product_right(grad, down_ref[...])
    for k in range(2):
        lanes = slice(k * units, (k + 1) * units)
        pair_ref[:, lanes] = (grad_active * kept_ref[:, lanes].astype(F32)).astype(BF16)
    accumulated(
        acc_ref,
        product_left(grad, kept_ref[:, 2 * units :]),
        lambda: pair_out(acc_ref, here_ref[0], mine_ref, other_ref),
    )


def part_pair_kernel(here_ref, rows_ref, pair_ref, mine_ref, other_ref, acc_ref):
    accumulated(
        acc_ref,
        product_left(rows_ref[...], pair_ref[...]),
        lambda: pair_out(acc_ref, here_ref[0], mine_ref, other_ref),
    )


def part_call(kernel, here, operands, fixed, outs, result, flops, behind=()):
    tokens = operands[0].shape[0]
    tile = 1024
    by_tokens = lambda width: pl.BlockSpec((tile, width), lambda i, h: (i, 0))
    entire = lambda shape: pl.BlockSpec(shape, lambda i, h: (0, 0))
    half = (result[0] // 2, result[1])
    return pl.pallas_call(
        ordered(kernel, len(behind)),
        grid_spec=pltpu.PrefetchScalarGridSpec(
            num_scalar_prefetch=1,
            grid=(tokens // tile,),
            in_specs=[pl.BlockSpec(memory_space=pl.ANY)] * len(behind)
            + [by_tokens(a.shape[1]) for a in operands]
            + [entire(a.shape) for a in fixed],
            out_specs=[by_tokens(width) for width in outs] + [entire(half)] * 2,
            scratch_shapes=[pltpu.VMEM(result, F32)],
        ),
        out_shape=[jax.ShapeDtypeStruct((tokens, width), BF16) for width in outs]
        + [jax.ShapeDtypeStruct(half, BF16)] * 2,
        compiler_params=pltpu.CompilerParams(vmem_limit_bytes=VMEM_LIMIT),
        cost_estimate=SHORT,
    )(here, *behind, *operands, *fixed)


def part_down_call(here, grad, kept, down, behind):
    tokens, width = grad.shape
    units = down.shape[0]
    flops = 4 * tokens * width * units
    return part_call(
        part_down_kernel,
        here,
        (grad, kept),
        (down,),
        (2 * units,),
        (width, units),
        flops,
        behind,
    )


def part_pair_call(here, inner, pair, behind):
    (tokens, width), columns = inner.shape, pair.shape[1]
    flops = 2 * tokens * width * columns
    return part_call(
        part_pair_kernel, here, (inner, pair), (), (), (width, columns), flops, behind
    )


def back_join_kernel(
    behind_ref, mine_ref, come_ref, values_ref, base_ref, gain_ref, wide_ref, low_ref, sums_ref
):
    grad = mine_ref[...] + come_ref[...].astype(F32)
    values = values_ref[...]
    inverse = inverse_rms(values)
    normed = values * inverse
    scaled = grad * gain_ref[...]
    sums_ref[...] = jnp.sum(grad * normed, axis=0, keepdims=True)
    total = base_ref[...] + inverse * (scaled - normed * mean_last(scaled * normed))
    wide_ref[...] = total
    low_ref[...] = total.astype(BF16)


def back_join_call(behind, mine, come, values, base, gain):
    vmem = pl.BlockSpec(memory_space=pltpu.VMEM)
    shape = values.shape
    wide, low, sums = pl.pallas_call(
        back_join_kernel,
        in_specs=[pl.BlockSpec(memory_space=pl.ANY), *[vmem] * 5],
        out_specs=[vmem] * 3,
        out_shape=[
            jax.ShapeDtypeStruct(shape, F32),
            jax.ShapeDtypeStruct(shape, BF16),
            jax.ShapeDtypeStruct((1, shape[1]), F32),
        ],
        compiler_params=pltpu.CompilerParams(vmem_limit_bytes=VMEM_LIMIT),
        cost_estimate=SHORT,
    )(behind, mine, come, values, base, gain[None])
    return wide, low, sums[0]


def pair_join_kernel(count, *refs):
    *refs, out_ref = refs[count:]
    at = 0
    for mine_ref, come_ref in zip(refs[::2], refs[1::2]):
        size = mine_ref.shape[-1]
        total = mine_ref[...].astype(F32) + come_ref[...].astype(F32)
        out_ref[..., at : at + size] = total.astype(BF16)
        at += size


def pair_join_call(behind, pairs):
    vmem = pl.BlockSpec(memory_space=pltpu.VMEM)
    operands = [a for pair in pairs for a in pair]
    shape = (*operands[0].shape[:-1], sum(mine.shape[-1] for mine, _ in pairs))
    return pl.pallas_call(
        functools.partial(pair_join_kernel, len(behind)),
        in_specs=[pl.BlockSpec(memory_space=pl.ANY)] * len(behind) + [vmem] * len(operands),
        out_specs=vmem,
        out_shape=jax.ShapeDtypeStruct(shape, BF16),
        compiler_params=pltpu.CompilerParams(vmem_limit_bytes=VMEM_LIMIT),
        cost_estimate=SHORT,
    )(*behind, *operands)


def lines_kernel(behind_ref, arrived_ref, pair_ref, down_ref):
    plane, _, lanes = arrived_ref.shape
    lanes //= 3
    part = down_ref.shape[1] // plane
    for k in range(plane):
        rows = arrived_ref[k].astype(F32)
        at = slice(k * part, (k + 1) * part)
        pair_ref[0, :, at] = rows[:, :part]
        pair_ref[1, :, at] = rows[:, lanes : lanes + part]
        down_ref[:, at] = rows[:, 2 * lanes : 2 * lanes + part]


def lines_call(behind, arrived, units):
    vmem = pl.BlockSpec(memory_space=pltpu.VMEM)
    rows = arrived.shape[1]
    return pl.pallas_call(
        lines_kernel,
        in_specs=[pl.BlockSpec(memory_space=pl.ANY), vmem],
        out_specs=[vmem] * 2,
        out_shape=[
            jax.ShapeDtypeStruct((2, rows, units), F32),
            jax.ShapeDtypeStruct((rows, units), F32),
        ],
        compiler_params=pltpu.CompilerParams(vmem_limit_bytes=VMEM_LIMIT),
        cost_estimate=SHORT,
    )(behind, arrived)


def line_sums_kernel(places_ref, come_ref, mine_ref, other_ref, acc_ref):
    here = places_ref[0]
    count, rows, _ = mine_ref.shape
    for k in range(count):
        tiles = [come_ref[m * count + k].astype(F32) for m in range(come_ref.shape[0] // count)]
        acc_ref[...] = functools.reduce(jnp.add, tiles)
        mine_ref[k] = acc_ref[pl.ds(pl.multiple_of(here * rows, rows), rows)]
        other = acc_ref[pl.ds(pl.multiple_of((1 - here) * rows, rows), rows)]
        other_ref[k] = other.astype(BF16)


def line_sums_call(places, come):
    vmem = pl.BlockSpec(memory_space=pltpu.VMEM)
    plane, block, size = come.shape
    lines = (4, block // 2, size)
    return pl.pallas_call(
        line_sums_kernel,
        in_specs=[pl.BlockSpec(memory_space=pltpu.SMEM), vmem],
        out_specs=[vmem] * 2,
        out_shape=[jax.ShapeDtypeStruct(lines, F32), jax.ShapeDtypeStruct(lines, BF16)],
        scratch_shapes=[pltpu.VMEM((block, size), F32)],
        compiler_params=pltpu.CompilerParams(vmem_limit_bytes=VMEM_LIMIT),
        cost_estimate=SHORT,
    )(places, come)


def finish_kernel(
    places_ref, behind_ref, mine_ref, come_ref, kept_ref, sent_ref, acc_ref
):
    section = places_ref[1]
    short = kept_ref.shape[1]
    acc_ref[...] = mine_ref[...] + come_ref[...].astype(F32)
    kept_ref[...] = acc_ref[:, pl.ds(pl.multiple_of(section * short, short), short)]
    sent = acc_ref[:, pl.ds(pl.multiple_of((1 - section) * short, short), short)]
    sent_ref[...] = sent.astype(BF16)


def section_sums_kernel(behind_ref, small_ref, sums_ref):
    half = small_ref.shape[0] // 2
    for k in range(2):
        sums_ref[k] = jnp.sum(small_ref[k * half : (k + 1) * half], axis=0)


def section_sums_call(behind, small):
    vmem = pl.BlockSpec(memory_space=pltpu.VMEM)
    return pl.pallas_call(
        section_sums_kernel,
        in_specs=[pl.BlockSpec(memory_space=pl.ANY), vmem],
        out_specs=vmem,
        out_shape=jax.ShapeDtypeStruct((2, *small.shape[1:]), F32),
        compiler_params=pltpu.CompilerParams(vmem_limit_bytes=VMEM_LIMIT),
        cost_estimate=SHORT,
    )(behind, small)


def finish_call(places, behind, mine, come):
    vmem = pl.BlockSpec(memory_space=pltpu.VMEM)
    count, rows, size = mine.shape
    lines = (count, rows // 2, size)
    return pl.pallas_call(
        finish_kernel,
        in_specs=[
            pl.BlockSpec(memory_space=pltpu.SMEM),
            pl.BlockSpec(memory_space=pl.ANY),
            *[vmem] * 2,
        ],
        out_specs=[vmem] * 2,
        out_shape=[jax.ShapeDtypeStruct(lines, F32), jax.ShapeDtypeStruct(lines, BF16)],
        scratch_shapes=[pltpu.VMEM(mine.shape, F32)],
        compiler_params=pltpu.CompilerParams(vmem_limit_bytes=VMEM_LIMIT),
        cost_estimate=SHORT,
    )(places, behind, mine, come)


def mixer_in_kernel(
    places_ref, behind_ref, columns_ref, early_ref, late_ref, parts_ref, normed_ref, in_ref, sem
):
    section, y = places_ref[1], places_ref[2]

    def copy(all_ref):
        rows = normed_ref.shape[0]
        start = pl.multiple_of(y * rows, rows)
        return pltpu.make_async_copy(all_ref.at[pl.ds(start, rows)], normed_ref, sem)

    @pl.when(section == 0)
    def _():
        copy(early_ref).start()

    @pl.when(section > 0)
    def _():
        copy(late_ref).start()

    copy(early_ref).wait()
    mix = columns_ref.shape[1] - in_ref.shape[1]
    in_ref[...] = product_left(normed_ref[...], columns_ref[:, mix:])
    plane, block, _ = parts_ref.shape
    short = block // 4
    for k in range(plane):
        for half in range(2):
            for s in range(2):
                start = ((2 * s + half) * plane + k) * short
                place = (2 * half + s) * short
                rows_in = in_ref[start : start + short]
                parts_ref[k, place : place + short] = rows_in.astype(BF16)


def mixer_in_call(places, behind, columns, early, late, plane):
    vmem, any_space = pl.BlockSpec(memory_space=pltpu.VMEM), pl.BlockSpec(memory_space=pl.ANY)
    tokens, width = columns.shape[0], early.shape[1]
    size = columns.shape[1] - width // 4
    return pl.pallas_call(
        mixer_in_kernel,
        in_specs=[pl.BlockSpec(memory_space=pltpu.SMEM), any_space, vmem, any_space, any_space],
        out_specs=vmem,
        out_shape=jax.ShapeDtypeStruct((plane, width // plane, size), BF16),
        scratch_shapes=[
            pltpu.VMEM((tokens, width), BF16),
            pltpu.VMEM((width, size), F32),
            pltpu.SemaphoreType.DMA,
        ],
        compiler_params=pltpu.CompilerParams(vmem_limit_bytes=VMEM_LIMIT),
        cost_estimate=SHORT,
    )(places, behind, columns, early, late)


def mixer_out_kernel(places_ref, behind_ref, columns_ref, gated_ref, mine_ref, other_ref, out_ref):
    out_ref[...] = product_left(columns_ref[:, : out_ref.shape[0]], gated_ref[...])
    pair_out(out_ref, places_ref[0], mine_ref, other_ref)


def mixer_out_call(places, behind, columns, gated, mix):
    vmem = pl.BlockSpec(memory_space=pltpu.VMEM)
    channels = gated.shape[1]
    half = jax.ShapeDtypeStruct((mix // 2, channels), BF16)
    return pl.pallas_call(
        mixer_out_kernel,
        in_specs=[
            pl.BlockSpec(memory_space=pltpu.SMEM),
            pl.BlockSpec(memory_space=pl.ANY),
            vmem,
            vmem,
        ],
        out_specs=[vmem] * 2,
        out_shape=[half, half],
        scratch_shapes=[pltpu.VMEM((mix, channels), F32)],
        compiler_params=pltpu.CompilerParams(vmem_limit_bytes=VMEM_LIMIT),
        cost_estimate=SHORT,
    )(places, behind, columns, gated)


def load_all(copies):
    for copy in copies:
        copy.start()


def in_time(rows):
    half = rows.shape[0] // 4
    return jnp.concatenate([rows[k * half : (k + 1) * half] for k in (0, 2, 1, 3)], axis=0)


def rows_out(acc_ref, core, mine_ref, other_ref):
    half = mine_ref.shape[0]
    mine_ref[...] = acc_ref[pl.ds(pl.multiple_of(core * half, half), half)]
    rest = acc_ref[pl.ds(pl.multiple_of((1 - core) * half, half), half)]
    other_ref[...] = rest.astype(BF16)


def weight_copies(whole_ref, out_ref, in_buf, out_buf, sems, start):
    size = in_buf.shape[2]
    copies = [
        pltpu.make_async_copy(
            whole_ref.at[:, pl.ds(start + k * size, size)], in_buf.at[k], sems.at[k]
        )
        for k in range(in_buf.shape[0])
    ]
    return copies, pltpu.make_async_copy(out_ref, out_buf, sems.at[len(copies)])


def conv_taps(mixed, kernel, masks):
    terms = [mixed]
    for lag in range(1, len(masks) + 1):
        terms.append(pltpu.roll(mixed, lag, 0) * masks[lag - 1])
    taps = kernel.shape[0]
    total = kernel[taps - 1 : taps] * terms[0]
    for lag in range(1, taps):
        total = total + kernel[taps - 1 - lag : taps - lag] * terms[lag]
    return terms, total


def conv_forward_kernel(
    core_ref, rows_ref, kernel_ref, masks_ref, whole_ref, out_ref,
    proj_ref, gated_ref, mine_ref, other_ref, in_buf, out_buf, acc_ref, sems,
):
    copies, last = weight_copies(whole_ref, out_ref, in_buf, out_buf, sems, 0)
    load_all([*copies, last])
    rows = rows_ref[...]
    parts = []
    for k, copy in enumerate(copies):
        copy.wait()
        part = product(rows, in_buf[k])
        proj_ref[k] = part.astype(BF16)
        parts.append(in_time(part))
    masks = [masks_ref[lag] for lag in range(masks_ref.shape[0])]
    gated = []
    for at in range(0, parts[0].shape[1], 128):
        before, after, signal = [part[:, at : at + 128] for part in parts]
        _, total = conv_taps(before * signal, kernel_ref[:, at : at + 128], masks)
        gated.append((after * total).astype(BF16))
    gated = in_time(jnp.concatenate(gated, axis=1))
    gated_ref[...] = gated
    last.wait()
    acc_ref[...] = product(gated, out_buf[...])
    rows_out(acc_ref, core_ref[0], mine_ref, other_ref)


def tiles_out(tiles_ref, grad_ref, columns):
    count, rows, size = tiles_ref.shape
    step = grad_ref.shape[1] // (2 * count * count)
    for k in range(count):
        starts = range(k * step, grad_ref.shape[1], count * step)
        parts = [grad_ref[:, at : at + step] for at in starts]
        parts.append(columns(k))
        spare = size - sum(part.shape[1] for part in parts)
        tiles_ref[k] = jnp.concatenate([*parts, jnp.zeros((rows, spare), BF16)], axis=1)


def conv_backward_kernel(
    core_ref, grad_ref, kernel_ref, masks_ref, proj_ref, other_tiles_ref,
    whole_ref, out_ref, tiles_ref, taps_ref, mine_ref, other_ref, in_buf, out_buf, acc_ref, sems,
):
    copies, last = weight_copies(whole_ref, out_ref, in_buf, out_buf, sems, 0)
    load_all([last, *copies])
    last.wait()
    grad_gated = in_time(product_right(grad_ref[...], out_buf[...]))
    parts = [in_time(proj_ref[k].astype(F32)) for k in range(3)]
    masks = [masks_ref[lag] for lag in range(masks_ref.shape[0])]
    rows = grad_gated.shape[0]
    grads = [[], [], []]
    for at in range(0, grad_gated.shape[1], 128):
        before, after, signal = [part[:, at : at + 128] for part in parts]
        kernel = kernel_ref[:, at : at + 128]
        terms, total = conv_taps(before * signal, kernel, masks)
        grad = grad_gated[:, at : at + 128]
        grad_total = grad * after
        taps = kernel.shape[0]
        grad_mixed = kernel[taps - 1 : taps] * grad_total
        for lag in range(1, taps):
            sent = pltpu.roll(grad_total * masks[lag - 1], rows - lag, 0)
            grad_mixed = grad_mixed + kernel[taps - 1 - lag : taps - lag] * sent
        for lag in range(taps):
            taps_ref[taps - 1 - lag : taps - lag, at : at + 128] = jnp.sum(
                grad_total * terms[lag], axis=0, keepdims=True
            )
        for k, value in enumerate((grad_mixed * signal, grad * total, grad_mixed * before)):
            grads[k].append(value.astype(BF16))
    grads = [in_time(jnp.concatenate(g, axis=1)) for g in grads]
    step = grads[0].shape[1] // tiles_ref.shape[0]

    @pl.when(core_ref[1] == 0)
    def _():
        tiles_out(
            tiles_ref,
            grad_ref,
            lambda k: jnp.concatenate([g[:, k * step : (k + 1) * step] for g in grads], axis=1),
        )

    @pl.when(core_ref[1] > 0)
    def _():
        tiles_ref[...] = other_tiles_ref[...]

    for k, copy in enumerate(copies):
        copy.wait()
        part = product_right(grads[k], in_buf[k])
        acc_ref[...] = part if k == 0 else acc_ref[...] + part
    rows_out(acc_ref, core_ref[0], mine_ref, other_ref)


def head_kind(head):
    return min(max(head % (GROUP + 2) - GROUP + 1, 0), 2)


def lane_facts(rows):
    lane = lax.broadcasted_iota(jnp.int32, (rows, 128), 1)
    return lane < HEAD_DIM, lax.rem(lane, HEAD_DIM) < HEAD_DIM // 2


def head_scales(block, low):
    squares = block * block
    first = jnp.sum(jnp.where(low, squares, 0.0), axis=1, keepdims=True)
    second = jnp.sum(jnp.where(low, 0.0, squares), axis=1, keepdims=True)
    return lax.rsqrt(jnp.where(low, first, second) * (1.0 / HEAD_DIM) + EPSILON)


def block_gains(gains_ref, at):
    heads = [head_kind(2 * at), head_kind(2 * at + 1)]
    return heads, gains_ref[3 * heads[0] + heads[1] : 3 * heads[0] + heads[1] + 1]


def attention_forward_kernel(
    core_ref, rows_ref, gains_ref, tables_ref, mask_ref, whole_ref, out_ref,
    qkv_ref, ready_ref, gated_ref, mine_ref, other_ref, in_buf, out_buf, acc_ref, sems,
):
    copies, last = weight_copies(
        whole_ref, out_ref, in_buf, out_buf, sems, whole_ref.shape[1] - in_buf.shape[2]
    )
    load_all([*copies, last])
    copies[0].wait()
    qkv_ref[...] = product(rows_ref[...], in_buf[0])
    rows, width = qkv_ref.shape
    low, front = lane_facts(rows)
    cosine, sine = tables_ref[0], tables_ref[1]
    for at in range(width // 128):
        block = qkv_ref[:, at * 128 : (at + 1) * 128]
        heads, gains = block_gains(gains_ref, at)
        normed = block * head_scales(block, low) * gains
        turned = jnp.where(front, -pltpu.roll(normed, 96, 1), pltpu.roll(normed, 32, 1))
        ready = normed * cosine + turned * sine
        if heads[0] == 2:
            ready = jnp.where(low, block, ready)
        if heads[1] == 2:
            ready = jnp.where(low, ready, block)
        ready_ref[:, at * 128 : (at + 1) * 128] = ready.astype(BF16)
    half = rows // 4
    span = (GROUP + 2) * HEAD_DIM
    for m in range(2):
        mask = mask_ref[m] > 0
        mask = jnp.concatenate([mask] * GROUP, axis=0)
        for g in range(width // span):
            queries, keys, values = head_rows(ready_ref, m, half, g * span)
            weights = softmax_weights(queries, keys, mask)
            attended = product(weights.astype(BF16), values).astype(BF16)
            for j in range(GROUP):
                at = (g * GROUP + j) * HEAD_DIM
                head = attended[j * 2 * half : (j + 1) * 2 * half]
                gated_ref[m * half : (m + 1) * half, at : at + HEAD_DIM] = head[:half]
                gated_ref[(m + 2) * half : (m + 3) * half, at : at + HEAD_DIM] = head[half:]
    last.wait()
    acc_ref[...] = product(gated_ref[...], out_buf[...])
    rows_out(acc_ref, core_ref[0], mine_ref, other_ref)


def sequence(ref, m, half, at):
    columns = slice(at, at + HEAD_DIM)
    return jnp.concatenate(
        [ref[m * half : (m + 1) * half, columns], ref[(m + 2) * half : (m + 3) * half, columns]],
        axis=0,
    )


def head_rows(ref, m, half, at):
    heads = [sequence(ref, m, half, at + j * HEAD_DIM) for j in range(GROUP + 2)]
    return jnp.concatenate(heads[:GROUP], axis=0), heads[GROUP], heads[GROUP + 1]


def softmax_weights(queries, keys, mask):
    scores = jnp.where(mask, product_right(queries, keys) * HEAD_DIM ** (-0.5), MASKED_SCORE)
    terms = jnp.exp(scores - jnp.max(scores, axis=1, keepdims=True))
    return terms / jnp.sum(terms, axis=1, keepdims=True)


def attention_backward_kernel(
    core_ref, grad_ref, gains_ref, tables_ref, mask_ref, qkv_ref, ready_ref,
    whole_ref, out_ref, tiles_ref, heads_ref, mine_ref, other_ref,
    in_buf, out_buf, acc_ref, attended_ref, ready_grad_ref, proj_ref, sems,
):
    copies, last = weight_copies(
        whole_ref, out_ref, in_buf, out_buf, sems, whole_ref.shape[1] - in_buf.shape[2]
    )
    load_all([last, *copies])
    last.wait()
    attended_ref[...] = product_right(grad_ref[...], out_buf[...]).astype(BF16)
    rows, width = qkv_ref.shape
    half = rows // 4
    span = (GROUP + 2) * HEAD_DIM
    scale = HEAD_DIM ** (-0.5)
    for m in range(2):
        mask = mask_ref[m] > 0
        mask = jnp.concatenate([mask] * GROUP, axis=0)
        for g in range(width // span):
            queries, keys, values = head_rows(ready_ref, m, half, g * span)
            weights = softmax_weights(queries, keys, mask)
            grad = jnp.concatenate(
                [
                    sequence(attended_ref, m, half, (g * GROUP + j) * HEAD_DIM)
                    for j in range(GROUP)
                ],
                axis=0,
            )
            grad_values = product_left(weights.astype(BF16), grad)
            grad_weights = product_right(grad, values)
            mean = jnp.sum(grad_weights * weights, axis=1, keepdims=True)
            grad_scores = (weights * (grad_weights - mean)).astype(BF16)
            grad_queries = product(grad_scores, keys) * scale
            grad_keys = product_left(grad_scores, queries) * scale
            outs = [grad_queries[j * 2 * half : (j + 1) * 2 * half] for j in range(GROUP)]
            for j, out in enumerate([*outs, grad_keys, grad_values]):
                at = g * span + j * HEAD_DIM
                ready_grad_ref[m * half : (m + 1) * half, at : at + HEAD_DIM] = out[:half]
                ready_grad_ref[(m + 2) * half : (m + 3) * half, at : at + HEAD_DIM] = out[half:]
    low, front = lane_facts(rows)
    cosine, sine = tables_ref[0], tables_ref[1]
    for at in range(width // 128):
        lanes = slice(at * 128, (at + 1) * 128)
        block, grad = qkv_ref[:, lanes], ready_grad_ref[:, lanes]
        heads, gains = block_gains(gains_ref, at)
        inverse = head_scales(block, low)
        normed = block * inverse
        turned = grad * sine
        grad_normed = grad * cosine + jnp.where(
            front, pltpu.roll(turned, 96, 1), -pltpu.roll(turned, 32, 1)
        )
        heads_ref[at : at + 1] = jnp.sum(grad_normed * normed, axis=0, keepdims=True)
        grad_normed = grad_normed * gains
        along = grad_normed * normed
        first = jnp.sum(jnp.where(low, along, 0.0), axis=1, keepdims=True)
        second = jnp.sum(jnp.where(low, 0.0, along), axis=1, keepdims=True)
        mean = jnp.where(low, first, second) * (1.0 / HEAD_DIM)
        raw = inverse * (grad_normed - normed * mean)
        if heads[0] == 2:
            raw = jnp.where(low, grad, raw)
        if heads[1] == 2:
            raw = jnp.where(low, raw, grad)
        proj_ref[:, lanes] = raw.astype(BF16)
    step = width // tiles_ref.shape[0]
    tiles_out(tiles_ref, grad_ref, lambda k: proj_ref[:, k * step : (k + 1) * step])
    copies[0].wait()
    acc_ref[...] = product_right(proj_ref[...], in_buf[0])
    rows_out(acc_ref, core_ref[0], mine_ref, other_ref)


def mixer_call(
    kernel, core, operands, whole, weight_out, in_tiles, outs, scratch=(), behind=()
):
    vmem, any_space = pl.BlockSpec(memory_space=pltpu.VMEM), pl.BlockSpec(memory_space=pl.ANY)
    rows, width = operands[0].shape
    channels = weight_out.shape[0]
    outs = [*outs, ((rows // 2, width), F32), ((rows // 2, width), BF16)]
    return pl.pallas_call(
        ordered(kernel, len(behind)),
        in_specs=[
            pl.BlockSpec(memory_space=pltpu.SMEM),
            *[any_space] * len(behind),
            *[vmem] * len(operands),
            any_space,
            any_space,
        ],
        out_specs=[vmem] * len(outs),
        out_shape=[jax.ShapeDtypeStruct(*out) for out in outs],
        scratch_shapes=[
            pltpu.VMEM((in_tiles[0], width, in_tiles[1]), BF16),
            pltpu.VMEM((channels, width), BF16),
            pltpu.VMEM((rows, width), F32),
            *scratch,
            pltpu.SemaphoreType.DMA((in_tiles[0] + 1,)),
        ],
        compiler_params=pltpu.CompilerParams(vmem_limit_bytes=VMEM_LIMIT),
        cost_estimate=SHORT,
    )(core, *behind, *operands, whole, weight_out)


def conv_forward_call(core, rows, kernel, masks, whole, weight_out):
    count, channels = rows.shape[0], kernel.shape[1]
    outs = [((3, count, channels), BF16), ((count, channels), BF16)]
    operands = (rows, kernel, masks)
    return mixer_call(
        conv_forward_kernel, core, operands, whole, weight_out, (3, channels), outs
    )


def conv_backward_call(core, grad, kernel, masks, projected, tiles, whole, weight_out):
    count, width = grad.shape
    taps, channels = kernel.shape
    outs = [
        (tiles.shape, BF16),
        ((taps, channels), F32),
    ]
    operands = (grad, kernel, masks, projected, tiles)
    return mixer_call(
        conv_backward_kernel, core, operands, whole, weight_out, (3, channels), outs
    )


def attention_forward_call(core, rows, gains, tables, mask, whole, weight_out, qkv_width):
    count, channels = rows.shape[0], weight_out.shape[0]
    outs = [((count, qkv_width), F32), ((count, qkv_width), BF16), ((count, channels), BF16)]
    operands = (rows, gains, tables, mask)
    return mixer_call(
        attention_forward_kernel, core, operands, whole, weight_out, (1, qkv_width), outs
    )


def attention_backward_call(core, grad, gains, tables, mask, qkv, ready, whole, weight_out):
    count, width = grad.shape
    channels, qkv_width = weight_out.shape[0], qkv.shape[1]
    outs = [
        ((4, count, whole_lanes((width + 3 * channels) // 4)), BF16),
        ((qkv_width // 128, 128), F32),
    ]
    scratch = [
        pltpu.VMEM((count, channels), BF16),
        pltpu.VMEM((count, qkv_width), F32),
        pltpu.VMEM((count, qkv_width), BF16),
    ]
    operands = (grad, gains, tables, mask, qkv, ready)
    return mixer_call(
        attention_backward_kernel, core, operands, whole, weight_out, (1, qkv_width), outs, scratch
    )


def conv_masks(segments, taps):
    masks = []
    for lag in range(1, taps):
        same = (segments[:, lag:] == segments[:, :-lag]).astype(F32)
        same = jnp.pad(same, ((0, 0), (lag, 0))).reshape(-1, 1)
        masks.append(jnp.broadcast_to(same, (same.shape[0], 128)))
    return jnp.stack(masks)


def score_mask(segments):
    position = jnp.arange(segments.shape[1])
    allowed = position[:, None] >= position[None, :]
    return (allowed & (segments[:, :, None] == segments[:, None, :])).astype(F32)


def turn_tables(length):
    half = HEAD_DIM // 2
    exponent = jnp.arange(half, dtype=F32) * (2.0 / HEAD_DIM)
    frequency = jnp.exp(-exponent * jnp.log(ROPE_BASE))
    angles = jnp.arange(length, dtype=F32)[:, None] * frequency[None, :]
    tables = jnp.tile(jnp.stack([jnp.cos(angles), jnp.sin(angles)]), (1, 1, 4))
    tables = tables.reshape(2, 2, 1, length // 2, 128)
    return jnp.broadcast_to(tables, (2, 2, 2, length // 2, 128)).reshape(2, 2 * length, 128)


def gain_rows(head_gains):
    kinds = [head_gains[0], head_gains[1], jnp.ones_like(head_gains[0])]
    rows = [jnp.concatenate([a, b]) for a in kinds for b in kinds]
    return jnp.stack(rows)


def head_gain_sums(sums):
    heads = sums.reshape(-1, GROUP + 2, HEAD_DIM)
    return jnp.stack([heads[:, :GROUP].sum((0, 1)), heads[:, GROUP].sum(0)])


def local(
    inputs,
    out_cotangent,
    segments,
    norm_gains,
    conv_kernel,
    qk_gains,
    conv_in,
    attn_qkv,
    mixer_out,
    gate_up,
    down,
):
    section = lax.axis_index("xh")
    first = section == 0
    core = lax.axis_index("c")
    place = lax.axis_index("y") * 4 + lax.axis_index("z")
    xl = lax.axis_index("xl")
    plane = lax.axis_size("y") * lax.axis_size("z")

    shape = inputs.shape[1:]
    width = shape[-1]
    inputs, out_cotangent = inputs.reshape(-1, width), out_cotangent.reshape(-1, width)
    segments = segments[0]
    half = inputs.shape[0]
    rows = 2 * half
    channels = conv_in.shape[2]
    kernel = lax.dynamic_slice_in_dim(conv_kernel, core * channels, channels, 1).astype(F32)
    gains = lax.dynamic_index_in_dim(norm_gains, section, 0, keepdims=False).astype(F32)
    weight_out, weight_pair, weight_down = mixer_out[0], gate_up[0], down[0]
    hidden_units = weight_down.shape[0]
    part = hidden_units // plane
    in_width = 3 * channels
    qkv_width = attn_qkv.shape[1]
    y = lax.axis_index("y")
    core_scalar = jnp.stack([core, section]).astype(jnp.int32)
    xl_scalar = jnp.stack([xl, section, y]).astype(jnp.int32)

    def chosen(from_first, from_second):
        return jnp.where(first, from_first, from_second)

    def gathered(own, axes):
        return lax.all_gather(own, axes, tiled=True)


    both = jnp.concatenate([conv_in.reshape(-1, in_width), attn_qkv], axis=1)
    whole = gathered(both, ("xh", "xl", "y", "z"))

    lanes = -(-part // 256) * 256
    fill = lanes - part
    part_pair = jnp.concatenate(
        [
            jnp.pad(lax.dynamic_slice_in_dim(w, place * part, part, 1), ((0, 0), (0, fill)))
            for w in (weight_pair[0], weight_pair[1])
        ],
        axis=1,
    )
    part_down = lax.dynamic_slice_in_dim(weight_down, place * part, part, 0)
    part_down = jnp.pad(part_down, ((0, fill), (0, 0)))
    masks = conv_masks(segments, kernel.shape[0])
    mask = score_mask(segments)
    tables = turn_tables(segments.shape[1])
    head_gains = gain_rows(qk_gains.astype(F32))
    first_in = inputs.astype(F32)
    normed_own_0 = (normalize(first_in) * gains[0]).astype(BF16)
    normed_0 = spread(normed_own_0)
    cotangent_1 = spread(out_cotangent)
    whole, part_pair, part_down, masks, mask, tables, head_gains, normed_0, cotangent_1 = (
        lax.optimization_barrier(
            (whole, part_pair, part_down, masks, mask, tables, head_gains, normed_0, cotangent_1)
        )
    )

    def inner_norm(hidden):
        return (normalize(hidden) * gains[1]).astype(BF16)

    def inner_back(mine, other, hidden, grad):
        return back_join_call(core_scalar, mine, swapped(other, "c"), hidden, grad, gains[1])

    def mixer_back(grad_hidden, mine, other, layer_in, behind):
        come = swapped(other, "c")
        return back_join_call(behind, mine, come, layer_in, grad_hidden, gains[0])[1:]

    plane_axes = ("y", "z", "c")
    early = gathered(chosen(normed_own_0, out_cotangent), plane_axes)

    projected, gated_0, mine, other = conv_forward_call(
        core_scalar, normed_0, kernel, masks, whole, weight_out
    )
    hidden_0 = first_in + joined(mine, other)
    inner_0 = inner_norm(hidden_0)
    gate, up, mine, other = feed_forward_call(
        False, core_scalar, spread(inner_0), weight_pair, weight_down
    )
    result_0 = (hidden_0 + joined(mine, other)).astype(BF16)

    second_in = lax.ppermute(result_0, "xh", [(0, 1)]).astype(F32)
    normed_own_1 = (normalize(second_in) * gains[0]).astype(BF16)
    qkv, ready, gated_1, mine, other = attention_forward_call(
        core_scalar, spread(normed_own_1), head_gains, tables, mask, whole, weight_out, qkv_width
    )
    hidden_1 = second_in + joined(mine, other)
    inner_1 = inner_norm(hidden_1)
    mine, other, grad_mine, grad_other = ffn_both_call(
        core_scalar, spread(inner_1), cotangent_1, weight_pair, weight_down, (early,)
    )
    result_1 = (hidden_1 + joined(mine, other)).astype(BF16)

    inner_all = gathered(chosen(inner_0, inner_1), plane_axes)
    gated_z = gathered(chosen(gated_0, gated_1), "z")

    grad_hidden_1, grad_mix_1, gain_inner_1 = inner_back(
        grad_mine, grad_other, hidden_1, out_cotangent.astype(F32)
    )
    tiles_1, head_sums, mine, other = attention_backward_call(
        core_scalar,
        spread(grad_mix_1),
        head_gains,
        tables,
        mask,
        qkv,
        ready,
        whole,
        weight_out,
    )
    input_grad_1, gain_outer_1 = mixer_back(grad_hidden_1, mine, other, second_in, core_scalar)

    cotangent = lax.ppermute(input_grad_1, "xh", [(1, 0)])
    late = gathered(chosen(cotangent, normed_own_1), plane_axes)
    mine, other = feed_forward_call(
        True,
        core_scalar,
        spread(cotangent),
        weight_pair,
        weight_down,
        (gate, up),
        (inner_all,),
    )
    grad_hidden_0, grad_mix_0, gain_inner_0 = inner_back(
        mine, other, hidden_0, cotangent.astype(F32)
    )
    tiles, grad_kernel, mine, other = conv_backward_call(
        core_scalar,
        spread(grad_mix_0),
        kernel,
        masks,
        projected,
        tiles_1,
        whole,
        weight_out,
    )
    columns = exchanged(tiles, "z").reshape(4 * rows, -1)
    part_kept = part_forward_call((tiles,), inner_all, part_pair)

    def summed_over_pair(mine, other):
        return mine.astype(F32) + swapped(other, "xl").astype(F32)

    pair_grads, down_mine, down_other = lax.cond(
        first,
        lambda: part_down_call(xl_scalar, late, part_kept, part_down, (columns,)),
        lambda: part_down_call(xl_scalar, early, part_kept, part_down, (columns,)),
    )
    input_grad_0, gain_outer_0 = mixer_back(grad_hidden_0, mine, other, first_in, pair_grads)
    in_parts = mixer_in_call(xl_scalar, pair_grads, columns, early, late, plane)
    pair_mine, pair_other = part_pair_call(xl_scalar, inner_all, pair_grads, (in_parts,))
    out_mine, out_other = mixer_out_call(xl_scalar, pair_other, columns, gated_z, width // 4)

    full_kernel = lax.dynamic_update_slice(
        jnp.zeros(conv_kernel.shape, F32), grad_kernel, (0, core * channels)
    )
    small = jnp.concatenate(
        [
            chosen(gain_outer_0, gain_outer_1),
            chosen(gain_inner_0, gain_inner_1),
            full_kernel.reshape(-1),
            head_gain_sums(head_sums).reshape(-1),
        ]
    )
    count = small.shape[0]
    small = jnp.pad(small, (0, -count % 1024)).reshape(-1, 128)
    small = lax.all_gather(small, "c").sum(0)
    small_all = lax.all_gather(small, ("xh", "xl", "y", "z"))

    come = exchanged(in_parts, PLANE)
    line_mine, line_other = line_sums_call(xl_scalar, come)
    line_come = swapped(line_other, "xl")

    pairs = [(a, swapped(b, "xl")) for a, b in ((pair_mine, pair_other), (down_mine, down_other))]
    total = pair_join_call((in_parts,), pairs)
    arrived = exchanged(total.reshape(plane, -1, 3 * lanes), PLANE)

    kept_lines, sent_lines = finish_call(xl_scalar, total, line_mine, line_come)
    across = swapped(sent_lines, "xh")
    come = across.astype(F32)[:, :, : in_width // 4]
    kept_lines = kept_lines[:, :, : in_width // 4]
    lines = chosen(kept_lines, come).reshape(4, -1, 3, channels // 4)
    grad_conv_in = jnp.moveaxis(lines, 0, 2).reshape(conv_in.shape)
    lines = chosen(come, kept_lines)[:, :, : qkv_width // 4]
    grad_attn_qkv = jnp.moveaxis(lines, 0, 1).reshape(attn_qkv.shape)

    grad_gate_up, grad_down = lines_call(across, arrived, hidden_units)
    grad_gate_up, grad_down = grad_gate_up[None], grad_down.T[None]

    total = summed_over_pair(out_mine, out_other).reshape(4, -1, channels)
    sent = total.astype(BF16)
    lines = lax.dynamic_index_in_dim(total, y, 0, keepdims=False)
    for by in range(1, 4):
        block = lax.dynamic_index_in_dim(sent, (y + by) % 4, 0, keepdims=False)
        lines += lax.ppermute(block, "y", around(by)).astype(F32)
    grad_mixer_out = lines.T[None]

    pair = section_sums_call(grad_gate_up, small_all).reshape(2, -1)
    grad_norm_gains = jnp.stack([a[: 2 * width].reshape(2, width) for a in pair])
    grad_conv_kernel = pair[0][2 * width : 5 * width].reshape(conv_kernel.shape)
    grad_qk_gains = pair[1][5 * width : count].reshape(qk_gains.shape)

    activations = chosen(result_0, result_1).reshape(1, 1, *shape)
    input_grads = chosen(input_grad_0, input_grad_1).reshape(1, 1, *shape)
    return (
        activations,
        input_grads,
        grad_norm_gains,
        grad_conv_kernel,
        grad_qk_gains,
        grad_conv_in,
        grad_attn_qkv,
        grad_mixer_out,
        grad_gate_up,
        grad_down,
    )


def solution(mesh):
    wide = Mesh(mesh.devices.reshape(2, 2, 4, 4, 2), AXES)
    dp = ("xl", "y", "z")
    everyone = ("xh", "xl", "y", "z")
    in_specs = (
        P(dp, None, "c", None),
        P(dp, None, "c", None),
        P(dp, None, None),
        P(),
        P(),
        P(),
        P(everyone, None, "c"),
        P(everyone, "c"),
        P("xh", "c", None),
        P("xh", None, None, "c"),
        P("xh", "c", None),
    )
    out_specs = (
        P("xh", dp, None, "c", None),
        P("xh", dp, None, "c", None),
        P(),
        P(),
        P(),
        P(everyone, None, "c"),
        P(everyone, "c"),
        P("xh", "c", dp),
        P("xh", None, dp, "c"),
        P("xh", "c", dp),
    )
    return jax.shard_map(local, mesh=wide, in_specs=in_specs, out_specs=out_specs, check_vma=False)
```
